32 devices in a mesh: pipe: 2 (over x), dp: 4 (over y, core), tensor: 4 (over z).
Axes of the slice: x: 2, y: 2, z: 4, core: 2. Of those that a mesh axis runs over, the one named last changes fastest.
Arguments:
- section_rows: bfloat16 [2, 8, 2, 256, 768], P('pipe', 'dp', None, 'tensor'), may hold values from -6 to 6
- enc_lengths: int32 [8, 6], P('dp'), may hold values from 1 to 256, 512 in all within a row
- dec_lengths: int32 [8, 6], P('dp'), may hold values from 1 to 114, 256 in all within a row
- enc_buckets: int32 [1023], replicated, may hold values from 0 to 31
- dec_buckets: int32 [256], replicated, may hold values from 0 to 31
- norm_gains: float32 [2, 3, 768], P('pipe'), may hold values from 0.5 to 1.5
- rel_bias: float32 [2, 32, 12], P('pipe', None, 'tensor'), may hold values from -3 to 3
- query_key_w: bfloat16 [2, 2, 768, 768], P('pipe', None, 'dp', 'tensor'), may hold values from -0.078125 to 0.078125
- value_w: bfloat16 [2, 768, 768], P('pipe', 'dp', 'tensor'), may hold values from -0.21875 to 0.21875
- attn_out_w: bfloat16 [2, 768, 768], P('pipe', 'tensor', 'dp'), may hold values from -1 to 1
- cross_first: bfloat16 [2, 768, 768], P('pipe', 'dp', 'tensor'), may hold values from -0.078125 to 0.078125
- cross_second: bfloat16 [2, 768, 768], P('pipe', 'dp', 'tensor'), may hold values from -0.5 to 0.5
- ff_in: bfloat16 [2, 768, 3072], P('pipe', 'dp', 'tensor'), may hold values from -0.21875 to 0.21875
- ff_out: bfloat16 [2, 3072, 768], P('pipe', 'tensor', 'dp'), may hold values from -0.109375 to 0.109375
Outputs:
- section_out: float32 [2, 8, 2, 256, 768], P('pipe', 'dp', None, 'tensor')
- gain_grads: float32 [2, 3, 768], P('pipe', None, 'dp')
- bias_grads: float32 [2, 32, 12], P('pipe', 'dp', 'tensor')
- pair_grads: float32 [2, 2, 768, 768], P('pipe', None, 'dp', 'tensor')
- value_grads: float32 [2, 768, 768], P('pipe', 'dp', 'tensor')
- out_grads: float32 [2, 768, 768], P('pipe', 'tensor', 'dp')
- first_grads: float32 [2, 768, 768], P('pipe', 'dp', 'tensor')
- second_grads: float32 [2, 768, 768], P('pipe', 'dp', 'tensor')
- inner_grads: float32 [2, 768, 3072], P('pipe', 'dp', 'tensor')
- outer_grads: float32 [2, 3072, 768], P('pipe', 'tensor', 'dp')
The draws below stay inside these ranges and needn't reach their ends.
Inputs may be any that keep to these rules, and one draw needn't show every extreme that they name: `enc_lengths`: each row's 6 lengths sum to 512; one of them is exactly 256. `dec_lengths`: each row's 6 lengths sum to 256; one of them is exactly 114.
All inputs are finite; a program needn't handle non-finite values.
Results may differ from the reference program's by a relative error of at most 0.025.
Values may be sent and summed in bfloat16 or wider, within the bound.
A program may use at most 192 MiB of HBM per device.

```python
import math
import jax
import jax.numpy as jnp
import numpy as np
from jax import lax

D = 768
HEADS = 12
HEAD_DIM = 64
FF = 3072
BUCKETS = 32
HALF = 256
DEC_MAX = 114
SEGS = 6
HD = 768
ROWS = 8


def plant(drawn, rng, least, top_value):
    dims = drawn.shape
    place = [jax.random.randint(jax.random.fold_in(rng, axis), (), 0, dims[axis]) for axis in range(len(dims))]
    drawn = drawn.at[tuple(place)].set(least)
    longest = dims.index(max(dims))
    place[longest] = (place[longest] + 1) % dims[longest]
    return drawn.at[tuple(place)].set(top_value)


def levels(key, dims, pieces, smallest, top_value):
    def one(position, blocks):
        heights = jax.random.uniform(jax.random.fold_in(jax.random.fold_in(key, 6), position), (blocks,), jnp.float32, smallest / len(pieces), top_value / len(pieces))
        return jnp.repeat(jnp.exp(heights), dims[position] // blocks).reshape((-1,) + (1,) * (len(dims) - position - 1))

    loudness = one(*pieces[0])
    for cut in pieces[1:]:
        loudness = loudness * one(*cut)
    return loudness


def length_profile(number_of, total, most, skew):
    loads = [(1 << 20) // math.isqrt(grade ** skew) + 1 for grade in range(2, number_of + 1)]
    rest, counts = total - most - (number_of - 1), [1] * (number_of - 1)
    while rest > 0:
        candidates = [i for i in range(number_of - 1) if counts[i] < most]
        whole, left = sum([loads[i] for i in candidates]), rest
        for i in candidates:
            addition = min(most - counts[i], max(1, left * loads[i] // whole), rest)
            counts[i] = counts[i] + addition
            rest = rest - addition
    return np.array([most] + counts)


def uneven(stream_key, count, total, reach, slope):
    if count == 2:
        one = jax.random.randint(stream_key, (), max(1, total - reach), min(reach, total - 1) + 1)
        return jnp.stack([one, total - one])
    tallies = jnp.asarray(length_profile(count, total, reach, slope), jnp.int32)
    couples = (count - 1) // 2
    donor, receiver = tallies[1:1 + 2 * couples:2], tallies[2:2 + 2 * couples:2]
    room = jnp.minimum(donor - 1, reach - receiver)
    moved = jax.random.randint(jax.random.fold_in(stream_key, 1), (couples,), 0, 1 << 20) % (room + 1)
    tallies = tallies.at[1:1 + 2 * couples:2].set(donor - moved).at[2:2 + 2 * couples:2].set(receiver + moved)
    return tallies[jax.random.permutation(jax.random.fold_in(stream_key, 2), count)]


def gaussian(key, extent, scale, bound, pieces=(), held_as=jnp.bfloat16):
    result = jax.random.normal(key, extent, jnp.float32) * scale
    if len(pieces) > 0:
        result = levels(key, extent, pieces, -0.22, 0.18) * result
    return jnp.clip(result, min=-bound, max=bound).astype(held_as)


def setup_inputs(seed: int = 0) -> dict:
    key_list = jax.random.split(jax.random.key(seed), 15)
    section_rows = gaussian(key_list[0], (2, ROWS, 2, HALF, D), 1.0, 6.0, ((0, 2), (1, 4), (3, 4)))
    enc_lengths = jax.vmap(lambda own: uneven(own, SEGS, 2 * HALF, HALF, 1))(jax.random.split(key_list[1], ROWS)).reshape((ROWS, SEGS)).astype(jnp.int32)
    dec_lengths = jax.vmap(lambda own: uneven(own, SEGS, HALF, DEC_MAX, 1))(jax.random.split(key_list[2], ROWS)).reshape((ROWS, SEGS)).astype(jnp.int32)
    enc_buckets = plant(jax.random.randint(key_list[3], (4 * HALF - 1,), 0, BUCKETS), jax.random.fold_in(key_list[3], 1), 0, BUCKETS - 1).astype(jnp.int32)
    dec_buckets = plant(jax.random.randint(key_list[4], (HALF,), 0, BUCKETS), jax.random.fold_in(key_list[4], 1), 0, BUCKETS - 1).astype(jnp.int32)
    norm_gains = jnp.clip(1.0 + 0.1 * jax.random.normal(key_list[5], (2, 3, D), jnp.float32), 0.5, 1.5)
    rel_bias = gaussian(key_list[6], (2, BUCKETS, HEADS), 0.5, 3.0, ((0, 2), (2, 4)), jnp.float32)
    query_key_w = gaussian(key_list[7], (2, 2, D, HD), (D * 8) ** -0.5, 0.078125, ((0, 2), (2, 4), (3, 4)))
    value_w = gaussian(key_list[8], (2, D, HD), D ** -0.5, 0.21875, ((0, 2), (1, 4), (2, 4)))
    attn_out_w = gaussian(key_list[9], (2, HD, D), 32 ** -0.5, 1.0, ((0, 2), (1, 4), (2, 4)))
    cross_first = gaussian(key_list[10], (2, D, HD), (D * 8) ** -0.5, 0.078125, ((0, 2), (1, 4), (2, 4)))
    cross_second = gaussian(key_list[11], (2, D, HD), 160 ** -0.5, 0.5, ((0, 2), (1, 4), (2, 4)))
    ff_in = gaussian(key_list[12], (2, D, FF), D ** -0.5, 0.21875, ((0, 2), (1, 4), (2, 4)))
    ff_out = gaussian(key_list[13], (2, FF, D), FF ** -0.5, 0.109375, ((0, 2), (1, 4), (2, 4)))
    return dict(section_rows=section_rows, enc_lengths=enc_lengths, dec_lengths=dec_lengths, enc_buckets=enc_buckets, dec_buckets=dec_buckets, norm_gains=norm_gains, rel_bias=rel_bias, query_key_w=query_key_w, value_w=value_w, attn_out_w=attn_out_w, cross_first=cross_first, cross_second=cross_second, ff_in=ff_in, ff_out=ff_out)


EPSILON = 1e-06
NEGATIVE = -1000000000.0
HIGHEST = lax.Precision.HIGHEST

@jax.custom_vjp
def low(v):
    return lax.optimization_barrier(v.astype(jnp.bfloat16)).astype(jnp.float32)

@jax.custom_vjp
def low_back(v):
    return v

def low_keep(v):
    return (low(v), None)

def low_pass(kept, grad):
    return (grad,)

def back_keep(v):
    return (v, None)

def back_low(kept, grad):
    return (low(grad),)
low.defvjp(low_keep, low_pass)
low_back.defvjp(back_keep, back_low)

def rms_norm(inputs, gain_row):
    return inputs * lax.rsqrt(lax.optimization_barrier(jnp.mean(inputs * inputs, axis=-1, keepdims=True)) + EPSILON) * gain_row

def segment_ids(lengths, length):
    boundaries = jnp.cumsum(lengths).astype(jnp.int32)
    places = jnp.arange(length, dtype=jnp.int32)
    return lax.optimization_barrier(jnp.sum((places[:, None] >= boundaries[None, :]).astype(jnp.int32), axis=1))

def relative_field(bias_table, buckets, length):
    places = jnp.arange(length, dtype=jnp.int32)
    offsets = (places[:, None] - places[None, :] + length - 1).astype(jnp.int32)
    return jnp.transpose(bias_table[buckets[offsets]], (2, 0, 1))

def project(hidden, weight):
    return jnp.dot(hidden, weight, precision=HIGHEST)

def split_heads(matrix):
    return matrix.reshape(matrix.shape[0], HEADS, HEAD_DIM)

def attend(queries, key_rows, values, position_bias, allowed):
    scores = jnp.einsum('qhd,khd->hqk', queries, key_rows, precision=HIGHEST) + position_bias
    scores = low_back(jnp.where(allowed[None], scores, NEGATIVE))
    log_total = jax.scipy.special.logsumexp(scores, axis=-1, keepdims=True)
    attn_probs = low(jnp.exp(scores - log_total))
    mixture = jnp.einsum('hqk,khd->qhd', attn_probs, values, precision=HIGHEST)
    return low_back(low(mixture)).reshape(mixture.shape[0], HEADS * HEAD_DIM)

def self_block(residual, gain_row, projections, position_bias, allowed):
    w_query, w_key, w_value, w_out = projections
    hidden = low(rms_norm(residual, gain_row))
    queries = split_heads(low_back(low(project(hidden, w_query))))
    key_rows = split_heads(low_back(low(project(hidden, w_key))))
    values = split_heads(low_back(low(project(hidden, w_value))))
    mixture = attend(queries, key_rows, values, position_bias, allowed)
    return residual + low_back(project(mixture, w_out))

def feed_block(residual, gain_row, w_inner, w_outer):
    hidden = low(rms_norm(residual, gain_row))
    inner_sum = low_back(project(hidden, w_inner))
    active = low(jax.nn.gelu(inner_sum, approximate=False))
    return residual + low_back(project(active, w_outer))

def row_pass(params, enc_row, dec_row, enc_length, dec_length, enc_buckets, dec_buckets):
    gain_rows, bias_table, pair_w, value_w, out_w, first_w, second_w, inner_w, outer_w = params
    length = 2 * HALF
    enc_seg = segment_ids(enc_length, length)
    dec_seg = segment_ids(dec_length, HALF)
    places = jnp.arange(HALF, dtype=jnp.int32)
    enc_allowed = enc_seg[:, None] == enc_seg[None, :]
    dec_allowed = (dec_seg[:, None] == dec_seg[None, :]) & (places[:, None] >= places[None, :])
    cross_allowed = dec_seg[:, None] == enc_seg[None, :]
    enc_bias = relative_field(bias_table[0], enc_buckets, length)
    dec_table = jnp.concatenate([jnp.zeros((HALF - 1,), jnp.int32), dec_buckets.astype(jnp.int32)])
    dec_bias = relative_field(bias_table[1], dec_table, HALF)
    enc_resid = self_block(enc_row, gain_rows[0, 0], (pair_w[0, 0], pair_w[0, 1], value_w[0], out_w[0]), enc_bias, enc_allowed)
    enc_resid = feed_block(enc_resid, gain_rows[0, 1], inner_w[0], outer_w[0])
    encoded = low(rms_norm(enc_resid, gain_rows[0, 2]))
    cross_keys = split_heads(low_back(low(project(encoded, first_w[0]))))
    cross_values = split_heads(low_back(low(project(encoded, second_w[0]))))
    dec_resid = self_block(dec_row, gain_rows[1, 0], (pair_w[1, 0], pair_w[1, 1], value_w[1], out_w[1]), dec_bias, dec_allowed)
    cross_hidden = low(rms_norm(dec_resid, gain_rows[1, 1]))
    cross_queries = split_heads(low_back(low(project(cross_hidden, first_w[1]))))
    cross_mixture = attend(cross_queries, cross_keys, cross_values, 0.0, cross_allowed)
    dec_resid = dec_resid + low_back(project(cross_mixture, second_w[1].T))
    return feed_block(dec_resid, gain_rows[1, 2], inner_w[1], outer_w[1])

def reference(section_rows, enc_lengths, dec_lengths, enc_buckets, dec_buckets, norm_gains, rel_bias, query_key_w, value_w, attn_out_w, cross_first, cross_second, ff_in, ff_out):
    params = tuple((weight.astype(jnp.float32) for weight in (norm_gains, rel_bias, query_key_w, value_w, attn_out_w, cross_first, cross_second, ff_in, ff_out)))
    section_data = section_rows.astype(jnp.float32)
    enc_rows = section_data[0].reshape(ROWS, 2 * HALF, D)
    dec_rows = section_data[1, :, 0]
    cotangent = section_data[1, :, 1]

    def forward(params, enc_rows, dec_rows):

        def one_row(row_items):
            return row_pass(params, row_items[0], row_items[1], row_items[2], row_items[3], enc_buckets, dec_buckets)
        return lax.map(jax.checkpoint(one_row), (enc_rows, dec_rows, enc_lengths, dec_lengths))
    decoded, pull_back = jax.vjp(forward, params, enc_rows, dec_rows)
    grads_params, grad_enc, grad_dec = pull_back(cotangent)
    section_out = jnp.stack([grad_enc.reshape(ROWS, 2, HALF, D), jnp.stack([decoded, grad_dec], axis=1)])
    return (section_out, grads_params[0], grads_params[1], grads_params[2], grads_params[3], grads_params[4], grads_params[5], grads_params[6], grads_params[7], grads_params[8])
```

```python
import functools

import jax
import jax.numpy as jnp
from jax import lax
from jax.experimental import pallas as pl
from jax.experimental.pallas import tpu as pltpu
from jax.sharding import PartitionSpec as P

MESH = pl.DeviceIdType.MESH
F32 = jnp.float32
BF16 = jnp.bfloat16
EPSILON = 1e-06
NEGATIVE = -1000000000.0
HEAD_DIM = 64
CORES = 2
LANES = 128
VMEM_LIMIT = 60 << 20
ANY = pl.BlockSpec(memory_space=pl.ANY)
VMEM = pl.BlockSpec(memory_space=pltpu.VMEM)


def nn(a, b):
    return lax.dot_general(a, b, (((1,), (0,)), ((), ())), preferred_element_type=F32)


def nt(a, b):
    return lax.dot_general(a, b, (((1,), (1,)), ((), ())), preferred_element_type=F32)


def tn(a, b):
    return lax.dot_general(a, b, (((0,), (0,)), ((), ())), preferred_element_type=F32)


class Place:
    def __init__(self, tensor, dp):
        self.tensor = tensor
        self.groups = dp // CORES
        self.chips = tensor * self.groups
        self.pipe = lax.axis_index("pipe")
        self.d = lax.axis_index("dp")
        self.t = lax.axis_index("tensor")
        self.core = lax.rem(self.d, CORES)
        self.group = self.d // CORES
        odd = lax.rem(self.group, 2)
        self.ring = self.group * tensor + self.t + odd * (tensor - 1 - 2 * self.t)

    def at(self, ring):
        group = ring // self.tensor
        along = lax.rem(ring, self.tensor)
        odd = lax.rem(group, 2)
        return group, along + odd * (self.tensor - 1 - 2 * along)

    def neighbour(self, step):
        group, t = self.at(lax.rem(self.ring + step + self.chips, self.chips))
        return {"dp": group * CORES + self.core, "tensor": t}

    def sibling(self):
        return {"dp": self.group * CORES + 1 - self.core}


def meet(devices):
    barrier = pltpu.get_barrier_semaphore()
    for device in devices:
        pl.semaphore_signal(barrier, inc=1, device_id=device, device_id_type=MESH)
    pl.semaphore_wait(barrier, len(devices))


def halves(rows, columns):
    if rows % 32 == 0:
        return [(pl.ds(k * (rows // 2), rows // 2), pl.ds(0, columns)) for k in range(2)]
    cut = columns // LANES // 2 * LANES
    return [(pl.ds(0, rows), pl.ds(0, cut)), (pl.ds(0, rows), pl.ds(cut, columns - cut))]


def gather_kernel(
    tensor, dp, rows_ref, pack_ref, length_ref, table_ref, x_ref, w_ref, lengths_ref, tables_ref,
    local_sem, block_send, block_recv, pass_send, pass_recv, small_send, small_recv,
    ring_send, ring_recv, core_send, core_recv,
):
    here = Place(tensor, dp)
    c, t, chips = here.core, here.t, here.chips
    nrow = rows_ref.shape[0]
    sibling = here.sibling()
    to_right, to_left = here.neighbour(1), here.neighbour(-1)
    others = [{"tensor": lax.rem(t + k, tensor)} for k in range(1, tensor)]
    meet([to_right, to_left, sibling] + others)

    lengths = pltpu.make_async_remote_copy(
        length_ref, lengths_ref.at[c], small_send.at[0], small_recv.at[0], device_id=sibling, device_id_type=MESH
    )
    lengths.start()
    own_lengths = pltpu.make_async_copy(length_ref, lengths_ref.at[c], local_sem.at[0])
    own_lengths.start()
    own_table = pltpu.make_async_copy(table_ref, tables_ref.at[t], local_sem.at[1])
    own_table.start()
    tables = []
    for k in range(1, tensor):
        tables.append(
            pltpu.make_async_remote_copy(
                table_ref, tables_ref.at[t], small_send.at[k], small_recv.at[k], device_id=others[k - 1], device_id_type=MESH
            )
        )
        tables[-1].start()

    def to_chip(i):
        return pltpu.make_async_remote_copy(
            rows_ref.at[i], x_ref.at[:, t], block_send.at[i], block_recv.at[t],
            device_id={"tensor": nrow * c + i}, device_id_type=MESH,
        )

    def kept(i):
        return pltpu.make_async_copy(rows_ref.at[i], x_ref.at[:, t], local_sem.at[2])

    def kept_pass(i):
        return pltpu.make_async_remote_copy(
            rows_ref.at[i], x_ref.at[:, t], pass_send.at[t], pass_recv.at[t], device_id=sibling, device_id_type=MESH
        )

    def passed(s):
        return pltpu.make_async_remote_copy(
            x_ref.at[:, s], x_ref.at[:, s], pass_send.at[s], pass_recv.at[s], device_id=sibling, device_id_type=MESH
        )

    for i in range(nrow):
        mine = nrow * c + i == t

        @pl.when(mine)
        def _():
            kept(i).start()
            kept_pass(i).start()

        @pl.when(jnp.logical_not(mine))
        def _():
            to_chip(i).start()

    parts = halves(*pack_ref.shape)
    own_pack = pltpu.make_async_copy(pack_ref, w_ref.at[t, here.d], local_sem.at[3])
    own_pack.start()

    def shard(ring, part):
        group, at = here.at(ring)
        return w_ref.at[at, group * CORES + c, parts[part][0], parts[part][1]]

    def source(step, part):
        return lax.rem(here.ring + (1 if part else -1) * step + chips, chips)

    def onward(step, part, first=False):
        slot = shard(source(step, part), part)
        return pltpu.make_async_remote_copy(
            pack_ref.at[parts[part][0], parts[part][1]] if first else slot, slot,
            ring_send.at[part, step], ring_recv.at[part, step],
            device_id=to_left if part else to_right, device_id_type=MESH,
        )

    def across(step, part, first=False):
        slot = shard(source(step, part), part)
        return pltpu.make_async_remote_copy(
            pack_ref.at[parts[part][0], parts[part][1]] if first else slot, slot,
            core_send.at[part, step], core_recv.at[part, step], device_id=sibling, device_id_type=MESH,
        )

    for part in range(2):
        onward(0, part, True).start()
        across(0, part, True).start()

    takes = t // nrow == c
    for s in range(tensor):

        @pl.when(jnp.logical_and(takes, s != t))
        def _():
            pltpu.make_async_remote_copy(
                rows_ref.at[0], x_ref.at[:, s], block_send.at[0], block_recv.at[s], device_id=sibling, device_id_type=MESH
            ).wait_recv()
            passed(s).start()

    @pl.loop(1, chips)
    def _(step):
        for part in range(2):
            onward(step - 1, part).wait_recv()

            @pl.when(step < chips - 1)
            def _():
                onward(step, part).start()

            across(step, part).start()

    @pl.loop(0, chips)
    def _(step):
        for part in range(2):

            @pl.when(step < chips - 1)
            def _():
                onward(step, part).wait_send()

            across(step, part).wait_send()
            across(step, part).wait_recv()

    for i in range(nrow):
        mine = nrow * c + i == t

        @pl.when(mine)
        def _():
            kept(i).wait()
            kept_pass(i).wait_send()

        @pl.when(jnp.logical_not(mine))
        def _():
            to_chip(i).wait_send()

    for s in range(tensor):

        @pl.when(jnp.logical_and(takes, s != t))
        def _():
            passed(s).wait_send()

        @pl.when(jnp.logical_not(takes))
        def _():
            passed(s).wait_recv()

    lengths.wait()
    own_lengths.wait()
    own_table.wait()
    own_pack.wait()
    for table in tables:
        table.wait()


def gather(tensor, dp, rows, pack, lengths, table):
    chips = tensor * dp // CORES
    nrow, two, places, width = rows.shape
    sems = pltpu.SemaphoreType.DMA
    return pl.pallas_call(
        functools.partial(gather_kernel, tensor, dp),
        out_shape=(
            jax.ShapeDtypeStruct((two, tensor, places, width), rows.dtype),
            jax.ShapeDtypeStruct((tensor, dp) + pack.shape, pack.dtype),
            jax.ShapeDtypeStruct((CORES,) + lengths.shape, lengths.dtype),
            jax.ShapeDtypeStruct((tensor,) + table.shape, table.dtype),
        ),
        in_specs=[ANY] * 4,
        out_specs=(ANY,) * 4,
        scratch_shapes=[
            sems((4,)), sems((nrow,)), sems((tensor,)), sems((tensor,)), sems((tensor,)), sems((tensor,)), sems((tensor,)),
            sems((2, chips)), sems((2, chips)), sems((2, chips)), sems((2, chips)),
        ],
        compiler_params=pltpu.CompilerParams(collective_id=0, has_side_effects=True),
        name="gather",
    )(rows, pack, lengths, table)


def scatter_kernel(
    tensor, dp, grads_ref, small_ref, rows_ref, out_ref, small_out, rows_out,
    own, theirs, taken, small_own, small_theirs, small_taken, total,
    own_sem, core_send, core_recv, ring_send, ring_recv,
    sown_sem, score_send, score_recv, sring_send, sring_recv, block_send, block_recv, local_sem,
):
    here = Place(tensor, dp)
    c, t, chips = here.core, here.t, here.chips
    nrow = rows_out.shape[0]
    sibling = here.sibling()
    to_right, to_left = here.neighbour(1), here.neighbour(-1)
    line = [
        {"dp": here.group * CORES + lax.rem(c + j, CORES), "tensor": lax.rem(t + k, tensor)}
        for j in range(CORES)
        for k in range(tensor)
        if j + k > 0
    ]
    meet([to_right, to_left] + line)

    half = tensor // 2
    owner = t // nrow

    def block(k):
        place = here.pipe * (c * half + k % half) + (1 - here.pipe) * k
        which = here.pipe * (k // half) + (1 - here.pipe) * c
        return place, which

    def home(k):
        place, which = block(k)
        slot = rows_out.at[lax.rem(t, nrow), which]
        recv = block_recv.at[lax.rem(t, nrow), which]
        return (
            jnp.logical_and(place == t, owner == c),
            lambda: pltpu.make_async_copy(rows_ref.at[k], slot, recv),
            lambda: pltpu.make_async_remote_copy(
                rows_ref.at[k], slot, block_send.at[k], recv,
                device_id={"dp": here.group * CORES + owner, "tensor": place}, device_id_type=MESH,
            ),
        )

    for k in range(tensor):
        stays, inside, away = home(k)

        @pl.when(stays)
        def _():
            inside().start()

        @pl.when(jnp.logical_not(stays))
        def _():
            away().start()

    def across(ring):
        group, at = here.at(ring)
        return (
            pltpu.make_async_remote_copy(
                grads_ref.at[at, group * CORES + 1 - c], theirs.at[ring], core_send.at[ring], core_recv.at[ring],
                device_id=sibling, device_id_type=MESH,
            ),
            pltpu.make_async_remote_copy(
                small_ref.at[at, group * CORES + 1 - c], small_theirs.at[ring], score_send.at[ring], score_recv.at[ring],
                device_id=sibling, device_id_type=MESH,
            ),
        )

    def fetch(ring):
        group, at = here.at(ring)
        return (
            pltpu.make_async_copy(grads_ref.at[at, group * CORES + c], own.at[ring], own_sem.at[ring]),
            pltpu.make_async_copy(small_ref.at[at, group * CORES + c], small_own.at[ring], sown_sem.at[ring]),
        )

    def behind(step):
        return lax.rem(here.ring - step + chips, chips)

    def order(k):
        off = (2 * lax.rem(k, 2) - 1) * (k // 2 + 1) * (1 - k // (chips - 1))
        return lax.rem(here.ring + chips + off, chips)

    @pl.loop(0, chips)
    def _(k):
        for copy in across(order(k)) + fetch(order(k)):
            copy.start()

    rows, columns = out_ref.shape
    parts = halves(rows, columns)

    def add(ring, part, step, last):
        height = parts[part][0].size
        piece = 16 if height % 16 == 0 else height

        @pl.loop(0, height // piece)
        def _(k):
            at = pl.ds(pl.multiple_of(parts[part][0].start + k * piece, 8), piece)
            where = (at, parts[part][1])
            value = own[(ring,) + where].astype(F32) + theirs[(ring,) + where].astype(F32)
            if step is not None:
                value = value + taken[(step,) + where].astype(F32)
            if last:
                total[where] = value
            else:
                own[(ring,) + where] = value.astype(BF16)

    def onward(ring, step, part):
        where = (parts[part][0], parts[part][1])
        return pltpu.make_async_remote_copy(
            own.at[(ring,) + where], taken.at[(step,) + where], ring_send.at[part, step], ring_recv.at[part, step],
            device_id=to_left if part else to_right, device_id_type=MESH,
        )

    def small_onward(ring, step):
        return pltpu.make_async_remote_copy(
            small_own.at[ring], small_taken.at[step], sring_send.at[step], sring_recv.at[step],
            device_id=to_right, device_id_type=MESH,
        )

    def ready(ring):
        for copy in across(ring):
            copy.wait_recv()
        for copy in fetch(ring):
            copy.wait()

    def ahead(step):
        return lax.rem(here.ring + step, chips)

    half_chips = chips // 2

    @pl.loop(0, chips - 1)
    def _(step):
        right, left = behind(step + 1), ahead(step + 1)

        @pl.when(step < half_chips)
        def _():
            ready(right)

        @pl.when(step < chips - 1 - half_chips)
        def _():
            ready(left)

        @pl.when(step == 0)
        def _():
            add(right, 0, None, False)
            add(left, 1, None, False)
            small_own[right] = small_own[right] + small_theirs[right]

        @pl.when(step > 0)
        def _():
            onward(right, step - 1, 0).wait_recv()
            add(right, 0, step - 1, False)
            onward(right, step, 0).start()
            onward(left, step - 1, 1).wait_recv()
            add(left, 1, step - 1, False)
            onward(left, step, 1).start()
            small_onward(right, step - 1).wait_recv()
            small_own[right] = small_own[right] + small_theirs[right] + small_taken[step - 1]
            small_onward(right, step).start()

        @pl.when(step == 0)
        def _():
            onward(right, 0, 0).start()
            onward(left, 0, 1).start()
            small_onward(right, 0).start()

    ready(here.ring)
    for part in range(2):
        onward(here.ring, chips - 2, part).wait_recv()
        add(here.ring, part, chips - 2, True)
    small_onward(here.ring, chips - 2).wait_recv()
    small_out[...] = small_own[here.ring] + small_theirs[here.ring] + small_taken[chips - 2]
    finish = pltpu.make_async_copy(total, out_ref, local_sem.at[0])
    finish.start()

    @pl.loop(0, chips)
    def _(step):
        @pl.when(step < chips - 1)
        def _():
            onward(behind(step + 1), step, 0).wait_send()
            onward(ahead(step + 1), step, 1).wait_send()
            small_onward(behind(step + 1), step).wait_send()

        for copy in across(step):
            copy.wait_send()

    for k in range(tensor):
        stays, inside, away = home(k)

        @pl.when(jnp.logical_not(stays))
        def _():
            away().wait_send()

    for i in range(nrow):
        for which in range(2):
            pltpu.make_async_copy(rows_ref.at[0], rows_out.at[i, which], block_recv.at[i, which]).wait()
    finish.wait()


def scatter(tensor, dp, grads, small, rows, nrow):
    chips = tensor * dp // CORES
    shard = grads.shape[2:]
    tiny = small.shape[2:]
    sems = pltpu.SemaphoreType.DMA
    return pl.pallas_call(
        functools.partial(scatter_kernel, tensor, dp),
        out_shape=(
            jax.ShapeDtypeStruct(shard, F32),
            jax.ShapeDtypeStruct(tiny, F32),
            jax.ShapeDtypeStruct((nrow, 2) + rows.shape[1:], rows.dtype),
        ),
        in_specs=[ANY] * 3,
        out_specs=(ANY, VMEM, ANY),
        scratch_shapes=[
            pltpu.VMEM((chips,) + shard, BF16),
            pltpu.VMEM((chips,) + shard, BF16),
            pltpu.VMEM((chips - 1,) + shard, BF16),
            pltpu.VMEM((chips,) + tiny, F32),
            pltpu.VMEM((chips,) + tiny, F32),
            pltpu.VMEM((chips - 1,) + tiny, F32),
            pltpu.VMEM(shard, F32),
            sems((chips,)), sems((chips,)), sems((chips,)), sems((2, chips)), sems((2, chips)),
            sems((chips,)), sems((chips,)), sems((chips,)), sems((chips,)), sems((chips,)),
            sems((tensor,)), sems((nrow, 2)), sems((1,)),
        ],
        compiler_params=pltpu.CompilerParams(collective_id=1, has_side_effects=True, vmem_limit_bytes=VMEM_LIMIT),
        name="scatter",
    )(grads, small, rows)


KEY, VALUE, QUERY, OUT, FIRST, SECOND = range(6)


def rms(value):
    return lax.rsqrt(jnp.mean(value * value, axis=-1, keepdims=True) + EPSILON)


def in_rows(count, piece, body):
    @pl.loop(0, count // piece)
    def _(k):
        body(pl.ds(pl.multiple_of(k * piece, piece), piece))


def columns_of(count, body, piece=256):
    @pl.loop(0, count // piece)
    def _(k):
        body(pl.ds(pl.multiple_of(k * piece, piece), piece))


def normalize(source, gain, target, count):
    def body(at):
        value = source[at, :].astype(F32)
        target[at, :] = (value * rms(value) * gain).astype(BF16)

    in_rows(count, 32, body)


def normalize_back(source, gain, incoming, total, gain_out, count, fresh):
    gain_out[...] = jnp.zeros_like(gain_out)

    def body(at):
        value, back = source[at, :].astype(F32), incoming[at, :]
        scale = rms(value)
        unit = value * scale
        gain_out[...] += jnp.sum((back * unit).reshape(-1, 8, back.shape[-1]), axis=0)
        back = back * gain
        back = scale * (back - unit * jnp.mean(back * unit, axis=-1, keepdims=True))
        total[at, :] = back if fresh else total[at, :] + back

    in_rows(count, 32, body)


def project(left, weight, target, count):
    def body(at):
        target[0:count, at] = nn(left[0:count, :], weight[:, at]).astype(target.dtype)

    columns_of(weight.shape[1], body)


def project_back(left, weight, total, count, fresh):
    def body(at):
        value = nt(left[0:count, :], weight[at, :])
        total[0:count, at] = value if fresh else total[0:count, at] + value

    columns_of(weight.shape[0], body)


def lane_half(shape, part):
    return lax.broadcasted_iota(jnp.int32, shape, 1) // HEAD_DIM == part


def attend(keys, values, queries, mixture, probs, rows, span, pairs, mask, bias):
    @pl.loop(0, pairs)
    def _(pair):
        lanes = pl.ds(pl.multiple_of(pair * LANES, LANES), LANES)
        key, query = keys[0:span, lanes], queries[0:rows, lanes]
        value_t = values[0:span, lanes].T
        mixed = []
        for part in range(2):
            one = jnp.where(lane_half(query.shape, part), query, jnp.zeros_like(query))
            scores = nt(key, one) + mask[0:span, 0:rows]
            if bias is not None:
                scores = scores + bias(2 * pair + part)
            scores = jnp.exp(scores - jnp.max(scores, axis=0, keepdims=True))
            scores = (scores * (1.0 / jnp.sum(scores, axis=0, keepdims=True))).astype(BF16)
            probs[2 * pair + part, 0:span, 0:rows] = scores
            mixed.append(nn(value_t[part * HEAD_DIM : (part + 1) * HEAD_DIM, :], scores))
        mixture[0:rows, lanes] = jnp.concatenate(mixed, axis=0).T.astype(BF16)


def attend_back(keys, values, queries, back, probs, d_keys, d_values, d_queries, rows, span, pairs, each):
    @pl.loop(0, pairs)
    def _(pair):
        lanes = pl.ds(pl.multiple_of(pair * LANES, LANES), LANES)
        key, value = keys[0:span, lanes], values[0:span, lanes]
        query, given = queries[0:rows, lanes], back[0:rows, lanes]
        key_t = key.T
        d_key, d_value, d_query = None, None, []
        for part in range(2):
            side = lane_half(query.shape, part)
            query_one = jnp.where(side, query, jnp.zeros_like(query))
            given_one = jnp.where(side, given, jnp.zeros_like(given))
            prob = probs[2 * pair + part, 0:span, 0:rows]
            wide = prob.astype(F32)
            d_prob = nt(value, given_one)
            d_score = (wide * (d_prob - jnp.sum(wide * d_prob, axis=0, keepdims=True))).astype(BF16)
            if each is not None:
                each(2 * pair + part, d_score)
            of_key, of_value = nn(d_score, query_one), nn(prob, given_one)
            d_key = of_key if d_key is None else d_key + of_key
            d_value = of_value if d_value is None else d_value + of_value
            d_query.append(nn(key_t[part * HEAD_DIM : (part + 1) * HEAD_DIM, :], d_score))
        d_keys[0:span, lanes] = d_key.astype(BF16)
        d_values[0:span, lanes] = d_value.astype(BF16)
        d_queries[0:rows, lanes] = jnp.concatenate(d_query, axis=0).T.astype(BF16)


def segments(lengths_row, shape, axis, first):
    lane = lax.broadcasted_iota(jnp.int32, lengths_row.shape, 1)
    places = lax.broadcasted_iota(jnp.int32, shape, axis) + first
    ids = jnp.zeros(shape, jnp.int32)
    for c in range(SEGS_HELD):
        bound = jnp.sum(jnp.where(lane <= c, lengths_row, 0), axis=1, keepdims=True)
        ids = ids + (places >= bound).astype(jnp.int32)
    return ids


SEGS_HELD = 6


def block_kernel(
    tensor, dp, heads_at, x_ref, w_hbm, gain_ref, length_ref, table_ref, bucket_ref,
    grads_hbm, rows_out, gains_out, bias_out,
    raw, square, inner, outer, hidden, keys, values, queries, probs, mask, cross_mask, mixture,
    resid_mid, resid_top, d_resid, summed, second, third, slope, active, d_active, d_branch, branch,
    cross_keys, cross_values, cross_queries, cross_mixture, cross_probs, cross_back, cross_in, cross_in_back,
    d_cross_keys, d_cross_values, d_cross_queries, cross_taken, send_pair, send_back, joined,
    d_keys, d_values, d_queries, taken_pair, d_pair, turned, stage, vectors, diagonals, onehot, gain_parts,
    load_sem, stage_sem, send_sem, recv_sem,
):
    here = Place(tensor, dp)
    c, t = here.core, here.t
    width = x_ref.shape[1]
    tall = x_ref.shape[0]
    block = width // tensor
    half_width = width // 2
    sibling = here.sibling()
    across = [{"pipe": 1 - here.pipe, "dp": here.group * CORES + k} for k in range(CORES)]
    meet([sibling] + across)

    def loads(tt):
        return [
            pltpu.make_async_copy(w_hbm.at[tt, :, pl.ds(0, 6 * block)], raw.at[tt], load_sem.at[0, tt]),
            pltpu.make_async_copy(w_hbm.at[tt, :, pl.ds(6 * block, inner.shape[2])], inner.at[tt], load_sem.at[1, tt]),
            pltpu.make_async_copy(
                w_hbm.at[tt, :, pl.ds(6 * block + inner.shape[2], outer.shape[2])], outer.at[tt], load_sem.at[2, tt]
            ),
        ]

    for tt in range(tensor):
        loads(tt)[0].start()
    for tt in range(tensor):
        loads(tt)[1].start()
        loads(tt)[2].start()

    def move(source, target, sends, recvs, device):
        return pltpu.make_async_remote_copy(
            source, target, send_sem.at[sends], recv_sem.at[recvs], device_id=device, device_id_type=MESH
        )

    places = onehot.shape[1]
    buckets = lax.broadcasted_iota(jnp.int32, onehot.shape, 0) == bucket_ref[0:1, :]
    onehot[...] = buckets.astype(F32)
    for tt in range(tensor):
        vectors[pl.ds(8 * tt, 8), :] = lax.dot_general(
            table_ref[tt], onehot[...], (((1,), (0,)), ((), ())), precision=lax.Precision.HIGHEST, preferred_element_type=F32
        )
    nrow = tensor // CORES
    enc_row = length_ref[t // nrow, pl.ds(lax.rem(t, nrow), 1), :]
    dec_row = length_ref[t // nrow, pl.ds(nrow + lax.rem(t, nrow), 1), :]

    def masked(allowed):
        return jnp.where(allowed, 0.0, NEGATIVE).astype(F32)

    def vector_row(head):
        return (head // heads_at) * 8 + lax.rem(head, heads_at)

    def untangle():
        for tt in range(tensor):
            loads(tt)[0].wait()
            for k in range(6):
                square[k, :, tt * block : (tt + 1) * block] = raw[tt, :, k * block : (k + 1) * block]

    def self_forward(span, rows, first_row):
        def bias(head):
            pieces = []
            for j in range(span // LANES):
                start = pl.multiple_of(first_row + span - LANES - j * LANES, LANES)
                row = vectors[pl.ds(vector_row(head), 1), pl.ds(start, rows + LANES)]
                wide = jnp.broadcast_to(row, (LANES, rows + LANES))
                pieces.append(pltpu.roll(wide, rows + 1, 1, stride=1, stride_axis=0)[:, 0:rows])
            return jnp.concatenate(pieces, axis=0)

        normalize(x_ref, gain_ref[0:1, :], hidden, span)
        project(hidden, square.at[KEY], keys, span)
        project(hidden, square.at[VALUE], values, span)
        own = hidden.at[pl.ds(first_row, rows)]
        project(own, square.at[QUERY], queries, rows)
        attend(keys, values, queries, mixture, probs, rows, span, width // LANES, mask, bias)
        project_back(mixture, square.at[OUT], resid_mid, rows, True)

        def add(at):
            there = pl.ds(pl.multiple_of(first_row + at.start, 32), 32)
            resid_mid[at, :] += x_ref[there, :].astype(F32)

        in_rows(rows, 32, add)

    def feed_forward(rows):
        @pl.loop(0, tensor)
        def _(tt):
            def body(at):
                value = nn(second[0:rows, :], inner[tt, :, at])
                cdf = 0.5 * (1.0 + lax.erf(value * 0.7071067811865476))
                active[tt, 0:rows, at] = (value * cdf).astype(BF16)
                slope[tt, 0:rows, at] = cdf + value * jnp.exp(-0.5 * value * value) * 0.3989422804014327

            columns_of(inner.shape[2], body)

    def feed_out(target, rows):
        @pl.loop(0, tensor)
        def _(tt):
            def body(at):
                target[0:rows, at] += nt(active[tt, 0:rows, :], outer[tt, at, :])

            columns_of(width, body)

    def feed_back(rows, ready):
        summed[0:rows, :] = jnp.zeros((rows, width), F32)

        @pl.loop(0, tensor)
        def _(tt):
            def body(at):
                value = ready[tt, rows : 2 * rows, at] if ready is not None else nn(d_branch[0:rows, :], outer[tt, :, at])
                d_active[tt, 0:rows, at] = (value * slope[tt, 0:rows, at]).astype(BF16)

            columns_of(inner.shape[2], body)

            def back(at):
                summed[0:rows, at] += nt(d_active[tt, 0:rows, :], inner[tt, at, :])

            columns_of(width, back)

    def turn(left, rows):
        def body(at):
            turned[at, 0:rows] = left[0:rows, at].T

        columns_of(width, body, LANES)

    def feed_grads(rows, right, column):
        def out(tt, slot):
            return pltpu.make_async_copy(
                stage.at[slot], grads_hbm.at[tt, :, pl.ds(column, stage.shape[2])], stage_sem.at[slot]
            )

        @pl.loop(0, tensor)
        def _(tt):
            slot = lax.rem(tt, 2)

            @pl.when(tt >= 2)
            def _():
                out(tt, slot).wait()

            def body(at):
                stage[slot, :, at] = nn(turned[:, 0:rows], right[tt, 0:rows, at]).astype(BF16)

            columns_of(stage.shape[2], body)
            out(tt, slot).start()

        out(0, 0).wait()
        out(1, 1).wait()

    def square_grad(rows, right, which):
        for k in range(tensor // 2):
            value = nn(turned[:, 0:rows], right[0:rows, 2 * k * block : 2 * (k + 1) * block]).astype(BF16)
            raw[2 * k, :, which * block : (which + 1) * block] = value[:, 0:block]
            raw[2 * k + 1, :, which * block : (which + 1) * block] = value[:, block:]

    def to_bf16(source, target, rows):
        def body(at):
            target[at, :] = source[at, :].astype(BF16)

        in_rows(rows, 32, body)

    def gain_done(which):
        gains_out[which : which + 1, :] = jnp.sum(gain_parts[...], axis=0, keepdims=True)

    def self_backward(span, rows, first_row, mirror):
        to_bf16(d_resid, branch, rows)
        project(branch, square.at[OUT], d_branch, rows)
        diagonals[...] = jnp.zeros_like(diagonals)

        def each(head, d_score):
            for j in range(span // LANES):
                start = pl.multiple_of(first_row + span - LANES - j * LANES, LANES)
                piece = nn(mirror, d_score[j * LANES : (j + 1) * LANES, :])
                piece = jnp.concatenate([piece, jnp.zeros((LANES, LANES), F32)], axis=1)
                piece = pltpu.roll(piece, 0, 1, stride=1, stride_axis=0)
                at = (pl.ds(vector_row(head), 1), pl.ds(start, rows + LANES))
                diagonals[at] += jnp.sum(piece, axis=0, keepdims=True)

        attend_back(
            keys, values, queries, d_branch, probs, d_keys, d_values, d_queries, rows, span, width // LANES, each
        )
        far = pl.ds(pl.multiple_of((1 - c) * rows, rows), rows)
        near = pl.ds(pl.multiple_of(c * rows, rows), rows)
        trades = [
            move(source.at[far], taken_pair.at[k, pl.ds(0, rows)], 12 + k, 12 + k, sibling)
            for k, source in enumerate((d_keys, d_values))
        ]
        for trade in trades:
            trade.start()
        turn(branch, rows)
        square_grad(rows, mixture, OUT)
        for tt in range(tensor):
            bias_out[pl.ds(8 * tt, 8), :] = lax.dot_general(
                diagonals[pl.ds(8 * tt, 8), :], onehot[...], (((1,), (1,)), ((), ())),
                precision=lax.Precision.HIGHEST, preferred_element_type=F32,
            )
        for trade in trades:
            trade.wait_recv()
        for k, source in enumerate((d_keys, d_values)):
            d_pair[k, 0:rows, :] = (source[near, :].astype(F32) + taken_pair[k, 0:rows, :].astype(F32)).astype(BF16)
        project_back(d_queries, square.at[QUERY], summed, rows, True)
        project_back(d_pair.at[0], square.at[KEY], summed, rows, False)
        project_back(d_pair.at[1], square.at[VALUE], summed, rows, False)
        own = pl.ds(pl.multiple_of(first_row, rows), rows)
        normalize_back(x_ref.at[own], gain_ref[0:1, :], summed, d_resid, gain_parts, rows, False)
        gain_done(0)
        turn(hidden.at[own], rows)
        square_grad(rows, d_queries, QUERY)
        square_grad(rows, d_pair.at[0], KEY)
        square_grad(rows, d_pair.at[1], VALUE)
        for trade in trades:
            trade.wait_send()
        outs = [
            pltpu.make_async_copy(raw.at[tt], grads_hbm.at[tt, :, pl.ds(0, 6 * block)], load_sem.at[0, tt])
            for tt in range(tensor)
        ]
        for out in outs:
            out.start()
        for out in outs:
            out.wait()

    def wait_loads():
        for tt in range(tensor):
            loads(tt)[1].wait()
            loads(tt)[2].wait()

    mirror = (
        lax.broadcasted_iota(jnp.int32, (LANES, LANES), 0) + lax.broadcasted_iota(jnp.int32, (LANES, LANES), 1) == LANES - 1
    ).astype(BF16)
    gains_out[...] = jnp.zeros_like(gains_out)
    near_lanes = pl.ds(pl.multiple_of(c * half_width, half_width), half_width)
    far_lanes = pl.ds(pl.multiple_of((1 - c) * half_width, half_width), half_width)
    rows_e, span_e, rows_d, span_d = tall // 2, tall, tall // 4, tall // 2
    pairs_here = half_width // LANES

    def parts_of(array):
        return [array.at[pl.ds(k * rows_d, rows_d)] for k in range(CORES)]

    @pl.when(here.pipe == 0)
    def _():
        rows, span = rows_e, span_e
        first_row = pl.multiple_of(c * rows, rows)
        seg_rows = segments(enc_row, (span, 1), 0, 0)
        mask[...] = masked(seg_rows == segments(enc_row, (1, rows), 1, first_row))
        cross_mask[...] = masked(seg_rows == segments(dec_row, (1, span_d), 1, 0))
        untangle()
        self_forward(span, rows, first_row)
        wait_loads()
        normalize(resid_mid, gain_ref[1:2, :], second, rows)
        feed_forward(rows)
        resid_top[...] = resid_mid[...]
        feed_out(resid_top, rows)
        normalize(resid_top, gain_ref[2:3, :], third, rows)
        mine = pl.ds(first_row, rows)
        other = pl.ds(pl.multiple_of((1 - c) * rows, rows), rows)
        project(third, square.at[FIRST], d_pair.at[0], rows)
        project(third, square.at[SECOND], d_pair.at[1], rows)
        trades = []
        for k, held in enumerate((cross_keys, cross_values)):
            held[mine, :] = d_pair[k, :, near_lanes]
            send_pair[k] = d_pair[k, :, far_lanes]
            trades.append(move(send_pair.at[k], held.at[mine], k, k, sibling))
            trades[-1].start()
        for k, part in enumerate(parts_of(cross_queries)):
            move(part, part, 2 + k, 2 + k, across[k]).wait_recv()
        for k, held in enumerate((cross_keys, cross_values)):
            move(send_pair.at[k], held.at[other], k, k, sibling).wait_recv()
        attend(
            cross_keys, cross_values, cross_queries, cross_mixture, cross_probs, span_d, span, pairs_here, cross_mask, None
        )
        mixtures = [
            move(part, cross_in.at[c], 4 + k, 4 + c, across[k]) for k, part in enumerate(parts_of(cross_mixture))
        ]
        for mix in mixtures:
            mix.start()
        for k, part in enumerate(parts_of(cross_back)):
            move(part, part, 6 + k, 6 + k, across[k]).wait_recv()
        attend_back(
            cross_keys, cross_values, cross_queries, cross_back, cross_probs,
            d_cross_keys, d_cross_values, d_cross_queries, span_d, span, pairs_here, None,
        )
        returns = [
            move(d_cross.at[other], cross_taken.at[k], 10 + k, 10 + k, sibling)
            for k, d_cross in enumerate((d_cross_keys, d_cross_values))
        ]
        for back in returns:
            back.start()
        answers = [
            move(part, cross_in_back.at[c], 8 + k, 8 + c, across[k]) for k, part in enumerate(parts_of(d_cross_queries))
        ]
        for answer in answers:
            answer.start()
        for k, d_cross in enumerate((d_cross_keys, d_cross_values)):
            d_pair[k, :, near_lanes] = d_cross[mine, :]
            returns[k].wait_recv()
            d_pair[k, :, far_lanes] = cross_taken[k]
        project_back(d_pair.at[0], square.at[FIRST], summed, rows, True)
        project_back(d_pair.at[1], square.at[SECOND], summed, rows, False)
        normalize_back(resid_top, gain_ref[2:3, :], summed, d_resid, gain_parts, rows, True)
        gain_done(2)
        turn(third, rows)
        square_grad(rows, d_pair.at[0], FIRST)
        square_grad(rows, d_pair.at[1], SECOND)
        to_bf16(d_resid, d_branch, rows)
        feed_back(rows, None)
        normalize_back(resid_mid, gain_ref[1:2, :], summed, d_resid, gain_parts, rows, False)
        gain_done(1)
        turn(second, rows)
        feed_grads(rows, d_active, 6 * block)
        turn(d_branch, rows)
        feed_grads(rows, active, 6 * block + inner.shape[2])
        for copy in trades + mixtures + returns + answers:
            copy.wait_send()
        self_backward(span, rows, first_row, mirror)
        to_bf16(d_resid, rows_out, rows)

    @pl.when(here.pipe == 1)
    def _():
        rows, span = rows_d, span_d
        first_row = pl.multiple_of(c * rows, rows)
        key_at = lax.broadcasted_iota(jnp.int32, (span, rows), 0)
        query_at = lax.broadcasted_iota(jnp.int32, (span, rows), 1) + first_row
        same = segments(dec_row, (span, 1), 0, 0) == segments(dec_row, (1, rows), 1, first_row)
        mask[0:span, 0:rows] = masked(same & (query_at >= key_at))
        untangle()
        self_forward(span, rows, first_row)
        normalize(resid_mid, gain_ref[1:2, :], third, rows)
        project(third, square.at[FIRST], joined, rows)
        asks = []
        for k in range(CORES):
            send_pair[k, 0:rows, :] = joined[:, k * half_width : (k + 1) * half_width]
            asks.append(move(send_pair.at[k, pl.ds(0, rows)], parted(cross_queries, c, rows), 2 + k, 2 + c, across[k]))
            asks[-1].start()
        wait_loads()
        cotangent = pl.ds(pl.multiple_of(span + first_row, rows), rows)
        d_branch[0:rows, :] = x_ref[cotangent, :]

        @pl.loop(0, tensor)
        def _(tt):
            def body(at):
                slope[tt, rows : 2 * rows, at] = nn(d_branch[0:rows, :], outer[tt, :, at])

            columns_of(inner.shape[2], body)

        for k in range(CORES):
            move(cross_in.at[k], cross_in.at[k], 4 + k, 4 + k, across[k]).wait_recv()
            joined[:, k * half_width : (k + 1) * half_width] = cross_in[k]
        resid_top[0:rows, :] = resid_mid[0:rows, :]
        project_back(joined, square.at[SECOND], resid_top, rows, False)
        normalize(resid_top, gain_ref[2:3, :], second, rows)
        feed_forward(rows)
        feed_back(rows, slope)
        d_resid[0:rows, :] = d_branch[0:rows, :].astype(F32)
        normalize_back(resid_top, gain_ref[2:3, :], summed, d_resid, gain_parts, rows, False)
        gain_done(2)
        to_bf16(d_resid, branch, rows)
        project(branch, square.at[SECOND], d_queries, rows)
        tells = []
        for k in range(CORES):
            send_back[k] = d_queries[0:rows, k * half_width : (k + 1) * half_width]
            tells.append(move(send_back.at[k], parted(cross_back, c, rows), 6 + k, 6 + c, across[k]))
            tells[-1].start()
        feed_out(resid_top, rows)
        to_bf16(resid_top, rows_out, rows)
        turn(second, rows)
        feed_grads(rows, d_active, 6 * block)
        turn(d_branch, rows)
        feed_grads(rows, active, 6 * block + inner.shape[2])
        turn(branch, rows)
        square_grad(rows, joined, SECOND)
        for k in range(CORES):
            move(cross_in_back.at[k], cross_in_back.at[k], 8 + k, 8 + k, across[k]).wait_recv()
            joined[:, k * half_width : (k + 1) * half_width] = cross_in_back[k]
        project_back(joined, square.at[FIRST], summed, rows, True)
        normalize_back(resid_mid, gain_ref[1:2, :], summed, d_resid, gain_parts, rows, False)
        gain_done(1)
        turn(third, rows)
        square_grad(rows, joined, FIRST)
        for copy in asks + tells:
            copy.wait_send()
        self_backward(span, rows, first_row, mirror)
        to_bf16(d_resid, rows_out.at[pl.ds(rows, rows)], rows)


def parted(array, c, rows):
    return array.at[pl.ds(pl.multiple_of(c * rows, rows), rows)]


def blocks(tensor, dp, heads_at, rows, weights, gains, lengths, tables, buckets):
    tall, width = rows.shape
    block = width // tensor
    hidden_block = (weights.shape[2] - 6 * block) // 2
    half_rows, half_width = tall // 2, width // 2
    heads = heads_at * tensor
    ranges = buckets.shape[1]
    sems = pltpu.SemaphoreType.DMA

    def held(*shape, dtype=BF16):
        return pltpu.VMEM(shape, dtype)

    scratch = dict(
        raw=held(tensor, width, 6 * block),
        square=held(6, width, width),
        inner=held(tensor, width, hidden_block),
        outer=held(tensor, width, hidden_block),
        hidden=held(tall, width),
        keys=held(tall, width),
        values=held(tall, width),
        queries=held(half_rows, width),
        probs=held(heads, tall, half_rows),
        mask=held(tall, half_rows, dtype=F32),
        cross_mask=held(tall, half_rows, dtype=F32),
        mixture=held(half_rows, width),
        resid_mid=held(half_rows, width, dtype=F32),
        resid_top=held(half_rows, width, dtype=F32),
        d_resid=held(half_rows, width, dtype=F32),
        summed=held(half_rows, width, dtype=F32),
        second=held(half_rows, width),
        third=held(half_rows, width),
        slope=held(tensor, half_rows, hidden_block, dtype=F32),
        active=held(tensor, half_rows, hidden_block),
        d_active=held(tensor, half_rows, hidden_block),
        d_branch=held(half_rows, width),
        branch=held(half_rows, width),
        cross_keys=held(tall, half_width),
        cross_values=held(tall, half_width),
        cross_queries=held(half_rows, half_width),
        cross_mixture=held(half_rows, half_width),
        cross_probs=held(heads // CORES, tall, half_rows),
        cross_back=held(half_rows, half_width),
        cross_in=held(CORES, half_rows // 2, half_width),
        cross_in_back=held(CORES, half_rows // 2, half_width),
        d_cross_keys=held(tall, half_width),
        d_cross_values=held(tall, half_width),
        d_cross_queries=held(half_rows, half_width),
        cross_taken=held(CORES, half_rows, half_width),
        send_pair=held(CORES, half_rows, half_width),
        send_back=held(CORES, half_rows // 2, half_width),
        joined=held(half_rows // 2, width),
        d_keys=held(tall, width),
        d_values=held(tall, width),
        d_queries=held(half_rows, width),
        taken_pair=held(2, half_rows, width),
        d_pair=held(2, half_rows, width),
        turned=held(width, half_rows),
        stage=held(2, width, hidden_block),
        vectors=held(8 * tensor, ranges, dtype=F32),
        diagonals=held(8 * tensor, ranges, dtype=F32),
        onehot=held(LANES, ranges, dtype=F32),
        gain_parts=held(8, width, dtype=F32),
        load_sem=sems((3, tensor)),
        stage_sem=sems((2,)),
        send_sem=sems((14,)),
        recv_sem=sems((14,)),
    )
    return pl.pallas_call(
        functools.partial(block_kernel, tensor, dp, heads_at),
        out_shape=(
            jax.ShapeDtypeStruct(weights.shape, BF16),
            jax.ShapeDtypeStruct((half_rows, width), BF16),
            jax.ShapeDtypeStruct((8, width), F32),
            jax.ShapeDtypeStruct((8 * tensor, LANES), F32),
        ),
        in_specs=[VMEM, ANY] + [VMEM] * 4,
        out_specs=(ANY, VMEM, VMEM, VMEM),
        scratch_shapes=list(scratch.values()),
        compiler_params=pltpu.CompilerParams(collective_id=2, has_side_effects=True, vmem_limit_bytes=VMEM_LIMIT),
        name="blocks",
    )(rows, weights, gains, lengths, tables, buckets)


def pad_to(array, *shape):
    return jnp.pad(array, [(0, full - have) for full, have in zip(shape, array.shape)])


def shards(
    tensor, dp, section_rows, enc_lengths, dec_lengths, enc_buckets, dec_buckets, norm_gains, rel_bias,
    query_key_w, value_w, attn_out_w, cross_first, cross_second, ff_in, ff_out,
):
    nrow = section_rows.shape[1]
    depth, block = value_w.shape[1:]
    buckets, heads_at = rel_bias.shape[1:]
    on_encoder = lax.axis_index("pipe") == 0
    pack = jnp.concatenate(
        [query_key_w[0, 1], value_w[0], query_key_w[0, 0], attn_out_w[0].T, cross_first[0], cross_second[0], ff_in[0], ff_out[0].T],
        axis=1,
    )
    lengths = pad_to(jnp.concatenate([enc_lengths, dec_lengths], axis=0), 8, LANES)
    table = pad_to(rel_bias[0].T, 8, LANES)
    rows, weights, lengths, tables = gather(tensor, dp, section_rows[0], pack, lengths, table)
    ranges = -(-enc_buckets.shape[0] // LANES) * LANES
    dec_all = jnp.concatenate([jnp.zeros((dec_buckets.shape[0] - 1,), jnp.int32), dec_buckets])
    bucket_row = jnp.where(on_encoder, pad_to(enc_buckets, ranges), pad_to(dec_all, ranges))
    width = section_rows.shape[-1]
    grads, finished, gains, bias = blocks(
        tensor, dp, heads_at, rows.reshape(-1, width), weights.reshape(tensor, width, -1),
        pad_to(norm_gains[0], 8, width), lengths, tables, jnp.broadcast_to(bucket_row[None], (8, ranges)),
    )
    held = buckets // dp
    wide = -(-max(depth, held) // LANES) * LANES
    gain_part = pad_to(gains[:3].reshape(3, dp, depth).transpose(1, 0, 2), dp, 3, wide)
    bias_part = bias.reshape(tensor, 8, LANES)[:, :heads_at, :buckets].reshape(tensor, heads_at, dp, held)
    bias_part = pad_to(bias_part.transpose(0, 2, 1, 3), tensor, dp, 5, wide)
    small = jnp.concatenate([jnp.broadcast_to(gain_part[None], (tensor,) + gain_part.shape), bias_part], axis=2)
    total, tiny, home = scatter(
        tensor, dp, grads.reshape(tensor, dp, depth, -1), small, finished.reshape(tensor, -1, width), nrow
    )
    names = ("key", "value", "query", "out", "first", "second")
    part = {name: total[:, k * block : (k + 1) * block] for k, name in enumerate(names)}
    hidden_block = ff_in.shape[2]
    return (
        home.astype(F32)[None],
        tiny[:3, :depth][None],
        tiny[3 : 3 + heads_at, :held].T[None],
        jnp.stack([part["query"], part["key"]])[None],
        part["value"][None],
        part["out"].T[None],
        part["first"][None],
        part["second"][None],
        total[:, 6 * block : 6 * block + hidden_block][None],
        total[:, 6 * block + hidden_block :].T[None],
    )


def solution(mesh):
    sizes = dict(mesh.shape)
    return jax.shard_map(
        functools.partial(shards, sizes["tensor"], sizes["dp"]),
        mesh=mesh,
        in_specs=(
            P("pipe", "dp", None, "tensor", None),
            P("dp", None),
            P("dp", None),
            P(),
            P(),
            P("pipe", None, None),
            P("pipe", None, "tensor"),
            P("pipe", None, "dp", "tensor"),
            P("pipe", "dp", "tensor"),
            P("pipe", "tensor", "dp"),
            P("pipe", "dp", "tensor"),
            P("pipe", "dp", "tensor"),
            P("pipe", "dp", "tensor"),
            P("pipe", "tensor", "dp"),
        ),
        out_specs=(
            P("pipe", "dp", None, "tensor", None),
            P("pipe", None, "dp"),
            P("pipe", "dp", "tensor"),
            P("pipe", None, "dp", "tensor"),
            P("pipe", "dp", "tensor"),
            P("pipe", "tensor", "dp"),
            P("pipe", "dp", "tensor"),
            P("pipe", "dp", "tensor"),
            P("pipe", "dp", "tensor"),
            P("pipe", "tensor", "dp"),
        ),
        check_vma=False,
    )
```

```python
import functools
import types

import jax
import jax.numpy as jnp
from jax import lax
from jax.experimental import pallas as pl
from jax.experimental.pallas import tpu as pltpu
from jax.sharding import PartitionSpec as P

MESH = pl.DeviceIdType.MESH
F32 = jnp.float32
BF16 = jnp.bfloat16
EPSILON = 1e-06
NEGATIVE = -1000000000.0
HEAD_DIM = 64
CORES = 2
LANES = 128
VMEM_LIMIT = 62 << 20
ANY = pl.BlockSpec(memory_space=pl.ANY)
VMEM = pl.BlockSpec(memory_space=pltpu.VMEM)


def nn(a, b):
    return lax.dot_general(a, b, (((1,), (0,)), ((), ())), preferred_element_type=F32)


def nt(a, b):
    return lax.dot_general(a, b, (((1,), (1,)), ((), ())), preferred_element_type=F32)


def tn(a, b):
    return lax.dot_general(a, b, (((0,), (0,)), ((), ())), preferred_element_type=F32)


class Place:
    def __init__(self, tensor, dp):
        self.tensor = tensor
        self.groups = dp // CORES
        self.chips = tensor * self.groups
        self.pipe = lax.axis_index("pipe")
        self.d = lax.axis_index("dp")
        self.t = lax.axis_index("tensor")
        self.core = lax.rem(self.d, CORES)
        self.group = self.d // CORES
        odd = lax.rem(self.group, 2)
        self.ring = self.group * tensor + self.t + odd * (tensor - 1 - 2 * self.t)

    def at(self, ring):
        group = ring // self.tensor
        along = lax.rem(ring, self.tensor)
        odd = lax.rem(group, 2)
        return group, along + odd * (self.tensor - 1 - 2 * along)

    def neighbour(self, step):
        group, t = self.at(lax.rem(self.ring + step + self.chips, self.chips))
        return {"dp": group * CORES + self.core, "tensor": t}

    def sibling(self):
        return {"dp": self.group * CORES + 1 - self.core}


def meet(devices):
    barrier = pltpu.get_barrier_semaphore()
    for device in devices:
        pl.semaphore_signal(barrier, inc=1, device_id=device, device_id_type=MESH)
    pl.semaphore_wait(barrier, len(devices))


def halves(rows, columns):
    if rows % 32 == 0:
        return [(pl.ds(k * (rows // 2), rows // 2), pl.ds(0, columns)) for k in range(2)]
    cut = columns // LANES // 2 * LANES
    return [(pl.ds(0, rows), pl.ds(0, cut)), (pl.ds(0, rows), pl.ds(cut, columns - cut))]


def gather_kernel(
    tensor, dp, rows_ref, pack_ref, length_ref, table_ref, x_ref, w_ref, lengths_ref, tables_ref,
    local_sem, block_send, block_recv, pass_send, pass_recv, small_send, small_recv,
    ring_send, ring_recv, core_send, core_recv,
):
    here = Place(tensor, dp)
    c, t, chips = here.core, here.t, here.chips
    nrow = rows_ref.shape[0]
    sibling = here.sibling()
    to_right, to_left = here.neighbour(1), here.neighbour(-1)
    others = [{"tensor": lax.rem(t + k, tensor)} for k in range(1, tensor)]
    meet([to_right, to_left, sibling] + others)

    lengths = pltpu.make_async_remote_copy(
        length_ref, lengths_ref.at[c], small_send.at[0], small_recv.at[0], device_id=sibling, device_id_type=MESH
    )
    lengths.start()
    own_lengths = pltpu.make_async_copy(length_ref, lengths_ref.at[c], local_sem.at[0])
    own_lengths.start()
    own_table = pltpu.make_async_copy(table_ref, tables_ref.at[t], local_sem.at[1])
    own_table.start()
    tables = []
    for k in range(1, tensor):
        tables.append(
            pltpu.make_async_remote_copy(
                table_ref, tables_ref.at[t], small_send.at[k], small_recv.at[k], device_id=others[k - 1], device_id_type=MESH
            )
        )
        tables[-1].start()

    def to_chip(i):
        return pltpu.make_async_remote_copy(
            rows_ref.at[i], x_ref.at[:, t], block_send.at[i], block_recv.at[t],
            device_id={"tensor": nrow * c + i}, device_id_type=MESH,
        )

    def kept(i):
        return pltpu.make_async_copy(rows_ref.at[i], x_ref.at[:, t], local_sem.at[2])

    def kept_pass(i):
        return pltpu.make_async_remote_copy(
            rows_ref.at[i], x_ref.at[:, t], pass_send.at[t], pass_recv.at[t], device_id=sibling, device_id_type=MESH
        )

    def passed(s):
        return pltpu.make_async_remote_copy(
            x_ref.at[:, s], x_ref.at[:, s], pass_send.at[s], pass_recv.at[s], device_id=sibling, device_id_type=MESH
        )

    for i in range(nrow):
        mine = nrow * c + i == t

        @pl.when(mine)
        def _():
            kept(i).start()
            kept_pass(i).start()

        @pl.when(jnp.logical_not(mine))
        def _():
            to_chip(i).start()

    parts = halves(*pack_ref.shape)
    own_pack = pltpu.make_async_copy(pack_ref, w_ref.at[t, here.d], local_sem.at[3])
    own_pack.start()

    def shard(ring, part):
        group, at = here.at(ring)
        return w_ref.at[at, group * CORES + c, parts[part][0], parts[part][1]]

    def source(step, part):
        return lax.rem(here.ring + (1 if part else -1) * step + chips, chips)

    def onward(step, part, first=False):
        slot = shard(source(step, part), part)
        return pltpu.make_async_remote_copy(
            pack_ref.at[parts[part][0], parts[part][1]] if first else slot, slot,
            ring_send.at[part, step], ring_recv.at[part, step],
            device_id=to_left if part else to_right, device_id_type=MESH,
        )

    def across(step, part, first=False):
        slot = shard(source(step, part), part)
        return pltpu.make_async_remote_copy(
            pack_ref.at[parts[part][0], parts[part][1]] if first else slot, slot,
            core_send.at[part, step], core_recv.at[part, step], device_id=sibling, device_id_type=MESH,
        )

    for part in range(2):
        onward(0, part, True).start()
        across(0, part, True).start()

    takes = t // nrow == c
    for s in range(tensor):

        @pl.when(jnp.logical_and(takes, s != t))
        def _():
            pltpu.make_async_remote_copy(
                rows_ref.at[0], x_ref.at[:, s], block_send.at[0], block_recv.at[s], device_id=sibling, device_id_type=MESH
            ).wait_recv()
            passed(s).start()

    @pl.loop(1, chips)
    def _(step):
        for part in range(2):
            onward(step - 1, part).wait_recv()

            @pl.when(step < chips - 1)
            def _():
                onward(step, part).start()

            across(step, part).start()

    @pl.loop(0, chips)
    def _(step):
        for part in range(2):

            @pl.when(step < chips - 1)
            def _():
                onward(step, part).wait_send()

            across(step, part).wait_send()
            across(step, part).wait_recv()

    for i in range(nrow):
        mine = nrow * c + i == t

        @pl.when(mine)
        def _():
            kept(i).wait()
            kept_pass(i).wait_send()

        @pl.when(jnp.logical_not(mine))
        def _():
            to_chip(i).wait_send()

    for s in range(tensor):

        @pl.when(jnp.logical_and(takes, s != t))
        def _():
            passed(s).wait_send()

        @pl.when(jnp.logical_not(takes))
        def _():
            passed(s).wait_recv()

    lengths.wait()
    own_lengths.wait()
    own_table.wait()
    own_pack.wait()
    for table in tables:
        table.wait()


def gather(tensor, dp, rows, pack, lengths, table):
    chips = tensor * dp // CORES
    nrow, two, places, width = rows.shape
    sems = pltpu.SemaphoreType.DMA
    return pl.pallas_call(
        functools.partial(gather_kernel, tensor, dp),
        out_shape=(
            jax.ShapeDtypeStruct((two, tensor, places, width), rows.dtype),
            jax.ShapeDtypeStruct((tensor, dp) + pack.shape, pack.dtype),
            jax.ShapeDtypeStruct((CORES,) + lengths.shape, lengths.dtype),
            jax.ShapeDtypeStruct((tensor,) + table.shape, table.dtype),
        ),
        in_specs=[ANY] * 4,
        out_specs=(ANY,) * 4,
        scratch_shapes=[
            sems((4,)), sems((nrow,)), sems((tensor,)), sems((tensor,)), sems((tensor,)), sems((tensor,)), sems((tensor,)),
            sems((2, chips)), sems((2, chips)), sems((2, chips)), sems((2, chips)),
        ],
        compiler_params=pltpu.CompilerParams(collective_id=0, has_side_effects=True),
        name="gather",
    )(rows, pack, lengths, table)


def scatter_kernel(
    tensor, dp, grads_ref, small_ref, rows_ref, out_ref, small_out, rows_out,
    own, theirs, taken, small_own, small_theirs, small_taken, total,
    own_sem, core_send, core_recv, ring_send, ring_recv,
    sown_sem, score_send, score_recv, sring_send, sring_recv, block_send, block_recv, local_sem,
):
    here = Place(tensor, dp)
    c, t, chips = here.core, here.t, here.chips
    nrow = rows_out.shape[0]
    sibling = here.sibling()
    to_right, to_left = here.neighbour(1), here.neighbour(-1)
    line = [
        {"dp": here.group * CORES + lax.rem(c + j, CORES), "tensor": lax.rem(t + k, tensor)}
        for j in range(CORES)
        for k in range(tensor)
        if j + k > 0
    ]
    meet([to_right, to_left] + line)

    half = tensor // 2
    owner = t // nrow

    def block(k):
        place = here.pipe * (c * half + k % half) + (1 - here.pipe) * k
        which = here.pipe * (k // half) + (1 - here.pipe) * c
        return place, which

    def home(k):
        place, which = block(k)
        slot = rows_out.at[lax.rem(t, nrow), which]
        recv = block_recv.at[lax.rem(t, nrow), which]
        return (
            jnp.logical_and(place == t, owner == c),
            lambda: pltpu.make_async_copy(rows_ref.at[k], slot, recv),
            lambda: pltpu.make_async_remote_copy(
                rows_ref.at[k], slot, block_send.at[k], recv,
                device_id={"dp": here.group * CORES + owner, "tensor": place}, device_id_type=MESH,
            ),
        )

    for k in range(tensor):
        stays, inside, away = home(k)

        @pl.when(stays)
        def _():
            inside().start()

        @pl.when(jnp.logical_not(stays))
        def _():
            away().start()

    def across(ring):
        group, at = here.at(ring)
        return (
            pltpu.make_async_remote_copy(
                grads_ref.at[at, group * CORES + 1 - c], theirs.at[ring], core_send.at[ring], core_recv.at[ring],
                device_id=sibling, device_id_type=MESH,
            ),
            pltpu.make_async_remote_copy(
                small_ref.at[at, group * CORES + 1 - c], small_theirs.at[ring], score_send.at[ring], score_recv.at[ring],
                device_id=sibling, device_id_type=MESH,
            ),
        )

    def fetch(ring):
        group, at = here.at(ring)
        return (
            pltpu.make_async_copy(grads_ref.at[at, group * CORES + c], own.at[ring], own_sem.at[ring]),
            pltpu.make_async_copy(small_ref.at[at, group * CORES + c], small_own.at[ring], sown_sem.at[ring]),
        )

    def behind(step):
        return lax.rem(here.ring - step + chips, chips)

    def order(k):
        off = (2 * lax.rem(k, 2) - 1) * (k // 2 + 1) * (1 - k // (chips - 1))
        return lax.rem(here.ring + chips + off, chips)

    @pl.loop(0, chips)
    def _(k):
        for copy in across(order(k)) + fetch(order(k)):
            copy.start()

    rows, columns = out_ref.shape
    parts = halves(rows, columns)

    def add(ring, part, step, last):
        height = parts[part][0].size
        piece = 16 if height % 16 == 0 else height

        @pl.loop(0, height // piece)
        def _(k):
            at = pl.ds(pl.multiple_of(parts[part][0].start + k * piece, 8), piece)
            where = (at, parts[part][1])
            value = own[(ring,) + where].astype(F32) + theirs[(ring,) + where].astype(F32)
            if step is not None:
                value = value + taken[(step,) + where].astype(F32)
            if last:
                total[where] = value
            else:
                own[(ring,) + where] = value.astype(BF16)

    def onward(ring, step, part):
        where = (parts[part][0], parts[part][1])
        return pltpu.make_async_remote_copy(
            own.at[(ring,) + where], taken.at[(step,) + where], ring_send.at[part, step], ring_recv.at[part, step],
            device_id=to_left if part else to_right, device_id_type=MESH,
        )

    def small_onward(ring, step):
        return pltpu.make_async_remote_copy(
            small_own.at[ring], small_taken.at[step], sring_send.at[step], sring_recv.at[step],
            device_id=to_right, device_id_type=MESH,
        )

    def ready(ring):
        for copy in across(ring):
            copy.wait_recv()
        for copy in fetch(ring):
            copy.wait()

    def ahead(step):
        return lax.rem(here.ring + step, chips)

    half_chips = chips // 2

    @pl.loop(0, chips - 1)
    def _(step):
        right, left = behind(step + 1), ahead(step + 1)

        @pl.when(step < half_chips)
        def _():
            ready(right)

        @pl.when(step < chips - 1 - half_chips)
        def _():
            ready(left)

        @pl.when(step == 0)
        def _():
            add(right, 0, None, False)
            add(left, 1, None, False)
            small_own[right] = small_own[right] + small_theirs[right]

        @pl.when(step > 0)
        def _():
            onward(right, step - 1, 0).wait_recv()
            add(right, 0, step - 1, False)
            onward(right, step, 0).start()
            onward(left, step - 1, 1).wait_recv()
            add(left, 1, step - 1, False)
            onward(left, step, 1).start()
            small_onward(right, step - 1).wait_recv()
            small_own[right] = small_own[right] + small_theirs[right] + small_taken[step - 1]
            small_onward(right, step).start()

        @pl.when(step == 0)
        def _():
            onward(right, 0, 0).start()
            onward(left, 0, 1).start()
            small_onward(right, 0).start()

    ready(here.ring)
    for part in range(2):
        onward(here.ring, chips - 2, part).wait_recv()
        add(here.ring, part, chips - 2, True)
    small_onward(here.ring, chips - 2).wait_recv()
    small_out[...] = small_own[here.ring] + small_theirs[here.ring] + small_taken[chips - 2]
    finish = pltpu.make_async_copy(total, out_ref, local_sem.at[0])
    finish.start()

    @pl.loop(0, chips)
    def _(step):
        @pl.when(step < chips - 1)
        def _():
            onward(behind(step + 1), step, 0).wait_send()
            onward(ahead(step + 1), step, 1).wait_send()
            small_onward(behind(step + 1), step).wait_send()

        for copy in across(step):
            copy.wait_send()

    for k in range(tensor):
        stays, inside, away = home(k)

        @pl.when(jnp.logical_not(stays))
        def _():
            away().wait_send()

    for i in range(nrow):
        for which in range(2):
            pltpu.make_async_copy(rows_ref.at[0], rows_out.at[i, which], block_recv.at[i, which]).wait()
    finish.wait()


def scatter(tensor, dp, grads, small, rows, nrow):
    chips = tensor * dp // CORES
    shard = grads.shape[2:]
    tiny = small.shape[2:]
    sems = pltpu.SemaphoreType.DMA
    return pl.pallas_call(
        functools.partial(scatter_kernel, tensor, dp),
        out_shape=(
            jax.ShapeDtypeStruct(shard, F32),
            jax.ShapeDtypeStruct(tiny, F32),
            jax.ShapeDtypeStruct((nrow, 2) + rows.shape[1:], rows.dtype),
        ),
        in_specs=[ANY] * 3,
        out_specs=(ANY, VMEM, ANY),
        scratch_shapes=[
            pltpu.VMEM((chips,) + shard, BF16),
            pltpu.VMEM((chips,) + shard, BF16),
            pltpu.VMEM((chips - 1,) + shard, BF16),
            pltpu.VMEM((chips,) + tiny, F32),
            pltpu.VMEM((chips,) + tiny, F32),
            pltpu.VMEM((chips - 1,) + tiny, F32),
            pltpu.VMEM(shard, F32),
            sems((chips,)), sems((chips,)), sems((chips,)), sems((2, chips)), sems((2, chips)),
            sems((chips,)), sems((chips,)), sems((chips,)), sems((chips,)), sems((chips,)),
            sems((tensor,)), sems((nrow, 2)), sems((1,)),
        ],
        compiler_params=pltpu.CompilerParams(collective_id=1, has_side_effects=True, vmem_limit_bytes=VMEM_LIMIT),
        name="scatter",
    )(grads, small, rows)


KEY, VALUE, QUERY, OUT, FIRST, SECOND = range(6)
ATTN, CROSS, INNER, OUTER = range(4)
SEGS_HELD = 6


def rms(value):
    return lax.rsqrt(jnp.mean(value * value, axis=-1, keepdims=True) + EPSILON)


def in_rows(count, body, piece=32):
    @pl.loop(0, count // piece)
    def _(k):
        body(pl.ds(pl.multiple_of(k * piece, piece), piece))


def columns_of(count, body, piece=256):
    @pl.loop(0, count // piece)
    def _(k):
        body(pl.ds(pl.multiple_of(k * piece, piece), piece), k)


def normalize(source, gain, target, count):
    def body(at):
        value = source[at, :].astype(F32)
        target[at, :] = (value * rms(value) * gain).astype(BF16)

    in_rows(count, body)


def normalize_back(source, gain, incoming, total, gain_parts, count, fresh):
    gain_parts[...] = jnp.zeros_like(gain_parts)

    def body(at):
        value, back = source[at, :].astype(F32), incoming[at, :]
        scale = rms(value)
        unit = value * scale
        gain_parts[...] += jnp.sum((back * unit).reshape(-1, 8, back.shape[-1]), axis=0)
        back = back * gain
        back = scale * (back - unit * jnp.mean(back * unit, axis=-1, keepdims=True))
        total[at, :] = back if fresh else total[at, :] + back

    in_rows(count, body)


def project(left, weight, target, count):
    def body(at, k):
        target[0:count, at] = nn(left[0:count, :], weight[:, at]).astype(target.dtype)

    columns_of(weight.shape[1], body)


def project_back(left, weight, total, count, fresh):
    def body(at, k):
        value = nt(left[0:count, :], weight[at, :])
        total[0:count, at] = value if fresh else total[0:count, at] + value

    columns_of(weight.shape[0], body)


def to_bf16(source, target, rows):
    def body(at):
        target[at, :] = source[at, :].astype(BF16)

    in_rows(rows, body)


def turn(left, turned, rows):
    def body(at, k):
        turned[at, 0:rows] = left[0:rows, at].T

    columns_of(left.shape[1], body, LANES)


def lane_half(shape, part):
    return lax.broadcasted_iota(jnp.int32, shape, 1) // HEAD_DIM == part


def attend(keys, values, queries, mixture, probs, rows, span, pairs, mask, bias, after):
    @pl.loop(0, pairs)
    def _(pair):
        lanes = pl.ds(pl.multiple_of(pair * LANES, LANES), LANES)
        key, query = keys[0:span, lanes], queries[0:rows, lanes]
        value_t = values[0:span, lanes].T
        mixed = []
        for part in range(2):
            one = jnp.where(lane_half(query.shape, part), query, jnp.zeros_like(query))
            scores = nt(key, one) + mask[0:span, 0:rows]
            if bias is not None:
                scores = scores + bias(2 * pair + part)
            scores = jnp.exp(scores - jnp.max(scores, axis=0, keepdims=True))
            scores = (scores * (1.0 / jnp.sum(scores, axis=0, keepdims=True))).astype(BF16)
            probs[2 * pair + part, 0:span, 0:rows] = scores
            mixed.append(nn(value_t[part * HEAD_DIM : (part + 1) * HEAD_DIM, :], scores))
        mixture[0:rows, lanes] = jnp.concatenate(mixed, axis=0).T.astype(BF16)
        after(pair)


def attend_back(keys, values, queries, back, probs, rows, span, pairs, each, after):
    @pl.loop(0, pairs)
    def _(pair):
        lanes = pl.ds(pl.multiple_of(pair * LANES, LANES), LANES)
        key, value = keys[0:span, lanes], values[0:span, lanes]
        query, given = queries[0:rows, lanes], back[0:rows, lanes]
        key_t = key.T
        d_key, d_value, d_query = None, None, []
        for part in range(2):
            side = lane_half(query.shape, part)
            query_one = jnp.where(side, query, jnp.zeros_like(query))
            given_one = jnp.where(side, given, jnp.zeros_like(given))
            prob = probs[2 * pair + part, 0:span, 0:rows]
            wide = prob.astype(F32)
            d_prob = nt(value, given_one)
            d_score = (wide * (d_prob - jnp.sum(wide * d_prob, axis=0, keepdims=True))).astype(BF16)
            if each is not None:
                each(2 * pair + part, d_score)
            of_key, of_value = nn(d_score, query_one), nn(prob, given_one)
            d_key = of_key if d_key is None else d_key + of_key
            d_value = of_value if d_value is None else d_value + of_value
            d_query.append(nn(key_t[part * HEAD_DIM : (part + 1) * HEAD_DIM, :], d_score))
        keys[0:span, lanes] = d_key.astype(BF16)
        values[0:span, lanes] = d_value.astype(BF16)
        queries[0:rows, lanes] = jnp.concatenate(d_query, axis=0).T.astype(BF16)
        after(pair)


def segments(lengths_row, shape, axis, first):
    lane = lax.broadcasted_iota(jnp.int32, lengths_row.shape, 1)
    places = lax.broadcasted_iota(jnp.int32, shape, axis) + first
    ids = jnp.zeros(shape, jnp.int32)
    for c in range(SEGS_HELD):
        bound = jnp.sum(jnp.where(lane <= c, lengths_row, 0), axis=1, keepdims=True)
        ids = ids + (places >= bound).astype(jnp.int32)
    return ids


def masked(allowed):
    return jnp.where(allowed, 0.0, NEGATIVE).astype(F32)


def nothing(*unused):
    pass


def work(r, here, supply, drain, tensor, heads_at):
    c, t = here.core, here.t
    width = r.hidden.shape[1]
    tall = r.hidden.shape[0]
    block = width // tensor
    half_width = width // 2
    units = r.inner.shape[2]
    places = r.x.shape[2]
    sibling = here.sibling()
    across = [{"pipe": 1 - here.pipe, "dp": here.group * CORES + k} for k in range(CORES)]
    nrow = tensor // CORES
    rows_e, span_e, rows_d, span_d = tall // 2, tall, tall // 4, tall // 2
    pairs_here = half_width // LANES
    near_lanes = pl.ds(pl.multiple_of(c * half_width, half_width), half_width)
    far_lanes = pl.ds(pl.multiple_of((1 - c) * half_width, half_width), half_width)
    lane_halves = [slice(k * half_width, (k + 1) * half_width) for k in range(CORES)]

    def move(source, target, sends, recvs, device):
        return pltpu.make_async_remote_copy(
            source, target, r.send_sem.at[sends], r.recv_sem.at[recvs], device_id=device, device_id_type=MESH
        )

    def lengths_row(first):
        return r.lengths[t // nrow, pl.ds(first + lax.rem(t, nrow), 1), :]

    def vector_row(head):
        return (head // heads_at) * 8 + lax.rem(head, heads_at)

    def bias_vectors():
        buckets = lax.broadcasted_iota(jnp.int32, r.onehot.shape, 0) == r.buckets[0:1, :]
        r.onehot[...] = buckets.astype(F32)
        for tt in range(tensor):
            r.vectors[pl.ds(8 * tt, 8), :] = lax.dot_general(
                r.tables[tt][:, 0 : r.onehot.shape[0]], r.onehot[...], (((1,), (0,)), ((), ())),
                precision=lax.Precision.HIGHEST, preferred_element_type=F32,
            )

    def rows_ready(span, rows, first_block):
        @pl.loop(0, span // places)
        def _(k):
            value = r.x[k // tensor, lax.rem(k, tensor)].astype(F32)
            at = pl.ds(pl.multiple_of(k * places, places), places)
            r.hidden[at, :] = (value * rms(value) * r.gains[0:1, :]).astype(BF16)

        for k in range(rows // places):
            r.own_x[k * places : (k + 1) * places, :] = r.x[first_block // tensor, lax.rem(first_block, tensor) + k]

    def untangle(source, first, count):
        for tt in range(tensor):
            for k in range(count):
                r.square[first + k, :, tt * block : (tt + 1) * block] = source[tt, :, k * block : (k + 1) * block]

    def self_forward(span, rows, first_row, group, following):
        def bias(head):
            pieces = []
            for j in range(span // LANES):
                start = pl.multiple_of(first_row + span - LANES - j * LANES, LANES)
                row = r.vectors[pl.ds(vector_row(head), 1), pl.ds(start, rows + LANES)]
                wide = jnp.broadcast_to(row, (LANES, rows + LANES))
                pieces.append(pltpu.roll(wide, rows + 1, 1, stride=1, stride_axis=0)[:, 0:rows])
            return jnp.concatenate(pieces, axis=0)

        untangle(r.raw_a, KEY, 2)
        untangle(r.raw_a.at[:, :, pl.ds(2 * block, 2 * block)], QUERY, 2)
        project(r.hidden, r.square.at[KEY], r.keys, span)
        supply.tick(group, 0)
        project(r.hidden, r.square.at[VALUE], r.values, span)
        project(r.hidden.at[pl.ds(first_row, rows)], r.square.at[QUERY], r.queries, rows)
        supply.tick(group, 1)

        def after(pair):
            @pl.when(pair < supply.count - 3)
            def _():
                supply.tick(group, 2 + pair)

            if supply.count - 2 < 2 + width // LANES:

                @pl.when(pair == supply.count - 4)
                def _():
                    supply.begin(following)

        attend(r.keys, r.values, r.queries, r.mixture, r.probs, rows, span, width // LANES, r.mask, bias, after)
        project_back(r.mixture, r.square.at[OUT], r.resid_mid, rows, True)

        def add(at):
            r.resid_mid[at, :] += r.own_x[at, :].astype(F32)

        in_rows(rows, add)
        supply.ticks(group, supply.count - 1, supply.count)
        supply.finish(group)

    def every_other(group, n):
        @pl.when(lax.rem(n, 2) == 1)
        def _():
            supply.tick(group, lax.div(n, 2))

    def feed_forward(rows, group):
        @pl.loop(0, tensor)
        def _(tt):
            def body(at, k):
                value = nn(r.second[0:rows, :], r.inner[tt, :, at])
                cdf = 0.5 * (1.0 + lax.erf(value * 0.7071067811865476))
                r.ff[tt, 0:rows, at] = (value * cdf).astype(BF16)
                slope = cdf + value * jnp.exp(-0.5 * value * value) * 0.3989422804014327
                r.ff[tensor + tt, 0:rows, at] = slope.astype(BF16)
                if group is not None:
                    every_other(group, tt * (units // 256) + k)

            columns_of(units, body)

    def feed_out(target, rows, group):
        @pl.loop(0, tensor)
        def _(tt):
            def body(at, k):
                target[0:rows, at] += nt(r.ff[tt, 0:rows, :], r.outer[tt, at, :])
                if group is not None:
                    every_other(group, tt * (width // 256) + k)

            columns_of(width, body)

    def feed_back(rows, ready, group):
        r.summed[0:rows, :] = jnp.zeros((rows, width), F32)

        @pl.loop(0, tensor)
        def _(tt):
            def body(at, k):
                if ready:
                    value = r.ff[tensor + tt, rows : 2 * rows, at].astype(F32)
                else:
                    value = nn(r.d_branch[0:rows, :], r.outer[tt, :, at])
                r.ff[tensor + tt, 0:rows, at] = (value * r.ff[tensor + tt, 0:rows, at].astype(F32)).astype(BF16)

            columns_of(units, body)

            def back(at, k):
                r.summed[0:rows, at] += nt(r.ff[tensor + tt, 0:rows, :], r.inner[tt, at, :])

            columns_of(width, back)
            if group is not None:
                drain.tick(group, tt)

    def feed_grads(rows, turned, first, which, hook):
        @pl.loop(0, tensor)
        def _(tt):
            slot = lax.rem(tt, 2)

            @pl.when(tt >= 2)
            def _():
                drain.release(which, tt - 2, slot)

            def body(at, k):
                r.stage[slot, :, at] = nn(turned[:, 0:rows], r.ff[first + tt, 0:rows, at]).astype(BF16)
                hook(tt, k)

            columns_of(units, body)
            drain.emit(which, tt, slot)

        for tt in range(tensor - 2, tensor):
            drain.release(which, tt, tt % 2)

    def square_grads(rows, which, products, hook):
        for k in range(tensor // 2):
            for j, (turned, right) in enumerate(products):
                value = nn(turned[:, 0:rows], right[0:rows, 2 * k * block : 2 * (k + 1) * block]).astype(BF16)
                for slot in range(2):
                    r.stage[slot, :, j * block : (j + 1) * block] = value[:, slot * block : (slot + 1) * block]
            for slot in range(2):
                drain.emit(which, 2 * k + slot, slot)
            hook(k)
            for slot in range(2):
                drain.release(which, 2 * k + slot, slot)

    def gain_done(which):
        r.gains_out[which : which + 1, :] = jnp.sum(r.gain_parts[...], axis=0, keepdims=True)

    def self_backward(span, rows, first_row, group, send_rows):
        mirror = (
            lax.broadcasted_iota(jnp.int32, (LANES, LANES), 0) + lax.broadcasted_iota(jnp.int32, (LANES, LANES), 1)
            == LANES - 1
        ).astype(BF16)
        to_bf16(r.d_resid, r.branch, rows)
        project(r.branch, r.square.at[OUT], r.d_branch, rows)
        drain.tick(group, 0)
        r.diagonals[...] = jnp.zeros_like(r.diagonals)

        def each(head, d_score):
            for j in range(span // LANES):
                start = pl.multiple_of(first_row + span - LANES - j * LANES, LANES)
                piece = nn(mirror, d_score[j * LANES : (j + 1) * LANES, :])
                piece = jnp.concatenate([piece, jnp.zeros((LANES, LANES), F32)], axis=1)
                piece = pltpu.roll(piece, 0, 1, stride=1, stride_axis=0)
                at = (pl.ds(vector_row(head), 1), pl.ds(start, rows + LANES))
                r.diagonals[at] += jnp.sum(piece, axis=0, keepdims=True)

        pairs = width // LANES
        attend_back(
            r.keys, r.values, r.queries, r.d_branch, r.probs, rows, span, pairs, each,
            lambda pair: drain.tick(group, 1 + lax.div(pair, pairs // 2), lax.rem(pair, pairs // 2) == 1),
        )
        far = pl.ds(pl.multiple_of((1 - c) * rows, rows), rows)
        near = pl.ds(pl.multiple_of(c * rows, rows), rows)
        trades = [
            move(source.at[far], r.taken_pair.at[k, pl.ds(0, rows)], 12 + k, 12 + k, sibling)
            for k, source in enumerate((r.keys, r.values))
        ]
        for trade in trades:
            trade.start()
        turn(r.branch, r.turned, rows)
        turn(r.hidden.at[pl.ds(first_row, rows)], r.turned_more, rows)
        for tt in range(tensor):
            at = pl.ds(8 * tt, 8)
            r.bias_out[at, 0 : r.onehot.shape[0]] = lax.dot_general(
                r.diagonals[at, :], r.onehot[...], (((1,), (1,)), ((), ())),
                precision=lax.Precision.HIGHEST, preferred_element_type=F32,
            )
        project_back(r.queries, r.square.at[QUERY], r.summed, rows, True)
        for trade in trades:
            trade.wait_recv()
        for k, source in enumerate((r.keys, r.values)):
            r.d_pair[k, 0:rows, :] = (source[near, :].astype(F32) + r.taken_pair[k, 0:rows, :].astype(F32)).astype(BF16)
        project_back(r.d_pair.at[0], r.square.at[KEY], r.summed, rows, False)
        project_back(r.d_pair.at[1], r.square.at[VALUE], r.summed, rows, False)
        drain.tick(group, 3)
        normalize_back(r.own_x, r.gains[0:1, :], r.summed, r.d_resid, r.gain_parts, rows, False)
        gain_done(0)
        send_rows()
        drain.small_begin()
        products = [(r.turned_more, r.d_pair.at[0]), (r.turned_more, r.d_pair.at[1]), (r.turned_more, r.queries), (r.turned, r.mixture)]
        square_grads(rows, ATTN, products, nothing)
        for trade in trades:
            trade.wait_send()
        drain.ticks(group, 4, drain.count)
        drain.begin(ATTN)
        drain.end(group)
        drain.ticks(ATTN, 0, drain.count)
        drain.end(ATTN)

    def parts_of(array):
        return [array.at[pl.ds(k * rows_d, rows_d)] for k in range(CORES)]

    def part_here(array):
        return array.at[pl.ds(pl.multiple_of(c * rows_d, rows_d), rows_d)]

    r.gains_out[...] = jnp.zeros_like(r.gains_out)
    r.bias_out[...] = jnp.zeros_like(r.bias_out)
    supply.start()
    supply.ticks(ATTN, 0, 2)
    supply.small()
    bias_vectors()
    supply.rows()

    @pl.when(here.pipe == 0)
    def _():
        rows, span = rows_e, span_e
        first_row = pl.multiple_of(c * rows, rows)
        seg_rows = segments(lengths_row(0), (span, 1), 0, 0)
        r.mask[...] = masked(seg_rows == segments(lengths_row(0), (1, rows), 1, first_row))
        supply.ticks(ATTN, 2, 4)
        rows_ready(span, rows, c * tensor)
        supply.ticks(ATTN, 4, supply.count - 1)
        supply.begin(INNER)
        supply.ticks(ATTN, supply.count - 1, supply.count)
        supply.finish(ATTN)
        self_forward(span, rows, first_row, INNER, OUTER)
        normalize(r.resid_mid, r.gains[1:2, :], r.second, rows)
        feed_forward(rows, OUTER)
        supply.begin(CROSS)
        supply.ticks(OUTER, supply.count - 1, supply.count)
        supply.finish(OUTER)
        r.resid_top[...] = r.resid_mid[...]
        feed_out(r.resid_top, rows, CROSS)
        normalize(r.resid_top, r.gains[2:3, :], r.third, rows)
        r.mask[...] = masked(seg_rows == segments(lengths_row(nrow), (1, span_d), 1, 0))
        supply.ticks(CROSS, supply.count - 1, supply.count)
        supply.finish(CROSS)
        untangle(r.raw_c, FIRST, 2)
        mine = pl.ds(first_row, rows)
        other = pl.ds(pl.multiple_of((1 - c) * rows, rows), rows)
        project(r.third, r.square.at[FIRST], r.d_pair.at[0], rows)
        project(r.third, r.square.at[SECOND], r.d_pair.at[1], rows)
        trades = []
        for k, held in enumerate((r.cross_keys, r.cross_values)):
            held[mine, :] = r.d_pair[k, :, near_lanes]
            r.send_pair[k] = r.d_pair[k, :, far_lanes]
            trades.append(move(r.send_pair.at[k], held.at[mine], k, k, sibling))
            trades[-1].start()
        for k, part in enumerate(parts_of(r.cross_queries)):
            move(part, part, 2 + k, 2 + k, across[k]).wait_recv()
        for k, held in enumerate((r.cross_keys, r.cross_values)):
            move(r.send_pair.at[k], held.at[other], k, k, sibling).wait_recv()
        attend(
            r.cross_keys, r.cross_values, r.cross_queries, r.cross_mixture, r.cross_probs, span_d, span, pairs_here,
            r.mask, None, nothing,
        )
        mixtures = [
            move(part, r.cross_in.at[c], 4 + k, 4 + c, across[k]) for k, part in enumerate(parts_of(r.cross_mixture))
        ]
        for mix in mixtures:
            mix.start()
        supply.close()
        drain.free(0)
        turn(r.third, r.turned, rows)
        for k, part in enumerate(parts_of(r.cross_back)):
            move(part, part, 6 + k, 6 + k, across[k]).wait_recv()
        attend_back(
            r.cross_keys, r.cross_values, r.cross_queries, r.cross_back, r.cross_probs, span_d, span, pairs_here, None, nothing
        )
        returns = [
            move(d_cross.at[other], r.cross_taken.at[k], 10 + k, 10 + k, sibling)
            for k, d_cross in enumerate((r.cross_keys, r.cross_values))
        ]
        for back in returns:
            back.start()
        answers = [
            move(part, r.cross_in_back.at[c], 8 + k, 8 + c, across[k]) for k, part in enumerate(parts_of(r.cross_queries))
        ]
        for answer in answers:
            answer.start()
        for k, d_cross in enumerate((r.cross_keys, r.cross_values)):
            r.d_pair[k, :, near_lanes] = d_cross[mine, :]
            returns[k].wait_recv()
            r.d_pair[k, :, far_lanes] = r.cross_taken[k]
        drain.allow(0)
        square_grads(rows, CROSS, [(r.turned, r.d_pair.at[0]), (r.turned, r.d_pair.at[1])], nothing)
        drain.begin(CROSS)
        project_back(r.d_pair.at[0], r.square.at[FIRST], r.summed, rows, True)
        drain.tick(CROSS, 0)
        project_back(r.d_pair.at[1], r.square.at[SECOND], r.summed, rows, False)
        drain.tick(CROSS, 1)
        normalize_back(r.resid_top, r.gains[2:3, :], r.summed, r.d_resid, r.gain_parts, rows, True)
        gain_done(2)
        drain.tick(CROSS, 2)
        to_bf16(r.d_resid, r.d_branch, rows)
        turn(r.d_branch, r.turned, rows)
        drain.tick(CROSS, 3)
        feed_grads(rows, r.turned, 0, OUTER, nothing)
        drain.ticks(CROSS, 4, drain.count)
        drain.begin(OUTER)
        drain.end(CROSS)
        feed_back(rows, False, OUTER)
        drain.free(1)
        normalize_back(r.resid_mid, r.gains[1:2, :], r.summed, r.d_resid, r.gain_parts, rows, False)
        gain_done(1)
        turn(r.second, r.turned, rows)
        drain.allow(1)
        feed_grads(rows, r.turned, tensor, INNER, nothing)
        drain.ticks(OUTER, tensor, drain.count)
        drain.begin(INNER)
        drain.end(OUTER)
        for copy in trades + mixtures + returns + answers:
            copy.wait_send()

        def send_rows():
            to_bf16(r.d_resid, r.rows_out, rows)
            drain.home()

        self_backward(span, rows, first_row, INNER, send_rows)

    @pl.when(here.pipe == 1)
    def _():
        rows, span = rows_d, span_d
        first_row = pl.multiple_of(c * rows, rows)
        key_at = lax.broadcasted_iota(jnp.int32, (span, rows), 0)
        query_at = lax.broadcasted_iota(jnp.int32, (span, rows), 1) + first_row
        same = segments(lengths_row(nrow), (span, 1), 0, 0) == segments(lengths_row(nrow), (1, rows), 1, first_row)
        r.mask[0:span, 0:rows] = masked(same & (query_at >= key_at))
        supply.ticks(ATTN, 2, 4)
        first_block = c * (tensor // 2)
        rows_ready(span, rows, first_block)
        for k in range(rows // places):
            r.d_branch[k * places : (k + 1) * places, :] = r.x[1, first_block + k]
        supply.ticks(ATTN, 4, supply.count - 1)
        supply.begin(CROSS)
        supply.ticks(ATTN, supply.count - 1, supply.count)
        supply.finish(ATTN)
        self_forward(span, rows, first_row, CROSS, INNER)
        untangle(r.raw_c, FIRST, 2)
        normalize(r.resid_mid, r.gains[1:2, :], r.third, rows)
        project(r.third, r.square.at[FIRST], r.joined, rows)
        asks = []
        for k in range(CORES):
            r.send_pair[k, 0:rows, :] = r.joined[:, lane_halves[k]]
            asks.append(move(r.send_pair.at[k, pl.ds(0, rows)], part_here(r.cross_queries), 2 + k, 2 + c, across[k]))
            asks[-1].start()
        supply.ticks(INNER, 0, supply.count - 1)
        supply.begin(OUTER)
        supply.ticks(INNER, supply.count - 1, supply.count)
        supply.finish(INNER)
        supply.ticks(OUTER, 0, supply.count)
        supply.finish(OUTER)

        @pl.loop(0, tensor)
        def _(tt):
            def body(at, k):
                r.ff[tensor + tt, rows : 2 * rows, at] = nn(r.d_branch[0:rows, :], r.outer[tt, :, at]).astype(BF16)

            columns_of(units, body)

        supply.close()
        drain.free(0)
        r.resid_top[0:rows, :] = r.resid_mid[0:rows, :]
        for k in range(CORES):
            move(r.cross_in.at[k], r.cross_in.at[k], 4 + k, 4 + k, across[k]).wait_recv()
            r.joined[:, lane_halves[k]] = r.cross_in[k]
        project_back(r.joined, r.square.at[SECOND], r.resid_top, rows, False)
        normalize(r.resid_top, r.gains[2:3, :], r.second, rows)
        feed_forward(rows, None)
        feed_back(rows, True, None)
        r.d_resid[0:rows, :] = r.d_branch[0:rows, :].astype(F32)
        normalize_back(r.resid_top, r.gains[2:3, :], r.summed, r.d_resid, r.gain_parts, rows, False)
        gain_done(2)
        to_bf16(r.d_resid, r.branch, rows)
        project(r.branch, r.square.at[SECOND], r.d_pair.at[0], rows)
        tells = []
        for k in range(CORES):
            r.send_back[k] = r.d_pair[0, 0:rows, lane_halves[k]]
            tells.append(move(r.send_back.at[k], part_here(r.cross_back), 6 + k, 6 + c, across[k]))
            tells[-1].start()
        feed_out(r.resid_top, rows, None)
        drain.free(1)
        to_bf16(r.resid_top, r.rows_out, rows)
        turn(r.d_branch, r.turned, rows)
        drain.allow(0)
        feed_grads(rows, r.turned, 0, OUTER, nothing)
        drain.begin(OUTER)
        turn(r.second, r.turned, rows)
        drain.allow(1)
        feed_grads(rows, r.turned, tensor, INNER, lambda tt, k: drain.tick(OUTER, tt, k == 0))
        turn(r.branch, r.turned, rows)
        turn(r.third, r.turned_more, rows)
        drain.ticks(OUTER, tensor, drain.count)
        drain.begin(INNER)
        drain.end(OUTER)
        for k in range(CORES):
            move(r.cross_in_back.at[k], r.cross_in_back.at[k], 8 + k, 8 + k, across[k]).wait_recv()
            r.d_pair[1, 0:rows, lane_halves[k]] = r.cross_in_back[k]
        project_back(r.d_pair.at[1], r.square.at[FIRST], r.summed, rows, True)
        drain.tick(INNER, 0)
        normalize_back(r.resid_mid, r.gains[1:2, :], r.summed, r.d_resid, r.gain_parts, rows, False)
        gain_done(1)
        drain.tick(INNER, 1)
        square_grads(
            rows, CROSS, [(r.turned_more, r.d_pair.at[1]), (r.turned, r.joined)], lambda k: drain.tick(INNER, 2 + k)
        )
        drain.ticks(INNER, 2 + tensor // 2, drain.count)
        drain.begin(CROSS)
        drain.end(INNER)
        for copy in asks + tells:
            copy.wait_send()

        def send_rows():
            to_bf16(r.d_resid, r.rows_out.at[pl.ds(rows, rows)], rows)
            drain.home()

        self_backward(span, rows, first_row, CROSS, send_rows)

    drain.close()


def held(*shape, dtype=BF16):
    return pltpu.VMEM(shape, dtype)


def arrays(tensor, heads_at, places, width, units, ranges, kinds):
    tall = 2 * tensor * places
    block = width // tensor
    half_rows, half_width = tall // 2, width // 2
    heads = heads_at * tensor
    return dict(
        x=held(2, tensor, places, width),
        own_x=held(half_rows, width),
        raw_a=held(tensor, width, 4 * block),
        raw_c=held(tensor, width, 2 * block),
        square=held(6, width, width),
        inner=held(tensor, width, units),
        outer=held(tensor, width, units),
        hidden=held(tall, width),
        keys=held(tall, width),
        values=held(tall, width),
        queries=held(half_rows, width),
        probs=held(heads, tall, half_rows),
        mask=held(tall, half_rows, dtype=F32),
        mixture=held(half_rows, width),
        resid_mid=held(half_rows, width, dtype=F32),
        resid_top=held(half_rows, width, dtype=F32),
        d_resid=held(half_rows, width, dtype=F32),
        summed=held(half_rows, width, dtype=F32),
        second=held(half_rows, width),
        third=held(half_rows, width),
        ff=held(2 * tensor, half_rows, units),
        d_branch=held(half_rows, width),
        branch=held(half_rows, width),
        cross_keys=held(tall, half_width),
        cross_values=held(tall, half_width),
        cross_queries=held(half_rows, half_width),
        cross_mixture=held(half_rows, half_width),
        cross_probs=held(heads // CORES, tall, half_rows),
        cross_back=held(half_rows, half_width),
        cross_in=held(CORES, half_rows // 2, half_width),
        cross_in_back=held(CORES, half_rows // 2, half_width),
        cross_taken=held(CORES, half_rows, half_width),
        send_pair=held(CORES, half_rows, half_width),
        send_back=held(CORES, half_rows // 2, half_width),
        joined=held(half_rows // 2, width),
        taken_pair=held(2, half_rows, width),
        d_pair=held(2, half_rows, width),
        turned=held(width, half_rows),
        turned_more=held(width, half_rows),
        stage=held(2, width, units),
        vectors=held(8 * tensor, ranges, dtype=F32),
        diagonals=held(8 * tensor, ranges, dtype=F32),
        onehot=held(kinds, ranges, dtype=F32),
        gain_parts=held(8, width, dtype=F32),
        send_sem=pltpu.SemaphoreType.DMA((14,)),
        recv_sem=pltpu.SemaphoreType.DMA((14,)),
    )


def group_columns(block, units):
    return {ATTN: (0, 4 * block), CROSS: (4 * block, 2 * block), INNER: (6 * block, units), OUTER: (6 * block + units, units)}


def landing(r):
    return {ATTN: r.raw_a, CROSS: r.raw_c, INNER: r.inner, OUTER: r.outer}


class Loads:
    count = 7

    def __init__(self, r, tensor, x_hbm, w_hbm, sems):
        columns = group_columns(r.raw_a.shape[2] // 4, r.inner.shape[2])
        self.x = pltpu.make_async_copy(x_hbm, r.x, sems.at[4, 0])
        self.weights = [
            [
                pltpu.make_async_copy(w_hbm.at[tt, :, pl.ds(*columns[group])], target.at[tt], sems.at[group, tt])
                for tt in range(tensor)
            ]
            for group, target in landing(r).items()
        ]

    def start(self):
        self.x.start()
        for group in self.weights:
            for copy in group:
                copy.start()

    def rows(self):
        self.x.wait()

    def finish(self, group):
        for copy in self.weights[group]:
            copy.wait()

    small = begin = tick = ticks = close = nothing


class Stores:
    count = 5

    def __init__(self, r, grads_hbm, sems):
        self.columns = group_columns(r.raw_a.shape[2] // 4, r.inner.shape[2])
        self.r, self.grads, self.sems = r, grads_hbm, sems

    def copy(self, group, tt, slot):
        first, wide = self.columns[group]
        return pltpu.make_async_copy(
            self.r.stage.at[slot, :, pl.ds(0, wide)], self.grads.at[tt, :, pl.ds(first, wide)], self.sems.at[slot]
        )

    def emit(self, group, tt, slot):
        self.copy(group, tt, slot).start()

    def release(self, group, tt, slot):
        self.copy(group, tt, slot).wait()

    free = allow = begin = tick = ticks = end = home = small_begin = close = nothing


def blocks_kernel(tensor, dp, heads_at, names, *refs):
    here = Place(tensor, dp)
    r = types.SimpleNamespace(**dict(zip(names, refs)))
    across = [{"pipe": 1 - here.pipe, "dp": here.group * CORES + k} for k in range(CORES)]
    meet([here.sibling()] + across)
    work(r, here, Loads(r, tensor, r.x_hbm, r.w_hbm, r.load_sem), Stores(r, r.grads_hbm, r.stage_sem), tensor, heads_at)


def blocks(tensor, dp, heads_at, kinds, rows, weights, gains, lengths, tables, buckets):
    places, width = rows.shape[2:]
    units = (weights.shape[2] - 6 * (width // tensor)) // 2
    half_rows = tensor * places
    scratch = arrays(tensor, heads_at, places, width, units, buckets.shape[1], kinds)
    scratch["load_sem"] = pltpu.SemaphoreType.DMA((5, tensor))
    scratch["stage_sem"] = pltpu.SemaphoreType.DMA((2,))
    names = ["x_hbm", "w_hbm", "gains", "lengths", "tables", "buckets", "grads_hbm", "rows_out", "gains_out", "bias_out"]
    return pl.pallas_call(
        functools.partial(blocks_kernel, tensor, dp, heads_at, names + list(scratch)),
        out_shape=(
            jax.ShapeDtypeStruct(weights.shape, BF16),
            jax.ShapeDtypeStruct((half_rows, width), BF16),
            jax.ShapeDtypeStruct((8, width), F32),
            jax.ShapeDtypeStruct((8 * tensor, LANES), F32),
        ),
        in_specs=[ANY, ANY] + [VMEM] * 4,
        out_specs=(ANY, VMEM, VMEM, VMEM),
        scratch_shapes=list(scratch.values()),
        compiler_params=pltpu.CompilerParams(collective_id=2, has_side_effects=True, vmem_limit_bytes=VMEM_LIMIT),
        name="blocks",
    )(rows, weights, gains, lengths, tables, buckets)


class Rings:
    def __init__(self, r, here, tensor, dp):
        self.r, self.here, self.tensor, self.dp = r, here, tensor, dp
        self.depth = r.value_w.shape[0]
        self.hops = here.chips // 2
        self.count = 2 * self.hops - 1
        self.sibling = here.sibling()
        self.targets = [here.neighbour(1), here.neighbour(-1)]
        self.landing = landing(r)


    def block_out(self, i):
        r, t, c = self.r, self.here.t, self.here.core
        return pltpu.make_async_remote_copy(
            r.rows.at[i], r.x.at[:, t], r.block_send.at[i], r.block_recv.at[t],
            device_id={"tensor": r.rows.shape[0] * c + i}, device_id_type=MESH,
        )

    def block_kept(self, i):
        return pltpu.make_async_copy(self.r.rows.at[i], self.r.x.at[:, self.here.t], self.r.local_sem.at[0])

    def block_pass(self, source, s):
        r = self.r
        return pltpu.make_async_remote_copy(
            source, r.x.at[:, s], r.pass_send.at[s], r.pass_recv.at[s], device_id=self.sibling, device_id_type=MESH
        )

    def blocks(self, mine, others):
        for i in range(self.r.rows.shape[0]):
            here = self.r.rows.shape[0] * self.here.core + i == self.here.t

            @pl.when(here)
            def _():
                mine(i)

            @pl.when(jnp.logical_not(here))
            def _():
                others(i)

    def small_copies(self):
        r, t = self.r, self.here.t
        copies = [
            pltpu.make_async_remote_copy(
                r.lengths_in, r.lengths.at[self.here.core], r.small_send.at[0], r.small_recv.at[0],
                device_id=self.sibling, device_id_type=MESH,
            ),
            pltpu.make_async_copy(r.lengths_in, r.lengths.at[self.here.core], r.local_sem.at[1]),
            pltpu.make_async_copy(r.table_in, r.tables.at[t], r.local_sem.at[2]),
        ]
        for k in range(1, self.tensor):
            copies.append(
                pltpu.make_async_remote_copy(
                    r.table_in, r.tables.at[t], r.small_send.at[k], r.small_recv.at[k],
                    device_id={"tensor": lax.rem(t + k, self.tensor)}, device_id_type=MESH,
                )
            )
        return copies


    def slot(self, group, ring, sub):
        line, at = self.here.at(ring)
        half = self.depth // 2
        first = pl.multiple_of((line * CORES + self.here.core) * self.depth + half * sub, 16)
        return self.landing[group].at[at, pl.ds(first, half), :]

    def packed(self, group, sub):
        half = self.depth // 2
        wide = self.landing[group].shape[2]
        return self.r.stage.at[0, pl.ds(group * self.depth + half * sub, half), pl.ds(0, wide)]

    def copies(self, group, step, part, sub, first=False):
        r, here = self.r, self.here
        way = -1 if part else 1
        slot = self.slot(group, lax.rem(here.ring - way * step + here.chips, here.chips), sub)
        source = self.packed(group, sub) if first else slot
        onward = lambda: pltpu.make_async_remote_copy(
            source, slot, r.ring_send.at[group, part, sub, step], r.ring_recv.at[group, part, sub, step],
            device_id=self.targets[part], device_id_type=MESH,
        )
        over = lambda: pltpu.make_async_remote_copy(
            source, slot, r.core_send.at[group, part, sub, step], r.core_recv.at[group, part, sub, step],
            device_id=self.sibling, device_id_type=MESH,
        )
        return onward, over

    def own(self, group):
        wide = self.landing[group].shape[2]
        first = pl.multiple_of(self.here.d * self.depth, 16)
        return pltpu.make_async_copy(
            self.r.stage.at[0, pl.ds(group * self.depth, self.depth), pl.ds(0, wide)],
            self.landing[group].at[self.here.t, pl.ds(first, self.depth), :],
            self.r.own_sem.at[group],
        )

    def begin(self, group):
        for sub in range(2):
            for part in range(2):
                onward, over = self.copies(group, 0, part, sub, True)
                onward().start()
                if part == 0:
                    over().start()
        self.own(group).start()

    def tick(self, group, n):
        last = lax.div(n, self.count - 1)
        step = lax.div(n, 2) + 1
        for part in range(2):
            sub = lax.rem(n, 2) + last * part
            self.copies(group, step - 1, part, sub)[0]().wait_recv()
            onward, over = self.copies(group, step, part, sub)
            goes = jnp.logical_or(step < self.hops - 1, jnp.logical_and(step == self.hops - 1, sub == part))

            @pl.when(goes)
            def _():
                onward().start()

            over().start()

    def ticks(self, group, first, last):
        if first < last:

            @pl.loop(first, last)
            def _(n):
                self.tick(group, n)

    def finish(self, group):
        self.each_over(group, lambda copy: copy.wait_recv())
        self.own(group).wait()

    def each_over(self, group, do):
        for sub in range(2):
            do(self.copies(group, 0, 0, sub)[1]())
            do(self.copies(group, self.hops, sub, sub)[1]())

        @pl.loop(1, self.hops)
        def _(step):
            for part in range(2):
                for sub in range(2):
                    do(self.copies(group, step, part, sub)[1]())

    def start(self):
        r, depth = self.r, self.depth
        self.blocks(
            lambda i: (self.block_kept(i).start(), self.block_pass(r.rows.at[i], self.here.t).start()),
            lambda i: self.block_out(i).start(),
        )
        block = r.value_w.shape[1]

        def band(group, pieces):
            wide = pieces[0].shape[1]
            for k, piece in enumerate(pieces):
                r.stage[0, group * depth : (group + 1) * depth, k * wide : (k + 1) * wide] = piece

        band(ATTN, [r.query_key_w[1], r.value_w[...], r.query_key_w[0], r.out_w[...].T])
        self.begin(ATTN)
        for copy in self.small_copies():
            copy.start()
        band(INNER, [r.inner_w[...]])
        band(OUTER, [r.outer_w[...].T])
        band(CROSS, [r.first_w[...], r.second_w[...]])

    def small(self):
        for copy in self.small_copies():
            copy.wait()

    def rows(self):
        r, t = self.r, self.here.t
        takes = lax.div(t, r.rows.shape[0]) == self.here.core
        for s in range(self.tensor):

            @pl.when(jnp.logical_and(takes, s != t))
            def _():
                pltpu.make_async_remote_copy(
                    r.rows.at[0], r.x.at[:, s], r.block_send.at[0], r.block_recv.at[s],
                    device_id=self.sibling, device_id_type=MESH,
                ).wait_recv()
                self.block_pass(r.x.at[:, s], s).start()

        self.blocks(lambda i: self.block_kept(i).wait(), nothing)
        for s in range(self.tensor):

            @pl.when(jnp.logical_not(takes))
            def _():
                self.block_pass(r.x.at[:, s], s).wait_recv()

    def close(self):
        r, t = self.r, self.here.t
        takes = lax.div(t, r.rows.shape[0]) == self.here.core
        self.blocks(
            lambda i: self.block_pass(r.rows.at[i], t).wait_send(),
            lambda i: self.block_out(i).wait_send(),
        )
        for s in range(self.tensor):

            @pl.when(jnp.logical_and(takes, s != t))
            def _():
                self.block_pass(r.x.at[:, s], s).wait_send()

        for group in (ATTN, CROSS, INNER, OUTER):
            self.each_over(group, lambda copy: copy.wait_send())

            @pl.loop(0, self.hops - 1)
            def _(step):
                for part in range(2):
                    for sub in range(2):
                        self.copies(group, step, part, sub)[0]().wait_send()

            for part in range(2):
                self.copies(group, self.hops - 1, part, part)[0]().wait_send()


class Sums:
    def __init__(self, r, here, tensor, dp):
        self.r, self.here, self.tensor, self.dp = r, here, tensor, dp
        self.depth = r.value_w.shape[0]
        self.hops = here.chips // 2
        self.count = 2 * self.hops - 3
        self.sibling = here.sibling()
        self.targets = [here.neighbour(1), here.neighbour(-1)]
        self.box = {CROSS: r.raw_c, OUTER: r.raw_a, INNER: r.inner, ATTN: r.outer}
        self.kept = {CROSS: r.own_cross, OUTER: r.own_outer, INNER: r.own_inner, ATTN: r.ff}

    def free(self, k):
        for device in self.targets + [self.sibling]:
            pl.semaphore_signal(self.r.free_sem.at[k], inc=1, device_id=device, device_id_type=MESH)

    def allow(self, k):
        pl.semaphore_wait(self.r.free_sem.at[k], 3)

    def boxed(self, group, index, first, height):
        at = pl.ds(pl.multiple_of(lax.rem(index, self.dp) * self.depth + first, 16), height)
        return (lax.div(index, self.dp), at, slice(None))

    def taken(self, group, step, part, first, height):
        index = 0 if isinstance(step, int) and step == 0 else step + part * (self.hops - 1) * jnp.minimum(step, 1)
        return self.boxed(group, index, first, height)

    def theirs(self, group, ring, first, height):
        return self.boxed(group, self.here.chips - 1 + ring, first, height)

    def own(self, group, ring, first, height):
        return (ring, pl.ds(first, height), slice(None))

    def ring_of(self, line, at):
        return line * self.tensor + at + (line % 2) * (self.tensor - 1 - 2 * at)

    def pieces(self, group, tt, slot):
        r, depth = self.r, self.depth
        wide = self.box[group].shape[2]
        made = []
        for line in range(self.here.groups):
            ring = self.ring_of(line, tt)

            def rows_of(core):
                return r.stage.at[slot, pl.ds(pl.multiple_of((line * CORES + core) * depth, 16), depth), pl.ds(0, wide)]

            made.append(
                pltpu.make_async_copy(
                    rows_of(self.here.core), self.kept[group].at[self.own(group, ring, 0, depth)], r.kept_sem.at[group, ring]
                )
            )
            made.append(
                pltpu.make_async_remote_copy(
                    rows_of(1 - self.here.core), self.box[group].at[self.theirs(group, ring, 0, depth)],
                    r.pair_send.at[group, ring], r.pair_recv.at[group, ring], device_id=self.sibling, device_id_type=MESH,
                )
            )
        return made

    def emit(self, group, tt, slot):
        for piece in self.pieces(group, tt, slot):
            piece.start()

    def release(self, group, tt, slot):
        for k, piece in enumerate(self.pieces(group, tt, slot)):
            if k % 2:
                piece.wait_send()
            else:
                piece.wait()


    def rows_at(self, sub):
        half = self.depth // 2
        return pl.multiple_of(half * sub, 16), half

    def source(self, step, part):
        way = -1 if part else 1
        return lax.rem(self.here.ring + way * (self.hops - step) + self.here.chips, self.here.chips)

    def onward(self, group, step, part, sub):
        r = self.r
        first, height = self.rows_at(sub)
        return pltpu.make_async_remote_copy(
            self.kept[group].at[self.own(group, self.source(step, part), first, height)],
            self.box[group].at[self.taken(group, step, part, first, height)],
            r.sum_send.at[group, part, sub, step], r.sum_recv.at[group, part, sub, step],
            device_id=self.targets[part], device_id_type=MESH,
        )

    def here_sum(self, group, ring, first, height):
        value = self.kept[group][self.own(group, ring, first, height)].astype(F32)
        return value + self.box[group][self.theirs(group, ring, first, height)].astype(F32)

    def advance(self, group, step, part, sub, fresh=False):
        if not fresh:
            self.onward(group, step - 1, part, sub).wait_recv()
        first, height = self.rows_at(sub)
        value = self.here_sum(group, self.source(step, part), first, height)
        if not fresh:
            value = value + self.box[group][self.taken(group, step - 1, part, first, height)].astype(F32)
        self.kept[group][self.own(group, self.source(step, part), first, height)] = value.astype(BF16)
        self.onward(group, step, part, sub).start()

    def begin(self, group):
        @pl.loop(0, self.here.chips)
        def _(ring):
            pltpu.make_async_remote_copy(
                self.kept[group].at[self.own(group, ring, 0, self.depth)],
                self.box[group].at[self.theirs(group, ring, 0, self.depth)],
                self.r.pair_send.at[group, ring], self.r.pair_recv.at[group, ring], device_id=self.sibling, device_id_type=MESH,
            ).wait_recv()

        for part in range(2):
            self.advance(group, 0, part, part, True)
        for part in range(2):
            self.advance(group, 1, part, 1 - part, True)
        if group == ATTN:
            self.small_across().wait_recv()
            self.small_advance(0, 0, True)
            self.small_advance(1, 1, True)

    def tick(self, group, n, when=True):
        step, leads = lax.div(n + 1, 2) + 1, lax.rem(n, 2)

        @pl.when(when)
        def _():
            for part in range(2):
                self.advance(group, step, part, (1 - part) * leads + part * (1 - leads))
            if group == ATTN:

                @pl.when(leads == 0)
                def _():
                    self.small_advance(step, 0)

                    @pl.when(step > 1)
                    def _():
                        self.small_advance(step, 1)

    def ticks(self, group, first, last):
        if first < last:

            @pl.loop(first, last)
            def _(n):
                self.tick(group, n)

    def end(self, group):
        r, last = self.r, self.hops - 1
        for sub in range(2):
            first, height = self.rows_at(sub)
            value = self.here_sum(group, self.here.ring, first, height)
            for part in range(2):
                self.onward(group, last, part, sub).wait_recv()
                value = value + self.box[group][self.taken(group, last, part, first, height)].astype(F32)
            target = r.inner_out if group == INNER else r.total
            target[pl.ds(first, height), 0 : self.box[group].shape[2]] = value
        block = r.value_w.shape[1]
        if group == ATTN:
            r.pair_out[1] = r.total[:, 0:block]
            r.value_out[...] = r.total[:, block : 2 * block]
            r.pair_out[0] = r.total[:, 2 * block : 3 * block]
            r.out_out[...] = r.total[:, 3 * block : 4 * block].T
            at = self.small_at(self.here.ring)
            value = r.small[at] + r.small_theirs[at]
            for part in range(2):
                self.small_onward(last, part).wait_recv()
                value = value + r.small_taken[part, last]
            r.tiny_out[...] = value
        if group == CROSS:
            r.first_out[...] = r.total[:, 0:block]
            r.second_out[...] = r.total[:, block : 2 * block]
        if group == OUTER:
            r.outer_out[...] = r.total[...].T


    def small_at(self, ring):
        line, at = self.here.at(ring)
        return at, line * CORES + self.here.core

    def small_across(self):
        r = self.r
        return pltpu.make_async_remote_copy(
            r.small, r.small_theirs, r.small_sem.at[0], r.small_sem.at[1], device_id=self.sibling, device_id_type=MESH
        )

    def small_onward(self, step, part):
        r = self.r
        return pltpu.make_async_remote_copy(
            r.small_sent.at[part, step], r.small_taken.at[part, step], r.tiny_send.at[part, step], r.tiny_recv.at[part, step],
            device_id=self.targets[part], device_id_type=MESH,
        )

    def small_advance(self, step, part, fresh=False):
        at = self.small_at(self.source(step, part))
        value = self.r.small[at] + self.r.small_theirs[at]
        if not fresh:
            self.small_onward(step - 1, part).wait_recv()
            value = value + self.r.small_taken[part, step - 1]
        self.r.small_sent[part, step] = value
        self.small_onward(step, part).start()

    def small_begin(self):
        r, depth = self.r, self.depth
        r.small[...] = jnp.zeros_like(r.small)
        kinds = r.onehot.shape[0] // self.dp
        heads_at = self.heads_at
        for tt in range(self.tensor):
            for d in range(self.dp):
                r.small[tt, d, 0:3, 0:depth] = r.gains_out[0:3, d * depth : (d + 1) * depth]
                r.small[tt, d, 3 : 3 + heads_at, 0:kinds] = r.bias_out[
                    8 * tt : 8 * tt + heads_at, d * kinds : (d + 1) * kinds
                ]
        self.small_across().start()


    def home_copy(self, k):
        r, here, tensor = self.r, self.here, self.tensor
        nrow, half, places = r.home_in.shape[0], tensor // 2, r.home_in.shape[2]
        place = here.pipe * (here.core * half + k % half) + (1 - here.pipe) * k
        which = here.pipe * (k // half) + (1 - here.pipe) * here.core
        owner = lax.div(here.t, nrow)
        source = r.rows_out.at[pl.ds(k * places, places)]
        slot = r.home_in.at[lax.rem(here.t, nrow), which]
        recv = r.home_recv.at[lax.rem(here.t, nrow), which]
        return (
            jnp.logical_and(place == here.t, owner == here.core),
            lambda: pltpu.make_async_copy(source, slot, recv),
            lambda: pltpu.make_async_remote_copy(
                source, slot, r.home_send.at[k], recv,
                device_id={"dp": here.group * CORES + owner, "tensor": place}, device_id_type=MESH,
            ),
        )

    def home(self):
        for k in range(self.tensor):
            stays, inside, away = self.home_copy(k)

            @pl.when(stays)
            def _():
                inside().start()

            @pl.when(jnp.logical_not(stays))
            def _():
                away().start()

    def close(self):
        r = self.r
        places = r.home_in.shape[2]
        for i in range(r.home_in.shape[0]):
            for which in range(2):
                pltpu.make_async_copy(
                    r.rows_out.at[pl.ds(0, places)], r.home_in.at[i, which], r.home_recv.at[i, which]
                ).wait()
                r.home_out[i, which] = r.home_in[i, which].astype(F32)
        for k in range(self.tensor):
            stays, inside, away = self.home_copy(k)

            @pl.when(jnp.logical_not(stays))
            def _():
                away().wait_send()

        self.small_across().wait_send()

        for part in range(2):
            self.small_onward(0 + part, part).wait_send()
            for group in (ATTN, CROSS, INNER, OUTER):
                self.onward(group, 0, part, part).wait_send()
                self.onward(group, 1, part, 1 - part).wait_send()
                self.onward(group, 1, part, part).wait_send()
        self.small_onward(1, 0).wait_send()

        @pl.loop(2, self.hops)
        def _(step):
            for part in range(2):
                self.small_onward(step, part).wait_send()
                for group in (ATTN, CROSS, INNER, OUTER):
                    for sub in range(2):
                        self.onward(group, step, part, sub).wait_send()


def fits_fused(tensor, dp, depth, units, width):
    chips = tensor * dp // CORES
    return (
        depth % 32 == 0
        and 4 * depth <= width
        and chips <= 2 * tensor
        and chips == 2 * tensor == 8
        and units == width == 6 * LANES
    )


def fused_kernel(tensor, dp, heads_at, names, *refs):
    here = Place(tensor, dp)
    r = types.SimpleNamespace(**dict(zip(names, refs)))
    line = [
        {"dp": here.group * CORES + lax.rem(here.core + j, CORES), "tensor": lax.rem(here.t + k, tensor)}
        for j in range(CORES)
        for k in range(tensor)
        if j + k > 0
    ]
    across = [{"pipe": 1 - here.pipe, "dp": here.group * CORES + k} for k in range(CORES)]
    meet([here.neighbour(1), here.neighbour(-1)] + line + across)
    supply, drain = Rings(r, here, tensor, dp), Sums(r, here, tensor, dp)
    drain.heads_at = heads_at
    work(r, here, supply, drain, tensor, heads_at)


def fused(tensor, dp, heads_at, kinds, rows, lengths, table, gains, buckets, weights):
    nrow, two, places, width = rows.shape
    depth, block = weights[1].shape
    units = weights[5].shape[1]
    chips = tensor * dp // CORES
    wide = -(-max(depth, kinds // dp) // LANES) * LANES
    sems = pltpu.SemaphoreType.DMA
    scratch = arrays(tensor, heads_at, places, width, units, buckets.shape[1], kinds)
    scratch.update(
        lengths=pltpu.VMEM((CORES,) + lengths.shape, lengths.dtype),
        tables=pltpu.VMEM((tensor,) + table.shape, table.dtype),
        own_cross=held(chips, depth, 2 * block),
        own_outer=held(chips, depth, units),
        own_inner=held(chips, depth, units),
        total=held(depth, units, dtype=F32),
        rows_out=held(tensor * places, width),
        gains_out=held(8, width, dtype=F32),
        bias_out=held(8 * tensor, LANES, dtype=F32),
        home_in=held(nrow, two, places, width),
        small=held(tensor, dp, 8, wide, dtype=F32),
        small_theirs=held(tensor, dp, 8, wide, dtype=F32),
        small_sent=held(2, chips // 2, 8, wide, dtype=F32),
        small_taken=held(2, chips // 2, 8, wide, dtype=F32),
        block_send=sems((nrow,)), block_recv=sems((tensor,)), pass_send=sems((tensor,)), pass_recv=sems((tensor,)),
        local_sem=sems((3,)), small_send=sems((tensor,)), small_recv=sems((tensor,)), own_sem=sems((4,)),
        ring_send=sems((4, 2, 2, chips)), ring_recv=sems((4, 2, 2, chips)),
        core_send=sems((4, 2, 2, chips)), core_recv=sems((4, 2, 2, chips)),
        kept_sem=sems((4, chips)), pair_send=sems((4, chips)), pair_recv=sems((4, chips)),
        sum_send=sems((4, 2, 2, chips)), sum_recv=sems((4, 2, 2, chips)),
        small_sem=sems((2,)), tiny_send=sems((2, chips // 2)), tiny_recv=sems((2, chips // 2)),
        home_send=sems((tensor,)), home_recv=sems((nrow, two)),
        free_sem=pltpu.SemaphoreType.REGULAR((2,)),
    )
    inputs = ["rows", "lengths_in", "table_in", "gains", "buckets"]
    inputs += ["query_key_w", "value_w", "out_w", "first_w", "second_w", "inner_w", "outer_w"]
    outputs = dict(
        home_out=rows.shape, tiny_out=(8, wide), pair_out=(2, depth, block), value_out=(depth, block),
        out_out=(block, depth), first_out=(depth, block), second_out=(depth, block), inner_out=(depth, units),
        outer_out=(units, depth),
    )
    return pl.pallas_call(
        functools.partial(fused_kernel, tensor, dp, heads_at, inputs + list(outputs) + list(scratch)),
        out_shape=tuple(jax.ShapeDtypeStruct(shape, F32) for shape in outputs.values()),
        in_specs=[ANY] + [VMEM] * 11,
        out_specs=(VMEM,) * len(outputs),
        scratch_shapes=list(scratch.values()),
        compiler_params=pltpu.CompilerParams(collective_id=3, has_side_effects=True, vmem_limit_bytes=VMEM_LIMIT),
        name="fused",
    )(rows, lengths, table, gains, buckets, *weights)


def pad_to(array, *shape):
    return jnp.pad(array, [(0, full - have) for full, have in zip(shape, array.shape)])


def shards(
    tensor, dp, section_rows, enc_lengths, dec_lengths, enc_buckets, dec_buckets, norm_gains, rel_bias,
    query_key_w, value_w, attn_out_w, cross_first, cross_second, ff_in, ff_out,
):
    nrow = section_rows.shape[1]
    depth, block = value_w.shape[1:]
    kinds, heads_at = rel_bias.shape[1:]
    on_encoder = lax.axis_index("pipe") == 0
    lengths = pad_to(jnp.concatenate([enc_lengths, dec_lengths], axis=0), 8, LANES)
    table = pad_to(rel_bias[0].T, 8, LANES)
    ranges = -(-enc_buckets.shape[0] // LANES) * LANES
    dec_all = jnp.concatenate([jnp.zeros((dec_buckets.shape[0] - 1,), jnp.int32), dec_buckets])
    bucket_row = jnp.where(on_encoder, pad_to(enc_buckets, ranges), pad_to(dec_all, ranges))
    bucket_rows = jnp.broadcast_to(bucket_row[None], (8, ranges))
    width = section_rows.shape[-1]
    gains = pad_to(norm_gains[0], 8, width)
    held_kinds = kinds // dp
    weights = (query_key_w[0], value_w[0], attn_out_w[0], cross_first[0], cross_second[0], ff_in[0], ff_out[0])
    if fits_fused(tensor, dp, depth, ff_in.shape[2], width):
        home, tiny, pair, value, out, first, second, inner, outer = fused(
            tensor, dp, heads_at, kinds, section_rows[0], lengths, table, gains, bucket_rows, weights
        )
        grads = (pair, value, out, first, second, inner, outer)
    else:
        home, tiny, grads = in_three(
            tensor, dp, heads_at, kinds, section_rows[0], lengths, table, gains, bucket_rows, weights
        )
    return (
        home.astype(F32)[None],
        tiny[:3, :depth][None],
        tiny[3 : 3 + heads_at, :held_kinds].T[None],
    ) + tuple(grad[None] for grad in grads)


def in_three(tensor, dp, heads_at, kinds, section_rows, lengths, table, gains, buckets, weights):
    query_key, value, out, first, second, inner, outer = weights
    nrow, _, _, width = section_rows.shape
    depth, block = value.shape
    units = inner.shape[1]
    pack = jnp.concatenate([query_key[1], value, query_key[0], out.T, first, second, inner, outer.T], axis=1)
    rows, gathered, lengths, tables = gather(tensor, dp, section_rows, pack, lengths, table)
    grads, finished, gain_grads, bias = blocks(
        tensor, dp, heads_at, kinds, rows, gathered.reshape(tensor, width, -1), gains, lengths, tables, buckets
    )
    held_kinds = kinds // dp
    wide = -(-max(depth, held_kinds) // LANES) * LANES
    gain_part = pad_to(gain_grads[:3].reshape(3, dp, depth).transpose(1, 0, 2), dp, 3, wide)
    bias_part = bias.reshape(tensor, 8, LANES)[:, :heads_at, :kinds].reshape(tensor, heads_at, dp, held_kinds)
    bias_part = pad_to(bias_part.transpose(0, 2, 1, 3), tensor, dp, 5, wide)
    small = jnp.concatenate([jnp.broadcast_to(gain_part[None], (tensor,) + gain_part.shape), bias_part], axis=2)
    total, tiny, home = scatter(
        tensor, dp, grads.reshape(tensor, dp, depth, -1), small, finished.reshape(tensor, -1, width), nrow
    )
    key, value, query, out, first, second = [total[:, k * block : (k + 1) * block] for k in range(6)]
    inner, outer = total[:, 6 * block : 6 * block + units], total[:, 6 * block + units :]
    return home, tiny, (jnp.stack([query, key]), value, out.T, first, second, inner, outer.T)


def solution(mesh):
    sizes = dict(mesh.shape)
    return jax.shard_map(
        functools.partial(shards, sizes["tensor"], sizes["dp"]),
        mesh=mesh,
        in_specs=(
            P("pipe", "dp", None, "tensor", None),
            P("dp", None),
            P("dp", None),
            P(),
            P(),
            P("pipe", None, None),
            P("pipe", None, "tensor"),
            P("pipe", None, "dp", "tensor"),
            P("pipe", "dp", "tensor"),
            P("pipe", "tensor", "dp"),
            P("pipe", "dp", "tensor"),
            P("pipe", "dp", "tensor"),
            P("pipe", "dp", "tensor"),
            P("pipe", "tensor", "dp"),
        ),
        out_specs=(
            P("pipe", "dp", None, "tensor", None),
            P("pipe", None, "dp"),
            P("pipe", "dp", "tensor"),
            P("pipe", None, "dp", "tensor"),
            P("pipe", "dp", "tensor"),
            P("pipe", "tensor", "dp"),
            P("pipe", "dp", "tensor"),
            P("pipe", "dp", "tensor"),
            P("pipe", "dp", "tensor"),
            P("pipe", "tensor", "dp"),
        ),
        check_vma=False,
    )
```

```python
import functools
import types

import jax
import jax.numpy as jnp
from jax import lax
from jax.experimental import pallas as pl
from jax.experimental.pallas import tpu as pltpu
from jax.sharding import PartitionSpec as P

MESH = pl.DeviceIdType.MESH
F32 = jnp.float32
BF16 = jnp.bfloat16
EPSILON = 1e-06
NEGATIVE = -1000000000.0
HEAD_DIM = 64
CORES = 2
LANES = 128
VMEM_LIMIT = 62 << 20
ANY = pl.BlockSpec(memory_space=pl.ANY)
VMEM = pl.BlockSpec(memory_space=pltpu.VMEM)


def nn(a, b):
    return lax.dot_general(a, b, (((1,), (0,)), ((), ())), preferred_element_type=F32)


def nt(a, b):
    return lax.dot_general(a, b, (((1,), (1,)), ((), ())), preferred_element_type=F32)


def tn(a, b):
    return lax.dot_general(a, b, (((0,), (0,)), ((), ())), preferred_element_type=F32)


class Place:
    def __init__(self, tensor, dp):
        self.tensor = tensor
        self.groups = dp // CORES
        self.chips = tensor * self.groups
        self.pipe = lax.axis_index("pipe")
        self.d = lax.axis_index("dp")
        self.t = lax.axis_index("tensor")
        self.core = lax.rem(self.d, CORES)
        self.group = self.d // CORES
        odd = lax.rem(self.group, 2)
        self.ring = self.group * tensor + self.t + odd * (tensor - 1 - 2 * self.t)

    def at(self, ring):
        group = ring // self.tensor
        along = lax.rem(ring, self.tensor)
        odd = lax.rem(group, 2)
        return group, along + odd * (self.tensor - 1 - 2 * along)

    def neighbour(self, step):
        group, t = self.at(lax.rem(self.ring + step + self.chips, self.chips))
        return {"dp": group * CORES + self.core, "tensor": t}

    def sibling(self):
        return {"dp": self.group * CORES + 1 - self.core}


def meet(devices):
    barrier = pltpu.get_barrier_semaphore()
    for device in devices:
        pl.semaphore_signal(barrier, inc=1, device_id=device, device_id_type=MESH)
    pl.semaphore_wait(barrier, len(devices))


def halves(rows, columns):
    if rows % 32 == 0:
        return [(pl.ds(k * (rows // 2), rows // 2), pl.ds(0, columns)) for k in range(2)]
    cut = columns // LANES // 2 * LANES
    return [(pl.ds(0, rows), pl.ds(0, cut)), (pl.ds(0, rows), pl.ds(cut, columns - cut))]


def gather_kernel(
    tensor, dp, rows_ref, pack_ref, length_ref, table_ref, x_ref, w_ref, lengths_ref, tables_ref,
    local_sem, block_send, block_recv, pass_send, pass_recv, small_send, small_recv,
    ring_send, ring_recv, core_send, core_recv,
):
    here = Place(tensor, dp)
    c, t, chips = here.core, here.t, here.chips
    nrow = rows_ref.shape[0]
    sibling = here.sibling()
    to_right, to_left = here.neighbour(1), here.neighbour(-1)
    others = [{"tensor": lax.rem(t + k, tensor)} for k in range(1, tensor)]
    meet([to_right, to_left, sibling] + others)

    lengths = pltpu.make_async_remote_copy(
        length_ref, lengths_ref.at[c], small_send.at[0], small_recv.at[0], device_id=sibling, device_id_type=MESH
    )
    lengths.start()
    own_lengths = pltpu.make_async_copy(length_ref, lengths_ref.at[c], local_sem.at[0])
    own_lengths.start()
    own_table = pltpu.make_async_copy(table_ref, tables_ref.at[t], local_sem.at[1])
    own_table.start()
    tables = []
    for k in range(1, tensor):
        tables.append(
            pltpu.make_async_remote_copy(
                table_ref, tables_ref.at[t], small_send.at[k], small_recv.at[k], device_id=others[k - 1], device_id_type=MESH
            )
        )
        tables[-1].start()

    def to_chip(i):
        return pltpu.make_async_remote_copy(
            rows_ref.at[i], x_ref.at[:, t], block_send.at[i], block_recv.at[t],
            device_id={"tensor": nrow * c + i}, device_id_type=MESH,
        )

    def kept(i):
        return pltpu.make_async_copy(rows_ref.at[i], x_ref.at[:, t], local_sem.at[2])

    def kept_pass(i):
        return pltpu.make_async_remote_copy(
            rows_ref.at[i], x_ref.at[:, t], pass_send.at[t], pass_recv.at[t], device_id=sibling, device_id_type=MESH
        )

    def passed(s):
        return pltpu.make_async_remote_copy(
            x_ref.at[:, s], x_ref.at[:, s], pass_send.at[s], pass_recv.at[s], device_id=sibling, device_id_type=MESH
        )

    for i in range(nrow):
        mine = nrow * c + i == t

        @pl.when(mine)
        def _():
            kept(i).start()
            kept_pass(i).start()

        @pl.when(jnp.logical_not(mine))
        def _():
            to_chip(i).start()

    parts = halves(*pack_ref.shape)
    own_pack = pltpu.make_async_copy(pack_ref, w_ref.at[t, here.d], local_sem.at[3])
    own_pack.start()

    def shard(ring, part):
        group, at = here.at(ring)
        return w_ref.at[at, group * CORES + c, parts[part][0], parts[part][1]]

    def source(step, part):
        return lax.rem(here.ring + (1 if part else -1) * step + chips, chips)

    def onward(step, part, first=False):
        slot = shard(source(step, part), part)
        return pltpu.make_async_remote_copy(
            pack_ref.at[parts[part][0], parts[part][1]] if first else slot, slot,
            ring_send.at[part, step], ring_recv.at[part, step],
            device_id=to_left if part else to_right, device_id_type=MESH,
        )

    def across(step, part, first=False):
        slot = shard(source(step, part), part)
        return pltpu.make_async_remote_copy(
            pack_ref.at[parts[part][0], parts[part][1]] if first else slot, slot,
            core_send.at[part, step], core_recv.at[part, step], device_id=sibling, device_id_type=MESH,
        )

    for part in range(2):
        onward(0, part, True).start()
        across(0, part, True).start()

    takes = t // nrow == c
    for s in range(tensor):

        @pl.when(jnp.logical_and(takes, s != t))
        def _():
            pltpu.make_async_remote_copy(
                rows_ref.at[0], x_ref.at[:, s], block_send.at[0], block_recv.at[s], device_id=sibling, device_id_type=MESH
            ).wait_recv()
            passed(s).start()

    @pl.loop(1, chips)
    def _(step):
        for part in range(2):
            onward(step - 1, part).wait_recv()

            @pl.when(step < chips - 1)
            def _():
                onward(step, part).start()

            across(step, part).start()

    @pl.loop(0, chips)
    def _(step):
        for part in range(2):

            @pl.when(step < chips - 1)
            def _():
                onward(step, part).wait_send()

            across(step, part).wait_send()
            across(step, part).wait_recv()

    for i in range(nrow):
        mine = nrow * c + i == t

        @pl.when(mine)
        def _():
            kept(i).wait()
            kept_pass(i).wait_send()

        @pl.when(jnp.logical_not(mine))
        def _():
            to_chip(i).wait_send()

    for s in range(tensor):

        @pl.when(jnp.logical_and(takes, s != t))
        def _():
            passed(s).wait_send()

        @pl.when(jnp.logical_not(takes))
        def _():
            passed(s).wait_recv()

    lengths.wait()
    own_lengths.wait()
    own_table.wait()
    own_pack.wait()
    for table in tables:
        table.wait()


def gather(tensor, dp, rows, pack, lengths, table):
    chips = tensor * dp // CORES
    nrow, two, places, width = rows.shape
    sems = pltpu.SemaphoreType.DMA
    return pl.pallas_call(
        functools.partial(gather_kernel, tensor, dp),
        out_shape=(
            jax.ShapeDtypeStruct((two, tensor, places, width), rows.dtype),
            jax.ShapeDtypeStruct((tensor, dp) + pack.shape, pack.dtype),
            jax.ShapeDtypeStruct((CORES,) + lengths.shape, lengths.dtype),
            jax.ShapeDtypeStruct((tensor,) + table.shape, table.dtype),
        ),
        in_specs=[ANY] * 4,
        out_specs=(ANY,) * 4,
        scratch_shapes=[
            sems((4,)), sems((nrow,)), sems((tensor,)), sems((tensor,)), sems((tensor,)), sems((tensor,)), sems((tensor,)),
            sems((2, chips)), sems((2, chips)), sems((2, chips)), sems((2, chips)),
        ],
        compiler_params=pltpu.CompilerParams(collective_id=0, has_side_effects=True),
        name="gather",
    )(rows, pack, lengths, table)


def scatter_kernel(
    tensor, dp, grads_ref, small_ref, rows_ref, out_ref, small_out, rows_out,
    own, theirs, taken, small_own, small_theirs, small_taken, total,
    own_sem, core_send, core_recv, ring_send, ring_recv,
    sown_sem, score_send, score_recv, sring_send, sring_recv, block_send, block_recv, local_sem,
):
    here = Place(tensor, dp)
    c, t, chips = here.core, here.t, here.chips
    nrow = rows_out.shape[0]
    sibling = here.sibling()
    to_right, to_left = here.neighbour(1), here.neighbour(-1)
    line = [
        {"dp": here.group * CORES + lax.rem(c + j, CORES), "tensor": lax.rem(t + k, tensor)}
        for j in range(CORES)
        for k in range(tensor)
        if j + k > 0
    ]
    meet([to_right, to_left] + line)

    half = tensor // 2
    owner = t // nrow

    def block(k):
        place = here.pipe * (c * half + k % half) + (1 - here.pipe) * k
        which = here.pipe * (k // half) + (1 - here.pipe) * c
        return place, which

    def home(k):
        place, which = block(k)
        slot = rows_out.at[lax.rem(t, nrow), which]
        recv = block_recv.at[lax.rem(t, nrow), which]
        return (
            jnp.logical_and(place == t, owner == c),
            lambda: pltpu.make_async_copy(rows_ref.at[k], slot, recv),
            lambda: pltpu.make_async_remote_copy(
                rows_ref.at[k], slot, block_send.at[k], recv,
                device_id={"dp": here.group * CORES + owner, "tensor": place}, device_id_type=MESH,
            ),
        )

    for k in range(tensor):
        stays, inside, away = home(k)

        @pl.when(stays)
        def _():
            inside().start()

        @pl.when(jnp.logical_not(stays))
        def _():
            away().start()

    def across(ring):
        group, at = here.at(ring)
        return (
            pltpu.make_async_remote_copy(
                grads_ref.at[at, group * CORES + 1 - c], theirs.at[ring], core_send.at[ring], core_recv.at[ring],
                device_id=sibling, device_id_type=MESH,
            ),
            pltpu.make_async_remote_copy(
                small_ref.at[at, group * CORES + 1 - c], small_theirs.at[ring], score_send.at[ring], score_recv.at[ring],
                device_id=sibling, device_id_type=MESH,
            ),
        )

    def fetch(ring):
        group, at = here.at(ring)
        return (
            pltpu.make_async_copy(grads_ref.at[at, group * CORES + c], own.at[ring], own_sem.at[ring]),
            pltpu.make_async_copy(small_ref.at[at, group * CORES + c], small_own.at[ring], sown_sem.at[ring]),
        )

    def behind(step):
        return lax.rem(here.ring - step + chips, chips)

    def order(k):
        off = (2 * lax.rem(k, 2) - 1) * (k // 2 + 1) * (1 - k // (chips - 1))
        return lax.rem(here.ring + chips + off, chips)

    @pl.loop(0, chips)
    def _(k):
        for copy in across(order(k)) + fetch(order(k)):
            copy.start()

    rows, columns = out_ref.shape
    parts = halves(rows, columns)

    def add(ring, part, step, last):
        height = parts[part][0].size
        piece = 16 if height % 16 == 0 else height

        @pl.loop(0, height // piece)
        def _(k):
            at = pl.ds(pl.multiple_of(parts[part][0].start + k * piece, 8), piece)
            where = (at, parts[part][1])
            value = own[(ring,) + where].astype(F32) + theirs[(ring,) + where].astype(F32)
            if step is not None:
                value = value + taken[(step,) + where].astype(F32)
            if last:
                total[where] = value
            else:
                own[(ring,) + where] = value.astype(BF16)

    def onward(ring, step, part):
        where = (parts[part][0], parts[part][1])
        return pltpu.make_async_remote_copy(
            own.at[(ring,) + where], taken.at[(step,) + where], ring_send.at[part, step], ring_recv.at[part, step],
            device_id=to_left if part else to_right, device_id_type=MESH,
        )

    def small_onward(ring, step):
        return pltpu.make_async_remote_copy(
            small_own.at[ring], small_taken.at[step], sring_send.at[step], sring_recv.at[step],
            device_id=to_right, device_id_type=MESH,
        )

    def ready(ring):
        for copy in across(ring):
            copy.wait_recv()
        for copy in fetch(ring):
            copy.wait()

    def ahead(step):
        return lax.rem(here.ring + step, chips)

    half_chips = chips // 2

    @pl.loop(0, chips - 1)
    def _(step):
        right, left = behind(step + 1), ahead(step + 1)

        @pl.when(step < half_chips)
        def _():
            ready(right)

        @pl.when(step < chips - 1 - half_chips)
        def _():
            ready(left)

        @pl.when(step == 0)
        def _():
            add(right, 0, None, False)
            add(left, 1, None, False)
            small_own[right] = small_own[right] + small_theirs[right]

        @pl.when(step > 0)
        def _():
            onward(right, step - 1, 0).wait_recv()
            add(right, 0, step - 1, False)
            onward(right, step, 0).start()
            onward(left, step - 1, 1).wait_recv()
            add(left, 1, step - 1, False)
            onward(left, step, 1).start()
            small_onward(right, step - 1).wait_recv()
            small_own[right] = small_own[right] + small_theirs[right] + small_taken[step - 1]
            small_onward(right, step).start()

        @pl.when(step == 0)
        def _():
            onward(right, 0, 0).start()
            onward(left, 0, 1).start()
            small_onward(right, 0).start()

    ready(here.ring)
    for part in range(2):
        onward(here.ring, chips - 2, part).wait_recv()
        add(here.ring, part, chips - 2, True)
    small_onward(here.ring, chips - 2).wait_recv()
    small_out[...] = small_own[here.ring] + small_theirs[here.ring] + small_taken[chips - 2]
    finish = pltpu.make_async_copy(total, out_ref, local_sem.at[0])
    finish.start()

    @pl.loop(0, chips)
    def _(step):
        @pl.when(step < chips - 1)
        def _():
            onward(behind(step + 1), step, 0).wait_send()
            onward(ahead(step + 1), step, 1).wait_send()
            small_onward(behind(step + 1), step).wait_send()

        for copy in across(step):
            copy.wait_send()

    for k in range(tensor):
        stays, inside, away = home(k)

        @pl.when(jnp.logical_not(stays))
        def _():
            away().wait_send()

    for i in range(nrow):
        for which in range(2):
            pltpu.make_async_copy(rows_ref.at[0], rows_out.at[i, which], block_recv.at[i, which]).wait()
    finish.wait()


def scatter(tensor, dp, grads, small, rows, nrow):
    chips = tensor * dp // CORES
    shard = grads.shape[2:]
    tiny = small.shape[2:]
    sems = pltpu.SemaphoreType.DMA
    return pl.pallas_call(
        functools.partial(scatter_kernel, tensor, dp),
        out_shape=(
            jax.ShapeDtypeStruct(shard, F32),
            jax.ShapeDtypeStruct(tiny, F32),
            jax.ShapeDtypeStruct((nrow, 2) + rows.shape[1:], rows.dtype),
        ),
        in_specs=[ANY] * 3,
        out_specs=(ANY, VMEM, ANY),
        scratch_shapes=[
            pltpu.VMEM((chips,) + shard, BF16),
            pltpu.VMEM((chips,) + shard, BF16),
            pltpu.VMEM((chips - 1,) + shard, BF16),
            pltpu.VMEM((chips,) + tiny, F32),
            pltpu.VMEM((chips,) + tiny, F32),
            pltpu.VMEM((chips - 1,) + tiny, F32),
            pltpu.VMEM(shard, F32),
            sems((chips,)), sems((chips,)), sems((chips,)), sems((2, chips)), sems((2, chips)),
            sems((chips,)), sems((chips,)), sems((chips,)), sems((chips,)), sems((chips,)),
            sems((tensor,)), sems((nrow, 2)), sems((1,)),
        ],
        compiler_params=pltpu.CompilerParams(collective_id=1, has_side_effects=True, vmem_limit_bytes=VMEM_LIMIT),
        name="scatter",
    )(grads, small, rows)


KEY, VALUE, QUERY, OUT, FIRST, SECOND = range(6)
ATTN, CROSS, INNER, OUTER = range(4)
SEGS_HELD = 6


def rms(value):
    return lax.rsqrt(jnp.mean(value * value, axis=-1, keepdims=True) + EPSILON)


def in_rows(count, body, piece=32):
    @pl.loop(0, count // piece)
    def _(k):
        body(pl.ds(pl.multiple_of(k * piece, piece), piece))


def columns_of(count, body, piece=256):
    @pl.loop(0, count // piece)
    def _(k):
        body(pl.ds(pl.multiple_of(k * piece, piece), piece), k)


def normalize(source, gain, target, count):
    def body(at):
        value = source[at, :].astype(F32)
        target[at, :] = (value * rms(value) * gain).astype(BF16)

    in_rows(count, body)


def normalize_back(source, gain, incoming, total, gain_parts, count, fresh):
    gain_parts[...] = jnp.zeros_like(gain_parts)

    def body(at):
        value, back = source[at, :].astype(F32), incoming[at, :]
        scale = rms(value)
        unit = value * scale
        gain_parts[...] += jnp.sum((back * unit).reshape(-1, 8, back.shape[-1]), axis=0)
        back = back * gain
        back = scale * (back - unit * jnp.mean(back * unit, axis=-1, keepdims=True))
        total[at, :] = back if fresh else total[at, :] + back

    in_rows(count, body)


def project(left, weight, target, count):
    def body(at, k):
        target[0:count, at] = nn(left[0:count, :], weight[:, at]).astype(target.dtype)

    columns_of(weight.shape[1], body)


def project_back(left, weight, total, count, fresh):
    def body(at, k):
        value = nt(left[0:count, :], weight[at, :])
        total[0:count, at] = value if fresh else total[0:count, at] + value

    columns_of(weight.shape[0], body)


def to_bf16(source, target, rows):
    def body(at):
        target[at, :] = source[at, :].astype(BF16)

    in_rows(rows, body)


def turn(left, turned, rows):
    def body(at, k):
        turned[at, 0:rows] = left[0:rows, at].T

    columns_of(left.shape[1], body, LANES)


def lane_half(shape, part):
    return lax.broadcasted_iota(jnp.int32, shape, 1) // HEAD_DIM == part


def attend(keys, values, queries, mixture, probs, rows, span, pairs, mask, bias, after):
    @pl.loop(0, pairs)
    def _(pair):
        lanes = pl.ds(pl.multiple_of(pair * LANES, LANES), LANES)
        key, query = keys[0:span, lanes], queries[0:rows, lanes]
        value_t = values[0:span, lanes].T
        mixed = []
        for part in range(2):
            one = jnp.where(lane_half(query.shape, part), query, jnp.zeros_like(query))
            scores = nt(key, one) + mask[0:span, 0:rows]
            if bias is not None:
                scores = scores + bias(2 * pair + part)
            scores = jnp.exp(scores - jnp.max(scores, axis=0, keepdims=True))
            scores = (scores * (1.0 / jnp.sum(scores, axis=0, keepdims=True))).astype(BF16)
            probs[2 * pair + part, 0:span, 0:rows] = scores
            mixed.append(nn(value_t[part * HEAD_DIM : (part + 1) * HEAD_DIM, :], scores))
        mixture[0:rows, lanes] = jnp.concatenate(mixed, axis=0).T.astype(BF16)
        after(pair)


def attend_back(keys, values, queries, back, probs, rows, span, pairs, each, before, after):
    @pl.loop(0, pairs)
    def _(pair):
        before(pair)
        lanes = pl.ds(pl.multiple_of(pair * LANES, LANES), LANES)
        key, value = keys[0:span, lanes], values[0:span, lanes]
        query, given = queries[0:rows, lanes], back[0:rows, lanes]
        key_t = key.T
        d_key, d_value, d_query = None, None, []
        for part in range(2):
            side = lane_half(query.shape, part)
            query_one = jnp.where(side, query, jnp.zeros_like(query))
            given_one = jnp.where(side, given, jnp.zeros_like(given))
            prob = probs[2 * pair + part, 0:span, 0:rows]
            wide = prob.astype(F32)
            d_prob = nt(value, given_one)
            d_score = (wide * (d_prob - jnp.sum(wide * d_prob, axis=0, keepdims=True))).astype(BF16)
            if each is not None:
                each(2 * pair + part, d_score)
            of_key, of_value = nn(d_score, query_one), nn(prob, given_one)
            d_key = of_key if d_key is None else d_key + of_key
            d_value = of_value if d_value is None else d_value + of_value
            d_query.append(nn(key_t[part * HEAD_DIM : (part + 1) * HEAD_DIM, :], d_score))
        keys[0:span, lanes] = d_key.astype(BF16)
        values[0:span, lanes] = d_value.astype(BF16)
        queries[0:rows, lanes] = jnp.concatenate(d_query, axis=0).T.astype(BF16)
        after(pair)


def segments(lengths_row, shape, axis, first):
    lane = lax.broadcasted_iota(jnp.int32, lengths_row.shape, 1)
    places = lax.broadcasted_iota(jnp.int32, shape, axis) + first
    ids = jnp.zeros(shape, jnp.int32)
    for c in range(SEGS_HELD):
        bound = jnp.sum(jnp.where(lane <= c, lengths_row, 0), axis=1, keepdims=True)
        ids = ids + (places >= bound).astype(jnp.int32)
    return ids


def masked(allowed):
    return jnp.where(allowed, 0.0, NEGATIVE).astype(F32)


def nothing(*unused, **named):
    pass


def work(r, here, supply, drain, tensor, heads_at):
    c, t = here.core, here.t
    width = r.hidden.shape[1]
    tall = r.hidden.shape[0]
    block = width // tensor
    half_width = width // 2
    units = r.inner.shape[2]
    places = r.x.shape[2]
    sibling = here.sibling()
    across = [{"pipe": 1 - here.pipe, "dp": here.group * CORES + k} for k in range(CORES)]
    nrow = tensor // CORES
    rows_e, span_e, rows_d, span_d = tall // 2, tall, tall // 4, tall // 2
    pairs_here = half_width // LANES
    near_lanes = pl.ds(pl.multiple_of(c * half_width, half_width), half_width)
    far_lanes = pl.ds(pl.multiple_of((1 - c) * half_width, half_width), half_width)
    lane_halves = [slice(k * half_width, (k + 1) * half_width) for k in range(CORES)]

    def move(source, target, sends, recvs, device):
        return pltpu.make_async_remote_copy(
            source, target, r.send_sem.at[sends], r.recv_sem.at[recvs], device_id=device, device_id_type=MESH
        )

    def lengths_row(first):
        return r.lengths[t // nrow, pl.ds(first + lax.rem(t, nrow), 1), :]

    def pair_lanes(pair):
        return pl.ds(pair * LANES if isinstance(pair, int) else pl.multiple_of(pair * LANES, LANES), LANES)

    def vector_row(head):
        return (head // heads_at) * 8 + lax.rem(head, heads_at)

    def bias_vectors():
        buckets = lax.broadcasted_iota(jnp.int32, r.onehot.shape, 0) == r.buckets[0:1, :]
        r.onehot[...] = buckets.astype(F32)
        for tt in range(tensor):
            r.vectors[pl.ds(8 * tt, 8), :] = lax.dot_general(
                r.tables[tt][:, 0 : r.onehot.shape[0]], r.onehot[...], (((1,), (0,)), ((), ())),
                precision=lax.Precision.HIGHEST, preferred_element_type=F32,
            )

    def rows_ready(span, rows, first_block):
        @pl.loop(0, span // places)
        def _(k):
            value = r.x[k // tensor, lax.rem(k, tensor)].astype(F32)
            at = pl.ds(pl.multiple_of(k * places, places), places)
            r.hidden[at, :] = (value * rms(value) * r.gains[0]).astype(BF16)

        for k in range(rows // places):
            r.own_x[k * places : (k + 1) * places, :] = r.x[first_block // tensor, lax.rem(first_block, tensor) + k]

    def untangle(source, first, count):
        for tt in range(tensor):
            for k in range(count):
                r.square[first + k, :, tt * block : (tt + 1) * block] = source[tt, :, k * block : (k + 1) * block]

    def self_forward(span, rows, first_row, group):
        def bias(head):
            pieces = []
            for j in range(span // LANES):
                start = pl.multiple_of(first_row + span - LANES - j * LANES, LANES)
                row = r.vectors[pl.ds(vector_row(head), 1), pl.ds(start, rows + LANES)]
                wide = jnp.broadcast_to(row, (LANES, rows + LANES))
                pieces.append(pltpu.roll(wide, rows + 1, 1, stride=1, stride_axis=0)[:, 0:rows])
            return jnp.concatenate(pieces, axis=0)

        untangle(r.raw_a, KEY, 2)
        untangle(r.raw_a.at[:, :, pl.ds(2 * block, 2 * block)], QUERY, 2)
        project(r.hidden, r.square.at[KEY], r.keys, span)
        supply.pump()
        project(r.hidden, r.square.at[VALUE], r.values, span)
        project(r.hidden.at[pl.ds(first_row, rows)], r.square.at[QUERY], r.queries, rows)
        supply.pump()
        after = at_each(range(width // LANES), supply.pump)

        attend(r.keys, r.values, r.queries, r.mixture, r.probs, rows, span, width // LANES, r.mask, bias, after)
        project_back(r.mixture, r.square.at[OUT], r.resid_mid, rows, True)

        def add(at):
            r.resid_mid[at, :] += r.own_x[at, :].astype(F32)

        in_rows(rows, add)
        supply.pump(until=group)
        supply.finish(group)

    def at_each(places, do):
        def hook(n):
            for place in places:

                @pl.when(n == place)
                def _():
                    do()

        return hook

    def feed_forward(rows, hook=nothing):
        @pl.loop(0, tensor)
        def _(tt):
            def body(at, k):
                value = nn(r.second[0:rows, :], r.inner[tt, :, at])
                cdf = 0.5 * (1.0 + lax.erf(value * 0.7071067811865476))
                r.ff[tt, 0:rows, at] = (value * cdf).astype(BF16)
                slope = cdf + value * jnp.exp(-0.5 * value * value) * 0.3989422804014327
                r.ff[tensor + tt, 0:rows, at] = slope.astype(BF16)
                hook(tt * (units // 256) + k)

            columns_of(units, body)

    def feed_out(target, rows, hook=nothing):
        @pl.loop(0, tensor)
        def _(tt):
            def body(at, k):
                target[0:rows, at] += nt(r.ff[tt, 0:rows, :], r.outer[tt, at, :])
                hook(tt * (width // 256) + k)

            columns_of(width, body)

    def feed_back(rows, ready, hook=nothing):
        r.summed[0:rows, :] = jnp.zeros((rows, width), F32)

        @pl.loop(0, tensor)
        def _(tt):
            def body(at, k):
                if ready:
                    value = r.ff[tensor + tt, rows : 2 * rows, at].astype(F32)
                else:
                    value = nn(r.d_branch[0:rows, :], r.outer[tt, :, at])
                r.ff[tensor + tt, 0:rows, at] = (value * r.ff[tensor + tt, 0:rows, at].astype(F32)).astype(BF16)

            columns_of(units, body)

            def back(at, k):
                r.summed[0:rows, at] += nt(r.ff[tensor + tt, 0:rows, :], r.inner[tt, at, :])

            columns_of(width, back)
            hook(tt)

    def feed_grads(rows, turned, first, which, hook=nothing):
        @pl.loop(0, tensor)
        def _(tt):
            slot = lax.rem(tt, 2)

            @pl.when(tt >= 2)
            def _():
                drain.release(which, tt - 2, slot)

            def body(at, k):
                r.stage[slot, :, at] = nn(turned[:, 0:rows], r.ff[first + tt, 0:rows, at]).astype(BF16)
                hook(tt * (units // 256) + k)

            columns_of(units, body)
            drain.emit(which, tt, slot)

        for tt in range(tensor - 2, tensor):
            drain.release(which, tt, tt % 2)

    def square_grads(rows, which, products, hook):
        for k in range(tensor // 2):
            for j, (turned, right) in enumerate(products):
                value = nn(turned[:, 0:rows], right[0:rows, 2 * k * block : 2 * (k + 1) * block]).astype(BF16)
                for slot in range(2):
                    r.stage[slot, :, j * block : (j + 1) * block] = value[:, slot * block : (slot + 1) * block]
            for slot in range(2):
                drain.emit(which, 2 * k + slot, slot)
            hook(k)
            for slot in range(2):
                drain.release(which, 2 * k + slot, slot)

    def gain_done(which):
        r.gains_out[which : which + 1, :] = jnp.sum(r.gain_parts[...], axis=0, keepdims=True)

    def self_backward(span, rows, first_row, steps, send_rows):
        mirror = (
            lax.broadcasted_iota(jnp.int32, (LANES, LANES), 0) + lax.broadcasted_iota(jnp.int32, (LANES, LANES), 1)
            == LANES - 1
        ).astype(BF16)
        to_bf16(r.d_resid, r.branch, rows)
        project(r.branch, r.square.at[OUT], r.d_branch, rows)
        r.diagonals[...] = jnp.zeros_like(r.diagonals)

        def each(head, d_score):
            for j in range(span // LANES):
                start = pl.multiple_of(first_row + span - LANES - j * LANES, LANES)
                piece = nn(mirror, d_score[j * LANES : (j + 1) * LANES, :])
                piece = jnp.concatenate([piece, jnp.zeros((LANES, LANES), F32)], axis=1)
                piece = pltpu.roll(piece, 0, 1, stride=1, stride_axis=0)
                at = (pl.ds(vector_row(head), 1), pl.ds(start, rows + LANES))
                r.diagonals[at] += jnp.sum(piece, axis=0, keepdims=True)

        pairs = width // LANES
        attend_back(
            r.keys, r.values, r.queries, r.d_branch, r.probs, rows, span, pairs, each, nothing,
            at_each(range(pairs), steps),
        )
        far = pl.ds(pl.multiple_of((1 - c) * rows, rows), rows)
        near = pl.ds(pl.multiple_of(c * rows, rows), rows)
        trades = [
            move(source.at[far], r.taken_pair.at[k, pl.ds(0, rows)], 12 + k, 12 + k, sibling)
            for k, source in enumerate((r.keys, r.values))
        ]
        for trade in trades:
            trade.start()
        steps()
        turn(r.branch, r.turned, rows)
        turn(r.hidden.at[pl.ds(first_row, rows)], r.turned_more, rows)
        for tt in range(tensor):
            at = pl.ds(8 * tt, 8)
            r.bias_out[at, 0 : r.onehot.shape[0]] = lax.dot_general(
                r.diagonals[at, :], r.onehot[...], (((1,), (1,)), ((), ())),
                precision=lax.Precision.HIGHEST, preferred_element_type=F32,
            )
        steps()
        project_back(r.queries, r.square.at[QUERY], r.summed, rows, True)
        for trade in trades:
            trade.wait_recv()
        for k, source in enumerate((r.keys, r.values)):
            r.d_pair[k, 0:rows, :] = (source[near, :].astype(F32) + r.taken_pair[k, 0:rows, :].astype(F32)).astype(BF16)
        project_back(r.d_pair.at[0], r.square.at[KEY], r.summed, rows, False)
        project_back(r.d_pair.at[1], r.square.at[VALUE], r.summed, rows, False)
        steps()
        normalize_back(r.own_x, r.gains[0], r.summed, r.d_resid, r.gain_parts, rows, False)
        gain_done(0)
        send_rows()
        drain.small_begin()
        products = [(r.turned_more, r.d_pair.at[0]), (r.turned_more, r.d_pair.at[1]), (r.turned_more, r.queries), (r.turned, r.mixture)]
        square_grads(rows, ATTN, products, nothing)
        for trade in trades:
            trade.wait_send()
        steps()
        drain.begin(ATTN)
        steps()
        drain.home_done()
        drain.rest(ATTN, 1)

    def parts_of(array):
        return [array.at[pl.ds(k * rows_d, rows_d)] for k in range(CORES)]

    def part_here(array):
        return array.at[pl.ds(pl.multiple_of(c * rows_d, rows_d), rows_d)]

    r.gains_out[...] = jnp.zeros_like(r.gains_out)
    r.bias_out[...] = jnp.zeros_like(r.bias_out)
    supply.start()

    def entry():
        supply.pump(2)
        supply.small()
        bias_vectors()
        supply.pump(2)
        supply.rows()

    def schedule(*items):
        left = list(items)

        def steps():
            for name, group, *n in left.pop(0) if left else ():
                getattr(drain, name)(group, *n)

        return steps

    @pl.when(here.pipe == 0)
    def _():
        supply.resume(ATTN, INNER, OUTER, CROSS)
        drain.order(CROSS, OUTER, INNER, ATTN)
        entry()
        rows, span = rows_e, span_e
        first_row = pl.multiple_of(c * rows, rows)
        seg_rows = segments(lengths_row(0), (span, 1), 0, 0)
        r.mask[...] = masked(seg_rows == segments(lengths_row(0), (1, rows), 1, first_row))
        supply.pump()
        rows_ready(span, rows, c * tensor)
        supply.pump(until=ATTN)
        supply.finish(ATTN)
        self_forward(span, rows, first_row, INNER)
        normalize(r.resid_mid, r.gains[1], r.second, rows)
        feed_forward(rows, at_each((3, 7, 11), supply.pump))
        supply.pump(until=OUTER)
        supply.finish(OUTER)
        r.resid_top[...] = r.resid_mid[...]
        feed_out(r.resid_top, rows, at_each((3, 7, 11), supply.pump))
        normalize(r.resid_top, r.gains[2], r.third, rows)
        r.mask[...] = masked(seg_rows == segments(lengths_row(nrow), (1, span_d), 1, 0))
        supply.pump(until=CROSS)
        supply.finish(CROSS)
        untangle(r.raw_c, FIRST, 2)
        mine = pl.ds(first_row, rows)
        other = pl.ds(pl.multiple_of((1 - c) * rows, rows), rows)
        trades = []
        for k, held in enumerate((r.cross_keys, r.cross_values)):
            r.send_pair[k] = nn(r.third[...], r.square[FIRST + k, :, far_lanes]).astype(BF16)
            trades.append(move(r.send_pair.at[k], held.at[mine], k, k, sibling))
            trades[-1].start()
        for k, held in enumerate((r.cross_keys, r.cross_values)):
            held[mine, :] = nn(r.third[...], r.square[FIRST + k, :, near_lanes]).astype(BF16)
        for k, part in enumerate(parts_of(r.cross_queries)):
            move(part, part, 2 + k, 2 + k, across[k]).wait_recv()
        for k, held in enumerate((r.cross_keys, r.cross_values)):
            move(r.send_pair.at[k], held.at[other], k, k, sibling).wait_recv()

        def mixtures(pair):
            at = pair_lanes(pair)
            return [
                pltpu.make_async_remote_copy(
                    r.cross_mixture.at[pl.ds(k * rows_d, rows_d), at], r.cross_in.at[c, :, at],
                    r.mix_send.at[k, pair], r.mix_recv.at[c, pair], device_id=across[k], device_id_type=MESH,
                )
                for k in range(CORES)
            ]

        def arrived(pair):
            for k in range(CORES):
                part = r.cross_back.at[pl.ds(k * rows_d, rows_d), pair_lanes(pair)]
                pltpu.make_async_remote_copy(
                    part, part, r.back_send.at[k, pair], r.back_recv.at[k, pair], device_id=across[k], device_id_type=MESH
                ).wait_recv()

        def returns(pair):
            at = pair_lanes(pair)
            return [
                pltpu.make_async_remote_copy(
                    d_cross.at[other, at], r.cross_taken.at[k, :, at],
                    r.give_send.at[k, pair], r.give_recv.at[k, pair], device_id=sibling, device_id_type=MESH,
                )
                for k, d_cross in enumerate((r.cross_keys, r.cross_values))
            ]

        attend(
            r.cross_keys, r.cross_values, r.cross_queries, r.cross_mixture, r.cross_probs, span_d, span, pairs_here,
            r.mask, None, lambda pair: [mix.start() for mix in mixtures(pair)],
        )
        supply.close()
        drain.free(0)
        turn(r.third, r.turned, rows)
        attend_back(
            r.cross_keys, r.cross_values, r.cross_queries, r.cross_back, r.cross_probs, span_d, span, pairs_here, None,
            arrived, lambda pair: [back.start() for back in returns(pair)],
        )
        answers = [
            move(part, r.cross_in_back.at[c], 8 + k, 8 + c, across[k]) for k, part in enumerate(parts_of(r.cross_queries))
        ]
        for answer in answers:
            answer.start()
        for k, d_cross in enumerate((r.cross_keys, r.cross_values)):
            r.d_pair[k, :, near_lanes] = d_cross[mine, :]
        for pair in range(pairs_here):
            for back in returns(pair):
                back.wait_recv()
        for k in range(2):
            r.d_pair[k, :, far_lanes] = r.cross_taken[k]
        drain.allow(0)
        square_grads(rows, CROSS, [(r.turned, r.d_pair.at[0]), (r.turned, r.d_pair.at[1])], nothing)
        drain.begin(CROSS)
        project_back(r.d_pair.at[0], r.square.at[FIRST], r.summed, rows, True)
        drain.tick(CROSS, 0)
        project_back(r.d_pair.at[1], r.square.at[SECOND], r.summed, rows, False)
        drain.tick(CROSS, 1)
        normalize_back(r.resid_top, r.gains[2], r.summed, r.d_resid, r.gain_parts, rows, True)
        gain_done(2)
        to_bf16(r.d_resid, r.d_branch, rows)
        turn(r.d_branch, r.turned, rows)
        drain.tick(CROSS, 2)
        feed_grads(rows, r.turned, 0, OUTER, at_each((6,), lambda: drain.tick(CROSS, 3)))
        drain.begin(OUTER)
        steps = schedule(
            [("tick", CROSS, 4), ("tick", OUTER, 0)],
            [("end", CROSS)],
            [("tick", OUTER, 1)],
        )
        feed_back(rows, False, at_each((0, 1, 3), steps))
        drain.free(1)
        turn(r.second, r.turned, rows)
        drain.allow(1)
        feed_grads(rows, r.turned, tensor, INNER, at_each((7,), lambda: drain.tick(OUTER, 2)))
        drain.begin(INNER)
        normalize_back(r.resid_mid, r.gains[1], r.summed, r.d_resid, r.gain_parts, rows, False)
        gain_done(1)
        drain.tick(OUTER, 3)
        for copy in trades + answers:
            copy.wait_send()
        for pair in range(pairs_here):
            for copy in mixtures(pair) + returns(pair):
                copy.wait_send()

        def send_rows():
            to_bf16(r.d_resid, r.rows_out, rows)
            drain.home()

        steps = schedule(
            [("tick", INNER, 0)], [("tick", OUTER, 4)], [("tick", INNER, 1)], [("end", OUTER)], [("tick", INNER, 2)], [],
            [("tick", INNER, 3)], [], [], [],
            [("tick", INNER, 4), ("tick", ATTN, 0), ("end", INNER)],
        )
        self_backward(span, rows, first_row, steps, send_rows)

    @pl.when(here.pipe == 1)
    def _():
        supply.resume(ATTN, CROSS, INNER, OUTER)
        drain.order(OUTER, INNER, CROSS, ATTN)
        entry()
        rows, span = rows_d, span_d
        first_row = pl.multiple_of(c * rows, rows)
        key_at = lax.broadcasted_iota(jnp.int32, (span, rows), 0)
        query_at = lax.broadcasted_iota(jnp.int32, (span, rows), 1) + first_row
        same = segments(lengths_row(nrow), (span, 1), 0, 0) == segments(lengths_row(nrow), (1, rows), 1, first_row)
        r.mask[0:span, 0:rows] = masked(same & (query_at >= key_at))
        supply.pump()
        first_block = c * (tensor // 2)
        rows_ready(span, rows, first_block)
        for k in range(rows // places):
            r.d_branch[k * places : (k + 1) * places, :] = r.x[1, first_block + k]
        supply.pump(until=ATTN)
        supply.finish(ATTN)
        self_forward(span, rows, first_row, CROSS)
        untangle(r.raw_c, FIRST, 2)
        normalize(r.resid_mid, r.gains[1], r.third, rows)
        project(r.third, r.square.at[FIRST], r.joined, rows)
        asks = []
        for k in range(CORES):
            r.send_pair[k, 0:rows, :] = r.joined[:, lane_halves[k]]
            asks.append(move(r.send_pair.at[k, pl.ds(0, rows)], part_here(r.cross_queries), 2 + k, 2 + c, across[k]))
            asks[-1].start()
        supply.pump(until=INNER)
        supply.finish(INNER)
        supply.pump(until=OUTER)
        supply.finish(OUTER)

        @pl.loop(0, tensor)
        def _(tt):
            def body(at, k):
                r.ff[tensor + tt, rows : 2 * rows, at] = nn(r.d_branch[0:rows, :], r.outer[tt, :, at]).astype(BF16)

            columns_of(units, body)

        supply.close()
        drain.free(0)
        r.resid_top[0:rows, :] = r.resid_mid[0:rows, :]
        for k in range(CORES):
            for pair in range(pairs_here):
                part = r.cross_in.at[k, :, pair_lanes(pair)]
                pltpu.make_async_remote_copy(
                    part, part, r.mix_send.at[k, pair], r.mix_recv.at[k, pair], device_id=across[k], device_id_type=MESH
                ).wait_recv()
            r.joined[:, lane_halves[k]] = r.cross_in[k]
        project_back(r.joined, r.square.at[SECOND], r.resid_top, rows, False)
        normalize(r.resid_top, r.gains[2], r.second, rows)
        feed_forward(rows)
        feed_back(rows, True)
        r.d_resid[0:rows, :] = r.d_branch[0:rows, :].astype(F32)
        normalize_back(r.resid_top, r.gains[2], r.summed, r.d_resid, r.gain_parts, rows, False)
        gain_done(2)
        to_bf16(r.d_resid, r.branch, rows)
        tells = []
        for pair in range(pairs_here):
            for k in range(CORES):
                at = pair_lanes(pair)
                first = k * half_width + pair * LANES
                r.send_back[k, :, at] = nn(r.branch[0:rows, :], r.square[SECOND, :, first : first + LANES]).astype(BF16)
                tells.append(
                    pltpu.make_async_remote_copy(
                        r.send_back.at[k, :, at], r.cross_back.at[pl.ds(pl.multiple_of(c * rows, rows), rows), at],
                        r.back_send.at[k, pair], r.back_recv.at[c, pair], device_id=across[k], device_id_type=MESH,
                    )
                )
                tells[-1].start()
        feed_out(r.resid_top, rows)
        drain.free(1)
        to_bf16(r.resid_top, r.rows_out, rows)
        turn(r.d_branch, r.turned, rows)
        drain.allow(0)
        feed_grads(rows, r.turned, 0, OUTER)
        drain.begin(OUTER)
        turn(r.second, r.turned, rows)
        drain.allow(1)
        steps = schedule([("tick", OUTER, 0)], [("tick", OUTER, 1)])
        feed_grads(rows, r.turned, tensor, INNER, at_each((4, 10), steps))
        drain.begin(INNER)
        turn(r.branch, r.turned, rows)
        turn(r.third, r.turned_more, rows)
        for group, n in ((OUTER, 2), (INNER, 0), (OUTER, 3), (INNER, 1), (OUTER, 4)):
            drain.tick(group, n)
        drain.end(OUTER)
        for k in range(CORES):
            move(r.cross_in_back.at[k], r.cross_in_back.at[k], 8 + k, 8 + k, across[k]).wait_recv()
            r.d_pair[1, 0:rows, lane_halves[k]] = r.cross_in_back[k]
        project_back(r.d_pair.at[1], r.square.at[FIRST], r.summed, rows, True)
        drain.tick(INNER, 2)
        square_grads(rows, CROSS, [(r.turned_more, r.d_pair.at[1]), (r.turned, r.joined)], nothing)
        drain.begin(CROSS)
        normalize_back(r.resid_mid, r.gains[1], r.summed, r.d_resid, r.gain_parts, rows, False)
        gain_done(1)
        drain.tick(INNER, 3)
        for copy in asks + tells:
            copy.wait_send()

        def send_rows():
            to_bf16(r.d_resid, r.rows_out.at[pl.ds(rows, rows)], rows)
            drain.home()

        steps = schedule(
            [("tick", INNER, 4), ("tick", CROSS, 0)], [("end", INNER)], [("tick", CROSS, 1)], [], [("tick", CROSS, 2)], [],
            [("tick", CROSS, 3)], [], [], [("tick", CROSS, 4)],
            [("end", CROSS), ("tick", ATTN, 0)],
        )
        self_backward(span, rows, first_row, steps, send_rows)

    drain.close()


def held(*shape, dtype=BF16):
    return pltpu.VMEM(shape, dtype)


def arrays(tensor, heads_at, places, width, units, ranges, kinds):
    tall = 2 * tensor * places
    block = width // tensor
    half_rows, half_width = tall // 2, width // 2
    heads = heads_at * tensor
    return dict(
        x=held(2, tensor, places, width),
        own_x=held(half_rows, width),
        raw_a=held(tensor, width, 4 * block),
        raw_c=held(tensor, width, 2 * block),
        square=held(6, width, width),
        inner=held(tensor, width, units),
        outer=held(tensor, width, units),
        hidden=held(tall, width),
        keys=held(tall, width),
        values=held(tall, width),
        queries=held(half_rows, width),
        probs=held(heads, tall, half_rows),
        mask=held(tall, half_rows, dtype=F32),
        mixture=held(half_rows, width),
        resid_mid=held(half_rows, width, dtype=F32),
        resid_top=held(half_rows, width, dtype=F32),
        d_resid=held(half_rows, width, dtype=F32),
        summed=held(half_rows, width, dtype=F32),
        second=held(half_rows, width),
        third=held(half_rows, width),
        ff=held(2 * tensor, half_rows, units),
        d_branch=held(half_rows, width),
        branch=held(half_rows, width),
        cross_keys=held(tall, half_width),
        cross_values=held(tall, half_width),
        cross_queries=held(half_rows, half_width),
        cross_mixture=held(half_rows, half_width),
        cross_probs=held(heads // CORES, tall, half_rows),
        cross_back=held(half_rows, half_width),
        cross_in=held(CORES, half_rows // 2, half_width),
        cross_in_back=held(CORES, half_rows // 2, half_width),
        cross_taken=held(CORES, half_rows, half_width),
        send_pair=held(CORES, half_rows, half_width),
        send_back=held(CORES, half_rows // 2, half_width),
        joined=held(half_rows // 2, width),
        taken_pair=held(2, half_rows, width),
        d_pair=held(2, half_rows, width),
        turned=held(width, half_rows),
        turned_more=held(width, half_rows),
        stage=held(2, width, units),
        vectors=held(8 * tensor, ranges, dtype=F32),
        diagonals=held(8 * tensor, ranges, dtype=F32),
        onehot=held(kinds, ranges, dtype=F32),
        gain_parts=held(8, width, dtype=F32),
        send_sem=pltpu.SemaphoreType.DMA((14,)),
        recv_sem=pltpu.SemaphoreType.DMA((14,)),
        **{
            name: pltpu.SemaphoreType.DMA((CORES, half_width // LANES))
            for name in ("mix_send", "mix_recv", "back_send", "back_recv", "give_send", "give_recv")
        },
    )


def group_columns(block, units):
    return {ATTN: (0, 4 * block), CROSS: (4 * block, 2 * block), INNER: (6 * block, units), OUTER: (6 * block + units, units)}


def landing(r):
    return {ATTN: r.raw_a, CROSS: r.raw_c, INNER: r.inner, OUTER: r.outer}


class Loads:
    def __init__(self, r, tensor, x_hbm, w_hbm, sems):
        columns = group_columns(r.raw_a.shape[2] // 4, r.inner.shape[2])
        self.x = pltpu.make_async_copy(x_hbm, r.x, sems.at[4, 0])
        self.weights = [
            [
                pltpu.make_async_copy(w_hbm.at[tt, :, pl.ds(*columns[group])], target.at[tt], sems.at[group, tt])
                for tt in range(tensor)
            ]
            for group, target in landing(r).items()
        ]

    def start(self):
        self.x.start()
        for group in self.weights:
            for copy in group:
                copy.start()

    def rows(self):
        self.x.wait()

    def finish(self, group):
        for copy in self.weights[group]:
            copy.wait()

    small = resume = pump = close = nothing


class Stores:
    def __init__(self, r, grads_hbm, sems):
        self.columns = group_columns(r.raw_a.shape[2] // 4, r.inner.shape[2])
        self.r, self.grads, self.sems = r, grads_hbm, sems

    def copy(self, group, tt, slot):
        first, wide = self.columns[group]
        return pltpu.make_async_copy(
            self.r.stage.at[slot, :, pl.ds(0, wide)], self.grads.at[tt, :, pl.ds(first, wide)], self.sems.at[slot]
        )

    def emit(self, group, tt, slot):
        self.copy(group, tt, slot).start()

    def release(self, group, tt, slot):
        self.copy(group, tt, slot).wait()

    order = free = allow = begin = tick = rest = end = home = home_done = small_begin = close = nothing


def blocks_kernel(tensor, dp, heads_at, names, *refs):
    here = Place(tensor, dp)
    r = types.SimpleNamespace(**dict(zip(names, refs)))
    across = [{"pipe": 1 - here.pipe, "dp": here.group * CORES + k} for k in range(CORES)]
    meet([here.sibling()] + across)
    work(r, here, Loads(r, tensor, r.x_hbm, r.w_hbm, r.load_sem), Stores(r, r.grads_hbm, r.stage_sem), tensor, heads_at)


def blocks(tensor, dp, heads_at, kinds, rows, weights, gains, lengths, tables, buckets):
    places, width = rows.shape[2:]
    units = (weights.shape[2] - 6 * (width // tensor)) // 2
    half_rows = tensor * places
    scratch = arrays(tensor, heads_at, places, width, units, buckets.shape[1], kinds)
    scratch["load_sem"] = pltpu.SemaphoreType.DMA((5, tensor))
    scratch["stage_sem"] = pltpu.SemaphoreType.DMA((2,))
    names = ["x_hbm", "w_hbm", "gains", "lengths", "tables", "buckets", "grads_hbm", "rows_out", "gains_out", "bias_out"]
    return pl.pallas_call(
        functools.partial(blocks_kernel, tensor, dp, heads_at, names + list(scratch)),
        out_shape=(
            jax.ShapeDtypeStruct(weights.shape, BF16),
            jax.ShapeDtypeStruct((half_rows, width), BF16),
            jax.ShapeDtypeStruct((8, width), F32),
            jax.ShapeDtypeStruct((8 * tensor, LANES), F32),
        ),
        in_specs=[ANY, ANY] + [VMEM] * 4,
        out_specs=(ANY, VMEM, VMEM, VMEM),
        scratch_shapes=list(scratch.values()),
        compiler_params=pltpu.CompilerParams(collective_id=2, has_side_effects=True, vmem_limit_bytes=VMEM_LIMIT),
        name="blocks",
    )(rows, weights, gains, lengths, tables, buckets)


class Rings:
    def __init__(self, r, here, tensor, dp):
        self.r, self.here, self.tensor, self.dp = r, here, tensor, dp
        self.depth = r.value_w.shape[0]
        self.hops = here.chips // 2
        self.count = 2 * self.hops - 1
        self.sibling = here.sibling()
        self.targets = [here.neighbour(1), here.neighbour(-1)]
        self.landing = landing(r)
        self.groups = []
        self.plan = []


    def order(self, *groups):
        steps = []
        for k, group in enumerate(groups):
            steps.append((4 * k - 0.5, k, self.begin, group, None))
            steps += [(4 * k + n, k, self.tick, group, n) for n in range(self.count)]
        steps.sort(key=lambda step: step[:2])
        self.groups = list(groups)
        self.plan = [step[2:] for step in steps]

    def resume(self, *groups):
        self.order(*groups)
        self.plan.pop(0)

    def pump(self, count=1, until=None):
        while self.plan and (count > 0 if until is None else any(step[1] == until for step in self.plan)):
            do, group, n = self.plan.pop(0)
            do(group) if n is None else do(group, n)
            count -= 0 if n is None else 1


    def block_out(self, i):
        r, t, c = self.r, self.here.t, self.here.core
        return pltpu.make_async_remote_copy(
            r.rows.at[i], r.x.at[:, t], r.block_send.at[i], r.block_recv.at[t],
            device_id={"tensor": r.rows.shape[0] * c + i}, device_id_type=MESH,
        )

    def block_kept(self, i):
        return pltpu.make_async_copy(self.r.rows.at[i], self.r.x.at[:, self.here.t], self.r.local_sem.at[0])

    def block_pass(self, source, s):
        r = self.r
        return pltpu.make_async_remote_copy(
            source, r.x.at[:, s], r.pass_send.at[s], r.pass_recv.at[s], device_id=self.sibling, device_id_type=MESH
        )

    def blocks(self, mine, others):
        for i in range(self.r.rows.shape[0]):
            here = self.r.rows.shape[0] * self.here.core + i == self.here.t

            @pl.when(here)
            def _():
                mine(i)

            @pl.when(jnp.logical_not(here))
            def _():
                others(i)

    def small_copies(self):
        r, t = self.r, self.here.t
        copies = [
            pltpu.make_async_remote_copy(
                r.lengths_in, r.lengths.at[self.here.core], r.small_send.at[0], r.small_recv.at[0],
                device_id=self.sibling, device_id_type=MESH,
            ),
            pltpu.make_async_copy(r.lengths_in, r.lengths.at[self.here.core], r.local_sem.at[1]),
            pltpu.make_async_copy(r.table_in, r.tables.at[t], r.local_sem.at[2]),
        ]
        for k in range(1, self.tensor):
            copies.append(
                pltpu.make_async_remote_copy(
                    r.table_in, r.tables.at[t], r.small_send.at[k], r.small_recv.at[k],
                    device_id={"tensor": lax.rem(t + k, self.tensor)}, device_id_type=MESH,
                )
            )
        return copies


    def rows_of(self, ring):
        line, at = self.here.at(ring)
        return at, pl.multiple_of((line * CORES + self.here.core) * self.depth, 16)

    def ring_at(self, step, part):
        way = -1 if part else 1
        return lax.rem(self.here.ring - way * step + self.here.chips, self.here.chips)

    def onward(self, group, step, part, sub):
        r, half = self.r, self.depth // 2
        at, first = self.rows_of(self.ring_at(step, part))
        target = self.landing[group]
        slot = target.at[at, pl.ds(pl.multiple_of(first + half * sub, 16), half), :]
        packed = r.stage.at[0, pl.ds(group * self.depth + half * sub, half), pl.ds(0, target.shape[2])]
        sems = (self.groups.index(group) % 2, part, sub, step)
        return pltpu.make_async_remote_copy(
            packed if step == 0 else slot, slot, r.ring_send.at[sems], r.ring_recv.at[sems],
            device_id=self.targets[part], device_id_type=MESH,
        )

    def over(self, group, ring, first_time=False):
        r = self.r
        at, first = self.rows_of(ring)
        target = self.landing[group]
        slot = target.at[at, pl.ds(first, self.depth), :]
        packed = r.stage.at[0, pl.ds(group * self.depth, self.depth), pl.ds(0, target.shape[2])]
        return pltpu.make_async_remote_copy(
            packed if first_time else slot, slot, r.over_send.at[group, ring], r.over_recv.at[group, ring],
            device_id=self.sibling, device_id_type=MESH,
        )

    def own(self, group):
        wide = self.landing[group].shape[2]
        first = pl.multiple_of(self.here.d * self.depth, 16)
        return pltpu.make_async_copy(
            self.r.stage.at[0, pl.ds(group * self.depth, self.depth), pl.ds(0, wide)],
            self.landing[group].at[self.here.t, pl.ds(first, self.depth), :],
            self.r.own_sem.at[group],
        )

    def begin(self, group):
        place = self.groups.index(group)
        if place >= 2:
            self.sends_done(self.groups[place - 2])
        for sub in range(2):
            for part in range(2):
                self.onward(group, 0, part, sub).start()
        self.over(group, self.here.ring, True).start()
        self.own(group).start()

    def tick(self, group, n):
        step, last = n // 2 + 1, n == self.count - 1
        for part in range(2):
            sub = part if last else n % 2
            self.onward(group, step - 1, part, sub).wait_recv()
            if not last and (step < self.hops - 1 or sub == part):
                self.onward(group, step, part, sub).start()
        if last:
            self.over(group, self.ring_at(step, 0)).start()
        elif n % 2:
            for part in range(2):
                self.over(group, self.ring_at(step, part)).start()

    def sends_done(self, group):
        for part in range(2):
            for sub in range(2):
                for step in range(self.hops):
                    if step < self.hops - 1 or sub == part:
                        self.onward(group, step, part, sub).wait_send()

    def finish(self, group):
        @pl.loop(0, self.here.chips)
        def _(ring):
            self.over(group, ring).wait_recv()

        self.own(group).wait()

    def start(self):
        r, depth = self.r, self.depth
        nrow = r.rows.shape[0]
        r.lengths_in[...] = jnp.zeros_like(r.lengths_in)
        r.lengths_in[0:nrow, 0 : r.enc_lengths.shape[1]] = r.enc_lengths[...]
        r.lengths_in[nrow : 2 * nrow, 0 : r.dec_lengths.shape[1]] = r.dec_lengths[...]
        r.table_in[...] = jnp.zeros_like(r.table_in)
        for k in range(r.bias_w.shape[0]):
            r.table_in[k : k + 1, 0 : r.bias_w.shape[2]] = r.bias_w[k]
        self.blocks(
            lambda i: (self.block_kept(i).start(), self.block_pass(r.rows.at[i], self.here.t).start()),
            lambda i: self.block_out(i).start(),
        )
        block = r.value_w.shape[1]

        def band(group, pieces):
            wide = pieces[0].shape[1]
            for k, piece in enumerate(pieces):
                r.stage[0, group * depth : (group + 1) * depth, k * wide : (k + 1) * wide] = piece

        band(ATTN, [r.query_key_w[1], r.value_w[...], r.query_key_w[0], r.out_w[...].T])
        self.order(ATTN)
        self.begin(ATTN)
        for copy in self.small_copies():
            copy.start()
        band(INNER, [r.inner_w[...]])
        band(OUTER, [r.outer_w[...]])
        band(CROSS, [r.first_w[...], r.second_w[...]])

    def small(self):
        for copy in self.small_copies():
            copy.wait()

    def rows(self):
        r, t = self.r, self.here.t
        takes = lax.div(t, r.rows.shape[0]) == self.here.core
        for s in range(self.tensor):

            @pl.when(jnp.logical_and(takes, s != t))
            def _():
                pltpu.make_async_remote_copy(
                    r.rows.at[0], r.x.at[:, s], r.block_send.at[0], r.block_recv.at[s],
                    device_id=self.sibling, device_id_type=MESH,
                ).wait_recv()
                self.block_pass(r.x.at[:, s], s).start()

        self.blocks(lambda i: self.block_kept(i).wait(), nothing)
        for s in range(self.tensor):

            @pl.when(jnp.logical_not(takes))
            def _():
                self.block_pass(r.x.at[:, s], s).wait_recv()

    def close(self):
        r, t = self.r, self.here.t
        takes = lax.div(t, r.rows.shape[0]) == self.here.core
        self.blocks(
            lambda i: self.block_pass(r.rows.at[i], t).wait_send(),
            lambda i: self.block_out(i).wait_send(),
        )
        for s in range(self.tensor):

            @pl.when(jnp.logical_and(takes, s != t))
            def _():
                self.block_pass(r.x.at[:, s], s).wait_send()

        for group in self.groups[-2:]:
            self.sends_done(group)
        for group in self.groups:

            @pl.loop(0, self.here.chips)
            def _(ring):
                self.over(group, ring).wait_send()


class Sums:
    def __init__(self, r, here, tensor, dp):
        self.r, self.here, self.tensor, self.dp = r, here, tensor, dp
        self.depth = r.value_w.shape[0]
        self.hops = here.chips // 2
        self.count = 2 * self.hops - 3
        self.sibling = here.sibling()
        self.targets = [here.neighbour(1), here.neighbour(-1)]
        self.box = {CROSS: r.raw_c, OUTER: r.raw_a, INNER: r.inner, ATTN: r.outer}
        self.kept = {CROSS: r.own_cross, OUTER: r.own_outer, INNER: r.own_inner, ATTN: r.ff}
        self.groups = []

    def order(self, *groups):
        self.groups = list(groups)

    def free(self, k):
        for device in self.targets + [self.sibling]:
            pl.semaphore_signal(self.r.free_sem.at[k], inc=1, device_id=device, device_id_type=MESH)

    def allow(self, k):
        pl.semaphore_wait(self.r.free_sem.at[k], 3)

    def boxed(self, group, index, first, height):
        if isinstance(index, int):
            return (index // self.dp, pl.ds(pl.multiple_of(index % self.dp * self.depth + first, 16), height), slice(None))
        at = pl.ds(pl.multiple_of(lax.rem(index, self.dp) * self.depth + first, 16), height)
        return (lax.div(index, self.dp), at, slice(None))

    def taken(self, group, step, part, first, height):
        index = step + part * (self.hops - 1) if step else 0
        return self.boxed(group, index, first, height)

    def theirs(self, group, ring, first, height):
        return self.boxed(group, self.here.chips - 1 + ring, first, height)

    def own(self, group, ring, first, height):
        return (ring, pl.ds(first, height), slice(None))

    def ring_of(self, line, at):
        return line * self.tensor + at + (line % 2) * (self.tensor - 1 - 2 * at)

    def pieces(self, group, tt, slot):
        r, depth = self.r, self.depth
        wide = self.box[group].shape[2]
        made = []
        for line in range(self.here.groups):
            ring = self.ring_of(line, tt)

            def rows_of(core):
                return r.stage.at[slot, pl.ds(pl.multiple_of((line * CORES + core) * depth, 16), depth), pl.ds(0, wide)]

            made.append(
                pltpu.make_async_copy(
                    rows_of(self.here.core), self.kept[group].at[self.own(group, ring, 0, depth)], r.kept_sem.at[slot, line]
                )
            )
            made.append(
                pltpu.make_async_remote_copy(
                    rows_of(1 - self.here.core), self.box[group].at[self.theirs(group, ring, 0, depth)],
                    r.over_send.at[group, ring], r.over_recv.at[group, ring], device_id=self.sibling, device_id_type=MESH,
                )
            )
        return made

    def emit(self, group, tt, slot):
        for piece in self.pieces(group, tt, slot):
            piece.start()

    def release(self, group, tt, slot):
        for k, piece in enumerate(self.pieces(group, tt, slot)):
            if k % 2:
                piece.wait_send()
            else:
                piece.wait()


    def rows_at(self, sub):
        half = self.depth // 2
        return half * sub, half

    def source(self, step, part):
        way = -1 if part else 1
        return lax.rem(self.here.ring + way * (self.hops - step) + self.here.chips, self.here.chips)

    def onward(self, group, step, part, sub):
        r = self.r
        first, height = self.rows_at(sub)
        sems = (self.groups.index(group) % 2, part, sub, step)
        return pltpu.make_async_remote_copy(
            self.kept[group].at[self.own(group, self.source(step, part), first, height)],
            self.box[group].at[self.taken(group, step, part, first, height)],
            r.ring_send.at[sems], r.ring_recv.at[sems],
            device_id=self.targets[part], device_id_type=MESH,
        )

    def here_sum(self, group, ring, first, height):
        value = self.kept[group][self.own(group, ring, first, height)].astype(F32)
        return value + self.box[group][self.theirs(group, ring, first, height)].astype(F32)

    def advance(self, group, step, part, sub, fresh=False):
        if not fresh:
            self.onward(group, step - 1, part, sub).wait_recv()
        first, height = self.rows_at(sub)
        value = self.here_sum(group, self.source(step, part), first, height)
        if not fresh:
            value = value + self.box[group][self.taken(group, step - 1, part, first, height)].astype(F32)
        self.kept[group][self.own(group, self.source(step, part), first, height)] = value.astype(BF16)
        self.onward(group, step, part, sub).start()

    def begin(self, group):
        @pl.loop(0, self.here.chips)
        def _(ring):
            pltpu.make_async_remote_copy(
                self.kept[group].at[self.own(group, ring, 0, self.depth)],
                self.box[group].at[self.theirs(group, ring, 0, self.depth)],
                self.r.over_send.at[group, ring], self.r.over_recv.at[group, ring], device_id=self.sibling, device_id_type=MESH,
            ).wait_recv()

        place = self.groups.index(group)
        if place >= 2:
            self.sends_done(self.groups[place - 2])
        for part in range(2):
            self.advance(group, 0, part, part, True)
        for part in range(2):
            self.advance(group, 1, part, 1 - part, True)
        if group == ATTN:
            self.small_across().wait_recv()
            self.small_advance(0, 0, True)
            self.small_advance(1, 1, True)

    def tick(self, group, n):
        step, leads = (n + 1) // 2 + 1, n % 2
        for part in range(2):
            self.advance(group, step, part, 1 - part if leads else part)
        if group == ATTN and not leads:
            self.small_advance(step, 0)
            if step > 1:
                self.small_advance(step, 1)

    def sends_done(self, group):
        for part in range(2):
            self.onward(group, 0, part, part).wait_send()
            for step in range(1, self.hops):
                for sub in range(2):
                    self.onward(group, step, part, sub).wait_send()

    def rest(self, group, first):
        for n in range(first, self.count):
            self.tick(group, n)
        self.end(group)
        for group in self.groups[-2:]:
            self.sends_done(group)

    def end(self, group):
        r, last = self.r, self.hops - 1
        for sub in range(2):
            first, height = self.rows_at(sub)
            value = self.here_sum(group, self.here.ring, first, height)
            for part in range(2):
                self.onward(group, last, part, sub).wait_recv()
                value = value + self.box[group][self.taken(group, last, part, first, height)].astype(F32)
            target = r.inner_out if group == INNER else r.total
            target[pl.ds(first, height), 0 : self.box[group].shape[2]] = value
        block = r.value_w.shape[1]
        if group == ATTN:
            r.pair_out[1] = r.total[:, 0:block]
            r.value_out[...] = r.total[:, block : 2 * block]
            r.pair_out[0] = r.total[:, 2 * block : 3 * block]
            r.out_out[...] = r.total[:, 3 * block : 4 * block].T
            at = self.small_at(self.here.ring)
            value = r.small[at] + r.small_theirs[at]
            for part in range(2):
                self.small_onward(last, part).wait_recv()
                value = value + r.small_taken[part, last]
            for k in range(3):
                r.gain_out[k] = value[k : k + 1, 0 : self.depth]
            for k in range(self.heads_at):
                r.kind_out[k] = value[3 + k : 4 + k, 0 : r.kind_out.shape[2]]
        if group == CROSS:
            r.first_out[...] = r.total[:, 0:block]
            r.second_out[...] = r.total[:, block : 2 * block]
        if group == OUTER:
            r.outer_out[...] = r.total[...]


    def small_at(self, ring):
        line, at = self.here.at(ring)
        return at, line * CORES + self.here.core

    def small_across(self):
        r = self.r
        return pltpu.make_async_remote_copy(
            r.small, r.small_theirs, r.small_sem.at[0], r.small_sem.at[1], device_id=self.sibling, device_id_type=MESH
        )

    def small_onward(self, step, part):
        r = self.r
        return pltpu.make_async_remote_copy(
            r.small_sent.at[part, step], r.small_taken.at[part, step], r.tiny_send.at[part, step], r.tiny_recv.at[part, step],
            device_id=self.targets[part], device_id_type=MESH,
        )

    def small_advance(self, step, part, fresh=False):
        at = self.small_at(self.source(step, part))
        value = self.r.small[at] + self.r.small_theirs[at]
        if not fresh:
            self.small_onward(step - 1, part).wait_recv()
            value = value + self.r.small_taken[part, step - 1]
        self.r.small_sent[part, step] = value
        self.small_onward(step, part).start()

    def small_begin(self):
        r, depth = self.r, self.depth
        r.small[...] = jnp.zeros_like(r.small)
        kinds = r.onehot.shape[0] // self.dp
        heads_at = self.heads_at
        for tt in range(self.tensor):
            for d in range(self.dp):
                r.small[tt, d, 0:3, 0:depth] = r.gains_out[0:3, d * depth : (d + 1) * depth]
                r.small[tt, d, 3 : 3 + heads_at, 0:kinds] = r.bias_out[
                    8 * tt : 8 * tt + heads_at, d * kinds : (d + 1) * kinds
                ]
        self.small_across().start()


    def home_copy(self, k):
        r, here, tensor = self.r, self.here, self.tensor
        nrow, half, places = r.home_in.shape[0], tensor // 2, r.home_in.shape[2]
        place = here.pipe * (here.core * half + k % half) + (1 - here.pipe) * k
        which = here.pipe * (k // half) + (1 - here.pipe) * here.core
        owner = lax.div(here.t, nrow)
        source = r.rows_out.at[pl.ds(k * places, places)]
        slot = r.home_in.at[lax.rem(here.t, nrow), which]
        recv = r.home_recv.at[lax.rem(here.t, nrow), which]
        return (
            jnp.logical_and(place == here.t, owner == here.core),
            lambda: pltpu.make_async_copy(source, slot, recv),
            lambda: pltpu.make_async_remote_copy(
                source, slot, r.home_send.at[k], recv,
                device_id={"dp": here.group * CORES + owner, "tensor": place}, device_id_type=MESH,
            ),
        )

    def home(self):
        for k in range(self.tensor):
            stays, inside, away = self.home_copy(k)

            @pl.when(stays)
            def _():
                inside().start()

            @pl.when(jnp.logical_not(stays))
            def _():
                away().start()

    def home_done(self):
        r = self.r
        places = r.home_in.shape[2]
        for i in range(r.home_in.shape[0]):
            for which in range(2):
                pltpu.make_async_copy(
                    r.rows_out.at[pl.ds(0, places)], r.home_in.at[i, which], r.home_recv.at[i, which]
                ).wait()
                r.home_out[i, which] = r.home_in[i, which].astype(F32)

    def close(self):
        r = self.r
        for k in range(self.tensor):
            stays, inside, away = self.home_copy(k)

            @pl.when(jnp.logical_not(stays))
            def _():
                away().wait_send()

        self.small_across().wait_send()

        for part in range(2):
            for step in range(part, self.hops):
                self.small_onward(step, part).wait_send()


def fits_fused(tensor, dp, depth, units, width):
    chips = tensor * dp // CORES
    return (
        depth % 32 == 0
        and 4 * depth <= width
        and chips <= 2 * tensor
        and chips == 2 * tensor == 8
        and units == width == 6 * LANES
    )


def fused_kernel(tensor, dp, heads_at, names, *refs):
    here = Place(tensor, dp)
    r = types.SimpleNamespace(**dict(zip(names, refs)))
    line = [
        {"dp": here.group * CORES + lax.rem(here.core + j, CORES), "tensor": lax.rem(here.t + k, tensor)}
        for j in range(CORES)
        for k in range(tensor)
        if j + k > 0
    ]
    across = [{"pipe": 1 - here.pipe, "dp": here.group * CORES + k} for k in range(CORES)]
    meet([here.neighbour(1), here.neighbour(-1)] + line + across)
    supply, drain = Rings(r, here, tensor, dp), Sums(r, here, tensor, dp)
    drain.heads_at = heads_at
    work(r, here, supply, drain, tensor, heads_at)


def fused(tensor, dp, rows, enc_lengths, dec_lengths, gains, bias, buckets, weights):
    nrow, two, places, width = rows.shape
    depth, block = weights[1].shape
    units = weights[5].shape[1]
    heads_at, _, kinds = bias.shape
    chips = tensor * dp // CORES
    wide = -(-max(depth, kinds // dp) // LANES) * LANES
    sems = pltpu.SemaphoreType.DMA
    scratch = arrays(tensor, heads_at, places, width, units, buckets.shape[1], kinds)
    scratch.update(
        lengths_in=held(8, LANES, dtype=jnp.int32),
        table_in=held(8, LANES, dtype=F32),
        lengths=held(CORES, 8, LANES, dtype=jnp.int32),
        tables=held(tensor, 8, LANES, dtype=F32),
        own_cross=held(chips, depth, 2 * block),
        own_outer=held(chips, depth, units),
        own_inner=held(chips, depth, units),
        total=held(depth, units, dtype=F32),
        rows_out=held(tensor * places, width),
        gains_out=held(8, width, dtype=F32),
        bias_out=held(8 * tensor, LANES, dtype=F32),
        home_in=held(nrow, two, places, width),
        small=held(tensor, dp, 8, wide, dtype=F32),
        small_theirs=held(tensor, dp, 8, wide, dtype=F32),
        small_sent=held(2, chips // 2, 8, wide, dtype=F32),
        small_taken=held(2, chips // 2, 8, wide, dtype=F32),
        block_send=sems((nrow,)), block_recv=sems((tensor,)), pass_send=sems((tensor,)), pass_recv=sems((tensor,)),
        local_sem=sems((3,)), small_send=sems((tensor,)), small_recv=sems((tensor,)), own_sem=sems((4,)),
        ring_send=sems((2, 2, 2, chips // 2)), ring_recv=sems((2, 2, 2, chips // 2)),
        over_send=sems((4, chips)), over_recv=sems((4, chips)), kept_sem=sems((2, dp // CORES)),
        small_sem=sems((2,)), tiny_send=sems((2, chips // 2)), tiny_recv=sems((2, chips // 2)),
        home_send=sems((tensor,)), home_recv=sems((nrow, two)),
        free_sem=pltpu.SemaphoreType.REGULAR((2,)),
    )
    inputs = ["rows", "enc_lengths", "dec_lengths", "gains", "bias_w", "buckets"]
    inputs += ["query_key_w", "value_w", "out_w", "first_w", "second_w", "inner_w", "outer_w"]
    outputs = dict(
        home_out=rows.shape, gain_out=(3, 1, depth), kind_out=(heads_at, 1, kinds // dp), pair_out=(2, depth, block), value_out=(depth, block),
        out_out=(block, depth), first_out=(depth, block), second_out=(depth, block), inner_out=(depth, units),
        outer_out=(depth, units),
    )
    return pl.pallas_call(
        functools.partial(fused_kernel, tensor, dp, heads_at, inputs + list(outputs) + list(scratch)),
        out_shape=tuple(jax.ShapeDtypeStruct(shape, F32) for shape in outputs.values()),
        in_specs=[ANY] + [VMEM] * 12,
        out_specs=(VMEM,) * len(outputs),
        scratch_shapes=list(scratch.values()),
        compiler_params=pltpu.CompilerParams(collective_id=3, has_side_effects=True, vmem_limit_bytes=VMEM_LIMIT),
        name="fused",
    )(rows, enc_lengths, dec_lengths, gains, bias, buckets, *weights)


def pad_to(array, *shape):
    return jnp.pad(array, [(0, full - have) for full, have in zip(shape, array.shape)])


def shards(
    tensor, dp, section_rows, enc_lengths, dec_lengths, enc_buckets, dec_buckets, norm_gains, rel_bias,
    query_key_w, value_w, attn_out_w, cross_first, cross_second, ff_in, ff_out,
):
    depth = value_w.shape[1]
    width = section_rows.shape[-1]
    on_encoder = lax.axis_index("pipe") == 0
    ranges = -(-enc_buckets.shape[0] // LANES) * LANES
    dec_all = jnp.concatenate([jnp.zeros((dec_buckets.shape[0] - 1,), jnp.int32), dec_buckets])
    bucket_row = jnp.where(on_encoder, pad_to(enc_buckets, ranges), pad_to(dec_all, ranges))[None]
    gains = norm_gains.transpose(1, 0, 2)
    bias = rel_bias.transpose(2, 0, 1)
    weights = (query_key_w[0], value_w[0], attn_out_w[0], cross_first[0], cross_second[0], ff_in[0], ff_out[0].T)
    run = fused if fits_fused(tensor, dp, depth, ff_in.shape[2], width) else in_three
    home, gain, kind, *grads, outer = run(
        tensor, dp, section_rows[0], enc_lengths, dec_lengths, gains, bias, bucket_row, weights
    )
    if run is fused:
        home, gain, kind, *grads, outer = copied(home, gain, kind, *grads, outer)
    return (
        (home[None], gain.transpose(1, 0, 2), kind.transpose(1, 2, 0))
        + tuple(grad[None] for grad in grads)
        + (outer.T[None],)
    )


def copied(*results):
    def kernel(*refs):
        for source, target in zip(refs[: len(results)], refs[len(results) :]):
            target[...] = source[...]

    return pl.pallas_call(
        kernel,
        out_shape=tuple(jax.ShapeDtypeStruct(result.shape, result.dtype) for result in results),
        in_specs=[VMEM] * len(results),
        out_specs=(VMEM,) * len(results),
        name="copied",
    )(*results)


def in_three(tensor, dp, section_rows, enc_lengths, dec_lengths, gains, bias, buckets, weights):
    query_key, value, out, first, second, inner, outer = weights
    nrow, _, _, width = section_rows.shape
    heads_at, _, kinds = bias.shape
    lengths = pad_to(jnp.concatenate([enc_lengths, dec_lengths], axis=0), 8, LANES)
    table = pad_to(bias[:, 0], 8, LANES)
    depth, block = value.shape
    units = inner.shape[1]
    pack = jnp.concatenate([query_key[1], value, query_key[0], out.T, first, second, inner, outer], axis=1)
    rows, gathered, lengths, tables = gather(tensor, dp, section_rows, pack, lengths, table)
    grads, finished, gain_grads, bias = blocks(
        tensor, dp, heads_at, kinds, rows, gathered.reshape(tensor, width, -1), gains, lengths, tables, buckets
    )
    held_kinds = kinds // dp
    wide = -(-max(depth, held_kinds) // LANES) * LANES
    gain_part = pad_to(gain_grads[:3].reshape(3, dp, depth).transpose(1, 0, 2), dp, 3, wide)
    bias_part = bias.reshape(tensor, 8, LANES)[:, :heads_at, :kinds].reshape(tensor, heads_at, dp, held_kinds)
    bias_part = pad_to(bias_part.transpose(0, 2, 1, 3), tensor, dp, 5, wide)
    small = jnp.concatenate([jnp.broadcast_to(gain_part[None], (tensor,) + gain_part.shape), bias_part], axis=2)
    total, tiny, home = scatter(
        tensor, dp, grads.reshape(tensor, dp, depth, -1), small, finished.reshape(tensor, -1, width), nrow
    )
    key, value, query, out, first, second = [total[:, k * block : (k + 1) * block] for k in range(6)]
    inner, outer = total[:, 6 * block : 6 * block + units], total[:, 6 * block + units :]
    return (
        home.astype(F32), tiny[:3, None, :depth], tiny[3 : 3 + heads_at, None, :held_kinds],
        jnp.stack([query, key]), value, out.T, first, second, inner, outer,
    )


def solution(mesh):
    sizes = dict(mesh.shape)
    return jax.shard_map(
        functools.partial(shards, sizes["tensor"], sizes["dp"]),
        mesh=mesh,
        in_specs=(
            P("pipe", "dp", None, "tensor", None),
            P("dp", None),
            P("dp", None),
            P(),
            P(),
            P("pipe", None, None),
            P("pipe", None, "tensor"),
            P("pipe", None, "dp", "tensor"),
            P("pipe", "dp", "tensor"),
            P("pipe", "tensor", "dp"),
            P("pipe", "dp", "tensor"),
            P("pipe", "dp", "tensor"),
            P("pipe", "dp", "tensor"),
            P("pipe", "tensor", "dp"),
        ),
        out_specs=(
            P("pipe", "dp", None, "tensor", None),
            P("pipe", None, "dp"),
            P("pipe", "dp", "tensor"),
            P("pipe", None, "dp", "tensor"),
            P("pipe", "dp", "tensor"),
            P("pipe", "tensor", "dp"),
            P("pipe", "dp", "tensor"),
            P("pipe", "dp", "tensor"),
            P("pipe", "dp", "tensor"),
            P("pipe", "tensor", "dp"),
        ),
        check_vma=False,
    )
```

```python
import functools
import types

import jax
import jax.numpy as jnp
from jax import lax
from jax.experimental import pallas as pl
from jax.experimental.pallas import tpu as pltpu
from jax.sharding import PartitionSpec as P

MESH = pl.DeviceIdType.MESH
F32 = jnp.float32
BF16 = jnp.bfloat16
EPSILON = 1e-06
NEGATIVE = -1000000000.0
HEAD_DIM = 64
CORES = 2
LANES = 128
VMEM_LIMIT = 62 << 20
ANY = pl.BlockSpec(memory_space=pl.ANY)
VMEM = pl.BlockSpec(memory_space=pltpu.VMEM)


def nn(a, b):
    return lax.dot_general(a, b, (((1,), (0,)), ((), ())), preferred_element_type=F32)


def nt(a, b):
    return lax.dot_general(a, b, (((1,), (1,)), ((), ())), preferred_element_type=F32)


def tn(a, b):
    return lax.dot_general(a, b, (((0,), (0,)), ((), ())), preferred_element_type=F32)


class Place:
    def __init__(self, tensor, dp):
        self.tensor = tensor
        self.groups = dp // CORES
        self.chips = tensor * self.groups
        self.pipe = lax.axis_index("pipe")
        self.d = lax.axis_index("dp")
        self.t = lax.axis_index("tensor")
        self.core = lax.rem(self.d, CORES)
        self.group = self.d // CORES
        odd = lax.rem(self.group, 2)
        self.ring = self.group * tensor + self.t + odd * (tensor - 1 - 2 * self.t)

    def at(self, ring):
        group = ring // self.tensor
        along = lax.rem(ring, self.tensor)
        odd = lax.rem(group, 2)
        return group, along + odd * (self.tensor - 1 - 2 * along)

    def neighbour(self, step):
        group, t = self.at(lax.rem(self.ring + step + self.chips, self.chips))
        return {"dp": group * CORES + self.core, "tensor": t}

    def sibling(self):
        return {"dp": self.group * CORES + 1 - self.core}


def meet(devices):
    barrier = pltpu.get_barrier_semaphore()
    for device in devices:
        pl.semaphore_signal(barrier, inc=1, device_id=device, device_id_type=MESH)
    pl.semaphore_wait(barrier, len(devices))


def halves(rows, columns):
    if rows % 32 == 0:
        return [(pl.ds(k * (rows // 2), rows // 2), pl.ds(0, columns)) for k in range(2)]
    cut = columns // LANES // 2 * LANES
    return [(pl.ds(0, rows), pl.ds(0, cut)), (pl.ds(0, rows), pl.ds(cut, columns - cut))]


def gather_kernel(
    tensor, dp, rows_ref, pack_ref, length_ref, table_ref, x_ref, w_ref, lengths_ref, tables_ref,
    local_sem, block_send, block_recv, pass_send, pass_recv, small_send, small_recv,
    ring_send, ring_recv, core_send, core_recv,
):
    here = Place(tensor, dp)
    c, t, chips = here.core, here.t, here.chips
    nrow = rows_ref.shape[0]
    sibling = here.sibling()
    to_right, to_left = here.neighbour(1), here.neighbour(-1)
    others = [{"tensor": lax.rem(t + k, tensor)} for k in range(1, tensor)]
    meet([to_right, to_left, sibling] + others)

    lengths = pltpu.make_async_remote_copy(
        length_ref, lengths_ref.at[c], small_send.at[0], small_recv.at[0], device_id=sibling, device_id_type=MESH
    )
    lengths.start()
    own_lengths = pltpu.make_async_copy(length_ref, lengths_ref.at[c], local_sem.at[0])
    own_lengths.start()
    own_table = pltpu.make_async_copy(table_ref, tables_ref.at[t], local_sem.at[1])
    own_table.start()
    tables = []
    for k in range(1, tensor):
        tables.append(
            pltpu.make_async_remote_copy(
                table_ref, tables_ref.at[t], small_send.at[k], small_recv.at[k], device_id=others[k - 1], device_id_type=MESH
            )
        )
        tables[-1].start()

    def to_chip(i):
        return pltpu.make_async_remote_copy(
            rows_ref.at[i], x_ref.at[:, t], block_send.at[i], block_recv.at[t],
            device_id={"tensor": nrow * c + i}, device_id_type=MESH,
        )

    def kept(i):
        return pltpu.make_async_copy(rows_ref.at[i], x_ref.at[:, t], local_sem.at[2])

    def kept_pass(i):
        return pltpu.make_async_remote_copy(
            rows_ref.at[i], x_ref.at[:, t], pass_send.at[t], pass_recv.at[t], device_id=sibling, device_id_type=MESH
        )

    def passed(s):
        return pltpu.make_async_remote_copy(
            x_ref.at[:, s], x_ref.at[:, s], pass_send.at[s], pass_recv.at[s], device_id=sibling, device_id_type=MESH
        )

    for i in range(nrow):
        mine = nrow * c + i == t

        @pl.when(mine)
        def _():
            kept(i).start()
            kept_pass(i).start()

        @pl.when(jnp.logical_not(mine))
        def _():
            to_chip(i).start()

    parts = halves(*pack_ref.shape)
    own_pack = pltpu.make_async_copy(pack_ref, w_ref.at[t, here.d], local_sem.at[3])
    own_pack.start()

    def shard(ring, part):
        group, at = here.at(ring)
        return w_ref.at[at, group * CORES + c, parts[part][0], parts[part][1]]

    def source(step, part):
        return lax.rem(here.ring + (1 if part else -1) * step + chips, chips)

    def onward(step, part, first=False):
        slot = shard(source(step, part), part)
        return pltpu.make_async_remote_copy(
            pack_ref.at[parts[part][0], parts[part][1]] if first else slot, slot,
            ring_send.at[part, step], ring_recv.at[part, step],
            device_id=to_left if part else to_right, device_id_type=MESH,
        )

    def across(step, part, first=False):
        slot = shard(source(step, part), part)
        return pltpu.make_async_remote_copy(
            pack_ref.at[parts[part][0], parts[part][1]] if first else slot, slot,
            core_send.at[part, step], core_recv.at[part, step], device_id=sibling, device_id_type=MESH,
        )

    for part in range(2):
        onward(0, part, True).start()
        across(0, part, True).start()

    takes = t // nrow == c
    for s in range(tensor):

        @pl.when(jnp.logical_and(takes, s != t))
        def _():
            pltpu.make_async_remote_copy(
                rows_ref.at[0], x_ref.at[:, s], block_send.at[0], block_recv.at[s], device_id=sibling, device_id_type=MESH
            ).wait_recv()
            passed(s).start()

    @pl.loop(1, chips)
    def _(step):
        for part in range(2):
            onward(step - 1, part).wait_recv()

            @pl.when(step < chips - 1)
            def _():
                onward(step, part).start()

            across(step, part).start()

    @pl.loop(0, chips)
    def _(step):
        for part in range(2):

            @pl.when(step < chips - 1)
            def _():
                onward(step, part).wait_send()

            across(step, part).wait_send()
            across(step, part).wait_recv()

    for i in range(nrow):
        mine = nrow * c + i == t

        @pl.when(mine)
        def _():
            kept(i).wait()
            kept_pass(i).wait_send()

        @pl.when(jnp.logical_not(mine))
        def _():
            to_chip(i).wait_send()

    for s in range(tensor):

        @pl.when(jnp.logical_and(takes, s != t))
        def _():
            passed(s).wait_send()

        @pl.when(jnp.logical_not(takes))
        def _():
            passed(s).wait_recv()

    lengths.wait()
    own_lengths.wait()
    own_table.wait()
    own_pack.wait()
    for table in tables:
        table.wait()


def gather(tensor, dp, rows, pack, lengths, table):
    chips = tensor * dp // CORES
    nrow, two, places, width = rows.shape
    sems = pltpu.SemaphoreType.DMA
    return pl.pallas_call(
        functools.partial(gather_kernel, tensor, dp),
        out_shape=(
            jax.ShapeDtypeStruct((two, tensor, places, width), rows.dtype),
            jax.ShapeDtypeStruct((tensor, dp) + pack.shape, pack.dtype),
            jax.ShapeDtypeStruct((CORES,) + lengths.shape, lengths.dtype),
            jax.ShapeDtypeStruct((tensor,) + table.shape, table.dtype),
        ),
        in_specs=[ANY] * 4,
        out_specs=(ANY,) * 4,
        scratch_shapes=[
            sems((4,)), sems((nrow,)), sems((tensor,)), sems((tensor,)), sems((tensor,)), sems((tensor,)), sems((tensor,)),
            sems((2, chips)), sems((2, chips)), sems((2, chips)), sems((2, chips)),
        ],
        compiler_params=pltpu.CompilerParams(collective_id=0, has_side_effects=True),
        name="gather",
    )(rows, pack, lengths, table)


def scatter_kernel(
    tensor, dp, grads_ref, small_ref, rows_ref, out_ref, small_out, rows_out,
    own, theirs, taken, small_own, small_theirs, small_taken, total,
    own_sem, core_send, core_recv, ring_send, ring_recv,
    sown_sem, score_send, score_recv, sring_send, sring_recv, block_send, block_recv, local_sem,
):
    here = Place(tensor, dp)
    c, t, chips = here.core, here.t, here.chips
    nrow = rows_out.shape[0]
    sibling = here.sibling()
    to_right, to_left = here.neighbour(1), here.neighbour(-1)
    line = [
        {"dp": here.group * CORES + lax.rem(c + j, CORES), "tensor": lax.rem(t + k, tensor)}
        for j in range(CORES)
        for k in range(tensor)
        if j + k > 0
    ]
    meet([to_right, to_left] + line)

    half = tensor // 2
    owner = t // nrow

    def block(k):
        place = here.pipe * (c * half + k % half) + (1 - here.pipe) * k
        which = here.pipe * (k // half) + (1 - here.pipe) * c
        return place, which

    def home(k):
        place, which = block(k)
        slot = rows_out.at[lax.rem(t, nrow), which]
        recv = block_recv.at[lax.rem(t, nrow), which]
        return (
            jnp.logical_and(place == t, owner == c),
            lambda: pltpu.make_async_copy(rows_ref.at[k], slot, recv),
            lambda: pltpu.make_async_remote_copy(
                rows_ref.at[k], slot, block_send.at[k], recv,
                device_id={"dp": here.group * CORES + owner, "tensor": place}, device_id_type=MESH,
            ),
        )

    for k in range(tensor):
        stays, inside, away = home(k)

        @pl.when(stays)
        def _():
            inside().start()

        @pl.when(jnp.logical_not(stays))
        def _():
            away().start()

    def across(ring):
        group, at = here.at(ring)
        return (
            pltpu.make_async_remote_copy(
                grads_ref.at[at, group * CORES + 1 - c], theirs.at[ring], core_send.at[ring], core_recv.at[ring],
                device_id=sibling, device_id_type=MESH,
            ),
            pltpu.make_async_remote_copy(
                small_ref.at[at, group * CORES + 1 - c], small_theirs.at[ring], score_send.at[ring], score_recv.at[ring],
                device_id=sibling, device_id_type=MESH,
            ),
        )

    def fetch(ring):
        group, at = here.at(ring)
        return (
            pltpu.make_async_copy(grads_ref.at[at, group * CORES + c], own.at[ring], own_sem.at[ring]),
            pltpu.make_async_copy(small_ref.at[at, group * CORES + c], small_own.at[ring], sown_sem.at[ring]),
        )

    def behind(step):
        return lax.rem(here.ring - step + chips, chips)

    def order(k):
        off = (2 * lax.rem(k, 2) - 1) * (k // 2 + 1) * (1 - k // (chips - 1))
        return lax.rem(here.ring + chips + off, chips)

    @pl.loop(0, chips)
    def _(k):
        for copy in across(order(k)) + fetch(order(k)):
            copy.start()

    rows, columns = out_ref.shape
    parts = halves(rows, columns)

    def add(ring, part, step, last):
        height = parts[part][0].size
        piece = 16 if height % 16 == 0 else height

        @pl.loop(0, height // piece)
        def _(k):
            at = pl.ds(pl.multiple_of(parts[part][0].start + k * piece, 8), piece)
            where = (at, parts[part][1])
            value = own[(ring,) + where].astype(F32) + theirs[(ring,) + where].astype(F32)
            if step is not None:
                value = value + taken[(step,) + where].astype(F32)
            if last:
                total[where] = value
            else:
                own[(ring,) + where] = value.astype(BF16)

    def onward(ring, step, part):
        where = (parts[part][0], parts[part][1])
        return pltpu.make_async_remote_copy(
            own.at[(ring,) + where], taken.at[(step,) + where], ring_send.at[part, step], ring_recv.at[part, step],
            device_id=to_left if part else to_right, device_id_type=MESH,
        )

    def small_onward(ring, step):
        return pltpu.make_async_remote_copy(
            small_own.at[ring], small_taken.at[step], sring_send.at[step], sring_recv.at[step],
            device_id=to_right, device_id_type=MESH,
        )

    def ready(ring):
        for copy in across(ring):
            copy.wait_recv()
        for copy in fetch(ring):
            copy.wait()

    def ahead(step):
        return lax.rem(here.ring + step, chips)

    half_chips = chips // 2

    @pl.loop(0, chips - 1)
    def _(step):
        right, left = behind(step + 1), ahead(step + 1)

        @pl.when(step < half_chips)
        def _():
            ready(right)

        @pl.when(step < chips - 1 - half_chips)
        def _():
            ready(left)

        @pl.when(step == 0)
        def _():
            add(right, 0, None, False)
            add(left, 1, None, False)
            small_own[right] = small_own[right] + small_theirs[right]

        @pl.when(step > 0)
        def _():
            onward(right, step - 1, 0).wait_recv()
            add(right, 0, step - 1, False)
            onward(right, step, 0).start()
            onward(left, step - 1, 1).wait_recv()
            add(left, 1, step - 1, False)
            onward(left, step, 1).start()
            small_onward(right, step - 1).wait_recv()
            small_own[right] = small_own[right] + small_theirs[right] + small_taken[step - 1]
            small_onward(right, step).start()

        @pl.when(step == 0)
        def _():
            onward(right, 0, 0).start()
            onward(left, 0, 1).start()
            small_onward(right, 0).start()

    ready(here.ring)
    for part in range(2):
        onward(here.ring, chips - 2, part).wait_recv()
        add(here.ring, part, chips - 2, True)
    small_onward(here.ring, chips - 2).wait_recv()
    small_out[...] = small_own[here.ring] + small_theirs[here.ring] + small_taken[chips - 2]
    finish = pltpu.make_async_copy(total, out_ref, local_sem.at[0])
    finish.start()

    @pl.loop(0, chips)
    def _(step):
        @pl.when(step < chips - 1)
        def _():
            onward(behind(step + 1), step, 0).wait_send()
            onward(ahead(step + 1), step, 1).wait_send()
            small_onward(behind(step + 1), step).wait_send()

        for copy in across(step):
            copy.wait_send()

    for k in range(tensor):
        stays, inside, away = home(k)

        @pl.when(jnp.logical_not(stays))
        def _():
            away().wait_send()

    for i in range(nrow):
        for which in range(2):
            pltpu.make_async_copy(rows_ref.at[0], rows_out.at[i, which], block_recv.at[i, which]).wait()
    finish.wait()


def scatter(tensor, dp, grads, small, rows, nrow):
    chips = tensor * dp // CORES
    shard = grads.shape[2:]
    tiny = small.shape[2:]
    sems = pltpu.SemaphoreType.DMA
    return pl.pallas_call(
        functools.partial(scatter_kernel, tensor, dp),
        out_shape=(
            jax.ShapeDtypeStruct(shard, F32),
            jax.ShapeDtypeStruct(tiny, F32),
            jax.ShapeDtypeStruct((nrow, 2) + rows.shape[1:], rows.dtype),
        ),
        in_specs=[ANY] * 3,
        out_specs=(ANY, VMEM, ANY),
        scratch_shapes=[
            pltpu.VMEM((chips,) + shard, BF16),
            pltpu.VMEM((chips,) + shard, BF16),
            pltpu.VMEM((chips - 1,) + shard, BF16),
            pltpu.VMEM((chips,) + tiny, F32),
            pltpu.VMEM((chips,) + tiny, F32),
            pltpu.VMEM((chips - 1,) + tiny, F32),
            pltpu.VMEM(shard, F32),
            sems((chips,)), sems((chips,)), sems((chips,)), sems((2, chips)), sems((2, chips)),
            sems((chips,)), sems((chips,)), sems((chips,)), sems((chips,)), sems((chips,)),
            sems((tensor,)), sems((nrow, 2)), sems((1,)),
        ],
        compiler_params=pltpu.CompilerParams(collective_id=1, has_side_effects=True, vmem_limit_bytes=VMEM_LIMIT),
        name="scatter",
    )(grads, small, rows)


KEY, VALUE, QUERY, OUT, FIRST, SECOND = range(6)
ATTN, CROSS, INNER, OUTER = range(4)
SEGS_HELD = 6


def rms(value):
    return lax.rsqrt(jnp.mean(value * value, axis=-1, keepdims=True) + EPSILON)


def in_rows(count, body, piece=32):
    @pl.loop(0, count // piece)
    def _(k):
        body(pl.ds(pl.multiple_of(k * piece, piece), piece))


def columns_of(count, body, piece=256):
    @pl.loop(0, count // piece)
    def _(k):
        body(pl.ds(pl.multiple_of(k * piece, piece), piece), k)


def normalize(source, gain, target, count):
    def body(at):
        value = source[at, :].astype(F32)
        target[at, :] = (value * rms(value) * gain).astype(BF16)

    in_rows(count, body)


def normalize_back(source, gain, incoming, total, gain_parts, count, fresh):
    gain_parts[...] = jnp.zeros_like(gain_parts)

    def body(at):
        value, back = source[at, :].astype(F32), incoming[at, :]
        scale = rms(value)
        unit = value * scale
        gain_parts[...] += jnp.sum((back * unit).reshape(-1, 8, back.shape[-1]), axis=0)
        back = back * gain
        back = scale * (back - unit * jnp.mean(back * unit, axis=-1, keepdims=True))
        total[at, :] = back if fresh else total[at, :] + back

    in_rows(count, body)


def project(left, weight, target, count):
    def body(at, k):
        target[0:count, at] = nn(left[0:count, :], weight[:, at]).astype(target.dtype)

    columns_of(weight.shape[1], body)


def project_back(left, weight, total, count, fresh):
    def body(at, k):
        value = nt(left[0:count, :], weight[at, :])
        total[0:count, at] = value if fresh else total[0:count, at] + value

    columns_of(weight.shape[0], body)


def to_bf16(source, target, rows):
    def body(at):
        target[at, :] = source[at, :].astype(BF16)

    in_rows(rows, body)


def turn(left, turned, rows):
    def body(at, k):
        turned[at, 0:rows] = left[0:rows, at].T

    columns_of(left.shape[1], body, LANES)


def lane_half(shape, part):
    return lax.broadcasted_iota(jnp.int32, shape, 1) // HEAD_DIM == part


def attend(keys, values, queries, mixture, probs, rows, span, pairs, mask, bias, after):
    @pl.loop(0, pairs)
    def _(pair):
        lanes = pl.ds(pl.multiple_of(pair * LANES, LANES), LANES)
        key, query = keys[0:span, lanes], queries[0:rows, lanes]
        value_t = values[0:span, lanes].T
        mixed = []
        for part in range(2):
            one = jnp.where(lane_half(query.shape, part), query, jnp.zeros_like(query))
            scores = nt(key, one) + mask[0:span, 0:rows]
            if bias is not None:
                scores = scores + bias(2 * pair + part)
            scores = jnp.exp(scores - jnp.max(scores, axis=0, keepdims=True))
            scores = (scores * (1.0 / jnp.sum(scores, axis=0, keepdims=True))).astype(BF16)
            probs[2 * pair + part, 0:span, 0:rows] = scores
            mixed.append(nn(value_t[part * HEAD_DIM : (part + 1) * HEAD_DIM, :], scores))
        mixture[0:rows, lanes] = jnp.concatenate(mixed, axis=0).T.astype(BF16)
        after(pair)


def attend_back(keys, values, queries, back, probs, rows, span, pairs, each, before, after):
    @pl.loop(0, pairs)
    def _(pair):
        before(pair)
        lanes = pl.ds(pl.multiple_of(pair * LANES, LANES), LANES)
        key, value = keys[0:span, lanes], values[0:span, lanes]
        query, given = queries[0:rows, lanes], back[0:rows, lanes]
        key_t = key.T
        d_key, d_value, d_query = None, None, []
        for part in range(2):
            side = lane_half(query.shape, part)
            query_one = jnp.where(side, query, jnp.zeros_like(query))
            given_one = jnp.where(side, given, jnp.zeros_like(given))
            prob = probs[2 * pair + part, 0:span, 0:rows]
            wide = prob.astype(F32)
            d_prob = nt(value, given_one)
            d_score = (wide * (d_prob - jnp.sum(wide * d_prob, axis=0, keepdims=True))).astype(BF16)
            if each is not None:
                each(2 * pair + part, d_score)
            of_key, of_value = nn(d_score, query_one), nn(prob, given_one)
            d_key = of_key if d_key is None else d_key + of_key
            d_value = of_value if d_value is None else d_value + of_value
            d_query.append(nn(key_t[part * HEAD_DIM : (part + 1) * HEAD_DIM, :], d_score))
        keys[0:span, lanes] = d_key.astype(BF16)
        values[0:span, lanes] = d_value.astype(BF16)
        queries[0:rows, lanes] = jnp.concatenate(d_query, axis=0).T.astype(BF16)
        after(pair)


def segments(lengths_row, shape, axis, first):
    lane = lax.broadcasted_iota(jnp.int32, lengths_row.shape, 1)
    places = lax.broadcasted_iota(jnp.int32, shape, axis) + first
    ids = jnp.zeros(shape, jnp.int32)
    for c in range(SEGS_HELD):
        bound = jnp.sum(jnp.where(lane <= c, lengths_row, 0), axis=1, keepdims=True)
        ids = ids + (places >= bound).astype(jnp.int32)
    return ids


def masked(allowed):
    return jnp.where(allowed, 0.0, NEGATIVE).astype(F32)


def nothing(*unused, **named):
    pass


def work(r, here, supply, drain, tensor, heads_at):
    c, t = here.core, here.t
    width = r.hidden.shape[1]
    tall = r.hidden.shape[0]
    block = width // tensor
    half_width = width // 2
    units = r.inner.shape[2]
    places = r.x.shape[2]
    sibling = here.sibling()
    across = [{"pipe": 1 - here.pipe, "dp": here.group * CORES + k} for k in range(CORES)]
    nrow = tensor // CORES
    rows_e, span_e, rows_d, span_d = tall // 2, tall, tall // 4, tall // 2
    pairs_here = half_width // LANES
    near_lanes = pl.ds(pl.multiple_of(c * half_width, half_width), half_width)
    far_lanes = pl.ds(pl.multiple_of((1 - c) * half_width, half_width), half_width)
    lane_halves = [slice(k * half_width, (k + 1) * half_width) for k in range(CORES)]

    def move(source, target, sends, recvs, device):
        return pltpu.make_async_remote_copy(
            source, target, r.send_sem.at[sends], r.recv_sem.at[recvs], device_id=device, device_id_type=MESH
        )

    def lengths_row(first):
        return r.lengths[t // nrow, pl.ds(first + lax.rem(t, nrow), 1), :]

    def pair_lanes(pair):
        return pl.ds(pair * LANES if isinstance(pair, int) else pl.multiple_of(pair * LANES, LANES), LANES)

    def vector_row(head):
        return (head // heads_at) * 8 + lax.rem(head, heads_at)

    def bias_vectors():
        buckets = lax.broadcasted_iota(jnp.int32, r.onehot.shape, 0) == r.buckets[0:1, :]
        r.onehot[...] = buckets.astype(F32)
        for tt in range(tensor):
            r.vectors[pl.ds(8 * tt, 8), :] = lax.dot_general(
                r.tables[tt][:, 0 : r.onehot.shape[0]], r.onehot[...], (((1,), (0,)), ((), ())),
                precision=lax.Precision.HIGHEST, preferred_element_type=F32,
            )

    def rows_ready(span, rows, first_block):
        @pl.loop(0, span // places)
        def _(k):
            value = r.x[k // tensor, lax.rem(k, tensor)].astype(F32)
            at = pl.ds(pl.multiple_of(k * places, places), places)
            r.hidden[at, :] = (value * rms(value) * r.gains[0]).astype(BF16)

        for k in range(rows // places):
            r.own_x[k * places : (k + 1) * places, :] = r.x[first_block // tensor, lax.rem(first_block, tensor) + k]

    def untangle(source, first, count):
        for tt in range(tensor):
            for k in range(count):
                r.square[first + k, :, tt * block : (tt + 1) * block] = source[tt, :, k * block : (k + 1) * block]

    def self_forward(span, rows, first_row, group):
        def bias(head):
            pieces = []
            for j in range(span // LANES):
                start = pl.multiple_of(first_row + span - LANES - j * LANES, LANES)
                row = r.vectors[pl.ds(vector_row(head), 1), pl.ds(start, rows + LANES)]
                wide = jnp.broadcast_to(row, (LANES, rows + LANES))
                pieces.append(pltpu.roll(wide, rows + 1, 1, stride=1, stride_axis=0)[:, 0:rows])
            return jnp.concatenate(pieces, axis=0)

        untangle(r.raw_a, KEY, 2)
        untangle(r.raw_a.at[:, :, pl.ds(2 * block, 2 * block)], QUERY, 2)
        project(r.hidden, r.square.at[KEY], r.keys, span)
        supply.pump()
        project(r.hidden, r.square.at[VALUE], r.values, span)
        project(r.hidden.at[pl.ds(first_row, rows)], r.square.at[QUERY], r.queries, rows)
        supply.pump()
        after = at_each(range(width // LANES), supply.pump)

        attend(r.keys, r.values, r.queries, r.mixture, r.probs, rows, span, width // LANES, r.mask, bias, after)
        project_back(r.mixture, r.square.at[OUT], r.resid_mid, rows, True)

        def add(at):
            r.resid_mid[at, :] += r.own_x[at, :].astype(F32)

        in_rows(rows, add)
        supply.pump(until=group)
        supply.finish(group)

    def at_each(places, do):
        def hook(n):
            for place in places:

                @pl.when(n == place)
                def _():
                    do()

        return hook

    def feed_forward(rows, hook=nothing):
        @pl.loop(0, tensor)
        def _(tt):
            def body(at, k):
                value = nn(r.second[0:rows, :], r.inner[tt, :, at])
                cdf = 0.5 * (1.0 + lax.erf(value * 0.7071067811865476))
                r.ff[tt, 0:rows, at] = (value * cdf).astype(BF16)
                slope = cdf + value * jnp.exp(-0.5 * value * value) * 0.3989422804014327
                r.ff[tensor + tt, 0:rows, at] = slope.astype(BF16)
                hook(tt * (units // 256) + k)

            columns_of(units, body)

    def feed_out(target, rows, hook=nothing):
        @pl.loop(0, tensor)
        def _(tt):
            def body(at, k):
                target[0:rows, at] += nt(r.ff[tt, 0:rows, :], r.outer[tt, at, :])
                hook(tt * (width // 256) + k)

            columns_of(width, body)

    def feed_back(rows, ready, hook=nothing):
        r.summed[0:rows, :] = jnp.zeros((rows, width), F32)

        @pl.loop(0, tensor)
        def _(tt):
            def body(at, k):
                if ready:
                    value = r.ff[tensor + tt, rows : 2 * rows, at].astype(F32)
                else:
                    value = nn(r.d_branch[0:rows, :], r.outer[tt, :, at])
                r.ff[tensor + tt, 0:rows, at] = (value * r.ff[tensor + tt, 0:rows, at].astype(F32)).astype(BF16)

            columns_of(units, body)

            def back(at, k):
                r.summed[0:rows, at] += nt(r.ff[tensor + tt, 0:rows, :], r.inner[tt, at, :])

            columns_of(width, back)
            hook(tt)

    def feed_grads(rows, turned, first, which, hook=nothing):
        @pl.loop(0, tensor)
        def _(tt):
            slot = lax.rem(tt, 2)

            @pl.when(tt >= 2)
            def _():
                drain.release(which, tt - 2, slot)

            def body(at, k):
                r.stage[slot, :, at] = nn(turned[:, 0:rows], r.ff[first + tt, 0:rows, at]).astype(BF16)
                hook(tt * (units // 256) + k)

            columns_of(units, body)
            drain.emit(which, tt, slot)

        for tt in range(tensor - 2, tensor):
            drain.release(which, tt, tt % 2)

    def square_grads(rows, which, products, hook):
        for k in range(tensor // 2):
            for j, (turned, right) in enumerate(products):
                value = nn(turned[:, 0:rows], right[0:rows, 2 * k * block : 2 * (k + 1) * block]).astype(BF16)
                for slot in range(2):
                    r.stage[slot, :, j * block : (j + 1) * block] = value[:, slot * block : (slot + 1) * block]
            for slot in range(2):
                drain.emit(which, 2 * k + slot, slot)
            hook(k)
            for slot in range(2):
                drain.release(which, 2 * k + slot, slot)

    def gain_done(which):
        r.gains_out[which : which + 1, :] = jnp.sum(r.gain_parts[...], axis=0, keepdims=True)

    def self_backward(span, rows, first_row, steps, send_rows):
        mirror = (
            lax.broadcasted_iota(jnp.int32, (LANES, LANES), 0) + lax.broadcasted_iota(jnp.int32, (LANES, LANES), 1)
            == LANES - 1
        ).astype(BF16)
        to_bf16(r.d_resid, r.branch, rows)
        project(r.branch, r.square.at[OUT], r.d_branch, rows)
        r.diagonals[...] = jnp.zeros_like(r.diagonals)

        def each(head, d_score):
            for j in range(span // LANES):
                start = pl.multiple_of(first_row + span - LANES - j * LANES, LANES)
                piece = nn(mirror, d_score[j * LANES : (j + 1) * LANES, :])
                piece = jnp.concatenate([piece, jnp.zeros((LANES, LANES), F32)], axis=1)
                piece = pltpu.roll(piece, 0, 1, stride=1, stride_axis=0)
                at = (pl.ds(vector_row(head), 1), pl.ds(start, rows + LANES))
                r.diagonals[at] += jnp.sum(piece, axis=0, keepdims=True)

        pairs = width // LANES
        attend_back(
            r.keys, r.values, r.queries, r.d_branch, r.probs, rows, span, pairs, each, nothing,
            at_each(range(pairs), steps),
        )
        far = pl.ds(pl.multiple_of((1 - c) * rows, rows), rows)
        near = pl.ds(pl.multiple_of(c * rows, rows), rows)
        trades = [
            move(source.at[far], r.taken_pair.at[k, pl.ds(0, rows)], 12 + k, 12 + k, sibling)
            for k, source in enumerate((r.keys, r.values))
        ]
        for trade in trades:
            trade.start()
        steps()
        turn(r.branch, r.turned, rows)
        turn(r.hidden.at[pl.ds(first_row, rows)], r.turned_more, rows)
        for tt in range(tensor):
            at = pl.ds(8 * tt, 8)
            r.bias_out[at, 0 : r.onehot.shape[0]] = lax.dot_general(
                r.diagonals[at, :], r.onehot[...], (((1,), (1,)), ((), ())),
                precision=lax.Precision.HIGHEST, preferred_element_type=F32,
            )
        steps()
        project_back(r.queries, r.square.at[QUERY], r.summed, rows, True)
        for trade in trades:
            trade.wait_recv()
        for k, source in enumerate((r.keys, r.values)):
            r.d_pair[k, 0:rows, :] = (source[near, :].astype(F32) + r.taken_pair[k, 0:rows, :].astype(F32)).astype(BF16)
        project_back(r.d_pair.at[0], r.square.at[KEY], r.summed, rows, False)
        project_back(r.d_pair.at[1], r.square.at[VALUE], r.summed, rows, False)
        steps()
        normalize_back(r.own_x, r.gains[0], r.summed, r.d_resid, r.gain_parts, rows, False)
        gain_done(0)
        send_rows()
        drain.small_begin()
        products = [(r.turned_more, r.d_pair.at[0]), (r.turned_more, r.d_pair.at[1]), (r.turned_more, r.queries), (r.turned, r.mixture)]
        square_grads(rows, ATTN, products, nothing)
        for trade in trades:
            trade.wait_send()
        steps()
        drain.begin(ATTN)
        steps()
        drain.home_done()
        drain.rest(ATTN, 2)

    def parts_of(array):
        return [array.at[pl.ds(k * rows_d, rows_d)] for k in range(CORES)]

    def part_here(array):
        return array.at[pl.ds(pl.multiple_of(c * rows_d, rows_d), rows_d)]

    r.gains_out[...] = jnp.zeros_like(r.gains_out)
    r.bias_out[...] = jnp.zeros_like(r.bias_out)
    supply.start()

    def entry():
        supply.pump(2)
        supply.small()
        bias_vectors()
        supply.pump(2)
        supply.rows()

    def schedule(*items):
        left = list(items)

        def steps():
            for name, group, *n in left.pop(0) if left else ():
                getattr(drain, name)(group, *n)

        return steps

    @pl.when(here.pipe == 0)
    def _():
        supply.resume(ATTN, INNER, OUTER, CROSS)
        drain.order(CROSS, OUTER, INNER, ATTN)
        entry()
        rows, span = rows_e, span_e
        first_row = pl.multiple_of(c * rows, rows)
        seg_rows = segments(lengths_row(0), (span, 1), 0, 0)
        r.mask[...] = masked(seg_rows == segments(lengths_row(0), (1, rows), 1, first_row))
        supply.pump()
        rows_ready(span, rows, c * tensor)
        supply.pump(until=ATTN)
        supply.finish(ATTN)
        self_forward(span, rows, first_row, INNER)
        normalize(r.resid_mid, r.gains[1], r.second, rows)
        feed_forward(rows, at_each((3, 7, 11), supply.pump))
        supply.pump(until=OUTER)
        supply.finish(OUTER)
        r.resid_top[...] = r.resid_mid[...]
        feed_out(r.resid_top, rows, at_each((3, 7, 11), supply.pump))
        normalize(r.resid_top, r.gains[2], r.third, rows)
        r.mask[...] = masked(seg_rows == segments(lengths_row(nrow), (1, span_d), 1, 0))
        supply.pump(until=CROSS)
        supply.finish(CROSS)
        untangle(r.raw_c, FIRST, 2)
        mine = pl.ds(first_row, rows)
        other = pl.ds(pl.multiple_of((1 - c) * rows, rows), rows)
        trades = []
        for k, held in enumerate((r.cross_keys, r.cross_values)):
            r.send_pair[k] = nn(r.third[...], r.square[FIRST + k, :, far_lanes]).astype(BF16)
            trades.append(move(r.send_pair.at[k], held.at[mine], k, k, sibling))
            trades[-1].start()
        for k, held in enumerate((r.cross_keys, r.cross_values)):
            held[mine, :] = nn(r.third[...], r.square[FIRST + k, :, near_lanes]).astype(BF16)
        for k, part in enumerate(parts_of(r.cross_queries)):
            move(part, part, 2 + k, 2 + k, across[k]).wait_recv()
        for k, held in enumerate((r.cross_keys, r.cross_values)):
            move(r.send_pair.at[k], held.at[other], k, k, sibling).wait_recv()

        def mixtures(pair):
            at = pair_lanes(pair)
            return [
                pltpu.make_async_remote_copy(
                    r.cross_mixture.at[pl.ds(k * rows_d, rows_d), at], r.cross_in.at[c, :, at],
                    r.mix_send.at[k, pair], r.mix_recv.at[c, pair], device_id=across[k], device_id_type=MESH,
                )
                for k in range(CORES)
            ]

        def arrived(pair):
            for k in range(CORES):
                part = r.cross_back.at[pl.ds(k * rows_d, rows_d), pair_lanes(pair)]
                pltpu.make_async_remote_copy(
                    part, part, r.back_send.at[k, pair], r.back_recv.at[k, pair], device_id=across[k], device_id_type=MESH
                ).wait_recv()

        def returns(pair):
            at = pair_lanes(pair)
            return [
                pltpu.make_async_remote_copy(
                    d_cross.at[other, at], r.cross_taken.at[k, :, at],
                    r.give_send.at[k, pair], r.give_recv.at[k, pair], device_id=sibling, device_id_type=MESH,
                )
                for k, d_cross in enumerate((r.cross_keys, r.cross_values))
            ]

        attend(
            r.cross_keys, r.cross_values, r.cross_queries, r.cross_mixture, r.cross_probs, span_d, span, pairs_here,
            r.mask, None, lambda pair: [mix.start() for mix in mixtures(pair)],
        )
        supply.close()
        drain.free(0)
        turn(r.third, r.turned, rows)
        attend_back(
            r.cross_keys, r.cross_values, r.cross_queries, r.cross_back, r.cross_probs, span_d, span, pairs_here, None,
            arrived, lambda pair: [back.start() for back in returns(pair)],
        )
        answers = [
            move(part, r.cross_in_back.at[c], 8 + k, 8 + c, across[k]) for k, part in enumerate(parts_of(r.cross_queries))
        ]
        for answer in answers:
            answer.start()
        for k, d_cross in enumerate((r.cross_keys, r.cross_values)):
            r.d_pair[k, :, near_lanes] = d_cross[mine, :]
        for pair in range(pairs_here):
            for back in returns(pair):
                back.wait_recv()
        for k in range(2):
            r.d_pair[k, :, far_lanes] = r.cross_taken[k]
        drain.allow(0)
        square_grads(rows, CROSS, [(r.turned, r.d_pair.at[0]), (r.turned, r.d_pair.at[1])], nothing)
        drain.begin(CROSS)
        project_back(r.d_pair.at[0], r.square.at[FIRST], r.summed, rows, True)
        drain.tick(CROSS, 0)
        project_back(r.d_pair.at[1], r.square.at[SECOND], r.summed, rows, False)
        drain.tick(CROSS, 1)
        normalize_back(r.resid_top, r.gains[2], r.summed, r.d_resid, r.gain_parts, rows, True)
        gain_done(2)
        to_bf16(r.d_resid, r.d_branch, rows)
        turn(r.d_branch, r.turned, rows)
        drain.tick(CROSS, 2)
        feed_grads(rows, r.turned, 0, OUTER, at_each((6,), lambda: drain.tick(CROSS, 3)))
        drain.begin(OUTER)
        steps = schedule([("tick", CROSS, 4)], [("tick", OUTER, 0)], [("tick", OUTER, 1)], [("end", CROSS)])
        feed_back(rows, False, at_each(range(tensor), steps))
        drain.free(1)
        turn(r.second, r.turned, rows)
        drain.allow(1)
        feed_grads(rows, r.turned, tensor, INNER, at_each((2,), lambda: drain.tick(OUTER, 2)))
        drain.begin(INNER)
        drain.tick(OUTER, 3)
        normalize_back(r.resid_mid, r.gains[1], r.summed, r.d_resid, r.gain_parts, rows, False)
        gain_done(1)
        drain.tick(OUTER, 4)
        for copy in trades + answers:
            copy.wait_send()
        for pair in range(pairs_here):
            for copy in mixtures(pair) + returns(pair):
                copy.wait_send()

        def send_rows():
            to_bf16(r.d_resid, r.rows_out, rows)
            drain.home()

        steps = schedule(
            [("tick", INNER, 0)], [], [("tick", INNER, 1)], [("end", OUTER)], [("tick", INNER, 2)], [],
            [("tick", INNER, 3)], [], [], [],
            [("tick", INNER, 4), ("tick", ATTN, 0), ("tick", ATTN, 1), ("end", INNER)],
        )
        self_backward(span, rows, first_row, steps, send_rows)

    @pl.when(here.pipe == 1)
    def _():
        supply.resume(ATTN, CROSS, INNER, OUTER)
        drain.order(OUTER, INNER, CROSS, ATTN)
        entry()
        rows, span = rows_d, span_d
        first_row = pl.multiple_of(c * rows, rows)
        key_at = lax.broadcasted_iota(jnp.int32, (span, rows), 0)
        query_at = lax.broadcasted_iota(jnp.int32, (span, rows), 1) + first_row
        same = segments(lengths_row(nrow), (span, 1), 0, 0) == segments(lengths_row(nrow), (1, rows), 1, first_row)
        r.mask[0:span, 0:rows] = masked(same & (query_at >= key_at))
        supply.pump()
        first_block = c * (tensor // 2)
        rows_ready(span, rows, first_block)
        for k in range(rows // places):
            r.d_branch[k * places : (k + 1) * places, :] = r.x[1, first_block + k]
        supply.pump(until=ATTN)
        supply.finish(ATTN)
        self_forward(span, rows, first_row, CROSS)
        untangle(r.raw_c, FIRST, 2)
        normalize(r.resid_mid, r.gains[1], r.third, rows)
        project(r.third, r.square.at[FIRST], r.joined, rows)
        asks = []
        for k in range(CORES):
            r.send_pair[k, 0:rows, :] = r.joined[:, lane_halves[k]]
            asks.append(move(r.send_pair.at[k, pl.ds(0, rows)], part_here(r.cross_queries), 2 + k, 2 + c, across[k]))
            asks[-1].start()
        supply.pump(until=INNER)
        supply.finish(INNER)
        supply.pump(until=OUTER)
        supply.finish(OUTER)

        @pl.loop(0, tensor)
        def _(tt):
            def body(at, k):
                r.ff[tensor + tt, rows : 2 * rows, at] = nn(r.d_branch[0:rows, :], r.outer[tt, :, at]).astype(BF16)

            columns_of(units, body)

        supply.close()
        drain.free(0)
        r.resid_top[0:rows, :] = r.resid_mid[0:rows, :]
        for k in range(CORES):
            for pair in range(pairs_here):
                part = r.cross_in.at[k, :, pair_lanes(pair)]
                pltpu.make_async_remote_copy(
                    part, part, r.mix_send.at[k, pair], r.mix_recv.at[k, pair], device_id=across[k], device_id_type=MESH
                ).wait_recv()
            r.joined[:, lane_halves[k]] = r.cross_in[k]
        project_back(r.joined, r.square.at[SECOND], r.resid_top, rows, False)
        normalize(r.resid_top, r.gains[2], r.second, rows)
        feed_forward(rows)
        feed_back(rows, True)
        r.d_resid[0:rows, :] = r.d_branch[0:rows, :].astype(F32)
        normalize_back(r.resid_top, r.gains[2], r.summed, r.d_resid, r.gain_parts, rows, False)
        gain_done(2)
        to_bf16(r.d_resid, r.branch, rows)
        tells = []
        for pair in range(pairs_here):
            for k in range(CORES):
                at = pair_lanes(pair)
                first = k * half_width + pair * LANES
                r.send_back[k, :, at] = nn(r.branch[0:rows, :], r.square[SECOND, :, first : first + LANES]).astype(BF16)
                tells.append(
                    pltpu.make_async_remote_copy(
                        r.send_back.at[k, :, at], r.cross_back.at[pl.ds(pl.multiple_of(c * rows, rows), rows), at],
                        r.back_send.at[k, pair], r.back_recv.at[c, pair], device_id=across[k], device_id_type=MESH,
                    )
                )
                tells[-1].start()
        feed_out(r.resid_top, rows)
        drain.free(1)
        to_bf16(r.resid_top, r.rows_out, rows)
        turn(r.d_branch, r.turned, rows)
        drain.allow(0)
        feed_grads(rows, r.turned, 0, OUTER)
        drain.begin(OUTER)
        turn(r.second, r.turned, rows)
        drain.allow(1)
        steps = schedule([("tick", OUTER, 0)], [("tick", OUTER, 1)])
        feed_grads(rows, r.turned, tensor, INNER, at_each((4, 10), steps))
        drain.begin(INNER)
        turn(r.branch, r.turned, rows)
        turn(r.third, r.turned_more, rows)
        for group, n in ((OUTER, 2), (OUTER, 3), (OUTER, 4), (INNER, 0), (INNER, 1)):
            drain.tick(group, n)
        drain.end(OUTER)
        for k in range(CORES):
            move(r.cross_in_back.at[k], r.cross_in_back.at[k], 8 + k, 8 + k, across[k]).wait_recv()
            r.d_pair[1, 0:rows, lane_halves[k]] = r.cross_in_back[k]
        project_back(r.d_pair.at[1], r.square.at[FIRST], r.summed, rows, True)
        drain.tick(INNER, 2)
        square_grads(rows, CROSS, [(r.turned_more, r.d_pair.at[1]), (r.turned, r.joined)], nothing)
        drain.begin(CROSS)
        normalize_back(r.resid_mid, r.gains[1], r.summed, r.d_resid, r.gain_parts, rows, False)
        gain_done(1)
        drain.tick(INNER, 3)
        for copy in asks + tells:
            copy.wait_send()

        def send_rows():
            to_bf16(r.d_resid, r.rows_out.at[pl.ds(rows, rows)], rows)
            drain.home()

        steps = schedule(
            [("tick", INNER, 4)], [("tick", CROSS, 0)], [("tick", CROSS, 1)], [("end", INNER)], [("tick", CROSS, 2)], [],
            [("tick", CROSS, 3)], [], [], [("tick", CROSS, 4)],
            [("tick", ATTN, 0), ("tick", ATTN, 1), ("end", CROSS)],
        )
        self_backward(span, rows, first_row, steps, send_rows)

    drain.close()


def held(*shape, dtype=BF16):
    return pltpu.VMEM(shape, dtype)


def arrays(tensor, heads_at, places, width, units, ranges, kinds):
    tall = 2 * tensor * places
    block = width // tensor
    half_rows, half_width = tall // 2, width // 2
    heads = heads_at * tensor
    return dict(
        x=held(2, tensor, places, width),
        own_x=held(half_rows, width),
        raw_a=held(tensor, width, 4 * block),
        raw_c=held(tensor, width, 2 * block),
        square=held(6, width, width),
        inner=held(tensor, width, units),
        outer=held(tensor, width, units),
        hidden=held(tall, width),
        keys=held(tall, width),
        values=held(tall, width),
        queries=held(half_rows, width),
        probs=held(heads, tall, half_rows),
        mask=held(tall, half_rows, dtype=F32),
        mixture=held(half_rows, width),
        resid_mid=held(half_rows, width, dtype=F32),
        resid_top=held(half_rows, width, dtype=F32),
        d_resid=held(half_rows, width, dtype=F32),
        summed=held(half_rows, width, dtype=F32),
        second=held(half_rows, width),
        third=held(half_rows, width),
        ff=held(2 * tensor, half_rows, units),
        d_branch=held(half_rows, width),
        branch=held(half_rows, width),
        cross_keys=held(tall, half_width),
        cross_values=held(tall, half_width),
        cross_queries=held(half_rows, half_width),
        cross_mixture=held(half_rows, half_width),
        cross_probs=held(heads // CORES, tall, half_rows),
        cross_back=held(half_rows, half_width),
        cross_in=held(CORES, half_rows // 2, half_width),
        cross_in_back=held(CORES, half_rows // 2, half_width),
        cross_taken=held(CORES, half_rows, half_width),
        send_pair=held(CORES, half_rows, half_width),
        send_back=held(CORES, half_rows // 2, half_width),
        joined=held(half_rows // 2, width),
        taken_pair=held(2, half_rows, width),
        d_pair=held(2, half_rows, width),
        turned=held(width, half_rows),
        turned_more=held(width, half_rows),
        stage=held(2, width, units),
        vectors=held(8 * tensor, ranges, dtype=F32),
        diagonals=held(8 * tensor, ranges, dtype=F32),
        onehot=held(kinds, ranges, dtype=F32),
        gain_parts=held(8, width, dtype=F32),
        send_sem=pltpu.SemaphoreType.DMA((14,)),
        recv_sem=pltpu.SemaphoreType.DMA((14,)),
        **{
            name: pltpu.SemaphoreType.DMA((CORES, half_width // LANES))
            for name in ("mix_send", "mix_recv", "back_send", "back_recv", "give_send", "give_recv")
        },
    )


def group_columns(block, units):
    return {ATTN: (0, 4 * block), CROSS: (4 * block, 2 * block), INNER: (6 * block, units), OUTER: (6 * block + units, units)}


def landing(r):
    return {ATTN: r.raw_a, CROSS: r.raw_c, INNER: r.inner, OUTER: r.outer}


class Loads:
    def __init__(self, r, tensor, x_hbm, w_hbm, sems):
        columns = group_columns(r.raw_a.shape[2] // 4, r.inner.shape[2])
        self.x = pltpu.make_async_copy(x_hbm, r.x, sems.at[4, 0])
        self.weights = [
            [
                pltpu.make_async_copy(w_hbm.at[tt, :, pl.ds(*columns[group])], target.at[tt], sems.at[group, tt])
                for tt in range(tensor)
            ]
            for group, target in landing(r).items()
        ]

    def start(self):
        self.x.start()
        for group in self.weights:
            for copy in group:
                copy.start()

    def rows(self):
        self.x.wait()

    def finish(self, group):
        for copy in self.weights[group]:
            copy.wait()

    small = resume = pump = close = nothing


class Stores:
    def __init__(self, r, grads_hbm, sems):
        self.columns = group_columns(r.raw_a.shape[2] // 4, r.inner.shape[2])
        self.r, self.grads, self.sems = r, grads_hbm, sems

    def copy(self, group, tt, slot):
        first, wide = self.columns[group]
        return pltpu.make_async_copy(
            self.r.stage.at[slot, :, pl.ds(0, wide)], self.grads.at[tt, :, pl.ds(first, wide)], self.sems.at[slot]
        )

    def emit(self, group, tt, slot):
        self.copy(group, tt, slot).start()

    def release(self, group, tt, slot):
        self.copy(group, tt, slot).wait()

    order = free = allow = begin = tick = rest = end = home = home_done = small_begin = close = nothing


def blocks_kernel(tensor, dp, heads_at, names, *refs):
    here = Place(tensor, dp)
    r = types.SimpleNamespace(**dict(zip(names, refs)))
    across = [{"pipe": 1 - here.pipe, "dp": here.group * CORES + k} for k in range(CORES)]
    meet([here.sibling()] + across)
    work(r, here, Loads(r, tensor, r.x_hbm, r.w_hbm, r.load_sem), Stores(r, r.grads_hbm, r.stage_sem), tensor, heads_at)


def blocks(tensor, dp, heads_at, kinds, rows, weights, gains, lengths, tables, buckets):
    places, width = rows.shape[2:]
    units = (weights.shape[2] - 6 * (width // tensor)) // 2
    half_rows = tensor * places
    scratch = arrays(tensor, heads_at, places, width, units, buckets.shape[1], kinds)
    scratch["load_sem"] = pltpu.SemaphoreType.DMA((5, tensor))
    scratch["stage_sem"] = pltpu.SemaphoreType.DMA((2,))
    names = ["x_hbm", "w_hbm", "gains", "lengths", "tables", "buckets", "grads_hbm", "rows_out", "gains_out", "bias_out"]
    return pl.pallas_call(
        functools.partial(blocks_kernel, tensor, dp, heads_at, names + list(scratch)),
        out_shape=(
            jax.ShapeDtypeStruct(weights.shape, BF16),
            jax.ShapeDtypeStruct((half_rows, width), BF16),
            jax.ShapeDtypeStruct((8, width), F32),
            jax.ShapeDtypeStruct((8 * tensor, LANES), F32),
        ),
        in_specs=[ANY, ANY] + [VMEM] * 4,
        out_specs=(ANY, VMEM, VMEM, VMEM),
        scratch_shapes=list(scratch.values()),
        compiler_params=pltpu.CompilerParams(collective_id=2, has_side_effects=True, vmem_limit_bytes=VMEM_LIMIT),
        name="blocks",
    )(rows, weights, gains, lengths, tables, buckets)


class Rings:
    def __init__(self, r, here, tensor, dp):
        self.r, self.here, self.tensor, self.dp = r, here, tensor, dp
        self.depth = r.value_w.shape[0]
        self.hops = here.chips // 2
        self.count = 2 * self.hops - 1
        self.sibling = here.sibling()
        self.targets = [here.neighbour(1), here.neighbour(-1)]
        self.landing = landing(r)
        self.groups = []
        self.plan = []


    def order(self, *groups):
        steps = []
        for k, group in enumerate(groups):
            steps.append((4 * k - 0.5, k, self.begin, group, None))
            late = {self.count - 3: 3.6, self.count - 2: 3.7, self.count - 1: 5.5}
            steps += [(4 * k + late.get(n, n), k, self.tick, group, n) for n in range(self.count)]
        steps.sort(key=lambda step: step[:2])
        self.groups = list(groups)
        self.plan = [step[2:] for step in steps]

    def resume(self, *groups):
        self.order(*groups)
        self.plan.pop(0)

    def pump(self, count=1, until=None):
        while self.plan and (count > 0 if until is None else any(step[1] == until for step in self.plan)):
            do, group, n = self.plan.pop(0)
            do(group) if n is None else do(group, n)
            count -= 0 if n is None else 1


    def block_out(self, i):
        r, t, c = self.r, self.here.t, self.here.core
        return pltpu.make_async_remote_copy(
            r.rows.at[i], r.x.at[:, t], r.block_send.at[i], r.block_recv.at[t],
            device_id={"tensor": r.rows.shape[0] * c + i}, device_id_type=MESH,
        )

    def block_kept(self, i):
        return pltpu.make_async_copy(self.r.rows.at[i], self.r.x.at[:, self.here.t], self.r.local_sem.at[0])

    def block_pass(self, source, s):
        r = self.r
        return pltpu.make_async_remote_copy(
            source, r.x.at[:, s], r.pass_send.at[s], r.pass_recv.at[s], device_id=self.sibling, device_id_type=MESH
        )

    def blocks(self, mine, others):
        for i in range(self.r.rows.shape[0]):
            here = self.r.rows.shape[0] * self.here.core + i == self.here.t

            @pl.when(here)
            def _():
                mine(i)

            @pl.when(jnp.logical_not(here))
            def _():
                others(i)

    def small_copies(self):
        r, t = self.r, self.here.t
        copies = [
            pltpu.make_async_remote_copy(
                r.lengths_in, r.lengths.at[self.here.core], r.small_send.at[0], r.small_recv.at[0],
                device_id=self.sibling, device_id_type=MESH,
            ),
            pltpu.make_async_copy(r.lengths_in, r.lengths.at[self.here.core], r.local_sem.at[1]),
            pltpu.make_async_copy(r.table_in, r.tables.at[t], r.local_sem.at[2]),
        ]
        for k in range(1, self.tensor):
            copies.append(
                pltpu.make_async_remote_copy(
                    r.table_in, r.tables.at[t], r.small_send.at[k], r.small_recv.at[k],
                    device_id={"tensor": lax.rem(t + k, self.tensor)}, device_id_type=MESH,
                )
            )
        return copies


    def rows_of(self, ring):
        line, at = self.here.at(ring)
        return at, pl.multiple_of((line * CORES + self.here.core) * self.depth, 16)

    def ring_at(self, step, part):
        way = -1 if part else 1
        return lax.rem(self.here.ring - way * step + self.here.chips, self.here.chips)

    def onward(self, group, step, part, sub):
        r, half = self.r, self.depth // 2
        at, first = self.rows_of(self.ring_at(step, part))
        target = self.landing[group]
        slot = target.at[at, pl.ds(pl.multiple_of(first + half * sub, 16), half), :]
        packed = r.stage.at[0, pl.ds(group * self.depth + half * sub, half), pl.ds(0, target.shape[2])]
        sems = (self.groups.index(group) % 2, part, sub, step)
        return pltpu.make_async_remote_copy(
            packed if step == 0 else slot, slot, r.ring_send.at[sems], r.ring_recv.at[sems],
            device_id=self.targets[part], device_id_type=MESH,
        )

    def over(self, group, ring, first_time=False):
        r = self.r
        at, first = self.rows_of(ring)
        target = self.landing[group]
        slot = target.at[at, pl.ds(first, self.depth), :]
        packed = r.stage.at[0, pl.ds(group * self.depth, self.depth), pl.ds(0, target.shape[2])]
        return pltpu.make_async_remote_copy(
            packed if first_time else slot, slot, r.over_send.at[group, ring], r.over_recv.at[group, ring],
            device_id=self.sibling, device_id_type=MESH,
        )

    def own(self, group):
        wide = self.landing[group].shape[2]
        first = pl.multiple_of(self.here.d * self.depth, 16)
        return pltpu.make_async_copy(
            self.r.stage.at[0, pl.ds(group * self.depth, self.depth), pl.ds(0, wide)],
            self.landing[group].at[self.here.t, pl.ds(first, self.depth), :],
            self.r.own_sem.at[group],
        )

    def begin(self, group):
        place = self.groups.index(group)
        if place >= 2:
            self.sends_done(self.groups[place - 2])
        for sub in range(2):
            for part in range(2):
                self.onward(group, 0, part, sub).start()
        self.over(group, self.here.ring, True).start()
        self.own(group).start()

    def tick(self, group, n):
        step, last = n // 2 + 1, n == self.count - 1
        for part in range(2):
            sub = part if last else n % 2
            self.onward(group, step - 1, part, sub).wait_recv()
            if not last and (step < self.hops - 1 or sub == part):
                self.onward(group, step, part, sub).start()
        if last:
            self.over(group, self.ring_at(step, 0)).start()
        elif n % 2:
            for part in range(2):
                self.over(group, self.ring_at(step, part)).start()

    def sends_done(self, group):
        for part in range(2):
            for sub in range(2):
                for step in range(self.hops):
                    if step < self.hops - 1 or sub == part:
                        self.onward(group, step, part, sub).wait_send()

    def finish(self, group):
        @pl.loop(0, self.here.chips)
        def _(ring):
            self.over(group, ring).wait_recv()

        self.own(group).wait()

    def start(self):
        r, depth = self.r, self.depth
        nrow = r.rows.shape[0]
        r.lengths_in[...] = jnp.zeros_like(r.lengths_in)
        r.lengths_in[0:nrow, 0 : r.enc_lengths.shape[1]] = r.enc_lengths[...]
        r.lengths_in[nrow : 2 * nrow, 0 : r.dec_lengths.shape[1]] = r.dec_lengths[...]
        r.table_in[...] = jnp.zeros_like(r.table_in)
        for k in range(r.bias_w.shape[0]):
            r.table_in[k : k + 1, 0 : r.bias_w.shape[2]] = r.bias_w[k]
        self.blocks(
            lambda i: (self.block_kept(i).start(), self.block_pass(r.rows.at[i], self.here.t).start()),
            lambda i: self.block_out(i).start(),
        )
        block = r.value_w.shape[1]

        def band(group, pieces):
            wide = pieces[0].shape[1]
            for k, piece in enumerate(pieces):
                r.stage[0, group * depth : (group + 1) * depth, k * wide : (k + 1) * wide] = piece

        band(ATTN, [r.query_key_w[1], r.value_w[...], r.query_key_w[0], r.out_w[...].T])
        self.order(ATTN)
        self.begin(ATTN)
        for copy in self.small_copies():
            copy.start()
        band(INNER, [r.inner_w[...]])
        band(OUTER, [r.outer_w[...]])
        band(CROSS, [r.first_w[...], r.second_w[...]])

    def small(self):
        for copy in self.small_copies():
            copy.wait()

    def rows(self):
        r, t = self.r, self.here.t
        takes = lax.div(t, r.rows.shape[0]) == self.here.core
        for s in range(self.tensor):

            @pl.when(jnp.logical_and(takes, s != t))
            def _():
                pltpu.make_async_remote_copy(
                    r.rows.at[0], r.x.at[:, s], r.block_send.at[0], r.block_recv.at[s],
                    device_id=self.sibling, device_id_type=MESH,
                ).wait_recv()
                self.block_pass(r.x.at[:, s], s).start()

        self.blocks(lambda i: self.block_kept(i).wait(), nothing)
        for s in range(self.tensor):

            @pl.when(jnp.logical_not(takes))
            def _():
                self.block_pass(r.x.at[:, s], s).wait_recv()

    def close(self):
        r, t = self.r, self.here.t
        takes = lax.div(t, r.rows.shape[0]) == self.here.core
        self.blocks(
            lambda i: self.block_pass(r.rows.at[i], t).wait_send(),
            lambda i: self.block_out(i).wait_send(),
        )
        for s in range(self.tensor):

            @pl.when(jnp.logical_and(takes, s != t))
            def _():
                self.block_pass(r.x.at[:, s], s).wait_send()

        for group in self.groups[-2:]:
            self.sends_done(group)
        for group in self.groups:

            @pl.loop(0, self.here.chips)
            def _(ring):
                self.over(group, ring).wait_send()


class Sums:
    def __init__(self, r, here, tensor, dp):
        self.r, self.here, self.tensor, self.dp = r, here, tensor, dp
        self.depth = r.value_w.shape[0]
        self.hops = here.chips // 2
        self.count = 2 * self.hops - 3
        self.sibling = here.sibling()
        self.targets = [here.neighbour(1), here.neighbour(-1)]
        self.box = {CROSS: r.raw_c, OUTER: r.raw_a, INNER: r.inner, ATTN: r.outer}
        self.kept = {CROSS: r.own_cross, OUTER: r.own_outer, INNER: r.own_inner, ATTN: r.ff}
        self.groups = []

    def order(self, *groups):
        self.groups = list(groups)

    def free(self, k):
        for device in self.targets + [self.sibling]:
            pl.semaphore_signal(self.r.free_sem.at[k], inc=1, device_id=device, device_id_type=MESH)

    def allow(self, k):
        pl.semaphore_wait(self.r.free_sem.at[k], 3)

    def boxed(self, group, index, first, height):
        if isinstance(index, int):
            return (index // self.dp, pl.ds(pl.multiple_of(index % self.dp * self.depth + first, 16), height), slice(None))
        at = pl.ds(pl.multiple_of(lax.rem(index, self.dp) * self.depth + first, 16), height)
        return (lax.div(index, self.dp), at, slice(None))

    def taken(self, group, step, part, first, height):
        index = step + part * (self.hops - 1) if step else 0
        return self.boxed(group, index, first, height)

    def theirs(self, group, ring, first, height):
        return self.boxed(group, self.here.chips - 1 + ring, first, height)

    def own(self, group, ring, first, height):
        return (ring, pl.ds(first, height), slice(None))

    def ring_of(self, line, at):
        return line * self.tensor + at + (line % 2) * (self.tensor - 1 - 2 * at)

    def pieces(self, group, tt, slot):
        r, depth = self.r, self.depth
        wide = self.box[group].shape[2]
        made = []
        for line in range(self.here.groups):
            ring = self.ring_of(line, tt)

            def rows_of(core):
                return r.stage.at[slot, pl.ds(pl.multiple_of((line * CORES + core) * depth, 16), depth), pl.ds(0, wide)]

            made.append(
                pltpu.make_async_copy(
                    rows_of(self.here.core), self.kept[group].at[self.own(group, ring, 0, depth)], r.kept_sem.at[slot, line]
                )
            )
            made.append(
                pltpu.make_async_remote_copy(
                    rows_of(1 - self.here.core), self.box[group].at[self.theirs(group, ring, 0, depth)],
                    r.over_send.at[group, ring], r.over_recv.at[group, ring], device_id=self.sibling, device_id_type=MESH,
                )
            )
        return made

    def emit(self, group, tt, slot):
        for piece in self.pieces(group, tt, slot):
            piece.start()

    def release(self, group, tt, slot):
        for k, piece in enumerate(self.pieces(group, tt, slot)):
            if k % 2:
                piece.wait_send()
            else:
                piece.wait()


    def rows_at(self, sub):
        half = self.depth // 2
        return half * sub, half

    def source(self, step, part):
        way = -1 if part else 1
        return lax.rem(self.here.ring + way * (self.hops - step) + self.here.chips, self.here.chips)

    def onward(self, group, step, part, sub):
        r = self.r
        first, height = self.rows_at(sub)
        sems = (self.groups.index(group) % 2, part, sub, step)
        return pltpu.make_async_remote_copy(
            self.kept[group].at[self.own(group, self.source(step, part), first, height)],
            self.box[group].at[self.taken(group, step, part, first, height)],
            r.ring_send.at[sems], r.ring_recv.at[sems],
            device_id=self.targets[part], device_id_type=MESH,
        )

    def here_sum(self, group, ring, first, height):
        value = self.kept[group][self.own(group, ring, first, height)].astype(F32)
        return value + self.box[group][self.theirs(group, ring, first, height)].astype(F32)

    def advance(self, group, step, part, sub, fresh=False):
        if not fresh:
            self.onward(group, step - 1, part, sub).wait_recv()
        first, height = self.rows_at(sub)
        value = self.here_sum(group, self.source(step, part), first, height)
        if not fresh:
            value = value + self.box[group][self.taken(group, step - 1, part, first, height)].astype(F32)
        self.kept[group][self.own(group, self.source(step, part), first, height)] = value.astype(BF16)
        self.onward(group, step, part, sub).start()

    def begin(self, group):
        @pl.loop(0, self.here.chips)
        def _(ring):
            pltpu.make_async_remote_copy(
                self.kept[group].at[self.own(group, ring, 0, self.depth)],
                self.box[group].at[self.theirs(group, ring, 0, self.depth)],
                self.r.over_send.at[group, ring], self.r.over_recv.at[group, ring], device_id=self.sibling, device_id_type=MESH,
            ).wait_recv()

        place = self.groups.index(group)
        if place >= 2:
            self.sends_done(self.groups[place - 2])
        for part in range(2):
            self.advance(group, 0, part, part, True)
        for part in range(2):
            self.advance(group, 1, part, 1 - part, True)
        if group == ATTN:
            self.small_across().wait_recv()
            self.small_advance(0, 0, True)
            self.small_advance(1, 1, True)

    def tick(self, group, n):
        step, leads = (n + 1) // 2 + 1, n % 2
        for part in range(2):
            self.advance(group, step, part, 1 - part if leads else part)
        if group == ATTN and not leads:
            self.small_advance(step, 0)
            if step > 1:
                self.small_advance(step, 1)

    def sends_done(self, group):
        for part in range(2):
            self.onward(group, 0, part, part).wait_send()
            for step in range(1, self.hops):
                for sub in range(2):
                    self.onward(group, step, part, sub).wait_send()

    def rest(self, group, first):
        for n in range(first, self.count):
            self.tick(group, n)
        self.end(group)
        for group in self.groups[-2:]:
            self.sends_done(group)

    def end(self, group):
        r, last = self.r, self.hops - 1
        for sub in range(2):
            first, height = self.rows_at(sub)
            value = self.here_sum(group, self.here.ring, first, height)
            for part in range(2):
                self.onward(group, last, part, sub).wait_recv()
                value = value + self.box[group][self.taken(group, last, part, first, height)].astype(F32)
            target = r.inner_out if group == INNER else r.total
            target[pl.ds(first, height), 0 : self.box[group].shape[2]] = value
        block = r.value_w.shape[1]
        if group == ATTN:
            r.pair_out[1] = r.total[:, 0:block]
            r.value_out[...] = r.total[:, block : 2 * block]
            r.pair_out[0] = r.total[:, 2 * block : 3 * block]
            r.out_out[...] = r.total[:, 3 * block : 4 * block].T
            at = self.small_at(self.here.ring)
            value = r.small[at] + r.small_theirs[at]
            for part in range(2):
                self.small_onward(last, part).wait_recv()
                value = value + r.small_taken[part, last]
            r.tiny_out[...] = value
        if group == CROSS:
            r.first_out[...] = r.total[:, 0:block]
            r.second_out[...] = r.total[:, block : 2 * block]
        if group == OUTER:
            r.outer_out[...] = r.total[...]


    def small_at(self, ring):
        line, at = self.here.at(ring)
        return at, line * CORES + self.here.core

    def small_across(self):
        r = self.r
        return pltpu.make_async_remote_copy(
            r.small, r.small_theirs, r.small_sem.at[0], r.small_sem.at[1], device_id=self.sibling, device_id_type=MESH
        )

    def small_onward(self, step, part):
        r = self.r
        return pltpu.make_async_remote_copy(
            r.small_sent.at[part, step], r.small_taken.at[part, step], r.tiny_send.at[part, step], r.tiny_recv.at[part, step],
            device_id=self.targets[part], device_id_type=MESH,
        )

    def small_advance(self, step, part, fresh=False):
        at = self.small_at(self.source(step, part))
        value = self.r.small[at] + self.r.small_theirs[at]
        if not fresh:
            self.small_onward(step - 1, part).wait_recv()
            value = value + self.r.small_taken[part, step - 1]
        self.r.small_sent[part, step] = value
        self.small_onward(step, part).start()

    def small_begin(self):
        r, depth = self.r, self.depth
        r.small[...] = jnp.zeros_like(r.small)
        kinds = r.onehot.shape[0] // self.dp
        heads_at = self.heads_at
        for tt in range(self.tensor):
            for d in range(self.dp):
                r.small[tt, d, 0:3, 0:depth] = r.gains_out[0:3, d * depth : (d + 1) * depth]
                r.small[tt, d, 3 : 3 + heads_at, 0:kinds] = r.bias_out[
                    8 * tt : 8 * tt + heads_at, d * kinds : (d + 1) * kinds
                ]
        self.small_across().start()


    def home_copy(self, k):
        r, here, tensor = self.r, self.here, self.tensor
        nrow, half, places = r.home_in.shape[0], tensor // 2, r.home_in.shape[2]
        place = here.pipe * (here.core * half + k % half) + (1 - here.pipe) * k
        which = here.pipe * (k // half) + (1 - here.pipe) * here.core
        owner = lax.div(here.t, nrow)
        source = r.rows_out.at[pl.ds(k * places, places)]
        slot = r.home_in.at[lax.rem(here.t, nrow), which]
        recv = r.home_recv.at[lax.rem(here.t, nrow), which]
        return (
            jnp.logical_and(place == here.t, owner == here.core),
            lambda: pltpu.make_async_copy(source, slot, recv),
            lambda: pltpu.make_async_remote_copy(
                source, slot, r.home_send.at[k], recv,
                device_id={"dp": here.group * CORES + owner, "tensor": place}, device_id_type=MESH,
            ),
        )

    def home(self):
        for k in range(self.tensor):
            stays, inside, away = self.home_copy(k)

            @pl.when(stays)
            def _():
                inside().start()

            @pl.when(jnp.logical_not(stays))
            def _():
                away().start()

    def home_done(self):
        r = self.r
        places = r.home_in.shape[2]
        for i in range(r.home_in.shape[0]):
            for which in range(2):
                pltpu.make_async_copy(
                    r.rows_out.at[pl.ds(0, places)], r.home_in.at[i, which], r.home_recv.at[i, which]
                ).wait()
                r.home_out[i, which] = r.home_in[i, which].astype(F32)

    def close(self):
        r = self.r
        for k in range(self.tensor):
            stays, inside, away = self.home_copy(k)

            @pl.when(jnp.logical_not(stays))
            def _():
                away().wait_send()

        self.small_across().wait_send()

        for part in range(2):
            for step in range(part, self.hops):
                self.small_onward(step, part).wait_send()


def fits_fused(tensor, dp, depth, units, width):
    chips = tensor * dp // CORES
    return (
        depth % 32 == 0
        and 4 * depth <= width
        and chips <= 2 * tensor
        and chips == 2 * tensor == 8
        and units == width == 6 * LANES
    )


def fused_kernel(tensor, dp, heads_at, names, *refs):
    here = Place(tensor, dp)
    r = types.SimpleNamespace(**dict(zip(names, refs)))
    line = [
        {"dp": here.group * CORES + lax.rem(here.core + j, CORES), "tensor": lax.rem(here.t + k, tensor)}
        for j in range(CORES)
        for k in range(tensor)
        if j + k > 0
    ]
    across = [{"pipe": 1 - here.pipe, "dp": here.group * CORES + k} for k in range(CORES)]
    meet([here.neighbour(1), here.neighbour(-1)] + line + across)
    supply, drain = Rings(r, here, tensor, dp), Sums(r, here, tensor, dp)
    drain.heads_at = heads_at
    work(r, here, supply, drain, tensor, heads_at)


def fused(tensor, dp, rows, enc_lengths, dec_lengths, gains, bias, buckets, weights):
    nrow, two, places, width = rows.shape
    depth, block = weights[1].shape
    units = weights[5].shape[1]
    heads_at, _, kinds = bias.shape
    chips = tensor * dp // CORES
    wide = -(-max(depth, kinds // dp) // LANES) * LANES
    sems = pltpu.SemaphoreType.DMA
    scratch = arrays(tensor, heads_at, places, width, units, buckets.shape[1], kinds)
    scratch.update(
        lengths_in=held(8, LANES, dtype=jnp.int32),
        table_in=held(8, LANES, dtype=F32),
        lengths=held(CORES, 8, LANES, dtype=jnp.int32),
        tables=held(tensor, 8, LANES, dtype=F32),
        own_cross=held(chips, depth, 2 * block),
        own_outer=held(chips, depth, units),
        own_inner=held(chips, depth, units),
        total=held(depth, units, dtype=F32),
        rows_out=held(tensor * places, width),
        gains_out=held(8, width, dtype=F32),
        bias_out=held(8 * tensor, LANES, dtype=F32),
        home_in=held(nrow, two, places, width),
        small=held(tensor, dp, 8, wide, dtype=F32),
        small_theirs=held(tensor, dp, 8, wide, dtype=F32),
        small_sent=held(2, chips // 2, 8, wide, dtype=F32),
        small_taken=held(2, chips // 2, 8, wide, dtype=F32),
        block_send=sems((nrow,)), block_recv=sems((tensor,)), pass_send=sems((tensor,)), pass_recv=sems((tensor,)),
        local_sem=sems((3,)), small_send=sems((tensor,)), small_recv=sems((tensor,)), own_sem=sems((4,)),
        ring_send=sems((2, 2, 2, chips // 2)), ring_recv=sems((2, 2, 2, chips // 2)),
        over_send=sems((4, chips)), over_recv=sems((4, chips)), kept_sem=sems((2, dp // CORES)),
        small_sem=sems((2,)), tiny_send=sems((2, chips // 2)), tiny_recv=sems((2, chips // 2)),
        home_send=sems((tensor,)), home_recv=sems((nrow, two)),
        free_sem=pltpu.SemaphoreType.REGULAR((2,)),
    )
    inputs = ["rows", "enc_lengths", "dec_lengths", "gains", "bias_w", "buckets"]
    inputs += ["query_key_w", "value_w", "out_w", "first_w", "second_w", "inner_w", "outer_w"]
    outputs = dict(
        home_out=rows.shape, tiny_out=(8, wide), pair_out=(2, depth, block), value_out=(depth, block),
        out_out=(block, depth), first_out=(depth, block), second_out=(depth, block), inner_out=(depth, units),
        outer_out=(depth, units),
    )
    return pl.pallas_call(
        functools.partial(fused_kernel, tensor, dp, heads_at, inputs + list(outputs) + list(scratch)),
        out_shape=tuple(jax.ShapeDtypeStruct(shape, F32) for shape in outputs.values()),
        in_specs=[ANY] + [VMEM] * 12,
        out_specs=(VMEM,) * len(outputs),
        scratch_shapes=list(scratch.values()),
        compiler_params=pltpu.CompilerParams(collective_id=3, has_side_effects=True, vmem_limit_bytes=VMEM_LIMIT),
        name="fused",
    )(rows, enc_lengths, dec_lengths, gains, bias, buckets, *weights)


def pad_to(array, *shape):
    return jnp.pad(array, [(0, full - have) for full, have in zip(shape, array.shape)])


def shards(
    tensor, dp, section_rows, enc_lengths, dec_lengths, enc_buckets, dec_buckets, norm_gains, rel_bias,
    query_key_w, value_w, attn_out_w, cross_first, cross_second, ff_in, ff_out,
):
    depth = value_w.shape[1]
    width = section_rows.shape[-1]
    on_encoder = lax.axis_index("pipe") == 0
    ranges = -(-enc_buckets.shape[0] // LANES) * LANES
    dec_all = jnp.concatenate([jnp.zeros((dec_buckets.shape[0] - 1,), jnp.int32), dec_buckets])
    bucket_row = jnp.where(on_encoder, pad_to(enc_buckets, ranges), pad_to(dec_all, ranges))[None]
    gains = norm_gains.transpose(1, 0, 2)
    bias = rel_bias.transpose(2, 0, 1)
    weights = (query_key_w[0], value_w[0], attn_out_w[0], cross_first[0], cross_second[0], ff_in[0], ff_out[0].T)
    run = fused if fits_fused(tensor, dp, depth, ff_in.shape[2], width) else in_three
    home, tiny, *grads, outer = run(
        tensor, dp, section_rows[0], enc_lengths, dec_lengths, gains, bias, bucket_row, weights
    )
    if run is fused:
        home, tiny, *grads, outer = copied(home, tiny, *grads, outer)
    heads_at, kinds = bias.shape[0], bias.shape[2] // dp
    return (
        (home[None], tiny[:3, :depth][None], tiny[3 : 3 + heads_at, :kinds].T[None])
        + tuple(grad[None] for grad in grads)
        + (outer.T[None],)
    )


def copied(*results):
    def kernel(*refs):
        for source, target in zip(refs[: len(results)], refs[len(results) :]):
            target[...] = source[...]

    return pl.pallas_call(
        kernel,
        out_shape=tuple(jax.ShapeDtypeStruct(result.shape, result.dtype) for result in results),
        in_specs=[VMEM] * len(results),
        out_specs=(VMEM,) * len(results),
        name="copied",
    )(*results)


def in_three(tensor, dp, section_rows, enc_lengths, dec_lengths, gains, bias, buckets, weights):
    query_key, value, out, first, second, inner, outer = weights
    nrow, _, _, width = section_rows.shape
    heads_at, _, kinds = bias.shape
    lengths = pad_to(jnp.concatenate([enc_lengths, dec_lengths], axis=0), 8, LANES)
    table = pad_to(bias[:, 0], 8, LANES)
    depth, block = value.shape
    units = inner.shape[1]
    pack = jnp.concatenate([query_key[1], value, query_key[0], out.T, first, second, inner, outer], axis=1)
    rows, gathered, lengths, tables = gather(tensor, dp, section_rows, pack, lengths, table)
    grads, finished, gain_grads, bias = blocks(
        tensor, dp, heads_at, kinds, rows, gathered.reshape(tensor, width, -1), gains, lengths, tables, buckets
    )
    held_kinds = kinds // dp
    wide = -(-max(depth, held_kinds) // LANES) * LANES
    gain_part = pad_to(gain_grads[:3].reshape(3, dp, depth).transpose(1, 0, 2), dp, 3, wide)
    bias_part = bias.reshape(tensor, 8, LANES)[:, :heads_at, :kinds].reshape(tensor, heads_at, dp, held_kinds)
    bias_part = pad_to(bias_part.transpose(0, 2, 1, 3), tensor, dp, 5, wide)
    small = jnp.concatenate([jnp.broadcast_to(gain_part[None], (tensor,) + gain_part.shape), bias_part], axis=2)
    total, tiny, home = scatter(
        tensor, dp, grads.reshape(tensor, dp, depth, -1), small, finished.reshape(tensor, -1, width), nrow
    )
    key, value, query, out, first, second = [total[:, k * block : (k + 1) * block] for k in range(6)]
    inner, outer = total[:, 6 * block : 6 * block + units], total[:, 6 * block + units :]
    return (
        home.astype(F32), tiny,
        jnp.stack([query, key]), value, out.T, first, second, inner, outer,
    )


def solution(mesh):
    sizes = dict(mesh.shape)
    return jax.shard_map(
        functools.partial(shards, sizes["tensor"], sizes["dp"]),
        mesh=mesh,
        in_specs=(
            P("pipe", "dp", None, "tensor", None),
            P("dp", None),
            P("dp", None),
            P(),
            P(),
            P("pipe", None, None),
            P("pipe", None, "tensor"),
            P("pipe", None, "dp", "tensor"),
            P("pipe", "dp", "tensor"),
            P("pipe", "tensor", "dp"),
            P("pipe", "dp", "tensor"),
            P("pipe", "dp", "tensor"),
            P("pipe", "dp", "tensor"),
            P("pipe", "tensor", "dp"),
        ),
        out_specs=(
            P("pipe", "dp", None, "tensor", None),
            P("pipe", None, "dp"),
            P("pipe", "dp", "tensor"),
            P("pipe", None, "dp", "tensor"),
            P("pipe", "dp", "tensor"),
            P("pipe", "tensor", "dp"),
            P("pipe", "dp", "tensor"),
            P("pipe", "dp", "tensor"),
            P("pipe", "dp", "tensor"),
            P("pipe", "tensor", "dp"),
        ),
        check_vma=False,
    )
```

```python
import functools
import types

import jax
import jax.numpy as jnp
from jax import lax
from jax.experimental import pallas as pl
from jax.experimental.pallas import tpu as pltpu
from jax.sharding import PartitionSpec as P

MESH = pl.DeviceIdType.MESH
F32 = jnp.float32
BF16 = jnp.bfloat16
EPSILON = 1e-06
NEGATIVE = -1000000000.0
HEAD_DIM = 64
CORES = 2
LANES = 128
VMEM_LIMIT = 62 << 20
ANY = pl.BlockSpec(memory_space=pl.ANY)
VMEM = pl.BlockSpec(memory_space=pltpu.VMEM)


def nn(a, b):
    return lax.dot_general(a, b, (((1,), (0,)), ((), ())), preferred_element_type=F32)


def nt(a, b):
    return lax.dot_general(a, b, (((1,), (1,)), ((), ())), preferred_element_type=F32)


def tn(a, b):
    return lax.dot_general(a, b, (((0,), (0,)), ((), ())), preferred_element_type=F32)


class Place:
    def __init__(self, tensor, dp):
        self.tensor = tensor
        self.groups = dp // CORES
        self.chips = tensor * self.groups
        self.pipe = lax.axis_index("pipe")
        self.d = lax.axis_index("dp")
        self.t = lax.axis_index("tensor")
        self.core = lax.rem(self.d, CORES)
        self.group = self.d // CORES
        odd = lax.rem(self.group, 2)
        self.ring = self.group * tensor + self.t + odd * (tensor - 1 - 2 * self.t)

    def at(self, ring):
        group = ring // self.tensor
        along = lax.rem(ring, self.tensor)
        odd = lax.rem(group, 2)
        return group, along + odd * (self.tensor - 1 - 2 * along)

    def neighbour(self, step):
        group, t = self.at(lax.rem(self.ring + step + self.chips, self.chips))
        return {"dp": group * CORES + self.core, "tensor": t}

    def sibling(self):
        return {"dp": self.group * CORES + 1 - self.core}


def meet(devices):
    barrier = pltpu.get_barrier_semaphore()
    for device in devices:
        pl.semaphore_signal(barrier, inc=1, device_id=device, device_id_type=MESH)
    pl.semaphore_wait(barrier, len(devices))


def halves(rows, columns):
    if rows % 32 == 0:
        return [(pl.ds(k * (rows // 2), rows // 2), pl.ds(0, columns)) for k in range(2)]
    cut = columns // LANES // 2 * LANES
    return [(pl.ds(0, rows), pl.ds(0, cut)), (pl.ds(0, rows), pl.ds(cut, columns - cut))]


def gather_kernel(
    tensor, dp, rows_ref, pack_ref, length_ref, table_ref, x_ref, w_ref, lengths_ref, tables_ref,
    local_sem, block_send, block_recv, pass_send, pass_recv, small_send, small_recv,
    ring_send, ring_recv, core_send, core_recv,
):
    here = Place(tensor, dp)
    c, t, chips = here.core, here.t, here.chips
    nrow = rows_ref.shape[0]
    sibling = here.sibling()
    to_right, to_left = here.neighbour(1), here.neighbour(-1)
    others = [{"tensor": lax.rem(t + k, tensor)} for k in range(1, tensor)]
    meet([to_right, to_left, sibling] + others)

    lengths = pltpu.make_async_remote_copy(
        length_ref, lengths_ref.at[c], small_send.at[0], small_recv.at[0], device_id=sibling, device_id_type=MESH
    )
    lengths.start()
    own_lengths = pltpu.make_async_copy(length_ref, lengths_ref.at[c], local_sem.at[0])
    own_lengths.start()
    own_table = pltpu.make_async_copy(table_ref, tables_ref.at[t], local_sem.at[1])
    own_table.start()
    tables = []
    for k in range(1, tensor):
        tables.append(
            pltpu.make_async_remote_copy(
                table_ref, tables_ref.at[t], small_send.at[k], small_recv.at[k], device_id=others[k - 1], device_id_type=MESH
            )
        )
        tables[-1].start()

    def to_chip(i):
        return pltpu.make_async_remote_copy(
            rows_ref.at[i], x_ref.at[:, t], block_send.at[i], block_recv.at[t],
            device_id={"tensor": nrow * c + i}, device_id_type=MESH,
        )

    def kept(i):
        return pltpu.make_async_copy(rows_ref.at[i], x_ref.at[:, t], local_sem.at[2])

    def kept_pass(i):
        return pltpu.make_async_remote_copy(
            rows_ref.at[i], x_ref.at[:, t], pass_send.at[t], pass_recv.at[t], device_id=sibling, device_id_type=MESH
        )

    def passed(s):
        return pltpu.make_async_remote_copy(
            x_ref.at[:, s], x_ref.at[:, s], pass_send.at[s], pass_recv.at[s], device_id=sibling, device_id_type=MESH
        )

    for i in range(nrow):
        mine = nrow * c + i == t

        @pl.when(mine)
        def _():
            kept(i).start()
            kept_pass(i).start()

        @pl.when(jnp.logical_not(mine))
        def _():
            to_chip(i).start()

    parts = halves(*pack_ref.shape)
    own_pack = pltpu.make_async_copy(pack_ref, w_ref.at[t, here.d], local_sem.at[3])
    own_pack.start()

    def shard(ring, part):
        group, at = here.at(ring)
        return w_ref.at[at, group * CORES + c, parts[part][0], parts[part][1]]

    def source(step, part):
        return lax.rem(here.ring + (1 if part else -1) * step + chips, chips)

    def onward(step, part, first=False):
        slot = shard(source(step, part), part)
        return pltpu.make_async_remote_copy(
            pack_ref.at[parts[part][0], parts[part][1]] if first else slot, slot,
            ring_send.at[part, step], ring_recv.at[part, step],
            device_id=to_left if part else to_right, device_id_type=MESH,
        )

    def across(step, part, first=False):
        slot = shard(source(step, part), part)
        return pltpu.make_async_remote_copy(
            pack_ref.at[parts[part][0], parts[part][1]] if first else slot, slot,
            core_send.at[part, step], core_recv.at[part, step], device_id=sibling, device_id_type=MESH,
        )

    for part in range(2):
        onward(0, part, True).start()
        across(0, part, True).start()

    takes = t // nrow == c
    for s in range(tensor):

        @pl.when(jnp.logical_and(takes, s != t))
        def _():
            pltpu.make_async_remote_copy(
                rows_ref.at[0], x_ref.at[:, s], block_send.at[0], block_recv.at[s], device_id=sibling, device_id_type=MESH
            ).wait_recv()
            passed(s).start()

    @pl.loop(1, chips)
    def _(step):
        for part in range(2):
            onward(step - 1, part).wait_recv()

            @pl.when(step < chips - 1)
            def _():
                onward(step, part).start()

            across(step, part).start()

    @pl.loop(0, chips)
    def _(step):
        for part in range(2):

            @pl.when(step < chips - 1)
            def _():
                onward(step, part).wait_send()

            across(step, part).wait_send()
            across(step, part).wait_recv()

    for i in range(nrow):
        mine = nrow * c + i == t

        @pl.when(mine)
        def _():
            kept(i).wait()
            kept_pass(i).wait_send()

        @pl.when(jnp.logical_not(mine))
        def _():
            to_chip(i).wait_send()

    for s in range(tensor):

        @pl.when(jnp.logical_and(takes, s != t))
        def _():
            passed(s).wait_send()

        @pl.when(jnp.logical_not(takes))
        def _():
            passed(s).wait_recv()

    lengths.wait()
    own_lengths.wait()
    own_table.wait()
    own_pack.wait()
    for table in tables:
        table.wait()


def gather(tensor, dp, rows, pack, lengths, table):
    chips = tensor * dp // CORES
    nrow, two, places, width = rows.shape
    sems = pltpu.SemaphoreType.DMA
    return pl.pallas_call(
        functools.partial(gather_kernel, tensor, dp),
        out_shape=(
            jax.ShapeDtypeStruct((two, tensor, places, width), rows.dtype),
            jax.ShapeDtypeStruct((tensor, dp) + pack.shape, pack.dtype),
            jax.ShapeDtypeStruct((CORES,) + lengths.shape, lengths.dtype),
            jax.ShapeDtypeStruct((tensor,) + table.shape, table.dtype),
        ),
        in_specs=[ANY] * 4,
        out_specs=(ANY,) * 4,
        scratch_shapes=[
            sems((4,)), sems((nrow,)), sems((tensor,)), sems((tensor,)), sems((tensor,)), sems((tensor,)), sems((tensor,)),
            sems((2, chips)), sems((2, chips)), sems((2, chips)), sems((2, chips)),
        ],
        compiler_params=pltpu.CompilerParams(collective_id=0, has_side_effects=True),
        name="gather",
    )(rows, pack, lengths, table)


def scatter_kernel(
    tensor, dp, grads_ref, small_ref, rows_ref, out_ref, small_out, rows_out,
    own, theirs, taken, small_own, small_theirs, small_taken, total,
    own_sem, core_send, core_recv, ring_send, ring_recv,
    sown_sem, score_send, score_recv, sring_send, sring_recv, block_send, block_recv, local_sem,
):
    here = Place(tensor, dp)
    c, t, chips = here.core, here.t, here.chips
    nrow = rows_out.shape[0]
    sibling = here.sibling()
    to_right, to_left = here.neighbour(1), here.neighbour(-1)
    line = [
        {"dp": here.group * CORES + lax.rem(c + j, CORES), "tensor": lax.rem(t + k, tensor)}
        for j in range(CORES)
        for k in range(tensor)
        if j + k > 0
    ]
    meet([to_right, to_left] + line)

    half = tensor // 2
    owner = t // nrow

    def block(k):
        place = here.pipe * (c * half + k % half) + (1 - here.pipe) * k
        which = here.pipe * (k // half) + (1 - here.pipe) * c
        return place, which

    def home(k):
        place, which = block(k)
        slot = rows_out.at[lax.rem(t, nrow), which]
        recv = block_recv.at[lax.rem(t, nrow), which]
        return (
            jnp.logical_and(place == t, owner == c),
            lambda: pltpu.make_async_copy(rows_ref.at[k], slot, recv),
            lambda: pltpu.make_async_remote_copy(
                rows_ref.at[k], slot, block_send.at[k], recv,
                device_id={"dp": here.group * CORES + owner, "tensor": place}, device_id_type=MESH,
            ),
        )

    for k in range(tensor):
        stays, inside, away = home(k)

        @pl.when(stays)
        def _():
            inside().start()

        @pl.when(jnp.logical_not(stays))
        def _():
            away().start()

    def across(ring):
        group, at = here.at(ring)
        return (
            pltpu.make_async_remote_copy(
                grads_ref.at[at, group * CORES + 1 - c], theirs.at[ring], core_send.at[ring], core_recv.at[ring],
                device_id=sibling, device_id_type=MESH,
            ),
            pltpu.make_async_remote_copy(
                small_ref.at[at, group * CORES + 1 - c], small_theirs.at[ring], score_send.at[ring], score_recv.at[ring],
                device_id=sibling, device_id_type=MESH,
            ),
        )

    def fetch(ring):
        group, at = here.at(ring)
        return (
            pltpu.make_async_copy(grads_ref.at[at, group * CORES + c], own.at[ring], own_sem.at[ring]),
            pltpu.make_async_copy(small_ref.at[at, group * CORES + c], small_own.at[ring], sown_sem.at[ring]),
        )

    def behind(step):
        return lax.rem(here.ring - step + chips, chips)

    def order(k):
        off = (2 * lax.rem(k, 2) - 1) * (k // 2 + 1) * (1 - k // (chips - 1))
        return lax.rem(here.ring + chips + off, chips)

    @pl.loop(0, chips)
    def _(k):
        for copy in across(order(k)) + fetch(order(k)):
            copy.start()

    rows, columns = out_ref.shape
    parts = halves(rows, columns)

    def add(ring, part, step, last):
        height = parts[part][0].size
        piece = 16 if height % 16 == 0 else height

        @pl.loop(0, height // piece)
        def _(k):
            at = pl.ds(pl.multiple_of(parts[part][0].start + k * piece, 8), piece)
            where = (at, parts[part][1])
            value = own[(ring,) + where].astype(F32) + theirs[(ring,) + where].astype(F32)
            if step is not None:
                value = value + taken[(step,) + where].astype(F32)
            if last:
                total[where] = value
            else:
                own[(ring,) + where] = value.astype(BF16)

    def onward(ring, step, part):
        where = (parts[part][0], parts[part][1])
        return pltpu.make_async_remote_copy(
            own.at[(ring,) + where], taken.at[(step,) + where], ring_send.at[part, step], ring_recv.at[part, step],
            device_id=to_left if part else to_right, device_id_type=MESH,
        )

    def small_onward(ring, step):
        return pltpu.make_async_remote_copy(
            small_own.at[ring], small_taken.at[step], sring_send.at[step], sring_recv.at[step],
            device_id=to_right, device_id_type=MESH,
        )

    def ready(ring):
        for copy in across(ring):
            copy.wait_recv()
        for copy in fetch(ring):
            copy.wait()

    def ahead(step):
        return lax.rem(here.ring + step, chips)

    half_chips = chips // 2

    @pl.loop(0, chips - 1)
    def _(step):
        right, left = behind(step + 1), ahead(step + 1)

        @pl.when(step < half_chips)
        def _():
            ready(right)

        @pl.when(step < chips - 1 - half_chips)
        def _():
            ready(left)

        @pl.when(step == 0)
        def _():
            add(right, 0, None, False)
            add(left, 1, None, False)
            small_own[right] = small_own[right] + small_theirs[right]

        @pl.when(step > 0)
        def _():
            onward(right, step - 1, 0).wait_recv()
            add(right, 0, step - 1, False)
            onward(right, step, 0).start()
            onward(left, step - 1, 1).wait_recv()
            add(left, 1, step - 1, False)
            onward(left, step, 1).start()
            small_onward(right, step - 1).wait_recv()
            small_own[right] = small_own[right] + small_theirs[right] + small_taken[step - 1]
            small_onward(right, step).start()

        @pl.when(step == 0)
        def _():
            onward(right, 0, 0).start()
            onward(left, 0, 1).start()
            small_onward(right, 0).start()

    ready(here.ring)
    for part in range(2):
        onward(here.ring, chips - 2, part).wait_recv()
        add(here.ring, part, chips - 2, True)
    small_onward(here.ring, chips - 2).wait_recv()
    small_out[...] = small_own[here.ring] + small_theirs[here.ring] + small_taken[chips - 2]
    finish = pltpu.make_async_copy(total, out_ref, local_sem.at[0])
    finish.start()

    @pl.loop(0, chips)
    def _(step):
        @pl.when(step < chips - 1)
        def _():
            onward(behind(step + 1), step, 0).wait_send()
            onward(ahead(step + 1), step, 1).wait_send()
            small_onward(behind(step + 1), step).wait_send()

        for copy in across(step):
            copy.wait_send()

    for k in range(tensor):
        stays, inside, away = home(k)

        @pl.when(jnp.logical_not(stays))
        def _():
            away().wait_send()

    for i in range(nrow):
        for which in range(2):
            pltpu.make_async_copy(rows_ref.at[0], rows_out.at[i, which], block_recv.at[i, which]).wait()
    finish.wait()


def scatter(tensor, dp, grads, small, rows, nrow):
    chips = tensor * dp // CORES
    shard = grads.shape[2:]
    tiny = small.shape[2:]
    sems = pltpu.SemaphoreType.DMA
    return pl.pallas_call(
        functools.partial(scatter_kernel, tensor, dp),
        out_shape=(
            jax.ShapeDtypeStruct(shard, F32),
            jax.ShapeDtypeStruct(tiny, F32),
            jax.ShapeDtypeStruct((nrow, 2) + rows.shape[1:], rows.dtype),
        ),
        in_specs=[ANY] * 3,
        out_specs=(ANY, VMEM, ANY),
        scratch_shapes=[
            pltpu.VMEM((chips,) + shard, BF16),
            pltpu.VMEM((chips,) + shard, BF16),
            pltpu.VMEM((chips - 1,) + shard, BF16),
            pltpu.VMEM((chips,) + tiny, F32),
            pltpu.VMEM((chips,) + tiny, F32),
            pltpu.VMEM((chips - 1,) + tiny, F32),
            pltpu.VMEM(shard, F32),
            sems((chips,)), sems((chips,)), sems((chips,)), sems((2, chips)), sems((2, chips)),
            sems((chips,)), sems((chips,)), sems((chips,)), sems((chips,)), sems((chips,)),
            sems((tensor,)), sems((nrow, 2)), sems((1,)),
        ],
        compiler_params=pltpu.CompilerParams(collective_id=1, has_side_effects=True, vmem_limit_bytes=VMEM_LIMIT),
        name="scatter",
    )(grads, small, rows)


KEY, VALUE, QUERY, OUT, FIRST, SECOND = range(6)
ATTN, CROSS, INNER, OUTER = range(4)
SEGS_HELD = 6


def rms(value):
    return lax.rsqrt(jnp.mean(value * value, axis=-1, keepdims=True) + EPSILON)


def in_rows(count, body, piece=32):
    @pl.loop(0, count // piece)
    def _(k):
        body(pl.ds(pl.multiple_of(k * piece, piece), piece))


def columns_of(count, body, piece=256):
    @pl.loop(0, count // piece)
    def _(k):
        body(pl.ds(pl.multiple_of(k * piece, piece), piece), k)


def normalize(source, gain, target, count):
    def body(at):
        value = source[at, :].astype(F32)
        target[at, :] = (value * rms(value) * gain).astype(BF16)

    in_rows(count, body)


def normalize_back(source, gain, incoming, total, gain_parts, count, fresh):
    gain_parts[...] = jnp.zeros_like(gain_parts)

    def body(at):
        value, back = source[at, :].astype(F32), incoming[at, :]
        scale = rms(value)
        unit = value * scale
        gain_parts[...] += jnp.sum((back * unit).reshape(-1, 8, back.shape[-1]), axis=0)
        back = back * gain
        back = scale * (back - unit * jnp.mean(back * unit, axis=-1, keepdims=True))
        total[at, :] = back if fresh else total[at, :] + back

    in_rows(count, body)


def project(left, weight, target, count):
    def body(at, k):
        target[0:count, at] = nn(left[0:count, :], weight[:, at]).astype(target.dtype)

    columns_of(weight.shape[1], body)


def project_back(left, weight, total, count, fresh):
    def body(at, k):
        value = nt(left[0:count, :], weight[at, :])
        total[0:count, at] = value if fresh else total[0:count, at] + value

    columns_of(weight.shape[0], body)


def to_bf16(source, target, rows):
    def body(at):
        target[at, :] = source[at, :].astype(BF16)

    in_rows(rows, body)


def turn(left, turned, rows):
    def body(at, k):
        turned[at, 0:rows] = left[0:rows, at].T

    columns_of(left.shape[1], body, LANES)


def lane_half(shape, part):
    return lax.broadcasted_iota(jnp.int32, shape, 1) // HEAD_DIM == part


def attend(keys, values, queries, mixture, probs, rows, span, pairs, mask, bias, after):
    @pl.loop(0, pairs)
    def _(pair):
        lanes = pl.ds(pl.multiple_of(pair * LANES, LANES), LANES)
        key, query = keys[0:span, lanes], queries[0:rows, lanes]
        value_t = values[0:span, lanes].T
        mixed = []
        for part in range(2):
            one = jnp.where(lane_half(query.shape, part), query, jnp.zeros_like(query))
            scores = nt(key, one) + mask[0:span, 0:rows]
            if bias is not None:
                scores = scores + bias(2 * pair + part)
            scores = jnp.exp(scores - jnp.max(scores, axis=0, keepdims=True))
            scores = (scores * (1.0 / jnp.sum(scores, axis=0, keepdims=True))).astype(BF16)
            probs[2 * pair + part, 0:span, 0:rows] = scores
            mixed.append(nn(value_t[part * HEAD_DIM : (part + 1) * HEAD_DIM, :], scores))
        mixture[0:rows, lanes] = jnp.concatenate(mixed, axis=0).T.astype(BF16)
        after(pair)


def attend_back(keys, values, queries, back, probs, rows, span, pairs, each, before, after):
    @pl.loop(0, pairs)
    def _(pair):
        before(pair)
        lanes = pl.ds(pl.multiple_of(pair * LANES, LANES), LANES)
        key, value = keys[0:span, lanes], values[0:span, lanes]
        query, given = queries[0:rows, lanes], back[0:rows, lanes]
        key_t = key.T
        d_key, d_value, d_query = None, None, []
        for part in range(2):
            side = lane_half(query.shape, part)
            query_one = jnp.where(side, query, jnp.zeros_like(query))
            given_one = jnp.where(side, given, jnp.zeros_like(given))
            prob = probs[2 * pair + part, 0:span, 0:rows]
            wide = prob.astype(F32)
            d_prob = nt(value, given_one)
            d_score = (wide * (d_prob - jnp.sum(wide * d_prob, axis=0, keepdims=True))).astype(BF16)
            if each is not None:
                each(2 * pair + part, d_score)
            of_key, of_value = nn(d_score, query_one), nn(prob, given_one)
            d_key = of_key if d_key is None else d_key + of_key
            d_value = of_value if d_value is None else d_value + of_value
            d_query.append(nn(key_t[part * HEAD_DIM : (part + 1) * HEAD_DIM, :], d_score))
        keys[0:span, lanes] = d_key.astype(BF16)
        values[0:span, lanes] = d_value.astype(BF16)
        queries[0:rows, lanes] = jnp.concatenate(d_query, axis=0).T.astype(BF16)
        after(pair)


def segments(lengths_row, shape, axis, first):
    lane = lax.broadcasted_iota(jnp.int32, lengths_row.shape, 1)
    places = lax.broadcasted_iota(jnp.int32, shape, axis) + first
    ids = jnp.zeros(shape, jnp.int32)
    for c in range(SEGS_HELD):
        bound = jnp.sum(jnp.where(lane <= c, lengths_row, 0), axis=1, keepdims=True)
        ids = ids + (places >= bound).astype(jnp.int32)
    return ids


def masked(allowed):
    return jnp.where(allowed, 0.0, NEGATIVE).astype(F32)


def nothing(*unused, **named):
    pass


def work(r, here, supply, drain, tensor, heads_at):
    c, t = here.core, here.t
    width = r.hidden.shape[1]
    tall = r.hidden.shape[0]
    block = width // tensor
    half_width = width // 2
    units = r.inner.shape[2]
    places = r.x.shape[2]
    sibling = here.sibling()
    across = [{"pipe": 1 - here.pipe, "dp": here.group * CORES + k} for k in range(CORES)]
    nrow = tensor // CORES
    rows_e, span_e, rows_d, span_d = tall // 2, tall, tall // 4, tall // 2
    pairs_here = half_width // LANES
    near_lanes = pl.ds(pl.multiple_of(c * half_width, half_width), half_width)
    far_lanes = pl.ds(pl.multiple_of((1 - c) * half_width, half_width), half_width)
    lane_halves = [slice(k * half_width, (k + 1) * half_width) for k in range(CORES)]

    def move(source, target, sends, recvs, device):
        return pltpu.make_async_remote_copy(
            source, target, r.send_sem.at[sends], r.recv_sem.at[recvs], device_id=device, device_id_type=MESH
        )

    def lengths_row(first):
        return r.lengths[t // nrow, pl.ds(first + lax.rem(t, nrow), 1), :]

    def pair_lanes(pair):
        return pl.ds(pair * LANES if isinstance(pair, int) else pl.multiple_of(pair * LANES, LANES), LANES)

    def vector_row(head):
        return (head // heads_at) * 8 + lax.rem(head, heads_at)

    def bias_vectors():
        buckets = lax.broadcasted_iota(jnp.int32, r.onehot.shape, 0) == r.buckets[0:1, :]
        r.onehot[...] = buckets.astype(F32)
        for tt in range(tensor):
            r.vectors[pl.ds(8 * tt, 8), :] = lax.dot_general(
                r.tables[tt][:, 0 : r.onehot.shape[0]], r.onehot[...], (((1,), (0,)), ((), ())),
                precision=lax.Precision.HIGHEST, preferred_element_type=F32,
            )

    def rows_ready(span, rows, first_block):
        @pl.loop(0, span // places)
        def _(k):
            value = r.x[k // tensor, lax.rem(k, tensor)].astype(F32)
            at = pl.ds(pl.multiple_of(k * places, places), places)
            r.hidden[at, :] = (value * rms(value) * r.gains[0]).astype(BF16)

        for k in range(rows // places):
            r.own_x[k * places : (k + 1) * places, :] = r.x[first_block // tensor, lax.rem(first_block, tensor) + k]

    def untangle(source, first, count):
        for tt in range(tensor):
            for k in range(count):
                r.square[first + k, :, tt * block : (tt + 1) * block] = source[tt, :, k * block : (k + 1) * block]

    def self_forward(span, rows, first_row, group):
        def bias(head):
            pieces = []
            for j in range(span // LANES):
                start = pl.multiple_of(first_row + span - LANES - j * LANES, LANES)
                row = r.vectors[pl.ds(vector_row(head), 1), pl.ds(start, rows + LANES)]
                wide = jnp.broadcast_to(row, (LANES, rows + LANES))
                pieces.append(pltpu.roll(wide, rows + 1, 1, stride=1, stride_axis=0)[:, 0:rows])
            return jnp.concatenate(pieces, axis=0)

        untangle(r.raw_a, KEY, 2)
        untangle(r.raw_a.at[:, :, pl.ds(2 * block, 2 * block)], QUERY, 2)
        project(r.hidden, r.square.at[KEY], r.keys, span)
        supply.pump()
        project(r.hidden, r.square.at[VALUE], r.values, span)
        project(r.hidden.at[pl.ds(first_row, rows)], r.square.at[QUERY], r.queries, rows)
        supply.pump()
        after = at_each(range(width // LANES), supply.pump)

        attend(r.keys, r.values, r.queries, r.mixture, r.probs, rows, span, width // LANES, r.mask, bias, after)
        project_back(r.mixture, r.square.at[OUT], r.resid_mid, rows, True)

        def add(at):
            r.resid_mid[at, :] += r.own_x[at, :].astype(F32)

        in_rows(rows, add)
        supply.pump(until=group)
        supply.finish(group)

    def at_each(places, do):
        def hook(n):
            for place in places:

                @pl.when(n == place)
                def _():
                    do()

        return hook

    def feed_forward(rows, hook=nothing):
        @pl.loop(0, tensor)
        def _(tt):
            def body(at, k):
                value = nn(r.second[0:rows, :], r.inner[tt, :, at])
                cdf = 0.5 * (1.0 + lax.erf(value * 0.7071067811865476))
                r.ff[tt, 0:rows, at] = (value * cdf).astype(BF16)
                slope = cdf + value * jnp.exp(-0.5 * value * value) * 0.3989422804014327
                r.ff[tensor + tt, 0:rows, at] = slope.astype(BF16)
                hook(tt * (units // 256) + k)

            columns_of(units, body)

    def feed_out(target, rows, hook=nothing):
        @pl.loop(0, tensor)
        def _(tt):
            def body(at, k):
                target[0:rows, at] += nt(r.ff[tt, 0:rows, :], r.outer[tt, at, :])
                hook(tt * (width // 256) + k)

            columns_of(width, body)

    def feed_back(rows, ready, hook=nothing):
        r.summed[0:rows, :] = jnp.zeros((rows, width), F32)

        @pl.loop(0, tensor)
        def _(tt):
            def body(at, k):
                if ready:
                    value = r.ff[tensor + tt, rows : 2 * rows, at].astype(F32)
                else:
                    value = nn(r.d_branch[0:rows, :], r.outer[tt, :, at])
                r.ff[tensor + tt, 0:rows, at] = (value * r.ff[tensor + tt, 0:rows, at].astype(F32)).astype(BF16)

            columns_of(units, body)

            def back(at, k):
                r.summed[0:rows, at] += nt(r.ff[tensor + tt, 0:rows, :], r.inner[tt, at, :])

            columns_of(width, back)
            hook(tt)

    def feed_grads(rows, turned, first, which, hook=nothing):
        @pl.loop(0, tensor)
        def _(tt):
            slot = lax.rem(tt, 2)

            @pl.when(tt >= 2)
            def _():
                drain.release(which, tt - 2, slot)

            def body(at, k):
                r.stage[slot, :, at] = nn(turned[:, 0:rows], r.ff[first + tt, 0:rows, at]).astype(BF16)
                hook(tt * (units // 256) + k)

            columns_of(units, body)
            drain.emit(which, tt, slot)

        for tt in range(tensor - 2, tensor):
            drain.release(which, tt, tt % 2)

    def square_grads(rows, which, products, hook):
        for k in range(tensor // 2):
            for j, (turned, right) in enumerate(products):
                value = nn(turned[:, 0:rows], right[0:rows, 2 * k * block : 2 * (k + 1) * block]).astype(BF16)
                for slot in range(2):
                    r.stage[slot, :, j * block : (j + 1) * block] = value[:, slot * block : (slot + 1) * block]
            for slot in range(2):
                drain.emit(which, 2 * k + slot, slot)
            hook(k)
            for slot in range(2):
                drain.release(which, 2 * k + slot, slot)

    def gain_done(which):
        r.gains_out[which : which + 1, :] = jnp.sum(r.gain_parts[...], axis=0, keepdims=True)

    def self_backward(span, rows, first_row, steps, send_rows):
        mirror = (
            lax.broadcasted_iota(jnp.int32, (LANES, LANES), 0) + lax.broadcasted_iota(jnp.int32, (LANES, LANES), 1)
            == LANES - 1
        ).astype(BF16)
        to_bf16(r.d_resid, r.branch, rows)
        project(r.branch, r.square.at[OUT], r.d_branch, rows)
        r.diagonals[...] = jnp.zeros_like(r.diagonals)

        def each(head, d_score):
            for j in range(span // LANES):
                start = pl.multiple_of(first_row + span - LANES - j * LANES, LANES)
                piece = nn(mirror, d_score[j * LANES : (j + 1) * LANES, :])
                piece = jnp.concatenate([piece, jnp.zeros((LANES, LANES), F32)], axis=1)
                piece = pltpu.roll(piece, 0, 1, stride=1, stride_axis=0)
                at = (pl.ds(vector_row(head), 1), pl.ds(start, rows + LANES))
                r.diagonals[at] += jnp.sum(piece, axis=0, keepdims=True)

        pairs = width // LANES
        attend_back(
            r.keys, r.values, r.queries, r.d_branch, r.probs, rows, span, pairs, each, nothing,
            at_each(range(pairs), steps),
        )
        far = pl.ds(pl.multiple_of((1 - c) * rows, rows), rows)
        near = pl.ds(pl.multiple_of(c * rows, rows), rows)
        trades = [
            move(source.at[far], r.taken_pair.at[k, pl.ds(0, rows)], 12 + k, 12 + k, sibling)
            for k, source in enumerate((r.keys, r.values))
        ]
        for trade in trades:
            trade.start()
        steps()
        turn(r.branch, r.turned, rows)
        turn(r.hidden.at[pl.ds(first_row, rows)], r.turned_more, rows)
        for tt in range(tensor):
            at = pl.ds(8 * tt, 8)
            r.bias_out[at, 0 : r.onehot.shape[0]] = lax.dot_general(
                r.diagonals[at, :], r.onehot[...], (((1,), (1,)), ((), ())),
                precision=lax.Precision.HIGHEST, preferred_element_type=F32,
            )
        steps()
        project_back(r.queries, r.square.at[QUERY], r.summed, rows, True)
        for trade in trades:
            trade.wait_recv()
        steps()
        for k, source in enumerate((r.keys, r.values)):
            r.d_pair[k, 0:rows, :] = (source[near, :].astype(F32) + r.taken_pair[k, 0:rows, :].astype(F32)).astype(BF16)
        project_back(r.d_pair.at[0], r.square.at[KEY], r.summed, rows, False)
        project_back(r.d_pair.at[1], r.square.at[VALUE], r.summed, rows, False)
        steps()
        normalize_back(r.own_x, r.gains[0], r.summed, r.d_resid, r.gain_parts, rows, False)
        gain_done(0)
        steps()
        send_rows()
        drain.small_begin()
        drain.allow(2)
        products = [(r.turned_more, r.d_pair.at[0]), (r.turned_more, r.d_pair.at[1]), (r.turned_more, r.queries), (r.turned, r.mixture)]
        square_grads(rows, ATTN, products, nothing)
        for trade in trades:
            trade.wait_send()
        steps()
        drain.begin(ATTN)
        steps()
        drain.rest(ATTN)

    def parts_of(array):
        return [array.at[pl.ds(k * rows_d, rows_d)] for k in range(CORES)]

    def part_here(array):
        return array.at[pl.ds(pl.multiple_of(c * rows_d, rows_d), rows_d)]

    r.gains_out[...] = jnp.zeros_like(r.gains_out)
    r.bias_out[...] = jnp.zeros_like(r.bias_out)
    supply.start()

    def entry():
        supply.pump(2)
        supply.small()
        bias_vectors()
        supply.pump(2)
        supply.rows()

    def schedule(*items):
        left = list(items)

        def steps():
            for name, group, *n in left.pop(0) if left else ():
                getattr(drain, name)(group, *n)

        return steps

    @pl.when(here.pipe == 0)
    def _():
        supply.resume(ATTN, INNER, OUTER, CROSS)
        drain.order(CROSS, OUTER, INNER, ATTN)
        entry()
        rows, span = rows_e, span_e
        first_row = pl.multiple_of(c * rows, rows)
        seg_rows = segments(lengths_row(0), (span, 1), 0, 0)
        r.mask[...] = masked(seg_rows == segments(lengths_row(0), (1, rows), 1, first_row))
        supply.pump()
        rows_ready(span, rows, c * tensor)
        supply.pump(until=ATTN)
        supply.finish(ATTN)
        self_forward(span, rows, first_row, INNER)
        normalize(r.resid_mid, r.gains[1], r.second, rows)
        feed_forward(rows, at_each((3, 7, 11), supply.pump))
        supply.pump(until=OUTER)
        supply.finish(OUTER)
        r.resid_top[...] = r.resid_mid[...]
        feed_out(r.resid_top, rows, at_each((3, 7, 11), supply.pump))
        normalize(r.resid_top, r.gains[2], r.third, rows)
        r.mask[...] = masked(seg_rows == segments(lengths_row(nrow), (1, span_d), 1, 0))
        supply.pump(until=CROSS)
        supply.finish(CROSS)
        untangle(r.raw_c, FIRST, 2)
        mine = pl.ds(first_row, rows)
        other = pl.ds(pl.multiple_of((1 - c) * rows, rows), rows)
        trades = []
        for k, held in enumerate((r.cross_keys, r.cross_values)):
            r.send_pair[k] = nn(r.third[...], r.square[FIRST + k, :, far_lanes]).astype(BF16)
            trades.append(move(r.send_pair.at[k], held.at[mine], k, k, sibling))
            trades[-1].start()
        for k, held in enumerate((r.cross_keys, r.cross_values)):
            held[mine, :] = nn(r.third[...], r.square[FIRST + k, :, near_lanes]).astype(BF16)
        for k, part in enumerate(parts_of(r.cross_queries)):
            move(part, part, 2 + k, 2 + k, across[k]).wait_recv()
        for k, held in enumerate((r.cross_keys, r.cross_values)):
            move(r.send_pair.at[k], held.at[other], k, k, sibling).wait_recv()

        def mixtures(pair):
            at = pair_lanes(pair)
            return [
                pltpu.make_async_remote_copy(
                    r.cross_mixture.at[pl.ds(k * rows_d, rows_d), at], r.cross_in.at[c, :, at],
                    r.mix_send.at[k, pair], r.mix_recv.at[c, pair], device_id=across[k], device_id_type=MESH,
                )
                for k in range(CORES)
            ]

        def arrived(pair):
            for k in range(CORES):
                part = r.cross_back.at[pl.ds(k * rows_d, rows_d), pair_lanes(pair)]
                pltpu.make_async_remote_copy(
                    part, part, r.back_send.at[k, pair], r.back_recv.at[k, pair], device_id=across[k], device_id_type=MESH
                ).wait_recv()

        def returns(pair):
            at = pair_lanes(pair)
            return [
                pltpu.make_async_remote_copy(
                    d_cross.at[other, at], r.cross_taken.at[k, :, at],
                    r.give_send.at[k, pair], r.give_recv.at[k, pair], device_id=sibling, device_id_type=MESH,
                )
                for k, d_cross in enumerate((r.cross_keys, r.cross_values))
            ]

        attend(
            r.cross_keys, r.cross_values, r.cross_queries, r.cross_mixture, r.cross_probs, span_d, span, pairs_here,
            r.mask, None, lambda pair: [mix.start() for mix in mixtures(pair)],
        )
        supply.close()
        drain.free(0)
        turn(r.third, r.turned, rows)
        attend_back(
            r.cross_keys, r.cross_values, r.cross_queries, r.cross_back, r.cross_probs, span_d, span, pairs_here, None,
            arrived, lambda pair: [back.start() for back in returns(pair)],
        )
        answers = [
            move(part, r.cross_in_back.at[c], 8 + k, 8 + c, across[k]) for k, part in enumerate(parts_of(r.cross_queries))
        ]
        for answer in answers:
            answer.start()
        for k, d_cross in enumerate((r.cross_keys, r.cross_values)):
            r.d_pair[k, :, near_lanes] = d_cross[mine, :]
        for pair in range(pairs_here):
            for back in returns(pair):
                back.wait_recv()
        for k in range(2):
            r.d_pair[k, :, far_lanes] = r.cross_taken[k]
        drain.allow(0)
        square_grads(rows, CROSS, [(r.turned, r.d_pair.at[0]), (r.turned, r.d_pair.at[1])], nothing)
        drain.begin(CROSS)
        project_back(r.d_pair.at[0], r.square.at[FIRST], r.summed, rows, True)
        project_back(r.d_pair.at[1], r.square.at[SECOND], r.summed, rows, False)
        normalize_back(r.resid_top, r.gains[2], r.summed, r.d_resid, r.gain_parts, rows, True)
        gain_done(2)
        to_bf16(r.d_resid, r.d_branch, rows)
        turn(r.d_branch, r.turned, rows)
        feed_grads(rows, r.turned, 0, OUTER, at_each((8,), lambda: drain.tick(CROSS, 0)))
        drain.tick(CROSS, 1)
        drain.begin(OUTER)
        feed_back(rows, False, at_each((0, 2), schedule([("tick", CROSS, 2)], [("tick", OUTER, 0)])))
        drain.free(1)
        drain.free(2)
        turn(r.second, r.turned, rows)
        drain.tick(CROSS, 3)
        drain.allow(1)
        feed_grads(rows, r.turned, tensor, INNER, at_each((5, 8), schedule([("tick", OUTER, 1)], [("tick", CROSS, 4)])))
        drain.begin(INNER)
        normalize_back(r.resid_mid, r.gains[1], r.summed, r.d_resid, r.gain_parts, rows, False)
        gain_done(1)
        for copy in trades + answers:
            copy.wait_send()
        for pair in range(pairs_here):
            for copy in mixtures(pair) + returns(pair):
                copy.wait_send()

        def send_rows():
            to_bf16(r.d_resid, r.rows_out, rows)
            drain.home()

        steps = schedule(
            [], [("tick", OUTER, 2)], [("tick", INNER, 0)], [("end", CROSS)], [("tick", OUTER, 3)], [],
            [("tick", INNER, 1), ("tick", INNER, 2), ("tick", OUTER, 4)], [], [], [], [("tick", INNER, 3)], [("tick", INNER, 4)],
            [("end", OUTER), ("tick", ATTN, 0), ("tick", ATTN, 1), ("tick", ATTN, 2), ("home_done", None)]
            + [("tick", ATTN, 3), ("tick", ATTN, 4), ("end", INNER)],
        )
        self_backward(span, rows, first_row, steps, send_rows)

    @pl.when(here.pipe == 1)
    def _():
        supply.resume(ATTN, CROSS, INNER, OUTER)
        drain.order(OUTER, INNER, CROSS, ATTN)
        entry()
        rows, span = rows_d, span_d
        first_row = pl.multiple_of(c * rows, rows)
        key_at = lax.broadcasted_iota(jnp.int32, (span, rows), 0)
        query_at = lax.broadcasted_iota(jnp.int32, (span, rows), 1) + first_row
        same = segments(lengths_row(nrow), (span, 1), 0, 0) == segments(lengths_row(nrow), (1, rows), 1, first_row)
        r.mask[0:span, 0:rows] = masked(same & (query_at >= key_at))
        supply.pump()
        first_block = c * (tensor // 2)
        rows_ready(span, rows, first_block)
        for k in range(rows // places):
            r.d_branch[k * places : (k + 1) * places, :] = r.x[1, first_block + k]
        supply.pump(until=ATTN)
        supply.finish(ATTN)
        self_forward(span, rows, first_row, CROSS)
        untangle(r.raw_c, FIRST, 2)
        normalize(r.resid_mid, r.gains[1], r.third, rows)
        project(r.third, r.square.at[FIRST], r.joined, rows)
        asks = []
        for k in range(CORES):
            r.send_pair[k, 0:rows, :] = r.joined[:, lane_halves[k]]
            asks.append(move(r.send_pair.at[k, pl.ds(0, rows)], part_here(r.cross_queries), 2 + k, 2 + c, across[k]))
            asks[-1].start()
        supply.pump(until=INNER)
        supply.finish(INNER)
        supply.pump(until=OUTER)
        supply.finish(OUTER)

        @pl.loop(0, tensor)
        def _(tt):
            def body(at, k):
                r.ff[tensor + tt, rows : 2 * rows, at] = nn(r.d_branch[0:rows, :], r.outer[tt, :, at]).astype(BF16)

            columns_of(units, body)

        supply.close()
        drain.free(0)
        r.resid_top[0:rows, :] = r.resid_mid[0:rows, :]
        for k in range(CORES):
            for pair in range(pairs_here):
                part = r.cross_in.at[k, :, pair_lanes(pair)]
                pltpu.make_async_remote_copy(
                    part, part, r.mix_send.at[k, pair], r.mix_recv.at[k, pair], device_id=across[k], device_id_type=MESH
                ).wait_recv()
            r.joined[:, lane_halves[k]] = r.cross_in[k]
        project_back(r.joined, r.square.at[SECOND], r.resid_top, rows, False)
        normalize(r.resid_top, r.gains[2], r.second, rows)
        feed_forward(rows)
        feed_back(rows, True)
        r.d_resid[0:rows, :] = r.d_branch[0:rows, :].astype(F32)
        normalize_back(r.resid_top, r.gains[2], r.summed, r.d_resid, r.gain_parts, rows, False)
        gain_done(2)
        to_bf16(r.d_resid, r.branch, rows)
        tells = []
        for pair in range(pairs_here):
            for k in range(CORES):
                at = pair_lanes(pair)
                first = k * half_width + pair * LANES
                r.send_back[k, :, at] = nn(r.branch[0:rows, :], r.square[SECOND, :, first : first + LANES]).astype(BF16)
                tells.append(
                    pltpu.make_async_remote_copy(
                        r.send_back.at[k, :, at], r.cross_back.at[pl.ds(pl.multiple_of(c * rows, rows), rows), at],
                        r.back_send.at[k, pair], r.back_recv.at[c, pair], device_id=across[k], device_id_type=MESH,
                    )
                )
                tells[-1].start()
        drain.free(1)
        turn(r.d_branch, r.turned, rows)
        drain.allow(0)
        feed_grads(rows, r.turned, 0, OUTER)
        drain.begin(OUTER)
        turn(r.second, r.turned, rows)
        drain.allow(1)
        feed_grads(rows, r.turned, tensor, INNER)
        drain.begin(INNER)
        feed_out(r.resid_top, rows, at_each((5,), lambda: drain.tick(OUTER, 0)))
        drain.free(2)
        to_bf16(r.resid_top, r.rows_out, rows)
        turn(r.branch, r.turned, rows)
        turn(r.third, r.turned_more, rows)
        for k in range(CORES):
            move(r.cross_in_back.at[k], r.cross_in_back.at[k], 8 + k, 8 + k, across[k]).wait_recv()
            r.d_pair[1, 0:rows, lane_halves[k]] = r.cross_in_back[k]
        project_back(r.d_pair.at[1], r.square.at[FIRST], r.summed, rows, True)
        square_grads(rows, CROSS, [(r.turned_more, r.d_pair.at[1]), (r.turned, r.joined)], nothing)
        drain.tick(OUTER, 1)
        normalize_back(r.resid_mid, r.gains[1], r.summed, r.d_resid, r.gain_parts, rows, False)
        gain_done(1)
        for copy in asks + tells:
            copy.wait_send()

        def send_rows():
            to_bf16(r.d_resid, r.rows_out.at[pl.ds(rows, rows)], rows)
            drain.home()

        steps = schedule(
            [], [("tick", INNER, 0)], [], [("tick", INNER, 1)], [("tick", OUTER, 2)], [],
            [("tick", OUTER, 3)], [], [("tick", INNER, 2), ("tick", OUTER, 4)], [("begin", CROSS)],
            [("tick", INNER, 3), ("tick", INNER, 4)], [],
            [("end", OUTER), ("tick", CROSS, 0), ("tick", ATTN, 0), ("tick", CROSS, 1), ("end", INNER), ("tick", ATTN, 1)]
            + [("tick", ATTN, 2), ("tick", CROSS, 2), ("home_done", None), ("tick", ATTN, 3), ("tick", ATTN, 4)]
            + [("tick", CROSS, 3), ("tick", CROSS, 4), ("end", CROSS)],
        )
        self_backward(span, rows, first_row, steps, send_rows)

    drain.close()


def held(*shape, dtype=BF16):
    return pltpu.VMEM(shape, dtype)


def arrays(tensor, heads_at, places, width, units, ranges, kinds):
    tall = 2 * tensor * places
    block = width // tensor
    half_rows, half_width = tall // 2, width // 2
    heads = heads_at * tensor
    return dict(
        x=held(2, tensor, places, width),
        own_x=held(half_rows, width),
        raw_a=held(tensor, width, 4 * block),
        raw_c=held(tensor, width, 2 * block),
        square=held(6, width, width),
        inner=held(tensor, width, units),
        outer=held(tensor, width, units),
        hidden=held(tall, width),
        keys=held(tall, width),
        values=held(tall, width),
        queries=held(half_rows, width),
        probs=held(heads, tall, half_rows),
        mask=held(tall, half_rows, dtype=F32),
        mixture=held(half_rows, width),
        resid_mid=held(half_rows, width, dtype=F32),
        resid_top=held(half_rows, width, dtype=F32),
        d_resid=held(half_rows, width, dtype=F32),
        summed=held(half_rows, width, dtype=F32),
        second=held(half_rows, width),
        third=held(half_rows, width),
        ff=held(2 * tensor, half_rows, units),
        d_branch=held(half_rows, width),
        branch=held(half_rows, width),
        cross_keys=held(tall, half_width),
        cross_values=held(tall, half_width),
        cross_queries=held(half_rows, half_width),
        cross_mixture=held(half_rows, half_width),
        cross_probs=held(heads // CORES, tall, half_rows),
        cross_back=held(half_rows, half_width),
        cross_in=held(CORES, half_rows // 2, half_width),
        cross_in_back=held(CORES, half_rows // 2, half_width),
        cross_taken=held(CORES, half_rows, half_width),
        send_pair=held(CORES, half_rows, half_width),
        send_back=held(CORES, half_rows // 2, half_width),
        joined=held(half_rows // 2, width),
        taken_pair=held(2, half_rows, width),
        d_pair=held(2, half_rows, width),
        turned=held(width, half_rows),
        turned_more=held(width, half_rows),
        stage=held(2, width, units),
        vectors=held(8 * tensor, ranges, dtype=F32),
        diagonals=held(8 * tensor, ranges, dtype=F32),
        onehot=held(kinds, ranges, dtype=F32),
        gain_parts=held(8, width, dtype=F32),
        send_sem=pltpu.SemaphoreType.DMA((14,)),
        recv_sem=pltpu.SemaphoreType.DMA((14,)),
        **{
            name: pltpu.SemaphoreType.DMA((CORES, half_width // LANES))
            for name in ("mix_send", "mix_recv", "back_send", "back_recv", "give_send", "give_recv")
        },
    )


def group_columns(block, units):
    return {ATTN: (0, 4 * block), CROSS: (4 * block, 2 * block), INNER: (6 * block, units), OUTER: (6 * block + units, units)}


def landing(r):
    return {ATTN: r.raw_a, CROSS: r.raw_c, INNER: r.inner, OUTER: r.outer}


class Loads:
    def __init__(self, r, tensor, x_hbm, w_hbm, sems):
        columns = group_columns(r.raw_a.shape[2] // 4, r.inner.shape[2])
        self.x = pltpu.make_async_copy(x_hbm, r.x, sems.at[4, 0])
        self.weights = [
            [
                pltpu.make_async_copy(w_hbm.at[tt, :, pl.ds(*columns[group])], target.at[tt], sems.at[group, tt])
                for tt in range(tensor)
            ]
            for group, target in landing(r).items()
        ]

    def start(self):
        self.x.start()
        for group in self.weights:
            for copy in group:
                copy.start()

    def rows(self):
        self.x.wait()

    def finish(self, group):
        for copy in self.weights[group]:
            copy.wait()

    small = resume = pump = close = nothing


class Stores:
    def __init__(self, r, grads_hbm, sems):
        self.columns = group_columns(r.raw_a.shape[2] // 4, r.inner.shape[2])
        self.r, self.grads, self.sems = r, grads_hbm, sems

    def copy(self, group, tt, slot):
        first, wide = self.columns[group]
        return pltpu.make_async_copy(
            self.r.stage.at[slot, :, pl.ds(0, wide)], self.grads.at[tt, :, pl.ds(first, wide)], self.sems.at[slot]
        )

    def emit(self, group, tt, slot):
        self.copy(group, tt, slot).start()

    def release(self, group, tt, slot):
        self.copy(group, tt, slot).wait()

    order = free = allow = begin = tick = rest = end = home = home_done = small_begin = close = nothing


def blocks_kernel(tensor, dp, heads_at, names, *refs):
    here = Place(tensor, dp)
    r = types.SimpleNamespace(**dict(zip(names, refs)))
    across = [{"pipe": 1 - here.pipe, "dp": here.group * CORES + k} for k in range(CORES)]
    meet([here.sibling()] + across)
    work(r, here, Loads(r, tensor, r.x_hbm, r.w_hbm, r.load_sem), Stores(r, r.grads_hbm, r.stage_sem), tensor, heads_at)


def blocks(tensor, dp, heads_at, kinds, rows, weights, gains, lengths, tables, buckets):
    places, width = rows.shape[2:]
    units = (weights.shape[2] - 6 * (width // tensor)) // 2
    half_rows = tensor * places
    scratch = arrays(tensor, heads_at, places, width, units, buckets.shape[1], kinds)
    scratch["load_sem"] = pltpu.SemaphoreType.DMA((5, tensor))
    scratch["stage_sem"] = pltpu.SemaphoreType.DMA((2,))
    names = ["x_hbm", "w_hbm", "gains", "lengths", "tables", "buckets", "grads_hbm", "rows_out", "gains_out", "bias_out"]
    return pl.pallas_call(
        functools.partial(blocks_kernel, tensor, dp, heads_at, names + list(scratch)),
        out_shape=(
            jax.ShapeDtypeStruct(weights.shape, BF16),
            jax.ShapeDtypeStruct((half_rows, width), BF16),
            jax.ShapeDtypeStruct((8, width), F32),
            jax.ShapeDtypeStruct((8 * tensor, LANES), F32),
        ),
        in_specs=[ANY, ANY] + [VMEM] * 4,
        out_specs=(ANY, VMEM, VMEM, VMEM),
        scratch_shapes=list(scratch.values()),
        compiler_params=pltpu.CompilerParams(collective_id=2, has_side_effects=True, vmem_limit_bytes=VMEM_LIMIT),
        name="blocks",
    )(rows, weights, gains, lengths, tables, buckets)


class Rings:
    def __init__(self, r, here, tensor, dp):
        self.r, self.here, self.tensor, self.dp = r, here, tensor, dp
        self.depth = r.value_w.shape[0]
        self.hops = here.chips // 2
        self.count = 2 * self.hops - 1
        self.sibling = here.sibling()
        self.targets = [here.neighbour(1), here.neighbour(-1)]
        self.landing = landing(r)
        self.groups = []
        self.plan = []


    def order(self, *groups):
        steps = []
        for k, group in enumerate(groups):
            steps.append((4 * k - 0.5, k, self.begin, group, None))
            late = {self.count - 3: 3.6, self.count - 2: 3.7, self.count - 1: 5.5}
            steps += [(4 * k + late.get(n, n), k, self.tick, group, n) for n in range(self.count)]
        steps.sort(key=lambda step: step[:2])
        self.groups = list(groups)
        self.plan = [step[2:] for step in steps]

    def resume(self, *groups):
        self.order(*groups)
        self.plan.pop(0)

    def pump(self, count=1, until=None):
        while self.plan and (count > 0 if until is None else any(step[1] == until for step in self.plan)):
            do, group, n = self.plan.pop(0)
            do(group) if n is None else do(group, n)
            count -= 0 if n is None else 1


    def block_out(self, i):
        r, t, c = self.r, self.here.t, self.here.core
        return pltpu.make_async_remote_copy(
            r.rows.at[i], r.x.at[:, t], r.block_send.at[i], r.block_recv.at[t],
            device_id={"tensor": r.rows.shape[0] * c + i}, device_id_type=MESH,
        )

    def block_kept(self, i):
        return pltpu.make_async_copy(self.r.rows.at[i], self.r.x.at[:, self.here.t], self.r.local_sem.at[0])

    def block_pass(self, source, s):
        r = self.r
        return pltpu.make_async_remote_copy(
            source, r.x.at[:, s], r.pass_send.at[s], r.pass_recv.at[s], device_id=self.sibling, device_id_type=MESH
        )

    def blocks(self, mine, others):
        for i in range(self.r.rows.shape[0]):
            here = self.r.rows.shape[0] * self.here.core + i == self.here.t

            @pl.when(here)
            def _():
                mine(i)

            @pl.when(jnp.logical_not(here))
            def _():
                others(i)

    def small_copies(self):
        r, t = self.r, self.here.t
        copies = [
            pltpu.make_async_remote_copy(
                r.lengths_in, r.lengths.at[self.here.core], r.small_send.at[0], r.small_recv.at[0],
                device_id=self.sibling, device_id_type=MESH,
            ),
            pltpu.make_async_copy(r.lengths_in, r.lengths.at[self.here.core], r.local_sem.at[1]),
            pltpu.make_async_copy(r.table_in, r.tables.at[t], r.local_sem.at[2]),
        ]
        for k in range(1, self.tensor):
            copies.append(
                pltpu.make_async_remote_copy(
                    r.table_in, r.tables.at[t], r.small_send.at[k], r.small_recv.at[k],
                    device_id={"tensor": lax.rem(t + k, self.tensor)}, device_id_type=MESH,
                )
            )
        return copies


    def rows_of(self, ring):
        line, at = self.here.at(ring)
        return at, pl.multiple_of((line * CORES + self.here.core) * self.depth, 16)

    def ring_at(self, step, part):
        way = -1 if part else 1
        return lax.rem(self.here.ring - way * step + self.here.chips, self.here.chips)

    def onward(self, group, step, part, sub):
        r, half = self.r, self.depth // 2
        at, first = self.rows_of(self.ring_at(step, part))
        target = self.landing[group]
        slot = target.at[at, pl.ds(pl.multiple_of(first + half * sub, 16), half), :]
        packed = r.stage.at[0, pl.ds(group * self.depth + half * sub, half), pl.ds(0, target.shape[2])]
        place = self.groups.index(group) % 2
        return pltpu.make_async_remote_copy(
            packed if step == 0 else slot, slot, r.ring_send.at[place, part, sub, step], r.ring_recv.at[group, part, sub, step],
            device_id=self.targets[part], device_id_type=MESH,
        )

    def over(self, group, ring, first_time=False):
        r = self.r
        at, first = self.rows_of(ring)
        target = self.landing[group]
        slot = target.at[at, pl.ds(first, self.depth), :]
        packed = r.stage.at[0, pl.ds(group * self.depth, self.depth), pl.ds(0, target.shape[2])]
        return pltpu.make_async_remote_copy(
            packed if first_time else slot, slot, r.over_send.at[group, ring], r.over_recv.at[group, ring],
            device_id=self.sibling, device_id_type=MESH,
        )

    def own(self, group):
        wide = self.landing[group].shape[2]
        first = pl.multiple_of(self.here.d * self.depth, 16)
        return pltpu.make_async_copy(
            self.r.stage.at[0, pl.ds(group * self.depth, self.depth), pl.ds(0, wide)],
            self.landing[group].at[self.here.t, pl.ds(first, self.depth), :],
            self.r.own_sem.at[group],
        )

    def begin(self, group):
        place = self.groups.index(group)
        if place >= 2:
            self.sends_done(self.groups[place - 2])
        for sub in range(2):
            for part in range(2):
                self.onward(group, 0, part, sub).start()
        self.over(group, self.here.ring, True).start()
        self.own(group).start()

    def tick(self, group, n):
        step, last = n // 2 + 1, n == self.count - 1
        for part in range(2):
            sub = part if last else n % 2
            self.onward(group, step - 1, part, sub).wait_recv()
            if not last and (step < self.hops - 1 or sub == part):
                self.onward(group, step, part, sub).start()
        if last:
            self.over(group, self.ring_at(step, 0)).start()
        elif n % 2:
            for part in range(2):
                self.over(group, self.ring_at(step, part)).start()

    def sends_done(self, group):
        for part in range(2):
            for sub in range(2):
                for step in range(self.hops):
                    if step < self.hops - 1 or sub == part:
                        self.onward(group, step, part, sub).wait_send()

    def finish(self, group):
        @pl.loop(0, self.here.chips)
        def _(ring):
            self.over(group, ring).wait_recv()

        self.own(group).wait()

    def start(self):
        r, depth = self.r, self.depth
        nrow = r.rows.shape[0]
        r.lengths_in[...] = jnp.zeros_like(r.lengths_in)
        r.lengths_in[0:nrow, 0 : r.enc_lengths.shape[1]] = r.enc_lengths[...]
        r.lengths_in[nrow : 2 * nrow, 0 : r.dec_lengths.shape[1]] = r.dec_lengths[...]
        r.table_in[...] = jnp.zeros_like(r.table_in)
        for k in range(r.bias_w.shape[0]):
            r.table_in[k : k + 1, 0 : r.bias_w.shape[2]] = r.bias_w[k]
        self.blocks(
            lambda i: (self.block_kept(i).start(), self.block_pass(r.rows.at[i], self.here.t).start()),
            lambda i: self.block_out(i).start(),
        )
        block = r.value_w.shape[1]

        def band(group, pieces):
            wide = pieces[0].shape[1]
            for k, piece in enumerate(pieces):
                r.stage[0, group * depth : (group + 1) * depth, k * wide : (k + 1) * wide] = piece

        band(ATTN, [r.query_key_w[1], r.value_w[...], r.query_key_w[0], r.out_w[...].T])
        self.order(ATTN)
        self.begin(ATTN)
        for copy in self.small_copies():
            copy.start()
        band(INNER, [r.inner_w[...]])
        band(OUTER, [r.outer_w[...]])
        band(CROSS, [r.first_w[...], r.second_w[...]])

    def small(self):
        for copy in self.small_copies():
            copy.wait()

    def rows(self):
        r, t = self.r, self.here.t
        takes = lax.div(t, r.rows.shape[0]) == self.here.core
        for s in range(self.tensor):

            @pl.when(jnp.logical_and(takes, s != t))
            def _():
                pltpu.make_async_remote_copy(
                    r.rows.at[0], r.x.at[:, s], r.block_send.at[0], r.block_recv.at[s],
                    device_id=self.sibling, device_id_type=MESH,
                ).wait_recv()
                self.block_pass(r.x.at[:, s], s).start()

        self.blocks(lambda i: self.block_kept(i).wait(), nothing)
        for s in range(self.tensor):

            @pl.when(jnp.logical_not(takes))
            def _():
                self.block_pass(r.x.at[:, s], s).wait_recv()

    def close(self):
        r, t = self.r, self.here.t
        takes = lax.div(t, r.rows.shape[0]) == self.here.core
        self.blocks(
            lambda i: self.block_pass(r.rows.at[i], t).wait_send(),
            lambda i: self.block_out(i).wait_send(),
        )
        for s in range(self.tensor):

            @pl.when(jnp.logical_and(takes, s != t))
            def _():
                self.block_pass(r.x.at[:, s], s).wait_send()

        for group in self.groups[-2:]:
            self.sends_done(group)
        for group in self.groups:

            @pl.loop(0, self.here.chips)
            def _(ring):
                self.over(group, ring).wait_send()


class Sums:
    def __init__(self, r, here, tensor, dp):
        self.r, self.here, self.tensor, self.dp = r, here, tensor, dp
        self.depth = r.value_w.shape[0]
        self.hops = here.chips // 2
        self.count = 2 * self.hops - 3
        self.sibling = here.sibling()
        self.targets = [here.neighbour(1), here.neighbour(-1)]
        self.box = {CROSS: r.raw_c, OUTER: r.raw_a, INNER: r.inner, ATTN: r.outer}
        self.kept = {CROSS: r.own_cross, OUTER: r.own_outer, INNER: r.own_inner, ATTN: r.ff}
        self.groups = []

    def order(self, *groups):
        self.groups = list(groups)

    def free(self, k):
        for device in self.targets + [self.sibling]:
            pl.semaphore_signal(self.r.free_sem.at[k], inc=1, device_id=device, device_id_type=MESH)

    def allow(self, k):
        pl.semaphore_wait(self.r.free_sem.at[k], 3)

    def boxed(self, group, index, first, height):
        if isinstance(index, int):
            return (index // self.dp, pl.ds(pl.multiple_of(index % self.dp * self.depth + first, 16), height), slice(None))
        at = pl.ds(pl.multiple_of(lax.rem(index, self.dp) * self.depth + first, 16), height)
        return (lax.div(index, self.dp), at, slice(None))

    def taken(self, group, step, part, first, height):
        index = step + part * (self.hops - 1) if step else 0
        return self.boxed(group, index, first, height)

    def theirs(self, group, ring, first, height):
        return self.boxed(group, self.here.chips - 1 + ring, first, height)

    def own(self, group, ring, first, height):
        return (ring, pl.ds(first, height), slice(None))

    def ring_of(self, line, at):
        return line * self.tensor + at + (line % 2) * (self.tensor - 1 - 2 * at)

    def pieces(self, group, tt, slot):
        r, depth = self.r, self.depth
        wide = self.box[group].shape[2]
        made = []
        for line in range(self.here.groups):
            ring = self.ring_of(line, tt)

            def rows_of(core):
                return r.stage.at[slot, pl.ds(pl.multiple_of((line * CORES + core) * depth, 16), depth), pl.ds(0, wide)]

            made.append(
                pltpu.make_async_copy(
                    rows_of(self.here.core), self.kept[group].at[self.own(group, ring, 0, depth)], r.kept_sem.at[slot, line]
                )
            )
            made.append(
                pltpu.make_async_remote_copy(
                    rows_of(1 - self.here.core), self.box[group].at[self.theirs(group, ring, 0, depth)],
                    r.over_send.at[group, ring], r.over_recv.at[group, ring], device_id=self.sibling, device_id_type=MESH,
                )
            )
        return made

    def emit(self, group, tt, slot):
        for piece in self.pieces(group, tt, slot):
            piece.start()

    def release(self, group, tt, slot):
        for k, piece in enumerate(self.pieces(group, tt, slot)):
            if k % 2:
                piece.wait_send()
            else:
                piece.wait()


    def rows_at(self, sub):
        half = self.depth // 2
        return half * sub, half

    def source(self, step, part):
        way = -1 if part else 1
        return lax.rem(self.here.ring + way * (self.hops - step) + self.here.chips, self.here.chips)

    def onward(self, group, step, part, sub):
        r = self.r
        first, height = self.rows_at(sub)
        place = self.groups.index(group) % 2
        return pltpu.make_async_remote_copy(
            self.kept[group].at[self.own(group, self.source(step, part), first, height)],
            self.box[group].at[self.taken(group, step, part, first, height)],
            r.ring_send.at[place, part, sub, step], r.ring_recv.at[group, part, sub, step],
            device_id=self.targets[part], device_id_type=MESH,
        )

    def here_sum(self, group, ring, first, height):
        value = self.kept[group][self.own(group, ring, first, height)].astype(F32)
        return value + self.box[group][self.theirs(group, ring, first, height)].astype(F32)

    def advance(self, group, step, part, sub, fresh=False):
        if not fresh:
            self.onward(group, step - 1, part, sub).wait_recv()
        first, height = self.rows_at(sub)
        value = self.here_sum(group, self.source(step, part), first, height)
        if not fresh:
            value = value + self.box[group][self.taken(group, step - 1, part, first, height)].astype(F32)
        self.kept[group][self.own(group, self.source(step, part), first, height)] = value.astype(BF16)
        self.onward(group, step, part, sub).start()

    def begin(self, group):
        @pl.loop(0, self.here.chips)
        def _(ring):
            pltpu.make_async_remote_copy(
                self.kept[group].at[self.own(group, ring, 0, self.depth)],
                self.box[group].at[self.theirs(group, ring, 0, self.depth)],
                self.r.over_send.at[group, ring], self.r.over_recv.at[group, ring], device_id=self.sibling, device_id_type=MESH,
            ).wait_recv()

        place = self.groups.index(group)
        if place >= 2:
            self.sends_done(self.groups[place - 2])
        for part in range(2):
            self.advance(group, 0, part, part, True)
        for part in range(2):
            self.advance(group, 1, part, 1 - part, True)
        if group == ATTN:
            self.small_across().wait_recv()
            self.small_advance(0, 0, True)
            self.small_advance(1, 1, True)

    def tick(self, group, n):
        step, leads = (n + 1) // 2 + 1, n % 2
        for part in range(2):
            self.advance(group, step, part, 1 - part if leads else part)
        if group == ATTN and not leads:
            self.small_advance(step, 0)
            if step > 1:
                self.small_advance(step, 1)

    def sends_done(self, group):
        for part in range(2):
            self.onward(group, 0, part, part).wait_send()
            for step in range(1, self.hops):
                for sub in range(2):
                    self.onward(group, step, part, sub).wait_send()

    def rest(self, group):
        self.end(group)
        for group in self.groups[-2:]:
            self.sends_done(group)

    def end(self, group):
        r, last = self.r, self.hops - 1
        for sub in range(2):
            first, height = self.rows_at(sub)
            value = self.here_sum(group, self.here.ring, first, height)
            for part in range(2):
                self.onward(group, last, part, sub).wait_recv()
                value = value + self.box[group][self.taken(group, last, part, first, height)].astype(F32)
            target = r.inner_out if group == INNER else r.total
            target[pl.ds(first, height), 0 : self.box[group].shape[2]] = value
        block = r.value_w.shape[1]
        if group == ATTN:
            r.pair_out[1] = r.total[:, 0:block]
            r.value_out[...] = r.total[:, block : 2 * block]
            r.pair_out[0] = r.total[:, 2 * block : 3 * block]
            r.out_out[...] = r.total[:, 3 * block : 4 * block].T
            at = self.small_at(self.here.ring)
            value = r.small[at] + r.small_theirs[at]
            for part in range(2):
                self.small_onward(last, part).wait_recv()
                value = value + r.small_taken[part, last]
            r.tiny_out[...] = value
        if group == CROSS:
            r.first_out[...] = r.total[:, 0:block]
            r.second_out[...] = r.total[:, block : 2 * block]
        if group == OUTER:
            r.outer_out[...] = r.total[...]


    def small_at(self, ring):
        line, at = self.here.at(ring)
        return at, line * CORES + self.here.core

    def small_across(self):
        r = self.r
        return pltpu.make_async_remote_copy(
            r.small, r.small_theirs, r.small_sem.at[0], r.small_sem.at[1], device_id=self.sibling, device_id_type=MESH
        )

    def small_onward(self, step, part):
        r = self.r
        return pltpu.make_async_remote_copy(
            r.small_sent.at[part, step], r.small_taken.at[part, step], r.tiny_send.at[part, step], r.tiny_recv.at[part, step],
            device_id=self.targets[part], device_id_type=MESH,
        )

    def small_advance(self, step, part, fresh=False):
        at = self.small_at(self.source(step, part))
        value = self.r.small[at] + self.r.small_theirs[at]
        if not fresh:
            self.small_onward(step - 1, part).wait_recv()
            value = value + self.r.small_taken[part, step - 1]
        self.r.small_sent[part, step] = value
        self.small_onward(step, part).start()

    def small_begin(self):
        r, depth = self.r, self.depth
        r.small[...] = jnp.zeros_like(r.small)
        kinds = r.onehot.shape[0] // self.dp
        heads_at = self.heads_at
        for tt in range(self.tensor):
            for d in range(self.dp):
                r.small[tt, d, 0:3, 0:depth] = r.gains_out[0:3, d * depth : (d + 1) * depth]
                r.small[tt, d, 3 : 3 + heads_at, 0:kinds] = r.bias_out[
                    8 * tt : 8 * tt + heads_at, d * kinds : (d + 1) * kinds
                ]
        self.small_across().start()


    def home_copy(self, k):
        r, here, tensor = self.r, self.here, self.tensor
        nrow, half, places = r.home_in.shape[0], tensor // 2, r.home_in.shape[2]
        place = here.pipe * (here.core * half + k % half) + (1 - here.pipe) * k
        which = here.pipe * (k // half) + (1 - here.pipe) * here.core
        owner = lax.div(here.t, nrow)
        source = r.rows_out.at[pl.ds(k * places, places)]
        slot = r.home_in.at[lax.rem(here.t, nrow), which]
        recv = r.home_recv.at[lax.rem(here.t, nrow), which]
        return (
            jnp.logical_and(place == here.t, owner == here.core),
            lambda: pltpu.make_async_copy(source, slot, recv),
            lambda: pltpu.make_async_remote_copy(
                source, slot, r.home_send.at[k], recv,
                device_id={"dp": here.group * CORES + owner, "tensor": place}, device_id_type=MESH,
            ),
        )

    def home(self):
        for k in range(self.tensor):
            stays, inside, away = self.home_copy(k)

            @pl.when(stays)
            def _():
                inside().start()

            @pl.when(jnp.logical_not(stays))
            def _():
                away().start()

    def home_done(self, unused=None):
        r = self.r
        places = r.home_in.shape[2]
        for i in range(r.home_in.shape[0]):
            for which in range(2):
                pltpu.make_async_copy(
                    r.rows_out.at[pl.ds(0, places)], r.home_in.at[i, which], r.home_recv.at[i, which]
                ).wait()
                r.home_out[i, which] = r.home_in[i, which].astype(F32)

    def close(self):
        r = self.r
        for k in range(self.tensor):
            stays, inside, away = self.home_copy(k)

            @pl.when(jnp.logical_not(stays))
            def _():
                away().wait_send()

        self.small_across().wait_send()

        for part in range(2):
            for step in range(part, self.hops):
                self.small_onward(step, part).wait_send()


def fits_fused(tensor, dp, depth, units, width):
    chips = tensor * dp // CORES
    return (
        depth % 32 == 0
        and 4 * depth <= width
        and chips <= 2 * tensor
        and chips == 2 * tensor == 8
        and units == width == 6 * LANES
    )


def fused_kernel(tensor, dp, heads_at, names, *refs):
    here = Place(tensor, dp)
    r = types.SimpleNamespace(**dict(zip(names, refs)))
    line = [
        {"dp": here.group * CORES + lax.rem(here.core + j, CORES), "tensor": lax.rem(here.t + k, tensor)}
        for j in range(CORES)
        for k in range(tensor)
        if j + k > 0
    ]
    across = [{"pipe": 1 - here.pipe, "dp": here.group * CORES + k} for k in range(CORES)]
    meet([here.neighbour(1), here.neighbour(-1)] + line + across)
    supply, drain = Rings(r, here, tensor, dp), Sums(r, here, tensor, dp)
    drain.heads_at = heads_at
    work(r, here, supply, drain, tensor, heads_at)


def fused(tensor, dp, rows, enc_lengths, dec_lengths, gains, bias, buckets, weights):
    nrow, two, places, width = rows.shape
    depth, block = weights[1].shape
    units = weights[5].shape[1]
    heads_at, _, kinds = bias.shape
    chips = tensor * dp // CORES
    wide = -(-max(depth, kinds // dp) // LANES) * LANES
    sems = pltpu.SemaphoreType.DMA
    scratch = arrays(tensor, heads_at, places, width, units, buckets.shape[1], kinds)
    scratch.update(
        lengths_in=held(8, LANES, dtype=jnp.int32),
        table_in=held(8, LANES, dtype=F32),
        lengths=held(CORES, 8, LANES, dtype=jnp.int32),
        tables=held(tensor, 8, LANES, dtype=F32),
        own_cross=held(chips, depth, 2 * block),
        own_outer=held(chips, depth, units),
        own_inner=held(chips, depth, units),
        total=held(depth, units, dtype=F32),
        rows_out=held(tensor * places, width),
        gains_out=held(8, width, dtype=F32),
        bias_out=held(8 * tensor, LANES, dtype=F32),
        home_in=held(nrow, two, places, width),
        small=held(tensor, dp, 8, wide, dtype=F32),
        small_theirs=held(tensor, dp, 8, wide, dtype=F32),
        small_sent=held(2, chips // 2, 8, wide, dtype=F32),
        small_taken=held(2, chips // 2, 8, wide, dtype=F32),
        block_send=sems((nrow,)), block_recv=sems((tensor,)), pass_send=sems((tensor,)), pass_recv=sems((tensor,)),
        local_sem=sems((3,)), small_send=sems((tensor,)), small_recv=sems((tensor,)), own_sem=sems((4,)),
        ring_send=sems((2, 2, 2, chips // 2)), ring_recv=sems((4, 2, 2, chips // 2)),
        over_send=sems((4, chips)), over_recv=sems((4, chips)), kept_sem=sems((2, dp // CORES)),
        small_sem=sems((2,)), tiny_send=sems((2, chips // 2)), tiny_recv=sems((2, chips // 2)),
        home_send=sems((tensor,)), home_recv=sems((nrow, two)),
        free_sem=pltpu.SemaphoreType.REGULAR((3,)),
    )
    inputs = ["rows", "enc_lengths", "dec_lengths", "gains", "bias_w", "buckets"]
    inputs += ["query_key_w", "value_w", "out_w", "first_w", "second_w", "inner_w", "outer_w"]
    outputs = dict(
        home_out=rows.shape, tiny_out=(8, wide), pair_out=(2, depth, block), value_out=(depth, block),
        out_out=(block, depth), first_out=(depth, block), second_out=(depth, block), inner_out=(depth, units),
        outer_out=(depth, units),
    )
    return pl.pallas_call(
        functools.partial(fused_kernel, tensor, dp, heads_at, inputs + list(outputs) + list(scratch)),
        out_shape=tuple(jax.ShapeDtypeStruct(shape, F32) for shape in outputs.values()),
        in_specs=[ANY] + [VMEM] * 12,
        out_specs=(VMEM,) * len(outputs),
        scratch_shapes=list(scratch.values()),
        compiler_params=pltpu.CompilerParams(collective_id=3, has_side_effects=True, vmem_limit_bytes=VMEM_LIMIT),
        name="fused",
    )(rows, enc_lengths, dec_lengths, gains, bias, buckets, *weights)


def pad_to(array, *shape):
    return jnp.pad(array, [(0, full - have) for full, have in zip(shape, array.shape)])


def shards(
    tensor, dp, section_rows, enc_lengths, dec_lengths, enc_buckets, dec_buckets, norm_gains, rel_bias,
    query_key_w, value_w, attn_out_w, cross_first, cross_second, ff_in, ff_out,
):
    depth = value_w.shape[1]
    width = section_rows.shape[-1]
    on_encoder = lax.axis_index("pipe") == 0
    ranges = -(-enc_buckets.shape[0] // LANES) * LANES
    dec_all = jnp.concatenate([jnp.zeros((dec_buckets.shape[0] - 1,), jnp.int32), dec_buckets])
    bucket_row = jnp.where(on_encoder, pad_to(enc_buckets, ranges), pad_to(dec_all, ranges))[None]
    gains = norm_gains.transpose(1, 0, 2)
    bias = rel_bias.transpose(2, 0, 1)
    weights = (query_key_w[0], value_w[0], attn_out_w[0], cross_first[0], cross_second[0], ff_in[0], ff_out[0].T)
    run = fused if fits_fused(tensor, dp, depth, ff_in.shape[2], width) else in_three
    home, tiny, *grads, outer = run(
        tensor, dp, section_rows[0], enc_lengths, dec_lengths, gains, bias, bucket_row, weights
    )
    heads_at, kinds = bias.shape[0], bias.shape[2] // dp
    return (
        (home[None], tiny[:3, :depth][None], tiny[3 : 3 + heads_at, :kinds].T[None])
        + tuple(grad[None] for grad in grads)
        + (outer.T[None],)
    )


def in_three(tensor, dp, section_rows, enc_lengths, dec_lengths, gains, bias, buckets, weights):
    query_key, value, out, first, second, inner, outer = weights
    nrow, _, _, width = section_rows.shape
    heads_at, _, kinds = bias.shape
    lengths = pad_to(jnp.concatenate([enc_lengths, dec_lengths], axis=0), 8, LANES)
    table = pad_to(bias[:, 0], 8, LANES)
    depth, block = value.shape
    units = inner.shape[1]
    pack = jnp.concatenate([query_key[1], value, query_key[0], out.T, first, second, inner, outer], axis=1)
    rows, gathered, lengths, tables = gather(tensor, dp, section_rows, pack, lengths, table)
    grads, finished, gain_grads, bias = blocks(
        tensor, dp, heads_at, kinds, rows, gathered.reshape(tensor, width, -1), gains, lengths, tables, buckets
    )
    held_kinds = kinds // dp
    wide = -(-max(depth, held_kinds) // LANES) * LANES
    gain_part = pad_to(gain_grads[:3].reshape(3, dp, depth).transpose(1, 0, 2), dp, 3, wide)
    bias_part = bias.reshape(tensor, 8, LANES)[:, :heads_at, :kinds].reshape(tensor, heads_at, dp, held_kinds)
    bias_part = pad_to(bias_part.transpose(0, 2, 1, 3), tensor, dp, 5, wide)
    small = jnp.concatenate([jnp.broadcast_to(gain_part[None], (tensor,) + gain_part.shape), bias_part], axis=2)
    total, tiny, home = scatter(
        tensor, dp, grads.reshape(tensor, dp, depth, -1), small, finished.reshape(tensor, -1, width), nrow
    )
    key, value, query, out, first, second = [total[:, k * block : (k + 1) * block] for k in range(6)]
    inner, outer = total[:, 6 * block : 6 * block + units], total[:, 6 * block + units :]
    return (
        home.astype(F32), tiny,
        jnp.stack([query, key]), value, out.T, first, second, inner, outer,
    )


def solution(mesh):
    sizes = dict(mesh.shape)
    return jax.shard_map(
        functools.partial(shards, sizes["tensor"], sizes["dp"]),
        mesh=mesh,
        in_specs=(
            P("pipe", "dp", None, "tensor", None),
            P("dp", None),
            P("dp", None),
            P(),
            P(),
            P("pipe", None, None),
            P("pipe", None, "tensor"),
            P("pipe", None, "dp", "tensor"),
            P("pipe", "dp", "tensor"),
            P("pipe", "tensor", "dp"),
            P("pipe", "dp", "tensor"),
            P("pipe", "dp", "tensor"),
            P("pipe", "dp", "tensor"),
            P("pipe", "tensor", "dp"),
        ),
        out_specs=(
            P("pipe", "dp", None, "tensor", None),
            P("pipe", None, "dp"),
            P("pipe", "dp", "tensor"),
            P("pipe", None, "dp", "tensor"),
            P("pipe", "dp", "tensor"),
            P("pipe", "tensor", "dp"),
            P("pipe", "dp", "tensor"),
            P("pipe", "dp", "tensor"),
            P("pipe", "dp", "tensor"),
            P("pipe", "tensor", "dp"),
        ),
        check_vma=False,
    )
```

```python
import functools
import types

import jax
import jax.numpy as jnp
from jax import lax
from jax.experimental import pallas as pl
from jax.experimental.pallas import tpu as pltpu
from jax.sharding import PartitionSpec as P

MESH = pl.DeviceIdType.MESH
F32 = jnp.float32
BF16 = jnp.bfloat16
EPSILON = 1e-06
NEGATIVE = -1000000000.0
HEAD_DIM = 64
CORES = 2
LANES = 128
VMEM_LIMIT = 62 << 20
ANY = pl.BlockSpec(memory_space=pl.ANY)
VMEM = pl.BlockSpec(memory_space=pltpu.VMEM)


def nn(a, b):
    return lax.dot_general(a, b, (((1,), (0,)), ((), ())), preferred_element_type=F32)


def nt(a, b):
    return lax.dot_general(a, b, (((1,), (1,)), ((), ())), preferred_element_type=F32)


def tn(a, b):
    return lax.dot_general(a, b, (((0,), (0,)), ((), ())), preferred_element_type=F32)


class Place:
    def __init__(self, tensor, dp):
        self.tensor = tensor
        self.groups = dp // CORES
        self.chips = tensor * self.groups
        self.pipe = lax.axis_index("pipe")
        self.d = lax.axis_index("dp")
        self.t = lax.axis_index("tensor")
        self.core = lax.rem(self.d, CORES)
        self.group = self.d // CORES
        odd = lax.rem(self.group, 2)
        self.ring = self.group * tensor + self.t + odd * (tensor - 1 - 2 * self.t)

    def at(self, ring):
        group = ring // self.tensor
        along = lax.rem(ring, self.tensor)
        odd = lax.rem(group, 2)
        return group, along + odd * (self.tensor - 1 - 2 * along)

    def neighbour(self, step):
        group, t = self.at(lax.rem(self.ring + step + self.chips, self.chips))
        return {"dp": group * CORES + self.core, "tensor": t}

    def sibling(self):
        return {"dp": self.group * CORES + 1 - self.core}


def meet(devices):
    barrier = pltpu.get_barrier_semaphore()
    for device in devices:
        pl.semaphore_signal(barrier, inc=1, device_id=device, device_id_type=MESH)
    pl.semaphore_wait(barrier, len(devices))


def halves(rows, columns):
    if rows % 32 == 0:
        return [(pl.ds(k * (rows // 2), rows // 2), pl.ds(0, columns)) for k in range(2)]
    cut = columns // LANES // 2 * LANES
    return [(pl.ds(0, rows), pl.ds(0, cut)), (pl.ds(0, rows), pl.ds(cut, columns - cut))]


def gather_kernel(
    tensor, dp, rows_ref, pack_ref, length_ref, table_ref, x_ref, w_ref, lengths_ref, tables_ref,
    local_sem, block_send, block_recv, pass_send, pass_recv, small_send, small_recv,
    ring_send, ring_recv, core_send, core_recv,
):
    here = Place(tensor, dp)
    c, t, chips = here.core, here.t, here.chips
    nrow = rows_ref.shape[0]
    sibling = here.sibling()
    to_right, to_left = here.neighbour(1), here.neighbour(-1)
    others = [{"tensor": lax.rem(t + k, tensor)} for k in range(1, tensor)]
    meet([to_right, to_left, sibling] + others)

    lengths = pltpu.make_async_remote_copy(
        length_ref, lengths_ref.at[c], small_send.at[0], small_recv.at[0], device_id=sibling, device_id_type=MESH
    )
    lengths.start()
    own_lengths = pltpu.make_async_copy(length_ref, lengths_ref.at[c], local_sem.at[0])
    own_lengths.start()
    own_table = pltpu.make_async_copy(table_ref, tables_ref.at[t], local_sem.at[1])
    own_table.start()
    tables = []
    for k in range(1, tensor):
        tables.append(
            pltpu.make_async_remote_copy(
                table_ref, tables_ref.at[t], small_send.at[k], small_recv.at[k], device_id=others[k - 1], device_id_type=MESH
            )
        )
        tables[-1].start()

    def to_chip(i):
        return pltpu.make_async_remote_copy(
            rows_ref.at[i], x_ref.at[:, t], block_send.at[i], block_recv.at[t],
            device_id={"tensor": nrow * c + i}, device_id_type=MESH,
        )

    def kept(i):
        return pltpu.make_async_copy(rows_ref.at[i], x_ref.at[:, t], local_sem.at[2])

    def kept_pass(i):
        return pltpu.make_async_remote_copy(
            rows_ref.at[i], x_ref.at[:, t], pass_send.at[t], pass_recv.at[t], device_id=sibling, device_id_type=MESH
        )

    def passed(s):
        return pltpu.make_async_remote_copy(
            x_ref.at[:, s], x_ref.at[:, s], pass_send.at[s], pass_recv.at[s], device_id=sibling, device_id_type=MESH
        )

    for i in range(nrow):
        mine = nrow * c + i == t

        @pl.when(mine)
        def _():
            kept(i).start()
            kept_pass(i).start()

        @pl.when(jnp.logical_not(mine))
        def _():
            to_chip(i).start()

    parts = halves(*pack_ref.shape)
    own_pack = pltpu.make_async_copy(pack_ref, w_ref.at[t, here.d], local_sem.at[3])
    own_pack.start()

    def shard(ring, part):
        group, at = here.at(ring)
        return w_ref.at[at, group * CORES + c, parts[part][0], parts[part][1]]

    def source(step, part):
        return lax.rem(here.ring + (1 if part else -1) * step + chips, chips)

    def onward(step, part, first=False):
        slot = shard(source(step, part), part)
        return pltpu.make_async_remote_copy(
            pack_ref.at[parts[part][0], parts[part][1]] if first else slot, slot,
            ring_send.at[part, step], ring_recv.at[part, step],
            device_id=to_left if part else to_right, device_id_type=MESH,
        )

    def across(step, part, first=False):
        slot = shard(source(step, part), part)
        return pltpu.make_async_remote_copy(
            pack_ref.at[parts[part][0], parts[part][1]] if first else slot, slot,
            core_send.at[part, step], core_recv.at[part, step], device_id=sibling, device_id_type=MESH,
        )

    for part in range(2):
        onward(0, part, True).start()
        across(0, part, True).start()

    takes = t // nrow == c
    for s in range(tensor):

        @pl.when(jnp.logical_and(takes, s != t))
        def _():
            pltpu.make_async_remote_copy(
                rows_ref.at[0], x_ref.at[:, s], block_send.at[0], block_recv.at[s], device_id=sibling, device_id_type=MESH
            ).wait_recv()
            passed(s).start()

    @pl.loop(1, chips)
    def _(step):
        for part in range(2):
            onward(step - 1, part).wait_recv()

            @pl.when(step < chips - 1)
            def _():
                onward(step, part).start()

            across(step, part).start()

    @pl.loop(0, chips)
    def _(step):
        for part in range(2):

            @pl.when(step < chips - 1)
            def _():
                onward(step, part).wait_send()

            across(step, part).wait_send()
            across(step, part).wait_recv()

    for i in range(nrow):
        mine = nrow * c + i == t

        @pl.when(mine)
        def _():
            kept(i).wait()
            kept_pass(i).wait_send()

        @pl.when(jnp.logical_not(mine))
        def _():
            to_chip(i).wait_send()

    for s in range(tensor):

        @pl.when(jnp.logical_and(takes, s != t))
        def _():
            passed(s).wait_send()

        @pl.when(jnp.logical_not(takes))
        def _():
            passed(s).wait_recv()

    lengths.wait()
    own_lengths.wait()
    own_table.wait()
    own_pack.wait()
    for table in tables:
        table.wait()


def gather(tensor, dp, rows, pack, lengths, table):
    chips = tensor * dp // CORES
    nrow, two, places, width = rows.shape
    sems = pltpu.SemaphoreType.DMA
    return pl.pallas_call(
        functools.partial(gather_kernel, tensor, dp),
        out_shape=(
            jax.ShapeDtypeStruct((two, tensor, places, width), rows.dtype),
            jax.ShapeDtypeStruct((tensor, dp) + pack.shape, pack.dtype),
            jax.ShapeDtypeStruct((CORES,) + lengths.shape, lengths.dtype),
            jax.ShapeDtypeStruct((tensor,) + table.shape, table.dtype),
        ),
        in_specs=[ANY] * 4,
        out_specs=(ANY,) * 4,
        scratch_shapes=[
            sems((4,)), sems((nrow,)), sems((tensor,)), sems((tensor,)), sems((tensor,)), sems((tensor,)), sems((tensor,)),
            sems((2, chips)), sems((2, chips)), sems((2, chips)), sems((2, chips)),
        ],
        compiler_params=pltpu.CompilerParams(collective_id=0, has_side_effects=True),
        name="gather",
    )(rows, pack, lengths, table)


def scatter_kernel(
    tensor, dp, grads_ref, small_ref, rows_ref, out_ref, small_out, rows_out,
    own, theirs, taken, small_own, small_theirs, small_taken, total,
    own_sem, core_send, core_recv, ring_send, ring_recv,
    sown_sem, score_send, score_recv, sring_send, sring_recv, block_send, block_recv, local_sem,
):
    here = Place(tensor, dp)
    c, t, chips = here.core, here.t, here.chips
    nrow = rows_out.shape[0]
    sibling = here.sibling()
    to_right, to_left = here.neighbour(1), here.neighbour(-1)
    line = [
        {"dp": here.group * CORES + lax.rem(c + j, CORES), "tensor": lax.rem(t + k, tensor)}
        for j in range(CORES)
        for k in range(tensor)
        if j + k > 0
    ]
    meet([to_right, to_left] + line)

    half = tensor // 2
    owner = t // nrow

    def block(k):
        place = here.pipe * (c * half + k % half) + (1 - here.pipe) * k
        which = here.pipe * (k // half) + (1 - here.pipe) * c
        return place, which

    def home(k):
        place, which = block(k)
        slot = rows_out.at[lax.rem(t, nrow), which]
        recv = block_recv.at[lax.rem(t, nrow), which]
        return (
            jnp.logical_and(place == t, owner == c),
            lambda: pltpu.make_async_copy(rows_ref.at[k], slot, recv),
            lambda: pltpu.make_async_remote_copy(
                rows_ref.at[k], slot, block_send.at[k], recv,
                device_id={"dp": here.group * CORES + owner, "tensor": place}, device_id_type=MESH,
            ),
        )

    for k in range(tensor):
        stays, inside, away = home(k)

        @pl.when(stays)
        def _():
            inside().start()

        @pl.when(jnp.logical_not(stays))
        def _():
            away().start()

    def across(ring):
        group, at = here.at(ring)
        return (
            pltpu.make_async_remote_copy(
                grads_ref.at[at, group * CORES + 1 - c], theirs.at[ring], core_send.at[ring], core_recv.at[ring],
                device_id=sibling, device_id_type=MESH,
            ),
            pltpu.make_async_remote_copy(
                small_ref.at[at, group * CORES + 1 - c], small_theirs.at[ring], score_send.at[ring], score_recv.at[ring],
                device_id=sibling, device_id_type=MESH,
            ),
        )

    def fetch(ring):
        group, at = here.at(ring)
        return (
            pltpu.make_async_copy(grads_ref.at[at, group * CORES + c], own.at[ring], own_sem.at[ring]),
            pltpu.make_async_copy(small_ref.at[at, group * CORES + c], small_own.at[ring], sown_sem.at[ring]),
        )

    def behind(step):
        return lax.rem(here.ring - step + chips, chips)

    def order(k):
        off = (2 * lax.rem(k, 2) - 1) * (k // 2 + 1) * (1 - k // (chips - 1))
        return lax.rem(here.ring + chips + off, chips)

    @pl.loop(0, chips)
    def _(k):
        for copy in across(order(k)) + fetch(order(k)):
            copy.start()

    rows, columns = out_ref.shape
    parts = halves(rows, columns)

    def add(ring, part, step, last):
        height = parts[part][0].size
        piece = 16 if height % 16 == 0 else height

        @pl.loop(0, height // piece)
        def _(k):
            at = pl.ds(pl.multiple_of(parts[part][0].start + k * piece, 8), piece)
            where = (at, parts[part][1])
            value = own[(ring,) + where].astype(F32) + theirs[(ring,) + where].astype(F32)
            if step is not None:
                value = value + taken[(step,) + where].astype(F32)
            if last:
                total[where] = value
            else:
                own[(ring,) + where] = value.astype(BF16)

    def onward(ring, step, part):
        where = (parts[part][0], parts[part][1])
        return pltpu.make_async_remote_copy(
            own.at[(ring,) + where], taken.at[(step,) + where], ring_send.at[part, step], ring_recv.at[part, step],
            device_id=to_left if part else to_right, device_id_type=MESH,
        )

    def small_onward(ring, step):
        return pltpu.make_async_remote_copy(
            small_own.at[ring], small_taken.at[step], sring_send.at[step], sring_recv.at[step],
            device_id=to_right, device_id_type=MESH,
        )

    def ready(ring):
        for copy in across(ring):
            copy.wait_recv()
        for copy in fetch(ring):
            copy.wait()

    def ahead(step):
        return lax.rem(here.ring + step, chips)

    half_chips = chips // 2

    @pl.loop(0, chips - 1)
    def _(step):
        right, left = behind(step + 1), ahead(step + 1)

        @pl.when(step < half_chips)
        def _():
            ready(right)

        @pl.when(step < chips - 1 - half_chips)
        def _():
            ready(left)

        @pl.when(step == 0)
        def _():
            add(right, 0, None, False)
            add(left, 1, None, False)
            small_own[right] = small_own[right] + small_theirs[right]

        @pl.when(step > 0)
        def _():
            onward(right, step - 1, 0).wait_recv()
            add(right, 0, step - 1, False)
            onward(right, step, 0).start()
            onward(left, step - 1, 1).wait_recv()
            add(left, 1, step - 1, False)
            onward(left, step, 1).start()
            small_onward(right, step - 1).wait_recv()
            small_own[right] = small_own[right] + small_theirs[right] + small_taken[step - 1]
            small_onward(right, step).start()

        @pl.when(step == 0)
        def _():
            onward(right, 0, 0).start()
            onward(left, 0, 1).start()
            small_onward(right, 0).start()

    ready(here.ring)
    for part in range(2):
        onward(here.ring, chips - 2, part).wait_recv()
        add(here.ring, part, chips - 2, True)
    small_onward(here.ring, chips - 2).wait_recv()
    small_out[...] = small_own[here.ring] + small_theirs[here.ring] + small_taken[chips - 2]
    finish = pltpu.make_async_copy(total, out_ref, local_sem.at[0])
    finish.start()

    @pl.loop(0, chips)
    def _(step):
        @pl.when(step < chips - 1)
        def _():
            onward(behind(step + 1), step, 0).wait_send()
            onward(ahead(step + 1), step, 1).wait_send()
            small_onward(behind(step + 1), step).wait_send()

        for copy in across(step):
            copy.wait_send()

    for k in range(tensor):
        stays, inside, away = home(k)

        @pl.when(jnp.logical_not(stays))
        def _():
            away().wait_send()

    for i in range(nrow):
        for which in range(2):
            pltpu.make_async_copy(rows_ref.at[0], rows_out.at[i, which], block_recv.at[i, which]).wait()
    finish.wait()


def scatter(tensor, dp, grads, small, rows, nrow):
    chips = tensor * dp // CORES
    shard = grads.shape[2:]
    tiny = small.shape[2:]
    sems = pltpu.SemaphoreType.DMA
    return pl.pallas_call(
        functools.partial(scatter_kernel, tensor, dp),
        out_shape=(
            jax.ShapeDtypeStruct(shard, F32),
            jax.ShapeDtypeStruct(tiny, F32),
            jax.ShapeDtypeStruct((nrow, 2) + rows.shape[1:], rows.dtype),
        ),
        in_specs=[ANY] * 3,
        out_specs=(ANY, VMEM, ANY),
        scratch_shapes=[
            pltpu.VMEM((chips,) + shard, BF16),
            pltpu.VMEM((chips,) + shard, BF16),
            pltpu.VMEM((chips - 1,) + shard, BF16),
            pltpu.VMEM((chips,) + tiny, F32),
            pltpu.VMEM((chips,) + tiny, F32),
            pltpu.VMEM((chips - 1,) + tiny, F32),
            pltpu.VMEM(shard, F32),
            sems((chips,)), sems((chips,)), sems((chips,)), sems((2, chips)), sems((2, chips)),
            sems((chips,)), sems((chips,)), sems((chips,)), sems((chips,)), sems((chips,)),
            sems((tensor,)), sems((nrow, 2)), sems((1,)),
        ],
        compiler_params=pltpu.CompilerParams(collective_id=1, has_side_effects=True, vmem_limit_bytes=VMEM_LIMIT),
        name="scatter",
    )(grads, small, rows)


KEY, VALUE, QUERY, OUT, FIRST, SECOND = range(6)
ATTN, CROSS, INNER, OUTER = range(4)
SEGS_HELD = 6


def rms(value):
    return lax.rsqrt(jnp.mean(value * value, axis=-1, keepdims=True) + EPSILON)


def in_rows(count, body, piece=32):
    @pl.loop(0, count // piece)
    def _(k):
        body(pl.ds(pl.multiple_of(k * piece, piece), piece))


def columns_of(count, body, piece=768):
    piece = min(piece, count)

    @pl.loop(0, count // piece)
    def _(k):
        body(pl.ds(pl.multiple_of(k * piece, piece), piece))


def normalize(source, gain, target, count):
    def body(at):
        value = source[at, :].astype(F32)
        target[at, :] = (value * rms(value) * gain).astype(BF16)

    in_rows(count, body)


def normalize_back(source, gain, incoming, total, gain_parts, count, fresh):
    gain_parts[...] = jnp.zeros_like(gain_parts)

    def body(at):
        value, back = source[at, :].astype(F32), incoming[at, :]
        scale = rms(value)
        unit = value * scale
        gain_parts[...] += jnp.sum((back * unit).reshape(-1, 8, back.shape[-1]), axis=0)
        back = back * gain
        back = scale * (back - unit * jnp.mean(back * unit, axis=-1, keepdims=True))
        total[at, :] = back if fresh else total[at, :] + back

    in_rows(count, body)


def project(left, weight, target, count):
    def body(at):
        target[0:count, at] = nn(left[0:count, :], weight[:, at]).astype(target.dtype)

    columns_of(weight.shape[1], body)


def project_back(left, weight, total, count, fresh):
    def body(at):
        value = nt(left[0:count, :], weight[at, :])
        total[0:count, at] = value if fresh else total[0:count, at] + value

    columns_of(weight.shape[0], body)


def to_bf16(source, target, rows):
    def body(at):
        target[at, :] = source[at, :].astype(BF16)

    in_rows(rows, body)


def turn(left, turned, rows):
    def body(at):
        turned[at, 0:rows] = left[0:rows, at].T

    columns_of(left.shape[1], body, LANES)


def lane_half(shape, part):
    return lax.broadcasted_iota(jnp.int32, shape, 1) // HEAD_DIM == part


def attend(keys, values, queries, mixture, probs, rows, span, pairs, mask, bias, after):
    @pl.loop(0, pairs)
    def _(pair):
        lanes = pl.ds(pl.multiple_of(pair * LANES, LANES), LANES)
        key, query = keys[0:span, lanes], queries[0:rows, lanes]
        value_t = values[0:span, lanes].T
        mixed = []
        for part in range(2):
            one = jnp.where(lane_half(query.shape, part), query, jnp.zeros_like(query))
            scores = nt(key, one) + mask[0:span, 0:rows]
            if bias is not None:
                scores = scores + bias(2 * pair + part)
            scores = jnp.exp(scores - jnp.max(scores, axis=0, keepdims=True))
            scores = (scores * (1.0 / jnp.sum(scores, axis=0, keepdims=True))).astype(BF16)
            probs[2 * pair + part, 0:span, 0:rows] = scores
            mixed.append(nn(value_t[part * HEAD_DIM : (part + 1) * HEAD_DIM, :], scores))
        mixture[0:rows, lanes] = jnp.concatenate(mixed, axis=0).T.astype(BF16)
        after(pair)


def attend_back(keys, values, queries, back, probs, rows, span, pairs, each, before, after):
    @pl.loop(0, pairs)
    def _(pair):
        before(pair)
        lanes = pl.ds(pl.multiple_of(pair * LANES, LANES), LANES)
        key, value = keys[0:span, lanes], values[0:span, lanes]
        query, given = queries[0:rows, lanes], back[0:rows, lanes]
        key_t = key.T
        d_key, d_value, d_query = None, None, []
        for part in range(2):
            side = lane_half(query.shape, part)
            query_one = jnp.where(side, query, jnp.zeros_like(query))
            given_one = jnp.where(side, given, jnp.zeros_like(given))
            prob = probs[2 * pair + part, 0:span, 0:rows]
            wide = prob.astype(F32)
            d_prob = nt(value, given_one)
            d_score = (wide * (d_prob - jnp.sum(wide * d_prob, axis=0, keepdims=True))).astype(BF16)
            if each is not None:
                each(2 * pair + part, d_score)
            of_key, of_value = nn(d_score, query_one), nn(prob, given_one)
            d_key = of_key if d_key is None else d_key + of_key
            d_value = of_value if d_value is None else d_value + of_value
            d_query.append(nn(key_t[part * HEAD_DIM : (part + 1) * HEAD_DIM, :], d_score))
        keys[0:span, lanes] = d_key.astype(BF16)
        values[0:span, lanes] = d_value.astype(BF16)
        queries[0:rows, lanes] = jnp.concatenate(d_query, axis=0).T.astype(BF16)
        after(pair)


def segments(lengths_row, shape, axis, first):
    lane = lax.broadcasted_iota(jnp.int32, lengths_row.shape, 1)
    places = lax.broadcasted_iota(jnp.int32, shape, axis) + first
    ids = jnp.zeros(shape, jnp.int32)
    for c in range(SEGS_HELD):
        bound = jnp.sum(jnp.where(lane <= c, lengths_row, 0), axis=1, keepdims=True)
        ids = ids + (places >= bound).astype(jnp.int32)
    return ids


def masked(allowed):
    return jnp.where(allowed, 0.0, NEGATIVE).astype(F32)


def nothing(*unused, **named):
    pass


def work(r, here, supply, drain, tensor, heads_at):
    c, t = here.core, here.t
    width = r.hidden.shape[1]
    tall = r.hidden.shape[0]
    block = width // tensor
    half_width = width // 2
    units = r.inner.shape[2]
    places = r.x.shape[2]
    sibling = here.sibling()
    across = [{"pipe": 1 - here.pipe, "dp": here.group * CORES + k} for k in range(CORES)]
    nrow = tensor // CORES
    rows_e, span_e, rows_d, span_d = tall // 2, tall, tall // 4, tall // 2
    pairs_here = half_width // LANES
    near_lanes = pl.ds(pl.multiple_of(c * half_width, half_width), half_width)
    far_lanes = pl.ds(pl.multiple_of((1 - c) * half_width, half_width), half_width)
    lane_halves = [slice(k * half_width, (k + 1) * half_width) for k in range(CORES)]

    def move(source, target, sends, recvs, device):
        return pltpu.make_async_remote_copy(
            source, target, r.send_sem.at[sends], r.recv_sem.at[recvs], device_id=device, device_id_type=MESH
        )

    def lengths_row(first):
        return r.lengths[t // nrow, pl.ds(first + lax.rem(t, nrow), 1), :]

    def pair_lanes(pair):
        return pl.ds(pair * LANES if isinstance(pair, int) else pl.multiple_of(pair * LANES, LANES), LANES)

    def vector_row(head):
        return (head // heads_at) * 8 + lax.rem(head, heads_at)

    def bias_vectors():
        buckets = lax.broadcasted_iota(jnp.int32, r.onehot.shape, 0) == r.buckets[0:1, :]
        r.onehot[...] = buckets.astype(F32)
        for tt in range(tensor):
            r.vectors[pl.ds(8 * tt, 8), :] = lax.dot_general(
                r.tables[tt][:, 0 : r.onehot.shape[0]], r.onehot[...], (((1,), (0,)), ((), ())),
                precision=lax.Precision.HIGHEST, preferred_element_type=F32,
            )

    def rows_ready(span, rows, first_block):
        @pl.loop(0, span // places)
        def _(k):
            value = r.x[k // tensor, lax.rem(k, tensor)].astype(F32)
            at = pl.ds(pl.multiple_of(k * places, places), places)
            r.hidden[at, :] = (value * rms(value) * r.gains[0]).astype(BF16)

        for k in range(rows // places):
            r.own_x[k * places : (k + 1) * places, :] = r.x[first_block // tensor, lax.rem(first_block, tensor) + k]

    def untangle(source, first, count):
        def body(at):
            for tt in range(tensor):
                for k in range(count):
                    r.square[first + k, at, tt * block : (tt + 1) * block] = source[tt, at, k * block : (k + 1) * block]

        in_rows(width, body, 128)

    def self_forward(span, rows, first_row, group):
        def bias(head):
            pieces = []
            for j in range(span // LANES):
                start = pl.multiple_of(first_row + span - LANES - j * LANES, LANES)
                row = r.vectors[pl.ds(vector_row(head), 1), pl.ds(start, rows + LANES)]
                wide = jnp.broadcast_to(row, (LANES, rows + LANES))
                pieces.append(pltpu.roll(wide, rows + 1, 1, stride=1, stride_axis=0)[:, 0:rows])
            return jnp.concatenate(pieces, axis=0)

        untangle(r.raw_a, KEY, 2)
        untangle(r.raw_a.at[:, :, pl.ds(2 * block, 2 * block)], QUERY, 2)
        project(r.hidden, r.square.at[KEY], r.keys, span)
        supply.pump()
        project(r.hidden, r.square.at[VALUE], r.values, span)
        project(r.hidden.at[pl.ds(first_row, rows)], r.square.at[QUERY], r.queries, rows)
        supply.pump()
        after = at_each(range(width // LANES), supply.pump)

        attend(r.keys, r.values, r.queries, r.mixture, r.probs, rows, span, width // LANES, r.mask, bias, after)
        project_back(r.mixture, r.square.at[OUT], r.resid_mid, rows, True)

        def add(at):
            r.resid_mid[at, :] += r.own_x[at, :].astype(F32)

        in_rows(rows, add)
        supply.pump(until=group)
        supply.finish(group)

    def at_each(places, do):
        def hook(n):
            for place in places:

                @pl.when(n == place)
                def _():
                    do()

        return hook

    def feed_forward(rows, hook=nothing):
        @pl.loop(0, tensor)
        def _(tt):
            def body(at):
                value = nn(r.second[0:rows, :], r.inner[tt, :, at])
                cdf = 0.5 * (1.0 + lax.erf(value * 0.7071067811865476))
                r.ff[tt, 0:rows, at] = (value * cdf).astype(BF16)
                slope = cdf + value * jnp.exp(-0.5 * value * value) * 0.3989422804014327
                r.ff[tensor + tt, 0:rows, at] = slope.astype(BF16)

            columns_of(units, body)
            hook(tt)

    def feed_out(target, rows, hook=nothing):
        @pl.loop(0, tensor)
        def _(tt):
            def body(at):
                target[0:rows, at] += nt(r.ff[tt, 0:rows, :], r.outer[tt, at, :])

            columns_of(width, body)
            hook(tt)

    def feed_back(rows, ready, hook=nothing):
        r.summed[0:rows, :] = jnp.zeros((rows, width), F32)

        @pl.loop(0, tensor)
        def _(tt):
            def body(at):
                if ready:
                    value = r.ff[tensor + tt, rows : 2 * rows, at].astype(F32)
                else:
                    value = nn(r.d_branch[0:rows, :], r.outer[tt, :, at])
                r.ff[tensor + tt, 0:rows, at] = (value * r.ff[tensor + tt, 0:rows, at].astype(F32)).astype(BF16)

            columns_of(units, body)

            def back(at):
                r.summed[0:rows, at] += nt(r.ff[tensor + tt, 0:rows, :], r.inner[tt, at, :])

            columns_of(width, back)
            hook(tt)

    def feed_grads(rows, turned, first, which, hook=nothing):
        @pl.loop(0, tensor)
        def _(tt):
            slot = lax.rem(tt, 2)

            @pl.when(tt >= 2)
            def _():
                drain.release(which, tt - 2, slot)

            def body(at):
                r.stage[slot, :, at] = nn(turned[:, 0:rows], r.ff[first + tt, 0:rows, at]).astype(BF16)

            columns_of(units, body)
            drain.emit(which, tt, slot)
            hook(tt)

        for tt in range(tensor - 2, tensor):
            drain.release(which, tt, tt % 2)

    def square_grads(rows, which, products, hook):
        for k in range(tensor // 2):
            for j, (turned, right) in enumerate(products):

                def body(at):
                    value = nn(turned[at, 0:rows], right[0:rows, 2 * k * block : 2 * (k + 1) * block]).astype(BF16)
                    for slot in range(2):
                        r.stage[slot, at, j * block : (j + 1) * block] = value[:, slot * block : (slot + 1) * block]

                in_rows(width, body, 256)
            for slot in range(2):
                drain.emit(which, 2 * k + slot, slot)
            hook(k)
            for slot in range(2):
                drain.release(which, 2 * k + slot, slot)

    def gain_done(which):
        r.gains_out[which : which + 1, :] = jnp.sum(r.gain_parts[...], axis=0, keepdims=True)

    def self_backward(span, rows, first_row, steps, send_rows):
        mirror = (
            lax.broadcasted_iota(jnp.int32, (LANES, LANES), 0) + lax.broadcasted_iota(jnp.int32, (LANES, LANES), 1)
            == LANES - 1
        ).astype(BF16)
        to_bf16(r.d_resid, r.branch, rows)
        project(r.branch, r.square.at[OUT], r.d_branch, rows)
        r.diagonals[...] = jnp.zeros_like(r.diagonals)

        def each(head, d_score):
            for j in range(span // LANES):
                start = pl.multiple_of(first_row + span - LANES - j * LANES, LANES)
                piece = nn(mirror, d_score[j * LANES : (j + 1) * LANES, :])
                piece = jnp.concatenate([piece, jnp.zeros((LANES, LANES), F32)], axis=1)
                piece = pltpu.roll(piece, 0, 1, stride=1, stride_axis=0)
                at = (pl.ds(vector_row(head), 1), pl.ds(start, rows + LANES))
                r.diagonals[at] += jnp.sum(piece, axis=0, keepdims=True)

        pairs = width // LANES
        attend_back(
            r.keys, r.values, r.queries, r.d_branch, r.probs, rows, span, pairs, each, nothing,
            at_each(range(pairs), steps),
        )
        far = pl.ds(pl.multiple_of((1 - c) * rows, rows), rows)
        near = pl.ds(pl.multiple_of(c * rows, rows), rows)
        trades = [
            move(source.at[far], r.taken_pair.at[k, pl.ds(0, rows)], 12 + k, 12 + k, sibling)
            for k, source in enumerate((r.keys, r.values))
        ]
        for trade in trades:
            trade.start()
        steps()
        turn(r.branch, r.turned, rows)
        turn(r.hidden.at[pl.ds(first_row, rows)], r.turned_more, rows)
        for tt in range(tensor):
            at = pl.ds(8 * tt, 8)
            r.bias_out[at, 0 : r.onehot.shape[0]] = lax.dot_general(
                r.diagonals[at, :], r.onehot[...], (((1,), (1,)), ((), ())),
                precision=lax.Precision.HIGHEST, preferred_element_type=F32,
            )
        steps()
        project_back(r.queries, r.square.at[QUERY], r.summed, rows, True)
        for trade in trades:
            trade.wait_recv()
        steps()
        for k, source in enumerate((r.keys, r.values)):
            r.d_pair[k, 0:rows, :] = (source[near, :].astype(F32) + r.taken_pair[k, 0:rows, :].astype(F32)).astype(BF16)
        project_back(r.d_pair.at[0], r.square.at[KEY], r.summed, rows, False)
        project_back(r.d_pair.at[1], r.square.at[VALUE], r.summed, rows, False)
        steps()
        normalize_back(r.own_x, r.gains[0], r.summed, r.d_resid, r.gain_parts, rows, False)
        gain_done(0)
        steps()
        send_rows()
        drain.small_begin()
        drain.allow(2)
        products = [(r.turned_more, r.d_pair.at[0]), (r.turned_more, r.d_pair.at[1]), (r.turned_more, r.queries), (r.turned, r.mixture)]
        square_grads(rows, ATTN, products, nothing)
        for trade in trades:
            trade.wait_send()
        steps()
        drain.begin(ATTN)
        steps()
        drain.rest(ATTN)

    def parts_of(array):
        return [array.at[pl.ds(k * rows_d, rows_d)] for k in range(CORES)]

    def part_here(array):
        return array.at[pl.ds(pl.multiple_of(c * rows_d, rows_d), rows_d)]

    r.gains_out[...] = jnp.zeros_like(r.gains_out)
    r.bias_out[...] = jnp.zeros_like(r.bias_out)
    supply.start()

    def entry():
        supply.pump(2)
        supply.small()
        bias_vectors()
        supply.pump(2)
        supply.rows()

    def schedule(*items):
        left = list(items)

        def steps():
            for name, group, *n in left.pop(0) if left else ():
                getattr(drain, name)(group, *n)

        return steps

    @pl.when(here.pipe == 0)
    def _():
        supply.resume(ATTN, INNER, OUTER, CROSS)
        drain.order(CROSS, OUTER, INNER, ATTN)
        entry()
        rows, span = rows_e, span_e
        first_row = pl.multiple_of(c * rows, rows)
        seg_rows = segments(lengths_row(0), (span, 1), 0, 0)
        r.mask[...] = masked(seg_rows == segments(lengths_row(0), (1, rows), 1, first_row))
        supply.pump()
        rows_ready(span, rows, c * tensor)
        supply.pump(until=ATTN)
        supply.finish(ATTN)
        self_forward(span, rows, first_row, INNER)
        normalize(r.resid_mid, r.gains[1], r.second, rows)
        feed_forward(rows, at_each((1, 2, 3), supply.pump))
        supply.pump(until=OUTER)
        supply.finish(OUTER)
        r.resid_top[...] = r.resid_mid[...]
        feed_out(r.resid_top, rows, at_each((1, 2, 3), supply.pump))
        normalize(r.resid_top, r.gains[2], r.third, rows)
        r.mask[...] = masked(seg_rows == segments(lengths_row(nrow), (1, span_d), 1, 0))
        supply.pump(until=CROSS)
        supply.finish(CROSS)
        untangle(r.raw_c, FIRST, 2)
        mine = pl.ds(first_row, rows)
        other = pl.ds(pl.multiple_of((1 - c) * rows, rows), rows)
        trades = []
        for k, held in enumerate((r.cross_keys, r.cross_values)):
            r.send_pair[k] = nn(r.third[...], r.square[FIRST + k, :, far_lanes]).astype(BF16)
            trades.append(move(r.send_pair.at[k], held.at[mine], k, k, sibling))
            trades[-1].start()
        for k, held in enumerate((r.cross_keys, r.cross_values)):
            held[mine, :] = nn(r.third[...], r.square[FIRST + k, :, near_lanes]).astype(BF16)
        for k, part in enumerate(parts_of(r.cross_queries)):
            move(part, part, 2 + k, 2 + k, across[k]).wait_recv()
        for k, held in enumerate((r.cross_keys, r.cross_values)):
            move(r.send_pair.at[k], held.at[other], k, k, sibling).wait_recv()

        def mixtures(pair):
            at = pair_lanes(pair)
            return [
                pltpu.make_async_remote_copy(
                    r.cross_mixture.at[pl.ds(k * rows_d, rows_d), at], r.cross_in.at[c, :, at],
                    r.mix_send.at[k, pair], r.mix_recv.at[c, pair], device_id=across[k], device_id_type=MESH,
                )
                for k in range(CORES)
            ]

        def arrived(pair):
            for k in range(CORES):
                part = r.cross_back.at[pl.ds(k * rows_d, rows_d), pair_lanes(pair)]
                pltpu.make_async_remote_copy(
                    part, part, r.back_send.at[k, pair], r.back_recv.at[k, pair], device_id=across[k], device_id_type=MESH
                ).wait_recv()

        def returns(pair):
            at = pair_lanes(pair)
            return [
                pltpu.make_async_remote_copy(
                    d_cross.at[other, at], r.cross_taken.at[k, :, at],
                    r.give_send.at[k, pair], r.give_recv.at[k, pair], device_id=sibling, device_id_type=MESH,
                )
                for k, d_cross in enumerate((r.cross_keys, r.cross_values))
            ]

        attend(
            r.cross_keys, r.cross_values, r.cross_queries, r.cross_mixture, r.cross_probs, span_d, span, pairs_here,
            r.mask, None, lambda pair: [mix.start() for mix in mixtures(pair)],
        )
        supply.close()
        drain.free(0)
        turn(r.third, r.turned, rows)
        attend_back(
            r.cross_keys, r.cross_values, r.cross_queries, r.cross_back, r.cross_probs, span_d, span, pairs_here, None,
            arrived, lambda pair: [back.start() for back in returns(pair)],
        )
        answers = [
            move(part, r.cross_in_back.at[c], 8 + k, 8 + c, across[k]) for k, part in enumerate(parts_of(r.cross_queries))
        ]
        for answer in answers:
            answer.start()
        for k, d_cross in enumerate((r.cross_keys, r.cross_values)):
            r.d_pair[k, :, near_lanes] = d_cross[mine, :]
        for pair in range(pairs_here):
            for back in returns(pair):
                back.wait_recv()
        for k in range(2):
            r.d_pair[k, :, far_lanes] = r.cross_taken[k]
        drain.allow(0)
        square_grads(rows, CROSS, [(r.turned, r.d_pair.at[0]), (r.turned, r.d_pair.at[1])], nothing)
        drain.begin(CROSS)
        project_back(r.d_pair.at[0], r.square.at[FIRST], r.summed, rows, True)
        project_back(r.d_pair.at[1], r.square.at[SECOND], r.summed, rows, False)
        normalize_back(r.resid_top, r.gains[2], r.summed, r.d_resid, r.gain_parts, rows, True)
        gain_done(2)
        to_bf16(r.d_resid, r.d_branch, rows)
        turn(r.d_branch, r.turned, rows)
        feed_grads(rows, r.turned, 0, OUTER, at_each((2,), lambda: drain.tick(CROSS, 0)))
        drain.tick(CROSS, 1)
        drain.begin(OUTER)
        feed_back(rows, False, at_each((1, 2), schedule([("tick", CROSS, 2)], [("tick", CROSS, 3)])))
        drain.free(1)
        drain.free(2)
        turn(r.second, r.turned, rows)
        drain.allow(1)
        feed_grads(rows, r.turned, tensor, INNER, at_each((1,), lambda: drain.tick(OUTER, 0)))
        normalize_back(r.resid_mid, r.gains[1], r.summed, r.d_resid, r.gain_parts, rows, False)
        gain_done(1)
        for copy in trades + answers:
            copy.wait_send()
        for pair in range(pairs_here):
            for copy in mixtures(pair) + returns(pair):
                copy.wait_send()

        def send_rows():
            to_bf16(r.d_resid, r.rows_out, rows)
            drain.home()

        steps = schedule(
            [("tick", CROSS, 4), ("begin", INNER), ("tick", OUTER, 1)], [("end", CROSS), ("tick", OUTER, 2)],
            [], [("tick", INNER, 0)], [], [],
            [], [], [("tick", INNER, 1)], [], [("tick", OUTER, 3), ("tick", OUTER, 4)], [],
            [("tick", INNER, 2), ("tick", ATTN, 0), ("end", OUTER), ("tick", INNER, 3), ("tick", ATTN, 1), ("tick", ATTN, 2)]
            + [("home_done", None), ("tick", INNER, 4), ("tick", ATTN, 3), ("tick", ATTN, 4), ("end", INNER)],
        )
        self_backward(span, rows, first_row, steps, send_rows)

    @pl.when(here.pipe == 1)
    def _():
        supply.resume(ATTN, CROSS, INNER, OUTER)
        drain.order(OUTER, INNER, CROSS, ATTN)
        entry()
        rows, span = rows_d, span_d
        first_row = pl.multiple_of(c * rows, rows)
        key_at = lax.broadcasted_iota(jnp.int32, (span, rows), 0)
        query_at = lax.broadcasted_iota(jnp.int32, (span, rows), 1) + first_row
        same = segments(lengths_row(nrow), (span, 1), 0, 0) == segments(lengths_row(nrow), (1, rows), 1, first_row)
        r.mask[0:span, 0:rows] = masked(same & (query_at >= key_at))
        supply.pump()
        first_block = c * (tensor // 2)
        rows_ready(span, rows, first_block)
        for k in range(rows // places):
            r.d_branch[k * places : (k + 1) * places, :] = r.x[1, first_block + k]
        supply.pump(until=ATTN)
        supply.finish(ATTN)
        self_forward(span, rows, first_row, CROSS)
        untangle(r.raw_c, FIRST, 2)
        normalize(r.resid_mid, r.gains[1], r.third, rows)
        project(r.third, r.square.at[FIRST], r.joined, rows)
        asks = []
        for k in range(CORES):
            r.send_pair[k, 0:rows, :] = r.joined[:, lane_halves[k]]
            asks.append(move(r.send_pair.at[k, pl.ds(0, rows)], part_here(r.cross_queries), 2 + k, 2 + c, across[k]))
            asks[-1].start()
        supply.pump(until=INNER)
        supply.finish(INNER)
        supply.pump(until=OUTER)
        supply.finish(OUTER)

        @pl.loop(0, tensor)
        def _(tt):
            def body(at):
                r.ff[tensor + tt, rows : 2 * rows, at] = nn(r.d_branch[0:rows, :], r.outer[tt, :, at]).astype(BF16)

            columns_of(units, body)

        supply.close()
        drain.free(0)
        r.resid_top[0:rows, :] = r.resid_mid[0:rows, :]
        for k in range(CORES):
            for pair in range(pairs_here):
                part = r.cross_in.at[k, :, pair_lanes(pair)]
                pltpu.make_async_remote_copy(
                    part, part, r.mix_send.at[k, pair], r.mix_recv.at[k, pair], device_id=across[k], device_id_type=MESH
                ).wait_recv()
            r.joined[:, lane_halves[k]] = r.cross_in[k]
        project_back(r.joined, r.square.at[SECOND], r.resid_top, rows, False)
        normalize(r.resid_top, r.gains[2], r.second, rows)
        feed_forward(rows)
        feed_back(rows, True)
        r.d_resid[0:rows, :] = r.d_branch[0:rows, :].astype(F32)
        normalize_back(r.resid_top, r.gains[2], r.summed, r.d_resid, r.gain_parts, rows, False)
        gain_done(2)
        to_bf16(r.d_resid, r.branch, rows)
        tells = []
        for pair in range(pairs_here):
            for k in range(CORES):
                at = pair_lanes(pair)
                first = k * half_width + pair * LANES
                r.send_back[k, :, at] = nn(r.branch[0:rows, :], r.square[SECOND, :, first : first + LANES]).astype(BF16)
                tells.append(
                    pltpu.make_async_remote_copy(
                        r.send_back.at[k, :, at], r.cross_back.at[pl.ds(pl.multiple_of(c * rows, rows), rows), at],
                        r.back_send.at[k, pair], r.back_recv.at[c, pair], device_id=across[k], device_id_type=MESH,
                    )
                )
                tells[-1].start()
        drain.free(1)
        turn(r.d_branch, r.turned, rows)
        drain.allow(0)
        feed_grads(rows, r.turned, 0, OUTER)
        drain.begin(OUTER)
        turn(r.second, r.turned, rows)
        drain.allow(1)
        feed_grads(rows, r.turned, tensor, INNER)
        drain.begin(INNER)
        feed_out(r.resid_top, rows, at_each((1,), lambda: drain.tick(OUTER, 0)))
        drain.free(2)
        to_bf16(r.resid_top, r.rows_out, rows)
        turn(r.branch, r.turned, rows)
        turn(r.third, r.turned_more, rows)
        for k in range(CORES):
            move(r.cross_in_back.at[k], r.cross_in_back.at[k], 8 + k, 8 + k, across[k]).wait_recv()
            r.d_pair[1, 0:rows, lane_halves[k]] = r.cross_in_back[k]
        project_back(r.d_pair.at[1], r.square.at[FIRST], r.summed, rows, True)
        square_grads(rows, CROSS, [(r.turned_more, r.d_pair.at[1]), (r.turned, r.joined)], nothing)
        drain.tick(OUTER, 1)
        normalize_back(r.resid_mid, r.gains[1], r.summed, r.d_resid, r.gain_parts, rows, False)
        gain_done(1)
        for copy in asks + tells:
            copy.wait_send()

        def send_rows():
            to_bf16(r.d_resid, r.rows_out.at[pl.ds(rows, rows)], rows)
            drain.home()

        steps = schedule(
            [], [("tick", INNER, 0)], [], [("tick", INNER, 1)], [("tick", OUTER, 2)], [],
            [("tick", OUTER, 3)], [], [("tick", INNER, 2), ("tick", OUTER, 4)], [("begin", CROSS)],
            [("tick", INNER, 3), ("tick", INNER, 4)], [],
            [("end", OUTER), ("tick", CROSS, 0), ("tick", ATTN, 0), ("tick", CROSS, 1), ("end", INNER), ("tick", ATTN, 1)]
            + [("tick", ATTN, 2), ("tick", CROSS, 2), ("home_done", None), ("tick", ATTN, 3), ("tick", ATTN, 4)]
            + [("tick", CROSS, 3), ("tick", CROSS, 4), ("end", CROSS)],
        )
        self_backward(span, rows, first_row, steps, send_rows)

    drain.close()


def held(*shape, dtype=BF16):
    return pltpu.VMEM(shape, dtype)


def arrays(tensor, heads_at, places, width, units, ranges, kinds):
    tall = 2 * tensor * places
    block = width // tensor
    half_rows, half_width = tall // 2, width // 2
    heads = heads_at * tensor
    return dict(
        x=held(2, tensor, places, width),
        own_x=held(half_rows, width),
        raw_a=held(tensor, width, 4 * block),
        raw_c=held(tensor, width, 2 * block),
        square=held(6, width, width),
        inner=held(tensor, width, units),
        outer=held(tensor, width, units),
        hidden=held(tall, width),
        keys=held(tall, width),
        values=held(tall, width),
        queries=held(half_rows, width),
        probs=held(heads, tall, half_rows),
        mask=held(tall, half_rows, dtype=F32),
        mixture=held(half_rows, width),
        resid_mid=held(half_rows, width, dtype=F32),
        resid_top=held(half_rows, width, dtype=F32),
        d_resid=held(half_rows, width, dtype=F32),
        summed=held(half_rows, width, dtype=F32),
        second=held(half_rows, width),
        third=held(half_rows, width),
        ff=held(2 * tensor, half_rows, units),
        d_branch=held(half_rows, width),
        branch=held(half_rows, width),
        cross_keys=held(tall, half_width),
        cross_values=held(tall, half_width),
        cross_queries=held(half_rows, half_width),
        cross_mixture=held(half_rows, half_width),
        cross_probs=held(heads // CORES, tall, half_rows),
        cross_back=held(half_rows, half_width),
        cross_in=held(CORES, half_rows // 2, half_width),
        cross_in_back=held(CORES, half_rows // 2, half_width),
        cross_taken=held(CORES, half_rows, half_width),
        send_pair=held(CORES, half_rows, half_width),
        send_back=held(CORES, half_rows // 2, half_width),
        joined=held(half_rows // 2, width),
        taken_pair=held(2, half_rows, width),
        d_pair=held(2, half_rows, width),
        turned=held(width, half_rows),
        turned_more=held(width, half_rows),
        stage=held(2, width, units),
        vectors=held(8 * tensor, ranges, dtype=F32),
        diagonals=held(8 * tensor, ranges, dtype=F32),
        onehot=held(kinds, ranges, dtype=F32),
        gain_parts=held(8, width, dtype=F32),
        send_sem=pltpu.SemaphoreType.DMA((14,)),
        recv_sem=pltpu.SemaphoreType.DMA((14,)),
        **{
            name: pltpu.SemaphoreType.DMA((CORES, half_width // LANES))
            for name in ("mix_send", "mix_recv", "back_send", "back_recv", "give_send", "give_recv")
        },
    )


def group_columns(block, units):
    return {ATTN: (0, 4 * block), CROSS: (4 * block, 2 * block), INNER: (6 * block, units), OUTER: (6 * block + units, units)}


def landing(r):
    return {ATTN: r.raw_a, CROSS: r.raw_c, INNER: r.inner, OUTER: r.outer}


class Loads:
    def __init__(self, r, tensor, x_hbm, w_hbm, sems):
        columns = group_columns(r.raw_a.shape[2] // 4, r.inner.shape[2])
        self.x = pltpu.make_async_copy(x_hbm, r.x, sems.at[4, 0])
        self.weights = [
            [
                pltpu.make_async_copy(w_hbm.at[tt, :, pl.ds(*columns[group])], target.at[tt], sems.at[group, tt])
                for tt in range(tensor)
            ]
            for group, target in landing(r).items()
        ]

    def start(self):
        self.x.start()
        for group in self.weights:
            for copy in group:
                copy.start()

    def rows(self):
        self.x.wait()

    def finish(self, group):
        for copy in self.weights[group]:
            copy.wait()

    small = resume = pump = close = nothing


class Stores:
    def __init__(self, r, grads_hbm, sems):
        self.columns = group_columns(r.raw_a.shape[2] // 4, r.inner.shape[2])
        self.r, self.grads, self.sems = r, grads_hbm, sems

    def copy(self, group, tt, slot):
        first, wide = self.columns[group]
        return pltpu.make_async_copy(
            self.r.stage.at[slot, :, pl.ds(0, wide)], self.grads.at[tt, :, pl.ds(first, wide)], self.sems.at[slot]
        )

    def emit(self, group, tt, slot):
        self.copy(group, tt, slot).start()

    def release(self, group, tt, slot):
        self.copy(group, tt, slot).wait()

    order = free = allow = begin = tick = rest = end = home = home_done = small_begin = close = nothing


def blocks_kernel(tensor, dp, heads_at, names, *refs):
    here = Place(tensor, dp)
    r = types.SimpleNamespace(**dict(zip(names, refs)))
    across = [{"pipe": 1 - here.pipe, "dp": here.group * CORES + k} for k in range(CORES)]
    meet([here.sibling()] + across)
    work(r, here, Loads(r, tensor, r.x_hbm, r.w_hbm, r.load_sem), Stores(r, r.grads_hbm, r.stage_sem), tensor, heads_at)


def blocks(tensor, dp, heads_at, kinds, rows, weights, gains, lengths, tables, buckets):
    places, width = rows.shape[2:]
    units = (weights.shape[2] - 6 * (width // tensor)) // 2
    half_rows = tensor * places
    scratch = arrays(tensor, heads_at, places, width, units, buckets.shape[1], kinds)
    scratch["load_sem"] = pltpu.SemaphoreType.DMA((5, tensor))
    scratch["stage_sem"] = pltpu.SemaphoreType.DMA((2,))
    names = ["x_hbm", "w_hbm", "gains", "lengths", "tables", "buckets", "grads_hbm", "rows_out", "gains_out", "bias_out"]
    return pl.pallas_call(
        functools.partial(blocks_kernel, tensor, dp, heads_at, names + list(scratch)),
        out_shape=(
            jax.ShapeDtypeStruct(weights.shape, BF16),
            jax.ShapeDtypeStruct((half_rows, width), BF16),
            jax.ShapeDtypeStruct((8, width), F32),
            jax.ShapeDtypeStruct((8 * tensor, LANES), F32),
        ),
        in_specs=[ANY, ANY] + [VMEM] * 4,
        out_specs=(ANY, VMEM, VMEM, VMEM),
        scratch_shapes=list(scratch.values()),
        compiler_params=pltpu.CompilerParams(collective_id=2, has_side_effects=True, vmem_limit_bytes=VMEM_LIMIT),
        name="blocks",
    )(rows, weights, gains, lengths, tables, buckets)


class Rings:
    def __init__(self, r, here, tensor, dp):
        self.r, self.here, self.tensor, self.dp = r, here, tensor, dp
        self.depth = r.value_w.shape[0]
        self.hops = here.chips // 2
        self.count = 2 * self.hops - 1
        self.sibling = here.sibling()
        self.targets = [here.neighbour(1), here.neighbour(-1)]
        self.landing = landing(r)
        self.groups = []
        self.plan = []


    def order(self, *groups):
        steps = []
        for k, group in enumerate(groups):
            steps.append((4 * k - 0.5, k, self.begin, group, None))
            late = {self.count - 3: 3.6, self.count - 2: 3.7, self.count - 1: 5.5}
            steps += [(4 * k + late.get(n, n), k, self.tick, group, n) for n in range(self.count)]
        steps.sort(key=lambda step: step[:2])
        self.groups = list(groups)
        self.plan = [step[2:] for step in steps]

    def resume(self, *groups):
        self.order(*groups)
        self.plan.pop(0)

    def pump(self, count=1, until=None):
        while self.plan and (count > 0 if until is None else any(step[1] == until for step in self.plan)):
            do, group, n = self.plan.pop(0)
            do(group) if n is None else do(group, n)
            count -= 0 if n is None else 1


    def block_out(self, i):
        r, t, c = self.r, self.here.t, self.here.core
        return pltpu.make_async_remote_copy(
            r.rows.at[i], r.x.at[:, t], r.block_send.at[i], r.block_recv.at[t],
            device_id={"tensor": r.rows.shape[0] * c + i}, device_id_type=MESH,
        )

    def block_kept(self, i):
        return pltpu.make_async_copy(self.r.rows.at[i], self.r.x.at[:, self.here.t], self.r.local_sem.at[0])

    def block_pass(self, source, s):
        r = self.r
        return pltpu.make_async_remote_copy(
            source, r.x.at[:, s], r.pass_send.at[s], r.pass_recv.at[s], device_id=self.sibling, device_id_type=MESH
        )

    def blocks(self, mine, others):
        for i in range(self.r.rows.shape[0]):
            here = self.r.rows.shape[0] * self.here.core + i == self.here.t

            @pl.when(here)
            def _():
                mine(i)

            @pl.when(jnp.logical_not(here))
            def _():
                others(i)

    def small_copies(self):
        r, t = self.r, self.here.t
        copies = [
            pltpu.make_async_remote_copy(
                r.lengths_in, r.lengths.at[self.here.core], r.small_send.at[0], r.small_recv.at[0],
                device_id=self.sibling, device_id_type=MESH,
            ),
            pltpu.make_async_copy(r.lengths_in, r.lengths.at[self.here.core], r.local_sem.at[1]),
            pltpu.make_async_copy(r.table_in, r.tables.at[t], r.local_sem.at[2]),
        ]
        for k in range(1, self.tensor):
            copies.append(
                pltpu.make_async_remote_copy(
                    r.table_in, r.tables.at[t], r.small_send.at[k], r.small_recv.at[k],
                    device_id={"tensor": lax.rem(t + k, self.tensor)}, device_id_type=MESH,
                )
            )
        return copies


    def rows_of(self, ring):
        line, at = self.here.at(ring)
        return at, pl.multiple_of((line * CORES + self.here.core) * self.depth, 16)

    def ring_at(self, step, part):
        way = -1 if part else 1
        return lax.rem(self.here.ring - way * step + self.here.chips, self.here.chips)

    def onward(self, group, step, part, sub):
        r, half = self.r, self.depth // 2
        at, first = self.rows_of(self.ring_at(step, part))
        target = self.landing[group]
        slot = target.at[at, pl.ds(pl.multiple_of(first + half * sub, 16), half), :]
        packed = r.stage.at[0, pl.ds(group * self.depth + half * sub, half), pl.ds(0, target.shape[2])]
        return pltpu.make_async_remote_copy(
            packed if step == 0 else slot, slot, r.ring_send.at[group, part, sub, step], r.ring_recv.at[group, part, sub, step],
            device_id=self.targets[part], device_id_type=MESH,
        )

    def over(self, group, ring, first_time=False):
        r = self.r
        at, first = self.rows_of(ring)
        target = self.landing[group]
        slot = target.at[at, pl.ds(first, self.depth), :]
        packed = r.stage.at[0, pl.ds(group * self.depth, self.depth), pl.ds(0, target.shape[2])]
        return pltpu.make_async_remote_copy(
            packed if first_time else slot, slot, r.over_send.at[group, ring], r.over_recv.at[group, ring],
            device_id=self.sibling, device_id_type=MESH,
        )

    def own(self, group):
        wide = self.landing[group].shape[2]
        first = pl.multiple_of(self.here.d * self.depth, 16)
        return pltpu.make_async_copy(
            self.r.stage.at[0, pl.ds(group * self.depth, self.depth), pl.ds(0, wide)],
            self.landing[group].at[self.here.t, pl.ds(first, self.depth), :],
            self.r.own_sem.at[group],
        )

    def begin(self, group):
        for sub in range(2):
            for part in range(2):
                self.onward(group, 0, part, sub).start()
        self.over(group, self.here.ring, True).start()
        self.own(group).start()

    def tick(self, group, n):
        step, last = n // 2 + 1, n == self.count - 1
        for part in range(2):
            sub = part if last else n % 2
            self.onward(group, step - 1, part, sub).wait_recv()
            if not last and (step < self.hops - 1 or sub == part):
                self.onward(group, step, part, sub).start()
        if last:
            self.over(group, self.ring_at(step, 0)).start()
        elif n % 2:
            for part in range(2):
                self.over(group, self.ring_at(step, part)).start()

    def sends_done(self, group):
        for part in range(2):
            for sub in range(2):
                for step in range(self.hops):
                    if step < self.hops - 1 or sub == part:
                        self.onward(group, step, part, sub).wait_send()

    def finish(self, group):
        @pl.loop(0, self.here.chips)
        def _(ring):
            self.over(group, ring).wait_recv()

        self.own(group).wait()

    def start(self):
        r, depth = self.r, self.depth
        nrow = r.rows.shape[0]
        r.lengths_in[...] = jnp.zeros_like(r.lengths_in)
        r.lengths_in[0:nrow, 0 : r.enc_lengths.shape[1]] = r.enc_lengths[...]
        r.lengths_in[nrow : 2 * nrow, 0 : r.dec_lengths.shape[1]] = r.dec_lengths[...]
        r.table_in[...] = jnp.zeros_like(r.table_in)
        for k in range(r.bias_w.shape[0]):
            r.table_in[k : k + 1, 0 : r.bias_w.shape[2]] = r.bias_w[k]
        self.blocks(
            lambda i: (self.block_kept(i).start(), self.block_pass(r.rows.at[i], self.here.t).start()),
            lambda i: self.block_out(i).start(),
        )
        block = r.value_w.shape[1]

        def band(group, pieces):
            wide = pieces[0].shape[1]
            for k, piece in enumerate(pieces):
                r.stage[0, group * depth : (group + 1) * depth, k * wide : (k + 1) * wide] = piece

        band(ATTN, [r.query_key_w[1], r.value_w[...], r.query_key_w[0], r.out_w[...].T])
        self.order(ATTN)
        self.begin(ATTN)
        for copy in self.small_copies():
            copy.start()
        band(INNER, [r.inner_w[...]])
        band(OUTER, [r.outer_w[...]])
        band(CROSS, [r.first_w[...], r.second_w[...]])

    def small(self):
        for copy in self.small_copies():
            copy.wait()

    def rows(self):
        r, t = self.r, self.here.t
        takes = lax.div(t, r.rows.shape[0]) == self.here.core
        for s in range(self.tensor):

            @pl.when(jnp.logical_and(takes, s != t))
            def _():
                pltpu.make_async_remote_copy(
                    r.rows.at[0], r.x.at[:, s], r.block_send.at[0], r.block_recv.at[s],
                    device_id=self.sibling, device_id_type=MESH,
                ).wait_recv()
                self.block_pass(r.x.at[:, s], s).start()

        self.blocks(lambda i: self.block_kept(i).wait(), nothing)
        for s in range(self.tensor):

            @pl.when(jnp.logical_not(takes))
            def _():
                self.block_pass(r.x.at[:, s], s).wait_recv()

    def close(self):
        r, t = self.r, self.here.t
        takes = lax.div(t, r.rows.shape[0]) == self.here.core
        self.blocks(
            lambda i: self.block_pass(r.rows.at[i], t).wait_send(),
            lambda i: self.block_out(i).wait_send(),
        )
        for s in range(self.tensor):

            @pl.when(jnp.logical_and(takes, s != t))
            def _():
                self.block_pass(r.x.at[:, s], s).wait_send()

        for group in self.groups:
            self.sends_done(group)

            @pl.loop(0, self.here.chips)
            def _(ring):
                self.over(group, ring).wait_send()


class Sums:
    def __init__(self, r, here, tensor, dp):
        self.r, self.here, self.tensor, self.dp = r, here, tensor, dp
        self.depth = r.value_w.shape[0]
        self.hops = here.chips // 2
        self.count = 2 * self.hops - 3
        self.sibling = here.sibling()
        self.targets = [here.neighbour(1), here.neighbour(-1)]
        self.box = {CROSS: r.raw_c, OUTER: r.raw_a, INNER: r.inner, ATTN: r.outer}
        self.kept = {CROSS: r.own_cross, OUTER: r.own_outer, INNER: r.own_inner, ATTN: r.ff}
        self.groups = []

    def order(self, *groups):
        self.groups = list(groups)

    def free(self, k):
        for device in self.targets + [self.sibling]:
            pl.semaphore_signal(self.r.free_sem.at[k], inc=1, device_id=device, device_id_type=MESH)

    def allow(self, k):
        pl.semaphore_wait(self.r.free_sem.at[k], 3)

    def boxed(self, group, index, first, height):
        if isinstance(index, int):
            return (index // self.dp, pl.ds(pl.multiple_of(index % self.dp * self.depth + first, 16), height), slice(None))
        at = pl.ds(pl.multiple_of(lax.rem(index, self.dp) * self.depth + first, 16), height)
        return (lax.div(index, self.dp), at, slice(None))

    def taken(self, group, step, part, first, height):
        index = step + part * (self.hops - 1) if step else 0
        return self.boxed(group, index, first, height)

    def theirs(self, group, ring, first, height):
        return self.boxed(group, self.here.chips - 1 + ring, first, height)

    def own(self, group, ring, first, height):
        return (ring, pl.ds(first, height), slice(None))

    def ring_of(self, line, at):
        return line * self.tensor + at + (line % 2) * (self.tensor - 1 - 2 * at)

    def pieces(self, group, tt, slot):
        r, depth = self.r, self.depth
        wide = self.box[group].shape[2]
        made = []
        for line in range(self.here.groups):
            ring = self.ring_of(line, tt)

            def rows_of(core):
                return r.stage.at[slot, pl.ds(pl.multiple_of((line * CORES + core) * depth, 16), depth), pl.ds(0, wide)]

            made.append(
                pltpu.make_async_copy(
                    rows_of(self.here.core), self.kept[group].at[self.own(group, ring, 0, depth)], r.kept_sem.at[slot, line]
                )
            )
            made.append(
                pltpu.make_async_remote_copy(
                    rows_of(1 - self.here.core), self.box[group].at[self.theirs(group, ring, 0, depth)],
                    r.over_send.at[group, ring], r.over_recv.at[group, ring], device_id=self.sibling, device_id_type=MESH,
                )
            )
        return made

    def emit(self, group, tt, slot):
        for piece in self.pieces(group, tt, slot):
            piece.start()

    def release(self, group, tt, slot):
        for k, piece in enumerate(self.pieces(group, tt, slot)):
            if k % 2:
                piece.wait_send()
            else:
                piece.wait()


    def rows_at(self, sub):
        half = self.depth // 2
        return half * sub, half

    def source(self, step, part):
        way = -1 if part else 1
        return lax.rem(self.here.ring + way * (self.hops - step) + self.here.chips, self.here.chips)

    def onward(self, group, step, part, sub):
        r = self.r
        first, height = self.rows_at(sub)
        return pltpu.make_async_remote_copy(
            self.kept[group].at[self.own(group, self.source(step, part), first, height)],
            self.box[group].at[self.taken(group, step, part, first, height)],
            r.ring_send.at[group, part, sub, step], r.ring_recv.at[group, part, sub, step],
            device_id=self.targets[part], device_id_type=MESH,
        )

    def here_sum(self, group, ring, first, height):
        value = self.kept[group][self.own(group, ring, first, height)].astype(F32)
        return value + self.box[group][self.theirs(group, ring, first, height)].astype(F32)

    def advance(self, group, step, part, sub, fresh=False):
        if not fresh:
            self.onward(group, step - 1, part, sub).wait_recv()
        ring = self.source(step, part)

        def add(first, height):
            value = self.here_sum(group, ring, first, height)
            if not fresh:
                value = value + self.box[group][self.taken(group, step - 1, part, first, height)].astype(F32)
            self.kept[group][self.own(group, ring, first, height)] = value.astype(BF16)

        self.in_pieces(sub, add)
        self.onward(group, step, part, sub).start()

    def in_pieces(self, sub, body):
        start, height = self.rows_at(sub)

        @pl.loop(0, height // 16)
        def _(k):
            body(pl.multiple_of(start + 16 * k, 16), 16)

    def begin(self, group):
        @pl.loop(0, self.here.chips)
        def _(ring):
            pltpu.make_async_remote_copy(
                self.kept[group].at[self.own(group, ring, 0, self.depth)],
                self.box[group].at[self.theirs(group, ring, 0, self.depth)],
                self.r.over_send.at[group, ring], self.r.over_recv.at[group, ring], device_id=self.sibling, device_id_type=MESH,
            ).wait_recv()

        for part in range(2):
            self.advance(group, 0, part, part, True)
        for part in range(2):
            self.advance(group, 1, part, 1 - part, True)
        if group == ATTN:
            self.small_across().wait_recv()
            self.small_advance(0, 0, True)
            self.small_advance(1, 1, True)

    def tick(self, group, n):
        step, leads = (n + 1) // 2 + 1, n % 2
        for part in range(2):
            self.advance(group, step, part, 1 - part if leads else part)
        if group == ATTN and not leads:
            self.small_advance(step, 0)
            if step > 1:
                self.small_advance(step, 1)

    def sends_done(self, group):
        for part in range(2):
            self.onward(group, 0, part, part).wait_send()
            for step in range(1, self.hops):
                for sub in range(2):
                    self.onward(group, step, part, sub).wait_send()

    def rest(self, group):
        self.end(group)
        for group in (ATTN, CROSS, INNER, OUTER):
            self.sends_done(group)

    def end(self, group):
        r, last = self.r, self.hops - 1
        for sub in range(2):
            for part in range(2):
                self.onward(group, last, part, sub).wait_recv()
            target = r.inner_out if group == INNER else r.total

            def add(first, height):
                value = self.here_sum(group, self.here.ring, first, height)
                for part in range(2):
                    value = value + self.box[group][self.taken(group, last, part, first, height)].astype(F32)
                target[pl.ds(first, height), 0 : self.box[group].shape[2]] = value

            self.in_pieces(sub, add)
        block = r.value_w.shape[1]
        if group == ATTN:
            r.pair_out[1] = r.total[:, 0:block]
            r.value_out[...] = r.total[:, block : 2 * block]
            r.pair_out[0] = r.total[:, 2 * block : 3 * block]
            r.out_out[...] = r.total[:, 3 * block : 4 * block].T
            at = self.small_at(self.here.ring)
            value = r.small[at] + r.small_theirs[at]
            for part in range(2):
                self.small_onward(last, part).wait_recv()
                value = value + r.small_taken[part, last]
            r.tiny_out[...] = value
        if group == CROSS:
            r.first_out[...] = r.total[:, 0:block]
            r.second_out[...] = r.total[:, block : 2 * block]
        if group == OUTER:
            r.outer_out[...] = r.total[...]


    def small_at(self, ring):
        line, at = self.here.at(ring)
        return at, line * CORES + self.here.core

    def small_across(self):
        r = self.r
        return pltpu.make_async_remote_copy(
            r.small, r.small_theirs, r.small_sem.at[0], r.small_sem.at[1], device_id=self.sibling, device_id_type=MESH
        )

    def small_onward(self, step, part):
        r = self.r
        return pltpu.make_async_remote_copy(
            r.small_sent.at[part, step], r.small_taken.at[part, step], r.tiny_send.at[part, step], r.tiny_recv.at[part, step],
            device_id=self.targets[part], device_id_type=MESH,
        )

    def small_advance(self, step, part, fresh=False):
        at = self.small_at(self.source(step, part))
        value = self.r.small[at] + self.r.small_theirs[at]
        if not fresh:
            self.small_onward(step - 1, part).wait_recv()
            value = value + self.r.small_taken[part, step - 1]
        self.r.small_sent[part, step] = value
        self.small_onward(step, part).start()

    def small_begin(self):
        r, depth = self.r, self.depth
        r.small[...] = jnp.zeros_like(r.small)
        kinds = r.onehot.shape[0] // self.dp
        heads_at = self.heads_at
        for tt in range(self.tensor):
            for d in range(self.dp):
                r.small[tt, d, 0:3, 0:depth] = r.gains_out[0:3, d * depth : (d + 1) * depth]
                r.small[tt, d, 3 : 3 + heads_at, 0:kinds] = r.bias_out[
                    8 * tt : 8 * tt + heads_at, d * kinds : (d + 1) * kinds
                ]
        self.small_across().start()


    def home_copy(self, k):
        r, here, tensor = self.r, self.here, self.tensor
        nrow, half, places = r.home_in.shape[0], tensor // 2, r.home_in.shape[2]
        place = here.pipe * (here.core * half + k % half) + (1 - here.pipe) * k
        which = here.pipe * (k // half) + (1 - here.pipe) * here.core
        owner = lax.div(here.t, nrow)
        source = r.rows_out.at[pl.ds(k * places, places)]
        slot = r.home_in.at[lax.rem(here.t, nrow), which]
        recv = r.home_recv.at[lax.rem(here.t, nrow), which]
        return (
            jnp.logical_and(place == here.t, owner == here.core),
            lambda: pltpu.make_async_copy(source, slot, recv),
            lambda: pltpu.make_async_remote_copy(
                source, slot, r.home_send.at[k], recv,
                device_id={"dp": here.group * CORES + owner, "tensor": place}, device_id_type=MESH,
            ),
        )

    def home(self):
        for k in range(self.tensor):
            stays, inside, away = self.home_copy(k)

            @pl.when(stays)
            def _():
                inside().start()

            @pl.when(jnp.logical_not(stays))
            def _():
                away().start()

    def home_done(self, unused=None):
        r = self.r
        places = r.home_in.shape[2]
        for i in range(r.home_in.shape[0]):
            for which in range(2):
                pltpu.make_async_copy(
                    r.rows_out.at[pl.ds(0, places)], r.home_in.at[i, which], r.home_recv.at[i, which]
                ).wait()
                r.home_out[i, which] = r.home_in[i, which].astype(F32)

    def close(self):
        r = self.r
        for k in range(self.tensor):
            stays, inside, away = self.home_copy(k)

            @pl.when(jnp.logical_not(stays))
            def _():
                away().wait_send()

        self.small_across().wait_send()

        for part in range(2):
            for step in range(part, self.hops):
                self.small_onward(step, part).wait_send()


def fits_fused(tensor, dp, depth, units, width):
    chips = tensor * dp // CORES
    return (
        depth % 32 == 0
        and 4 * depth <= width
        and chips <= 2 * tensor
        and chips == 2 * tensor == 8
        and units == width == 6 * LANES
    )


def fused_kernel(tensor, dp, heads_at, names, *refs):
    here = Place(tensor, dp)
    r = types.SimpleNamespace(**dict(zip(names, refs)))
    line = [
        {"dp": here.group * CORES + lax.rem(here.core + j, CORES), "tensor": lax.rem(here.t + k, tensor)}
        for j in range(CORES)
        for k in range(tensor)
        if j + k > 0
    ]
    across = [{"pipe": 1 - here.pipe, "dp": here.group * CORES + k} for k in range(CORES)]
    meet([here.neighbour(1), here.neighbour(-1)] + line + across)
    supply, drain = Rings(r, here, tensor, dp), Sums(r, here, tensor, dp)
    drain.heads_at = heads_at
    work(r, here, supply, drain, tensor, heads_at)


def fused(tensor, dp, rows, enc_lengths, dec_lengths, gains, bias, buckets, weights):
    nrow, two, places, width = rows.shape
    depth, block = weights[1].shape
    units = weights[5].shape[1]
    heads_at, _, kinds = bias.shape
    chips = tensor * dp // CORES
    wide = -(-max(depth, kinds // dp) // LANES) * LANES
    sems = pltpu.SemaphoreType.DMA
    scratch = arrays(tensor, heads_at, places, width, units, buckets.shape[1], kinds)
    scratch.update(
        lengths_in=held(8, LANES, dtype=jnp.int32),
        table_in=held(8, LANES, dtype=F32),
        lengths=held(CORES, 8, LANES, dtype=jnp.int32),
        tables=held(tensor, 8, LANES, dtype=F32),
        own_cross=held(chips, depth, 2 * block),
        own_outer=held(chips, depth, units),
        own_inner=held(chips, depth, units),
        total=held(depth, units, dtype=F32),
        rows_out=held(tensor * places, width),
        gains_out=held(8, width, dtype=F32),
        bias_out=held(8 * tensor, LANES, dtype=F32),
        home_in=held(nrow, two, places, width),
        small=held(tensor, dp, 8, wide, dtype=F32),
        small_theirs=held(tensor, dp, 8, wide, dtype=F32),
        small_sent=held(2, chips // 2, 8, wide, dtype=F32),
        small_taken=held(2, chips // 2, 8, wide, dtype=F32),
        block_send=sems((nrow,)), block_recv=sems((tensor,)), pass_send=sems((tensor,)), pass_recv=sems((tensor,)),
        local_sem=sems((3,)), small_send=sems((tensor,)), small_recv=sems((tensor,)), own_sem=sems((4,)),
        ring_send=sems((4, 2, 2, chips // 2)), ring_recv=sems((4, 2, 2, chips // 2)),
        over_send=sems((4, chips)), over_recv=sems((4, chips)), kept_sem=sems((2, dp // CORES)),
        small_sem=sems((2,)), tiny_send=sems((2, chips // 2)), tiny_recv=sems((2, chips // 2)),
        home_send=sems((tensor,)), home_recv=sems((nrow, two)),
        free_sem=pltpu.SemaphoreType.REGULAR((3,)),
    )
    inputs = ["rows", "enc_lengths", "dec_lengths", "gains", "bias_w", "buckets"]
    inputs += ["query_key_w", "value_w", "out_w", "first_w", "second_w", "inner_w", "outer_w"]
    outputs = dict(
        home_out=rows.shape, tiny_out=(8, wide), pair_out=(2, depth, block), value_out=(depth, block),
        out_out=(block, depth), first_out=(depth, block), second_out=(depth, block), inner_out=(depth, units),
        outer_out=(depth, units),
    )
    return pl.pallas_call(
        functools.partial(fused_kernel, tensor, dp, heads_at, inputs + list(outputs) + list(scratch)),
        out_shape=tuple(jax.ShapeDtypeStruct(shape, F32) for shape in outputs.values()),
        in_specs=[ANY] + [VMEM] * 12,
        out_specs=(VMEM,) * len(outputs),
        scratch_shapes=list(scratch.values()),
        compiler_params=pltpu.CompilerParams(collective_id=3, has_side_effects=True, vmem_limit_bytes=VMEM_LIMIT),
        name="fused",
    )(rows, enc_lengths, dec_lengths, gains, bias, buckets, *weights)


def pad_to(array, *shape):
    return jnp.pad(array, [(0, full - have) for full, have in zip(shape, array.shape)])


def shards(
    tensor, dp, section_rows, enc_lengths, dec_lengths, enc_buckets, dec_buckets, norm_gains, rel_bias,
    query_key_w, value_w, attn_out_w, cross_first, cross_second, ff_in, ff_out,
):
    depth = value_w.shape[1]
    width = section_rows.shape[-1]
    on_encoder = lax.axis_index("pipe") == 0
    ranges = -(-enc_buckets.shape[0] // LANES) * LANES
    dec_all = jnp.concatenate([jnp.zeros((dec_buckets.shape[0] - 1,), jnp.int32), dec_buckets])
    bucket_row = jnp.where(on_encoder, pad_to(enc_buckets, ranges), pad_to(dec_all, ranges))[None]
    gains = norm_gains.transpose(1, 0, 2)
    bias = rel_bias.transpose(2, 0, 1)
    weights = (query_key_w[0], value_w[0], attn_out_w[0], cross_first[0], cross_second[0], ff_in[0], ff_out[0].T)
    run = fused if fits_fused(tensor, dp, depth, ff_in.shape[2], width) else in_three
    home, tiny, *grads, outer = run(
        tensor, dp, section_rows[0], enc_lengths, dec_lengths, gains, bias, bucket_row, weights
    )
    if run is fused:
        home, tiny, *grads, outer = copied(home, tiny, *grads, outer)
    heads_at, kinds = bias.shape[0], bias.shape[2] // dp
    return (
        (home[None], tiny[:3, :depth][None], tiny[3 : 3 + heads_at, :kinds].T[None])
        + tuple(grad[None] for grad in grads)
        + (outer.T[None],)
    )


def copied(*results):
    def kernel(*refs):
        for source, target in zip(refs[: len(results)], refs[len(results) :]):
            target[...] = source[...]

    return pl.pallas_call(
        kernel,
        out_shape=tuple(jax.ShapeDtypeStruct(result.shape, result.dtype) for result in results),
        in_specs=[VMEM] * len(results),
        out_specs=(VMEM,) * len(results),
        name="copied",
    )(*results)


def in_three(tensor, dp, section_rows, enc_lengths, dec_lengths, gains, bias, buckets, weights):
    query_key, value, out, first, second, inner, outer = weights
    nrow, _, _, width = section_rows.shape
    heads_at, _, kinds = bias.shape
    lengths = pad_to(jnp.concatenate([enc_lengths, dec_lengths], axis=0), 8, LANES)
    table = pad_to(bias[:, 0], 8, LANES)
    depth, block = value.shape
    units = inner.shape[1]
    pack = jnp.concatenate([query_key[1], value, query_key[0], out.T, first, second, inner, outer], axis=1)
    rows, gathered, lengths, tables = gather(tensor, dp, section_rows, pack, lengths, table)
    grads, finished, gain_grads, bias = blocks(
        tensor, dp, heads_at, kinds, rows, gathered.reshape(tensor, width, -1), gains, lengths, tables, buckets
    )
    held_kinds = kinds // dp
    wide = -(-max(depth, held_kinds) // LANES) * LANES
    gain_part = pad_to(gain_grads[:3].reshape(3, dp, depth).transpose(1, 0, 2), dp, 3, wide)
    bias_part = bias.reshape(tensor, 8, LANES)[:, :heads_at, :kinds].reshape(tensor, heads_at, dp, held_kinds)
    bias_part = pad_to(bias_part.transpose(0, 2, 1, 3), tensor, dp, 5, wide)
    small = jnp.concatenate([jnp.broadcast_to(gain_part[None], (tensor,) + gain_part.shape), bias_part], axis=2)
    total, tiny, home = scatter(
        tensor, dp, grads.reshape(tensor, dp, depth, -1), small, finished.reshape(tensor, -1, width), nrow
    )
    key, value, query, out, first, second = [total[:, k * block : (k + 1) * block] for k in range(6)]
    inner, outer = total[:, 6 * block : 6 * block + units], total[:, 6 * block + units :]
    return (
        home.astype(F32), tiny,
        jnp.stack([query, key]), value, out.T, first, second, inner, outer,
    )


def solution(mesh):
    sizes = dict(mesh.shape)
    return jax.shard_map(
        functools.partial(shards, sizes["tensor"], sizes["dp"]),
        mesh=mesh,
        in_specs=(
            P("pipe", "dp", None, "tensor", None),
            P("dp", None),
            P("dp", None),
            P(),
            P(),
            P("pipe", None, None),
            P("pipe", None, "tensor"),
            P("pipe", None, "dp", "tensor"),
            P("pipe", "dp", "tensor"),
            P("pipe", "tensor", "dp"),
            P("pipe", "dp", "tensor"),
            P("pipe", "dp", "tensor"),
            P("pipe", "dp", "tensor"),
            P("pipe", "tensor", "dp"),
        ),
        out_specs=(
            P("pipe", "dp", None, "tensor", None),
            P("pipe", None, "dp"),
            P("pipe", "dp", "tensor"),
            P("pipe", None, "dp", "tensor"),
            P("pipe", "dp", "tensor"),
            P("pipe", "tensor", "dp"),
            P("pipe", "dp", "tensor"),
            P("pipe", "dp", "tensor"),
            P("pipe", "dp", "tensor"),
            P("pipe", "tensor", "dp"),
        ),
        check_vma=False,
    )
```

```python
import functools
import types

import jax
import jax.numpy as jnp
from jax import lax
from jax.experimental import pallas as pl
from jax.experimental.pallas import tpu as pltpu
from jax.sharding import PartitionSpec as P

MESH = pl.DeviceIdType.MESH
F32 = jnp.float32
BF16 = jnp.bfloat16
EPSILON = 1e-06
NEGATIVE = -1000000000.0
HEAD_DIM = 64
CORES = 2
LANES = 128
VMEM_LIMIT = 62 << 20
ANY = pl.BlockSpec(memory_space=pl.ANY)
VMEM = pl.BlockSpec(memory_space=pltpu.VMEM)


def nn(a, b):
    return lax.dot_general(a, b, (((1,), (0,)), ((), ())), preferred_element_type=F32)


def nt(a, b):
    return lax.dot_general(a, b, (((1,), (1,)), ((), ())), preferred_element_type=F32)


def tn(a, b):
    return lax.dot_general(a, b, (((0,), (0,)), ((), ())), preferred_element_type=F32)


class Place:
    def __init__(self, tensor, dp):
        self.tensor = tensor
        self.groups = dp // CORES
        self.chips = tensor * self.groups
        self.pipe = lax.axis_index("pipe")
        self.d = lax.axis_index("dp")
        self.t = lax.axis_index("tensor")
        self.core = lax.rem(self.d, CORES)
        self.group = self.d // CORES
        odd = lax.rem(self.group, 2)
        self.ring = self.group * tensor + self.t + odd * (tensor - 1 - 2 * self.t)

    def at(self, ring):
        group = ring // self.tensor
        along = lax.rem(ring, self.tensor)
        odd = lax.rem(group, 2)
        return group, along + odd * (self.tensor - 1 - 2 * along)

    def neighbour(self, step):
        group, t = self.at(lax.rem(self.ring + step + self.chips, self.chips))
        return {"dp": group * CORES + self.core, "tensor": t}

    def sibling(self):
        return {"dp": self.group * CORES + 1 - self.core}


def meet(devices):
    barrier = pltpu.get_barrier_semaphore()
    for device in devices:
        pl.semaphore_signal(barrier, inc=1, device_id=device, device_id_type=MESH)
    pl.semaphore_wait(barrier, len(devices))


def halves(rows, columns):
    if rows % 32 == 0:
        return [(pl.ds(k * (rows // 2), rows // 2), pl.ds(0, columns)) for k in range(2)]
    cut = columns // LANES // 2 * LANES
    return [(pl.ds(0, rows), pl.ds(0, cut)), (pl.ds(0, rows), pl.ds(cut, columns - cut))]


def gather_kernel(
    tensor, dp, rows_ref, pack_ref, length_ref, table_ref, x_ref, w_ref, lengths_ref, tables_ref,
    local_sem, block_send, block_recv, pass_send, pass_recv, small_send, small_recv,
    ring_send, ring_recv, core_send, core_recv,
):
    here = Place(tensor, dp)
    c, t, chips = here.core, here.t, here.chips
    nrow = rows_ref.shape[0]
    sibling = here.sibling()
    to_right, to_left = here.neighbour(1), here.neighbour(-1)
    others = [{"tensor": lax.rem(t + k, tensor)} for k in range(1, tensor)]
    meet([to_right, to_left, sibling] + others)

    lengths = pltpu.make_async_remote_copy(
        length_ref, lengths_ref.at[c], small_send.at[0], small_recv.at[0], device_id=sibling, device_id_type=MESH
    )
    lengths.start()
    own_lengths = pltpu.make_async_copy(length_ref, lengths_ref.at[c], local_sem.at[0])
    own_lengths.start()
    own_table = pltpu.make_async_copy(table_ref, tables_ref.at[t], local_sem.at[1])
    own_table.start()
    tables = []
    for k in range(1, tensor):
        tables.append(
            pltpu.make_async_remote_copy(
                table_ref, tables_ref.at[t], small_send.at[k], small_recv.at[k], device_id=others[k - 1], device_id_type=MESH
            )
        )
        tables[-1].start()

    def to_chip(i):
        return pltpu.make_async_remote_copy(
            rows_ref.at[i], x_ref.at[:, t], block_send.at[i], block_recv.at[t],
            device_id={"tensor": nrow * c + i}, device_id_type=MESH,
        )

    def kept(i):
        return pltpu.make_async_copy(rows_ref.at[i], x_ref.at[:, t], local_sem.at[2])

    def kept_pass(i):
        return pltpu.make_async_remote_copy(
            rows_ref.at[i], x_ref.at[:, t], pass_send.at[t], pass_recv.at[t], device_id=sibling, device_id_type=MESH
        )

    def passed(s):
        return pltpu.make_async_remote_copy(
            x_ref.at[:, s], x_ref.at[:, s], pass_send.at[s], pass_recv.at[s], device_id=sibling, device_id_type=MESH
        )

    for i in range(nrow):
        mine = nrow * c + i == t

        @pl.when(mine)
        def _():
            kept(i).start()
            kept_pass(i).start()

        @pl.when(jnp.logical_not(mine))
        def _():
            to_chip(i).start()

    parts = halves(*pack_ref.shape)
    own_pack = pltpu.make_async_copy(pack_ref, w_ref.at[t, here.d], local_sem.at[3])
    own_pack.start()

    def shard(ring, part):
        group, at = here.at(ring)
        return w_ref.at[at, group * CORES + c, parts[part][0], parts[part][1]]

    def source(step, part):
        return lax.rem(here.ring + (1 if part else -1) * step + chips, chips)

    def onward(step, part, first=False):
        slot = shard(source(step, part), part)
        return pltpu.make_async_remote_copy(
            pack_ref.at[parts[part][0], parts[part][1]] if first else slot, slot,
            ring_send.at[part, step], ring_recv.at[part, step],
            device_id=to_left if part else to_right, device_id_type=MESH,
        )

    def across(step, part, first=False):
        slot = shard(source(step, part), part)
        return pltpu.make_async_remote_copy(
            pack_ref.at[parts[part][0], parts[part][1]] if first else slot, slot,
            core_send.at[part, step], core_recv.at[part, step], device_id=sibling, device_id_type=MESH,
        )

    for part in range(2):
        onward(0, part, True).start()
        across(0, part, True).start()

    takes = t // nrow == c
    for s in range(tensor):

        @pl.when(jnp.logical_and(takes, s != t))
        def _():
            pltpu.make_async_remote_copy(
                rows_ref.at[0], x_ref.at[:, s], block_send.at[0], block_recv.at[s], device_id=sibling, device_id_type=MESH
            ).wait_recv()
            passed(s).start()

    @pl.loop(1, chips)
    def _(step):
        for part in range(2):
            onward(step - 1, part).wait_recv()

            @pl.when(step < chips - 1)
            def _():
                onward(step, part).start()

            across(step, part).start()

    @pl.loop(0, chips)
    def _(step):
        for part in range(2):

            @pl.when(step < chips - 1)
            def _():
                onward(step, part).wait_send()

            across(step, part).wait_send()
            across(step, part).wait_recv()

    for i in range(nrow):
        mine = nrow * c + i == t

        @pl.when(mine)
        def _():
            kept(i).wait()
            kept_pass(i).wait_send()

        @pl.when(jnp.logical_not(mine))
        def _():
            to_chip(i).wait_send()

    for s in range(tensor):

        @pl.when(jnp.logical_and(takes, s != t))
        def _():
            passed(s).wait_send()

        @pl.when(jnp.logical_not(takes))
        def _():
            passed(s).wait_recv()

    lengths.wait()
    own_lengths.wait()
    own_table.wait()
    own_pack.wait()
    for table in tables:
        table.wait()


def gather(tensor, dp, rows, pack, lengths, table):
    chips = tensor * dp // CORES
    nrow, two, places, width = rows.shape
    sems = pltpu.SemaphoreType.DMA
    return pl.pallas_call(
        functools.partial(gather_kernel, tensor, dp),
        out_shape=(
            jax.ShapeDtypeStruct((two, tensor, places, width), rows.dtype),
            jax.ShapeDtypeStruct((tensor, dp) + pack.shape, pack.dtype),
            jax.ShapeDtypeStruct((CORES,) + lengths.shape, lengths.dtype),
            jax.ShapeDtypeStruct((tensor,) + table.shape, table.dtype),
        ),
        in_specs=[ANY] * 4,
        out_specs=(ANY,) * 4,
        scratch_shapes=[
            sems((4,)), sems((nrow,)), sems((tensor,)), sems((tensor,)), sems((tensor,)), sems((tensor,)), sems((tensor,)),
            sems((2, chips)), sems((2, chips)), sems((2, chips)), sems((2, chips)),
        ],
        compiler_params=pltpu.CompilerParams(collective_id=0, has_side_effects=True),
        name="gather",
    )(rows, pack, lengths, table)


def scatter_kernel(
    tensor, dp, grads_ref, small_ref, rows_ref, out_ref, small_out, rows_out,
    own, theirs, taken, small_own, small_theirs, small_taken, total,
    own_sem, core_send, core_recv, ring_send, ring_recv,
    sown_sem, score_send, score_recv, sring_send, sring_recv, block_send, block_recv, local_sem,
):
    here = Place(tensor, dp)
    c, t, chips = here.core, here.t, here.chips
    nrow = rows_out.shape[0]
    sibling = here.sibling()
    to_right, to_left = here.neighbour(1), here.neighbour(-1)
    line = [
        {"dp": here.group * CORES + lax.rem(c + j, CORES), "tensor": lax.rem(t + k, tensor)}
        for j in range(CORES)
        for k in range(tensor)
        if j + k > 0
    ]
    meet([to_right, to_left] + line)

    half = tensor // 2
    owner = t // nrow

    def block(k):
        place = here.pipe * (c * half + k % half) + (1 - here.pipe) * k
        which = here.pipe * (k // half) + (1 - here.pipe) * c
        return place, which

    def home(k):
        place, which = block(k)
        slot = rows_out.at[lax.rem(t, nrow), which]
        recv = block_recv.at[lax.rem(t, nrow), which]
        return (
            jnp.logical_and(place == t, owner == c),
            lambda: pltpu.make_async_copy(rows_ref.at[k], slot, recv),
            lambda: pltpu.make_async_remote_copy(
                rows_ref.at[k], slot, block_send.at[k], recv,
                device_id={"dp": here.group * CORES + owner, "tensor": place}, device_id_type=MESH,
            ),
        )

    for k in range(tensor):
        stays, inside, away = home(k)

        @pl.when(stays)
        def _():
            inside().start()

        @pl.when(jnp.logical_not(stays))
        def _():
            away().start()

    def across(ring):
        group, at = here.at(ring)
        return (
            pltpu.make_async_remote_copy(
                grads_ref.at[at, group * CORES + 1 - c], theirs.at[ring], core_send.at[ring], core_recv.at[ring],
                device_id=sibling, device_id_type=MESH,
            ),
            pltpu.make_async_remote_copy(
                small_ref.at[at, group * CORES + 1 - c], small_theirs.at[ring], score_send.at[ring], score_recv.at[ring],
                device_id=sibling, device_id_type=MESH,
            ),
        )

    def fetch(ring):
        group, at = here.at(ring)
        return (
            pltpu.make_async_copy(grads_ref.at[at, group * CORES + c], own.at[ring], own_sem.at[ring]),
            pltpu.make_async_copy(small_ref.at[at, group * CORES + c], small_own.at[ring], sown_sem.at[ring]),
        )

    def behind(step):
        return lax.rem(here.ring - step + chips, chips)

    def order(k):
        off = (2 * lax.rem(k, 2) - 1) * (k // 2 + 1) * (1 - k // (chips - 1))
        return lax.rem(here.ring + chips + off, chips)

    @pl.loop(0, chips)
    def _(k):
        for copy in across(order(k)) + fetch(order(k)):
            copy.start()

    rows, columns = out_ref.shape
    parts = halves(rows, columns)

    def add(ring, part, step, last):
        height = parts[part][0].size
        piece = 16 if height % 16 == 0 else height

        @pl.loop(0, height // piece)
        def _(k):
            at = pl.ds(pl.multiple_of(parts[part][0].start + k * piece, 8), piece)
            where = (at, parts[part][1])
            value = own[(ring,) + where].astype(F32) + theirs[(ring,) + where].astype(F32)
            if step is not None:
                value = value + taken[(step,) + where].astype(F32)
            if last:
                total[where] = value
            else:
                own[(ring,) + where] = value.astype(BF16)

    def onward(ring, step, part):
        where = (parts[part][0], parts[part][1])
        return pltpu.make_async_remote_copy(
            own.at[(ring,) + where], taken.at[(step,) + where], ring_send.at[part, step], ring_recv.at[part, step],
            device_id=to_left if part else to_right, device_id_type=MESH,
        )

    def small_onward(ring, step):
        return pltpu.make_async_remote_copy(
            small_own.at[ring], small_taken.at[step], sring_send.at[step], sring_recv.at[step],
            device_id=to_right, device_id_type=MESH,
        )

    def ready(ring):
        for copy in across(ring):
            copy.wait_recv()
        for copy in fetch(ring):
            copy.wait()

    def ahead(step):
        return lax.rem(here.ring + step, chips)

    half_chips = chips // 2

    @pl.loop(0, chips - 1)
    def _(step):
        right, left = behind(step + 1), ahead(step + 1)

        @pl.when(step < half_chips)
        def _():
            ready(right)

        @pl.when(step < chips - 1 - half_chips)
        def _():
            ready(left)

        @pl.when(step == 0)
        def _():
            add(right, 0, None, False)
            add(left, 1, None, False)
            small_own[right] = small_own[right] + small_theirs[right]

        @pl.when(step > 0)
        def _():
            onward(right, step - 1, 0).wait_recv()
            add(right, 0, step - 1, False)
            onward(right, step, 0).start()
            onward(left, step - 1, 1).wait_recv()
            add(left, 1, step - 1, False)
            onward(left, step, 1).start()
            small_onward(right, step - 1).wait_recv()
            small_own[right] = small_own[right] + small_theirs[right] + small_taken[step - 1]
            small_onward(right, step).start()

        @pl.when(step == 0)
        def _():
            onward(right, 0, 0).start()
            onward(left, 0, 1).start()
            small_onward(right, 0).start()

    ready(here.ring)
    for part in range(2):
        onward(here.ring, chips - 2, part).wait_recv()
        add(here.ring, part, chips - 2, True)
    small_onward(here.ring, chips - 2).wait_recv()
    small_out[...] = small_own[here.ring] + small_theirs[here.ring] + small_taken[chips - 2]
    finish = pltpu.make_async_copy(total, out_ref, local_sem.at[0])
    finish.start()

    @pl.loop(0, chips)
    def _(step):
        @pl.when(step < chips - 1)
        def _():
            onward(behind(step + 1), step, 0).wait_send()
            onward(ahead(step + 1), step, 1).wait_send()
            small_onward(behind(step + 1), step).wait_send()

        for copy in across(step):
            copy.wait_send()

    for k in range(tensor):
        stays, inside, away = home(k)

        @pl.when(jnp.logical_not(stays))
        def _():
            away().wait_send()

    for i in range(nrow):
        for which in range(2):
            pltpu.make_async_copy(rows_ref.at[0], rows_out.at[i, which], block_recv.at[i, which]).wait()
    finish.wait()


def scatter(tensor, dp, grads, small, rows, nrow):
    chips = tensor * dp // CORES
    shard = grads.shape[2:]
    tiny = small.shape[2:]
    sems = pltpu.SemaphoreType.DMA
    return pl.pallas_call(
        functools.partial(scatter_kernel, tensor, dp),
        out_shape=(
            jax.ShapeDtypeStruct(shard, F32),
            jax.ShapeDtypeStruct(tiny, F32),
            jax.ShapeDtypeStruct((nrow, 2) + rows.shape[1:], rows.dtype),
        ),
        in_specs=[ANY] * 3,
        out_specs=(ANY, VMEM, ANY),
        scratch_shapes=[
            pltpu.VMEM((chips,) + shard, BF16),
            pltpu.VMEM((chips,) + shard, BF16),
            pltpu.VMEM((chips - 1,) + shard, BF16),
            pltpu.VMEM((chips,) + tiny, F32),
            pltpu.VMEM((chips,) + tiny, F32),
            pltpu.VMEM((chips - 1,) + tiny, F32),
            pltpu.VMEM(shard, F32),
            sems((chips,)), sems((chips,)), sems((chips,)), sems((2, chips)), sems((2, chips)),
            sems((chips,)), sems((chips,)), sems((chips,)), sems((chips,)), sems((chips,)),
            sems((tensor,)), sems((nrow, 2)), sems((1,)),
        ],
        compiler_params=pltpu.CompilerParams(collective_id=1, has_side_effects=True, vmem_limit_bytes=VMEM_LIMIT),
        name="scatter",
    )(grads, small, rows)


KEY, VALUE, QUERY, OUT, FIRST, SECOND = range(6)
ATTN, CROSS, INNER, OUTER = range(4)
SEGS_HELD = 6


def rms(value):
    return lax.rsqrt(jnp.mean(value * value, axis=-1, keepdims=True) + EPSILON)


def in_rows(count, body, piece=128):
    @pl.loop(0, count // piece)
    def _(k):
        body(pl.ds(pl.multiple_of(k * piece, piece), piece))


def columns_of(count, body, piece=768):
    piece = min(piece, count)

    @pl.loop(0, count // piece)
    def _(k):
        body(pl.ds(pl.multiple_of(k * piece, piece), piece))


def normalize(source, gain, target, count):
    def body(at):
        value = source[at, :].astype(F32)
        target[at, :] = (value * rms(value) * gain).astype(BF16)

    in_rows(count, body)


def normalize_back(source, gain, incoming, total, gain_parts, count, fresh):
    gain_parts[...] = jnp.zeros_like(gain_parts)

    def body(at):
        value, back = source[at, :].astype(F32), incoming[at, :]
        scale = rms(value)
        unit = value * scale
        gain_parts[...] += jnp.sum((back * unit).reshape(-1, 8, back.shape[-1]), axis=0)
        back = back * gain
        back = scale * (back - unit * jnp.mean(back * unit, axis=-1, keepdims=True))
        total[at, :] = back if fresh else total[at, :] + back

    in_rows(count, body)


def project(left, weight, target, count):
    def body(at):
        target[0:count, at] = nn(left[0:count, :], weight[:, at]).astype(target.dtype)

    columns_of(weight.shape[1], body)


def project_back(left, weight, total, count, fresh):
    def body(at):
        value = nt(left[0:count, :], weight[at, :])
        total[0:count, at] = value if fresh else total[0:count, at] + value

    columns_of(weight.shape[0], body)


def to_bf16(source, target, rows):
    def body(at):
        target[at, :] = source[at, :].astype(BF16)

    in_rows(rows, body)


def turn(left, turned, rows):
    def body(at):
        turned[at, 0:rows] = left[0:rows, at].T

    columns_of(left.shape[1], body, LANES)


def lane_half(shape, part):
    return lax.broadcasted_iota(jnp.int32, shape, 1) // HEAD_DIM == part


def attend(keys, values, queries, mixture, probs, rows, span, pairs, mask, bias, after):
    @pl.loop(0, pairs)
    def _(pair):
        lanes = pl.ds(pl.multiple_of(pair * LANES, LANES), LANES)
        key, query = keys[0:span, lanes], queries[0:rows, lanes]
        value_t = values[0:span, lanes].T
        mixed = []
        for part in range(2):
            one = jnp.where(lane_half(query.shape, part), query, jnp.zeros_like(query))
            scores = nt(key, one) + mask[0:span, 0:rows]
            if bias is not None:
                scores = scores + bias(2 * pair + part)
            scores = jnp.exp(scores - jnp.max(scores, axis=0, keepdims=True))
            scores = (scores * (1.0 / jnp.sum(scores, axis=0, keepdims=True))).astype(BF16)
            probs[2 * pair + part, 0:span, 0:rows] = scores
            mixed.append(nn(value_t[part * HEAD_DIM : (part + 1) * HEAD_DIM, :], scores))
        mixture[0:rows, lanes] = jnp.concatenate(mixed, axis=0).T.astype(BF16)
        after(pair)


def attend_back(keys, values, queries, back, probs, rows, span, pairs, each, before, after):
    @pl.loop(0, pairs)
    def _(pair):
        before(pair)
        lanes = pl.ds(pl.multiple_of(pair * LANES, LANES), LANES)
        key, value = keys[0:span, lanes], values[0:span, lanes]
        query, given = queries[0:rows, lanes], back[0:rows, lanes]
        key_t = key.T
        d_key, d_value, d_query = None, None, []
        for part in range(2):
            side = lane_half(query.shape, part)
            query_one = jnp.where(side, query, jnp.zeros_like(query))
            given_one = jnp.where(side, given, jnp.zeros_like(given))
            prob = probs[2 * pair + part, 0:span, 0:rows]
            wide = prob.astype(F32)
            d_prob = nt(value, given_one)
            d_score = (wide * (d_prob - jnp.sum(wide * d_prob, axis=0, keepdims=True))).astype(BF16)
            if each is not None:
                each(2 * pair + part, d_score)
            of_key, of_value = nn(d_score, query_one), nn(prob, given_one)
            d_key = of_key if d_key is None else d_key + of_key
            d_value = of_value if d_value is None else d_value + of_value
            d_query.append(nn(key_t[part * HEAD_DIM : (part + 1) * HEAD_DIM, :], d_score))
        keys[0:span, lanes] = d_key.astype(BF16)
        values[0:span, lanes] = d_value.astype(BF16)
        queries[0:rows, lanes] = jnp.concatenate(d_query, axis=0).T.astype(BF16)
        after(pair)


def segments(lengths_row, shape, axis, first):
    lane = lax.broadcasted_iota(jnp.int32, lengths_row.shape, 1)
    places = lax.broadcasted_iota(jnp.int32, shape, axis) + first
    ids = jnp.zeros(shape, jnp.int32)
    for c in range(SEGS_HELD):
        bound = jnp.sum(jnp.where(lane <= c, lengths_row, 0), axis=1, keepdims=True)
        ids = ids + (places >= bound).astype(jnp.int32)
    return ids


def masked(allowed):
    return jnp.where(allowed, 0.0, NEGATIVE).astype(F32)


def nothing(*unused, **named):
    pass


def work(r, here, supply, drain, tensor, heads_at):
    c, t = here.core, here.t
    width = r.hidden.shape[1]
    tall = r.hidden.shape[0]
    block = width // tensor
    half_width = width // 2
    units = r.inner.shape[2]
    places = r.x.shape[2]
    sibling = here.sibling()
    across = [{"pipe": 1 - here.pipe, "dp": here.group * CORES + k} for k in range(CORES)]
    nrow = tensor // CORES
    rows_e, span_e, rows_d, span_d = tall // 2, tall, tall // 4, tall // 2
    pairs_here = half_width // LANES
    near_lanes = pl.ds(pl.multiple_of(c * half_width, half_width), half_width)
    far_lanes = pl.ds(pl.multiple_of((1 - c) * half_width, half_width), half_width)
    lane_halves = [slice(k * half_width, (k + 1) * half_width) for k in range(CORES)]

    def move(source, target, sends, recvs, device):
        return pltpu.make_async_remote_copy(
            source, target, r.send_sem.at[sends], r.recv_sem.at[recvs], device_id=device, device_id_type=MESH
        )

    def lengths_row(first):
        return r.lengths[t // nrow, pl.ds(first + lax.rem(t, nrow), 1), :]

    def pair_lanes(pair):
        return pl.ds(pair * LANES if isinstance(pair, int) else pl.multiple_of(pair * LANES, LANES), LANES)

    def vector_row(head):
        return (head // heads_at) * 8 + lax.rem(head, heads_at)

    def bias_vectors():
        enc, dec = r.enc_buckets.shape[1], r.dec_buckets.shape[1]
        r.buckets[...] = jnp.zeros_like(r.buckets)

        @pl.when(here.pipe == 0)
        def _():
            r.buckets[0:1, 0:enc] = r.enc_buckets[...]

        @pl.when(here.pipe == 1)
        def _():
            r.buckets[0:1, dec - 1 : 2 * dec - 1] = r.dec_buckets[...]

        buckets = lax.broadcasted_iota(jnp.int32, r.onehot.shape, 0) == r.buckets[0:1, :]
        r.onehot[...] = buckets.astype(F32)
        for tt in range(tensor):
            r.vectors[pl.ds(8 * tt, 8), :] = lax.dot_general(
                r.tables[tt][:, 0 : r.onehot.shape[0]], r.onehot[...], (((1,), (0,)), ((), ())),
                precision=lax.Precision.HIGHEST, preferred_element_type=F32,
            )

    def rows_ready(span, rows, first_block):
        @pl.loop(0, span // places)
        def _(k):
            value = r.x[k // tensor, lax.rem(k, tensor)].astype(F32)
            at = pl.ds(pl.multiple_of(k * places, places), places)
            r.hidden[at, :] = (value * rms(value) * r.gains[0]).astype(BF16)

        for k in range(rows // places):
            r.own_x[k * places : (k + 1) * places, :] = r.x[first_block // tensor, lax.rem(first_block, tensor) + k]

    def untangle(source, first, count):
        def body(at):
            for tt in range(tensor):
                for k in range(count):
                    r.square[first + k, at, tt * block : (tt + 1) * block] = source[tt, at, k * block : (k + 1) * block]

        in_rows(width, body, 128)

    def self_forward(span, rows, first_row, group):
        def bias(head):
            pieces = []
            for j in range(span // LANES):
                start = pl.multiple_of(first_row + span - LANES - j * LANES, LANES)
                row = r.vectors[pl.ds(vector_row(head), 1), pl.ds(start, rows + LANES)]
                wide = jnp.broadcast_to(row, (LANES, rows + LANES))
                pieces.append(pltpu.roll(wide, rows + 1, 1, stride=1, stride_axis=0)[:, 0:rows])
            return jnp.concatenate(pieces, axis=0)

        untangle(r.raw_a, KEY, 2)
        untangle(r.raw_a.at[:, :, pl.ds(2 * block, 2 * block)], QUERY, 2)
        project(r.hidden, r.square.at[KEY], r.keys, span)
        supply.pump()
        project(r.hidden, r.square.at[VALUE], r.values, span)
        project(r.hidden.at[pl.ds(first_row, rows)], r.square.at[QUERY], r.queries, rows)
        supply.pump()
        after = at_each(range(width // LANES), supply.pump)

        attend(r.keys, r.values, r.queries, r.mixture, r.probs, rows, span, width // LANES, r.mask, bias, after)
        project_back(r.mixture, r.square.at[OUT], r.resid_mid, rows, True)

        def add(at):
            r.resid_mid[at, :] += r.own_x[at, :].astype(F32)

        in_rows(rows, add)
        supply.pump(until=group)
        supply.finish(group)

    def at_each(places, do):
        def hook(n):
            for place in places:

                @pl.when(n == place)
                def _():
                    do()

        return hook

    def feed_forward(rows, hook=nothing):
        @pl.loop(0, tensor)
        def _(tt):
            def body(at):
                value = nn(r.second[0:rows, :], r.inner[tt, :, at])
                cdf = 0.5 * (1.0 + lax.erf(value * 0.7071067811865476))
                r.ff[tt, 0:rows, at] = (value * cdf).astype(BF16)
                slope = cdf + value * jnp.exp(-0.5 * value * value) * 0.3989422804014327
                r.ff[tensor + tt, 0:rows, at] = slope.astype(BF16)

            columns_of(units, body)
            hook(tt)

    def feed_out(target, rows, hook=nothing):
        @pl.loop(0, tensor)
        def _(tt):
            def body(at):
                target[0:rows, at] += nt(r.ff[tt, 0:rows, :], r.outer[tt, at, :])

            columns_of(width, body)
            hook(tt)

    def feed_back(rows, ready, hook=nothing):
        r.summed[0:rows, :] = jnp.zeros((rows, width), F32)

        @pl.loop(0, tensor)
        def _(tt):
            def body(at):
                if ready:
                    value = r.ff[tensor + tt, rows : 2 * rows, at].astype(F32)
                else:
                    value = nn(r.d_branch[0:rows, :], r.outer[tt, :, at])
                r.ff[tensor + tt, 0:rows, at] = (value * r.ff[tensor + tt, 0:rows, at].astype(F32)).astype(BF16)

            columns_of(units, body)

            def back(at):
                r.summed[0:rows, at] += nt(r.ff[tensor + tt, 0:rows, :], r.inner[tt, at, :])

            columns_of(width, back)
            hook(tt)

    def feed_grads(rows, turned, first, which, hook=nothing):
        @pl.loop(0, tensor)
        def _(tt):
            slot = lax.rem(tt, 2)

            @pl.when(tt >= 2)
            def _():
                drain.release(which, tt - 2, slot)

            def body(at):
                r.stage[slot, :, at] = nn(turned[:, 0:rows], r.ff[first + tt, 0:rows, at]).astype(BF16)

            columns_of(units, body)
            drain.emit(which, tt, slot)
            hook(tt)

        for tt in range(tensor - 2, tensor):
            drain.release(which, tt, tt % 2)

    def square_grads(rows, which, products, hook):
        for k in range(tensor // 2):
            for j, (turned, right) in enumerate(products):

                def body(at):
                    value = nn(turned[at, 0:rows], right[0:rows, 2 * k * block : 2 * (k + 1) * block]).astype(BF16)
                    for slot in range(2):
                        r.stage[slot, at, j * block : (j + 1) * block] = value[:, slot * block : (slot + 1) * block]

                in_rows(width, body, 256)
            for slot in range(2):
                drain.emit(which, 2 * k + slot, slot)
            hook(k)
            for slot in range(2):
                drain.release(which, 2 * k + slot, slot)

    def gain_done(which):
        r.gains_out[which : which + 1, :] = jnp.sum(r.gain_parts[...], axis=0, keepdims=True)

    def self_backward(span, rows, first_row, steps, send_rows):
        mirror = (
            lax.broadcasted_iota(jnp.int32, (LANES, LANES), 0) + lax.broadcasted_iota(jnp.int32, (LANES, LANES), 1)
            == LANES - 1
        ).astype(BF16)
        to_bf16(r.d_resid, r.branch, rows)
        project(r.branch, r.square.at[OUT], r.d_branch, rows)
        r.diagonals[...] = jnp.zeros_like(r.diagonals)

        def each(head, d_score):
            for j in range(span // LANES):
                start = pl.multiple_of(first_row + span - LANES - j * LANES, LANES)
                piece = nn(mirror, d_score[j * LANES : (j + 1) * LANES, :])
                piece = jnp.concatenate([piece, jnp.zeros((LANES, LANES), F32)], axis=1)
                piece = pltpu.roll(piece, 0, 1, stride=1, stride_axis=0)
                at = (pl.ds(vector_row(head), 1), pl.ds(start, rows + LANES))
                r.diagonals[at] += jnp.sum(piece, axis=0, keepdims=True)

        pairs = width // LANES
        attend_back(
            r.keys, r.values, r.queries, r.d_branch, r.probs, rows, span, pairs, each, nothing,
            at_each(range(pairs), steps),
        )
        far = pl.ds(pl.multiple_of((1 - c) * rows, rows), rows)
        near = pl.ds(pl.multiple_of(c * rows, rows), rows)
        trades = [
            move(source.at[far], r.taken_pair.at[k, pl.ds(0, rows)], 12 + k, 12 + k, sibling)
            for k, source in enumerate((r.keys, r.values))
        ]
        for trade in trades:
            trade.start()
        steps()
        turn(r.branch, r.turned, rows)
        turn(r.hidden.at[pl.ds(first_row, rows)], r.turned_more, rows)
        for tt in range(tensor):
            at = pl.ds(8 * tt, 8)
            r.bias_out[at, 0 : r.onehot.shape[0]] = lax.dot_general(
                r.diagonals[at, :], r.onehot[...], (((1,), (1,)), ((), ())),
                precision=lax.Precision.HIGHEST, preferred_element_type=F32,
            )
        steps()
        project_back(r.queries, r.square.at[QUERY], r.summed, rows, True)
        for trade in trades:
            trade.wait_recv()
        steps()
        for k, source in enumerate((r.keys, r.values)):
            r.d_pair[k, 0:rows, :] = (source[near, :].astype(F32) + r.taken_pair[k, 0:rows, :].astype(F32)).astype(BF16)
        project_back(r.d_pair.at[0], r.square.at[KEY], r.summed, rows, False)
        project_back(r.d_pair.at[1], r.square.at[VALUE], r.summed, rows, False)
        steps()
        normalize_back(r.own_x, r.gains[0], r.summed, r.d_resid, r.gain_parts, rows, False)
        gain_done(0)
        steps()
        send_rows()
        drain.small_begin()
        drain.allow(2)
        products = [(r.turned_more, r.d_pair.at[0]), (r.turned_more, r.d_pair.at[1]), (r.turned_more, r.queries), (r.turned, r.mixture)]
        square_grads(rows, ATTN, products, nothing)
        for trade in trades:
            trade.wait_send()
        steps()
        drain.begin(ATTN)
        steps()
        drain.rest(ATTN)

    def parts_of(array):
        return [array.at[pl.ds(k * rows_d, rows_d)] for k in range(CORES)]

    def part_here(array):
        return array.at[pl.ds(pl.multiple_of(c * rows_d, rows_d), rows_d)]

    r.gains_out[...] = jnp.zeros_like(r.gains_out)
    r.bias_out[...] = jnp.zeros_like(r.bias_out)
    supply.start()

    def entry():
        supply.pump(2)
        supply.small()
        bias_vectors()
        supply.pump(2)
        supply.rows()

    def schedule(*items):
        left = list(items)

        def steps():
            for name, group, *n in left.pop(0) if left else ():
                getattr(drain, name)(group, *n)

        return steps

    @pl.when(here.pipe == 0)
    def _():
        supply.resume(ATTN, INNER, OUTER, CROSS)
        drain.order(CROSS, OUTER, INNER, ATTN)
        entry()
        rows, span = rows_e, span_e
        first_row = pl.multiple_of(c * rows, rows)
        seg_rows = segments(lengths_row(0), (span, 1), 0, 0)
        r.mask[...] = masked(seg_rows == segments(lengths_row(0), (1, rows), 1, first_row))
        supply.pump()
        rows_ready(span, rows, c * tensor)
        supply.pump(until=ATTN)
        supply.finish(ATTN)
        self_forward(span, rows, first_row, INNER)
        normalize(r.resid_mid, r.gains[1], r.second, rows)
        feed_forward(rows, at_each((1, 2, 3), supply.pump))
        supply.pump(until=OUTER)
        supply.finish(OUTER)
        r.resid_top[...] = r.resid_mid[...]
        feed_out(r.resid_top, rows, at_each((1, 2, 3), supply.pump))
        normalize(r.resid_top, r.gains[2], r.third, rows)
        r.mask[...] = masked(seg_rows == segments(lengths_row(nrow), (1, span_d), 1, 0))
        supply.pump(until=CROSS)
        supply.finish(CROSS)
        untangle(r.raw_c, FIRST, 2)
        mine = pl.ds(first_row, rows)
        other = pl.ds(pl.multiple_of((1 - c) * rows, rows), rows)
        trades = []
        for k, held in enumerate((r.cross_keys, r.cross_values)):
            r.send_pair[k] = nn(r.third[...], r.square[FIRST + k, :, far_lanes]).astype(BF16)
            trades.append(move(r.send_pair.at[k], held.at[mine], k, k, sibling))
            trades[-1].start()
        for k, held in enumerate((r.cross_keys, r.cross_values)):
            held[mine, :] = nn(r.third[...], r.square[FIRST + k, :, near_lanes]).astype(BF16)
        for k, part in enumerate(parts_of(r.cross_queries)):
            move(part, part, 2 + k, 2 + k, across[k]).wait_recv()
        for k, held in enumerate((r.cross_keys, r.cross_values)):
            move(r.send_pair.at[k], held.at[other], k, k, sibling).wait_recv()

        def mixtures(pair):
            at = pair_lanes(pair)
            return [
                pltpu.make_async_remote_copy(
                    r.cross_mixture.at[pl.ds(k * rows_d, rows_d), at], r.cross_in.at[c, :, at],
                    r.mix_send.at[k, pair], r.mix_recv.at[c, pair], device_id=across[k], device_id_type=MESH,
                )
                for k in range(CORES)
            ]

        def arrived(pair):
            for k in range(CORES):
                part = r.cross_back.at[pl.ds(k * rows_d, rows_d), pair_lanes(pair)]
                pltpu.make_async_remote_copy(
                    part, part, r.back_send.at[k, pair], r.back_recv.at[k, pair], device_id=across[k], device_id_type=MESH
                ).wait_recv()

        def returns(pair):
            at = pair_lanes(pair)
            return [
                pltpu.make_async_remote_copy(
                    d_cross.at[other, at], r.cross_taken.at[k, :, at],
                    r.give_send.at[k, pair], r.give_recv.at[k, pair], device_id=sibling, device_id_type=MESH,
                )
                for k, d_cross in enumerate((r.cross_keys, r.cross_values))
            ]

        attend(
            r.cross_keys, r.cross_values, r.cross_queries, r.cross_mixture, r.cross_probs, span_d, span, pairs_here,
            r.mask, None, lambda pair: [mix.start() for mix in mixtures(pair)],
        )
        supply.close()
        drain.free(0)
        turn(r.third, r.turned, rows)
        attend_back(
            r.cross_keys, r.cross_values, r.cross_queries, r.cross_back, r.cross_probs, span_d, span, pairs_here, None,
            arrived, lambda pair: [back.start() for back in returns(pair)],
        )
        answers = [
            move(part, r.cross_in_back.at[c], 8 + k, 8 + c, across[k]) for k, part in enumerate(parts_of(r.cross_queries))
        ]
        for answer in answers:
            answer.start()
        for k, d_cross in enumerate((r.cross_keys, r.cross_values)):
            r.d_pair[k, :, near_lanes] = d_cross[mine, :]
        for pair in range(pairs_here):
            for back in returns(pair):
                back.wait_recv()
        for k in range(2):
            r.d_pair[k, :, far_lanes] = r.cross_taken[k]
        drain.allow(0)
        square_grads(rows, CROSS, [(r.turned, r.d_pair.at[0]), (r.turned, r.d_pair.at[1])], nothing)
        drain.begin(CROSS)
        project_back(r.d_pair.at[0], r.square.at[FIRST], r.summed, rows, True)
        project_back(r.d_pair.at[1], r.square.at[SECOND], r.summed, rows, False)
        normalize_back(r.resid_top, r.gains[2], r.summed, r.d_resid, r.gain_parts, rows, True)
        gain_done(2)
        to_bf16(r.d_resid, r.d_branch, rows)
        turn(r.d_branch, r.turned, rows)
        feed_grads(rows, r.turned, 0, OUTER, at_each((2,), lambda: drain.tick(CROSS, 0)))
        drain.tick(CROSS, 1)
        drain.begin(OUTER)
        feed_back(rows, False, at_each((1, 2), schedule([("tick", CROSS, 2)], [("tick", CROSS, 3)])))
        drain.free(1)
        drain.free(2)
        turn(r.second, r.turned, rows)
        drain.allow(1)
        feed_grads(rows, r.turned, tensor, INNER, at_each((1,), lambda: drain.tick(OUTER, 0)))
        normalize_back(r.resid_mid, r.gains[1], r.summed, r.d_resid, r.gain_parts, rows, False)
        gain_done(1)
        for copy in trades + answers:
            copy.wait_send()
        for pair in range(pairs_here):
            for copy in mixtures(pair) + returns(pair):
                copy.wait_send()

        def send_rows():
            to_bf16(r.d_resid, r.rows_out, rows)
            drain.home()

        steps = schedule(
            [("tick", CROSS, 4), ("begin", INNER)], [("tick", OUTER, 1)],
            [], [("end", CROSS)], [], [("tick", OUTER, 2)],
            [("tick", INNER, 0)], [], [("tick", INNER, 1)], [], [("tick", OUTER, 3)], [("tick", OUTER, 4)],
            [("tick", INNER, 2), ("tick", ATTN, 0), ("end", OUTER), ("tick", INNER, 3), ("tick", ATTN, 1), ("tick", ATTN, 2)]
            + [("home_done", None), ("tick", INNER, 4), ("tick", ATTN, 3), ("tick", ATTN, 4), ("end", INNER)],
        )
        self_backward(span, rows, first_row, steps, send_rows)

    @pl.when(here.pipe == 1)
    def _():
        supply.resume(ATTN, CROSS, INNER, OUTER)
        drain.order(OUTER, INNER, CROSS, ATTN)
        entry()
        rows, span = rows_d, span_d
        first_row = pl.multiple_of(c * rows, rows)
        key_at = lax.broadcasted_iota(jnp.int32, (span, rows), 0)
        query_at = lax.broadcasted_iota(jnp.int32, (span, rows), 1) + first_row
        same = segments(lengths_row(nrow), (span, 1), 0, 0) == segments(lengths_row(nrow), (1, rows), 1, first_row)
        r.mask[0:span, 0:rows] = masked(same & (query_at >= key_at))
        supply.pump()
        first_block = c * (tensor // 2)
        rows_ready(span, rows, first_block)
        for k in range(rows // places):
            r.d_branch[k * places : (k + 1) * places, :] = r.x[1, first_block + k]
        supply.pump(until=ATTN)
        supply.finish(ATTN)
        self_forward(span, rows, first_row, CROSS)
        untangle(r.raw_c, FIRST, 2)
        normalize(r.resid_mid, r.gains[1], r.third, rows)
        project(r.third, r.square.at[FIRST], r.joined, rows)
        asks = []
        for k in range(CORES):
            r.send_pair[k, 0:rows, :] = r.joined[:, lane_halves[k]]
            asks.append(move(r.send_pair.at[k, pl.ds(0, rows)], part_here(r.cross_queries), 2 + k, 2 + c, across[k]))
            asks[-1].start()
        supply.pump(until=INNER)
        supply.finish(INNER)
        supply.pump(until=OUTER)
        supply.finish(OUTER)

        @pl.loop(0, tensor)
        def _(tt):
            def body(at):
                r.ff[tensor + tt, rows : 2 * rows, at] = nn(r.d_branch[0:rows, :], r.outer[tt, :, at]).astype(BF16)

            columns_of(units, body)

        supply.close()
        drain.free(0)
        r.resid_top[0:rows, :] = r.resid_mid[0:rows, :]
        for k in range(CORES):
            for pair in range(pairs_here):
                part = r.cross_in.at[k, :, pair_lanes(pair)]
                pltpu.make_async_remote_copy(
                    part, part, r.mix_send.at[k, pair], r.mix_recv.at[k, pair], device_id=across[k], device_id_type=MESH
                ).wait_recv()
            r.joined[:, lane_halves[k]] = r.cross_in[k]
        project_back(r.joined, r.square.at[SECOND], r.resid_top, rows, False)
        normalize(r.resid_top, r.gains[2], r.second, rows)
        feed_forward(rows)
        feed_back(rows, True)
        r.d_resid[0:rows, :] = r.d_branch[0:rows, :].astype(F32)
        normalize_back(r.resid_top, r.gains[2], r.summed, r.d_resid, r.gain_parts, rows, False)
        gain_done(2)
        to_bf16(r.d_resid, r.branch, rows)
        tells = []
        for pair in range(pairs_here):
            at = pair_lanes(pair)
            firsts = [k * half_width + pair * LANES for k in range(CORES)]
            both = jnp.concatenate([r.square[SECOND, :, first : first + LANES] for first in firsts], axis=1)
            value = nn(r.branch[0:rows, :], both).astype(BF16)
            for k in range(CORES):
                r.send_back[k, :, at] = value[:, k * LANES : (k + 1) * LANES]
                tells.append(
                    pltpu.make_async_remote_copy(
                        r.send_back.at[k, :, at], r.cross_back.at[pl.ds(pl.multiple_of(c * rows, rows), rows), at],
                        r.back_send.at[k, pair], r.back_recv.at[c, pair], device_id=across[k], device_id_type=MESH,
                    )
                )
                tells[-1].start()
        drain.free(1)
        turn(r.d_branch, r.turned, rows)
        drain.allow(0)
        feed_grads(rows, r.turned, 0, OUTER)
        drain.begin(OUTER)
        turn(r.second, r.turned, rows)
        drain.allow(1)
        feed_grads(rows, r.turned, tensor, INNER)
        drain.begin(INNER)
        feed_out(r.resid_top, rows, at_each((1,), lambda: drain.tick(OUTER, 0)))
        drain.free(2)
        to_bf16(r.resid_top, r.rows_out, rows)
        turn(r.branch, r.turned, rows)
        turn(r.third, r.turned_more, rows)
        for k in range(CORES):
            move(r.cross_in_back.at[k], r.cross_in_back.at[k], 8 + k, 8 + k, across[k]).wait_recv()
            r.d_pair[1, 0:rows, lane_halves[k]] = r.cross_in_back[k]
        project_back(r.d_pair.at[1], r.square.at[FIRST], r.summed, rows, True)
        square_grads(rows, CROSS, [(r.turned_more, r.d_pair.at[1]), (r.turned, r.joined)], nothing)
        drain.tick(OUTER, 1)
        normalize_back(r.resid_mid, r.gains[1], r.summed, r.d_resid, r.gain_parts, rows, False)
        gain_done(1)
        for copy in asks + tells:
            copy.wait_send()

        def send_rows():
            to_bf16(r.d_resid, r.rows_out.at[pl.ds(rows, rows)], rows)
            drain.home()

        steps = schedule(
            [], [("tick", INNER, 0)], [], [("tick", INNER, 1)], [("tick", OUTER, 2)], [],
            [("tick", OUTER, 3)], [], [("tick", INNER, 2), ("tick", OUTER, 4)], [("begin", CROSS)],
            [("tick", INNER, 3), ("tick", INNER, 4)], [],
            [("end", OUTER), ("tick", CROSS, 0), ("tick", ATTN, 0), ("tick", CROSS, 1), ("end", INNER), ("tick", ATTN, 1)]
            + [("tick", ATTN, 2), ("tick", CROSS, 2), ("home_done", None), ("tick", ATTN, 3), ("tick", ATTN, 4)]
            + [("tick", CROSS, 3), ("tick", CROSS, 4), ("end", CROSS)],
        )
        self_backward(span, rows, first_row, steps, send_rows)

    drain.close()


def held(*shape, dtype=BF16):
    return pltpu.VMEM(shape, dtype)


def arrays(tensor, heads_at, places, width, units, ranges, kinds):
    tall = 2 * tensor * places
    block = width // tensor
    half_rows, half_width = tall // 2, width // 2
    heads = heads_at * tensor
    return dict(
        x=held(2, tensor, places, width),
        own_x=held(half_rows, width),
        raw_a=held(tensor, width, 4 * block),
        raw_c=held(tensor, width, 2 * block),
        square=held(6, width, width),
        inner=held(tensor, width, units),
        outer=held(tensor, width, units),
        hidden=held(tall, width),
        keys=held(tall, width),
        values=held(tall, width),
        queries=held(half_rows, width),
        probs=held(heads, tall, half_rows),
        mask=held(tall, half_rows, dtype=F32),
        mixture=held(half_rows, width),
        resid_mid=held(half_rows, width, dtype=F32),
        resid_top=held(half_rows, width, dtype=F32),
        d_resid=held(half_rows, width, dtype=F32),
        summed=held(half_rows, width, dtype=F32),
        second=held(half_rows, width),
        third=held(half_rows, width),
        ff=held(2 * tensor, half_rows, units),
        d_branch=held(half_rows, width),
        branch=held(half_rows, width),
        cross_keys=held(tall, half_width),
        cross_values=held(tall, half_width),
        cross_queries=held(half_rows, half_width),
        cross_mixture=held(half_rows, half_width),
        cross_probs=held(heads // CORES, tall, half_rows),
        cross_back=held(half_rows, half_width),
        cross_in=held(CORES, half_rows // 2, half_width),
        cross_in_back=held(CORES, half_rows // 2, half_width),
        cross_taken=held(CORES, half_rows, half_width),
        send_pair=held(CORES, half_rows, half_width),
        send_back=held(CORES, half_rows // 2, half_width),
        joined=held(half_rows // 2, width),
        taken_pair=held(2, half_rows, width),
        d_pair=held(2, half_rows, width),
        turned=held(width, half_rows),
        turned_more=held(width, half_rows),
        stage=held(2, width, units),
        vectors=held(8 * tensor, ranges, dtype=F32),
        diagonals=held(8 * tensor, ranges, dtype=F32),
        onehot=held(kinds, ranges, dtype=F32),
        buckets=held(8, ranges, dtype=jnp.int32),
        gain_parts=held(8, width, dtype=F32),
        send_sem=pltpu.SemaphoreType.DMA((14,)),
        recv_sem=pltpu.SemaphoreType.DMA((14,)),
        **{
            name: pltpu.SemaphoreType.DMA((CORES, half_width // LANES))
            for name in ("mix_send", "mix_recv", "back_send", "back_recv", "give_send", "give_recv")
        },
    )


def group_columns(block, units):
    return {ATTN: (0, 4 * block), CROSS: (4 * block, 2 * block), INNER: (6 * block, units), OUTER: (6 * block + units, units)}


def landing(r):
    return {ATTN: r.raw_a, CROSS: r.raw_c, INNER: r.inner, OUTER: r.outer}


class Loads:
    def __init__(self, r, tensor, x_hbm, w_hbm, sems):
        columns = group_columns(r.raw_a.shape[2] // 4, r.inner.shape[2])
        self.x = pltpu.make_async_copy(x_hbm, r.x, sems.at[4, 0])
        self.weights = [
            [
                pltpu.make_async_copy(w_hbm.at[tt, :, pl.ds(*columns[group])], target.at[tt], sems.at[group, tt])
                for tt in range(tensor)
            ]
            for group, target in landing(r).items()
        ]

    def start(self):
        self.x.start()
        for group in self.weights:
            for copy in group:
                copy.start()

    def rows(self):
        self.x.wait()

    def finish(self, group):
        for copy in self.weights[group]:
            copy.wait()

    small = resume = pump = close = nothing


class Stores:
    def __init__(self, r, grads_hbm, sems):
        self.columns = group_columns(r.raw_a.shape[2] // 4, r.inner.shape[2])
        self.r, self.grads, self.sems = r, grads_hbm, sems

    def copy(self, group, tt, slot):
        first, wide = self.columns[group]
        return pltpu.make_async_copy(
            self.r.stage.at[slot, :, pl.ds(0, wide)], self.grads.at[tt, :, pl.ds(first, wide)], self.sems.at[slot]
        )

    def emit(self, group, tt, slot):
        self.copy(group, tt, slot).start()

    def release(self, group, tt, slot):
        self.copy(group, tt, slot).wait()

    order = free = allow = begin = tick = rest = end = home = home_done = small_begin = close = nothing


def blocks_kernel(tensor, dp, heads_at, names, *refs):
    here = Place(tensor, dp)
    r = types.SimpleNamespace(**dict(zip(names, refs)))
    across = [{"pipe": 1 - here.pipe, "dp": here.group * CORES + k} for k in range(CORES)]
    meet([here.sibling()] + across)
    work(r, here, Loads(r, tensor, r.x_hbm, r.w_hbm, r.load_sem), Stores(r, r.grads_hbm, r.stage_sem), tensor, heads_at)


def blocks(tensor, dp, heads_at, kinds, rows, weights, gains, lengths, tables, buckets):
    places, width = rows.shape[2:]
    units = (weights.shape[2] - 6 * (width // tensor)) // 2
    half_rows = tensor * places
    ranges = -(-buckets[0].shape[1] // LANES) * LANES
    scratch = arrays(tensor, heads_at, places, width, units, ranges, kinds)
    scratch["load_sem"] = pltpu.SemaphoreType.DMA((5, tensor))
    scratch["stage_sem"] = pltpu.SemaphoreType.DMA((2,))
    names = ["x_hbm", "w_hbm", "gains", "lengths", "tables", "enc_buckets", "dec_buckets", "grads_hbm", "rows_out", "gains_out", "bias_out"]
    return pl.pallas_call(
        functools.partial(blocks_kernel, tensor, dp, heads_at, names + list(scratch)),
        out_shape=(
            jax.ShapeDtypeStruct(weights.shape, BF16),
            jax.ShapeDtypeStruct((half_rows, width), BF16),
            jax.ShapeDtypeStruct((8, width), F32),
            jax.ShapeDtypeStruct((8 * tensor, LANES), F32),
        ),
        in_specs=[ANY, ANY] + [VMEM] * 5,
        out_specs=(ANY, VMEM, VMEM, VMEM),
        scratch_shapes=list(scratch.values()),
        compiler_params=pltpu.CompilerParams(collective_id=2, has_side_effects=True, vmem_limit_bytes=VMEM_LIMIT),
        name="blocks",
    )(rows, weights, gains, lengths, tables, *buckets)


def all_sends(r, box, group, depth, hops, targets):
    for part in range(2):
        sent = box.at[0, pl.ds(0, (2 * hops - 1) * depth // 2), :]
        pltpu.make_async_remote_copy(
            sent, sent, r.ring_send.at[group, part], r.ring_recv.at[group, part, 0, 0],
            device_id=targets[part], device_id_type=MESH,
        ).wait_send()


def all_over(r, box, group, here, depth):
    whole = box.at[pl.ds(0, here.chips * depth // box.shape[1])]
    return pltpu.make_async_remote_copy(
        whole, whole, r.over_send.at[group], r.over_recv.at[group], device_id=here.sibling(), device_id_type=MESH
    )


class Rings:
    def __init__(self, r, here, tensor, dp):
        self.r, self.here, self.tensor, self.dp = r, here, tensor, dp
        self.depth = r.value_w.shape[0]
        self.hops = here.chips // 2
        self.count = 2 * self.hops - 1
        self.sibling = here.sibling()
        self.targets = [here.neighbour(1), here.neighbour(-1)]
        self.landing = landing(r)
        self.groups = []
        self.plan = []


    def order(self, *groups):
        steps = []
        for k, group in enumerate(groups):
            steps.append((4 * k - 0.5, k, self.begin, group, None))
            late = {self.count - 3: 3.6, self.count - 2: 3.7, self.count - 1: 5.5}
            steps += [(4 * k + late.get(n, n), k, self.tick, group, n) for n in range(self.count)]
        steps.sort(key=lambda step: step[:2])
        self.groups = list(groups)
        self.plan = [step[2:] for step in steps]

    def resume(self, *groups):
        self.order(*groups)
        self.plan.pop(0)

    def pump(self, count=1, until=None):
        while self.plan and (count > 0 if until is None else any(step[1] == until for step in self.plan)):
            do, group, n = self.plan.pop(0)
            do(group) if n is None else do(group, n)
            count -= 0 if n is None else 1


    def block_out(self, i):
        r, t, c = self.r, self.here.t, self.here.core
        return pltpu.make_async_remote_copy(
            r.rows.at[i], r.x.at[:, t], r.block_send.at[i], r.block_recv.at[t],
            device_id={"tensor": r.rows.shape[0] * c + i}, device_id_type=MESH,
        )

    def block_kept(self, i):
        return pltpu.make_async_copy(self.r.rows.at[i], self.r.x.at[:, self.here.t], self.r.local_sem.at[0])

    def block_pass(self, source, s):
        r = self.r
        return pltpu.make_async_remote_copy(
            source, r.x.at[:, s], r.pass_send.at[s], r.pass_recv.at[s], device_id=self.sibling, device_id_type=MESH
        )

    def blocks(self, mine, others):
        for i in range(self.r.rows.shape[0]):
            here = self.r.rows.shape[0] * self.here.core + i == self.here.t

            @pl.when(here)
            def _():
                mine(i)

            @pl.when(jnp.logical_not(here))
            def _():
                others(i)

    def small_copies(self):
        r, t = self.r, self.here.t
        copies = [
            pltpu.make_async_remote_copy(
                r.lengths_in, r.lengths.at[self.here.core], r.small_send.at[0], r.small_recv.at[0],
                device_id=self.sibling, device_id_type=MESH,
            ),
            pltpu.make_async_copy(r.lengths_in, r.lengths.at[self.here.core], r.local_sem.at[1]),
            pltpu.make_async_copy(r.table_in, r.tables.at[t], r.local_sem.at[2]),
        ]
        for k in range(1, self.tensor):
            copies.append(
                pltpu.make_async_remote_copy(
                    r.table_in, r.tables.at[t], r.small_send.at[k], r.small_recv.at[k],
                    device_id={"tensor": lax.rem(t + k, self.tensor)}, device_id_type=MESH,
                )
            )
        return copies


    def rows_of(self, ring):
        line, at = self.here.at(ring)
        return at, pl.multiple_of((line * CORES + self.here.core) * self.depth, 16)

    def ring_at(self, step, part):
        way = -1 if part else 1
        return lax.rem(self.here.ring - way * step + self.here.chips, self.here.chips)

    def onward(self, group, step, part, sub):
        r, half = self.r, self.depth // 2
        at, first = self.rows_of(self.ring_at(step, part))
        target = self.landing[group]
        slot = target.at[at, pl.ds(pl.multiple_of(first + half * sub, 16), half), :]
        packed = r.stage.at[0, pl.ds(group * self.depth + half * sub, half), pl.ds(0, target.shape[2])]
        return pltpu.make_async_remote_copy(
            packed if step == 0 else slot, slot, r.ring_send.at[group, part], r.ring_recv.at[group, part, sub, step],
            device_id=self.targets[part], device_id_type=MESH,
        )

    def over(self, group, ring, first_time=False):
        r = self.r
        at, first = self.rows_of(ring)
        target = self.landing[group]
        slot = target.at[at, pl.ds(first, self.depth), :]
        packed = r.stage.at[0, pl.ds(group * self.depth, self.depth), pl.ds(0, target.shape[2])]
        return pltpu.make_async_remote_copy(
            packed if first_time else slot, slot, r.over_send.at[group], r.over_recv.at[group],
            device_id=self.sibling, device_id_type=MESH,
        )

    def own(self, group):
        wide = self.landing[group].shape[2]
        first = pl.multiple_of(self.here.d * self.depth, 16)
        return pltpu.make_async_copy(
            self.r.stage.at[0, pl.ds(group * self.depth, self.depth), pl.ds(0, wide)],
            self.landing[group].at[self.here.t, pl.ds(first, self.depth), :],
            self.r.own_sem.at[group],
        )

    def begin(self, group):
        for sub in range(2):
            for part in range(2):
                self.onward(group, 0, part, sub).start()
        self.over(group, self.here.ring, True).start()
        self.own(group).start()

    def tick(self, group, n):
        step, last = n // 2 + 1, n == self.count - 1
        for part in range(2):
            sub = part if last else n % 2
            self.onward(group, step - 1, part, sub).wait_recv()
            if not last and (step < self.hops - 1 or sub == part):
                self.onward(group, step, part, sub).start()
        if last:
            self.over(group, self.ring_at(step, 0)).start()
        elif n % 2:
            for part in range(2):
                self.over(group, self.ring_at(step, part)).start()

    def sends_done(self, group):
        all_sends(self.r, self.landing[group], group, self.depth, self.hops, self.targets)

    def finish(self, group):
        all_over(self.r, self.landing[group], group, self.here, self.depth).wait_recv()
        self.own(group).wait()

    def start(self):
        r, depth = self.r, self.depth
        block = r.value_w.shape[1]

        def band(group, pieces):
            wide = pieces[0].shape[1]
            for k, piece in enumerate(pieces):
                r.stage[0, group * depth : (group + 1) * depth, k * wide : (k + 1) * wide] = piece

        band(ATTN, [r.query_key_w[1], r.value_w[...], r.query_key_w[0], r.out_w[...].T])
        self.order(ATTN)
        self.begin(ATTN)
        nrow = r.rows.shape[0]
        r.lengths_in[...] = jnp.zeros_like(r.lengths_in)
        r.lengths_in[0:nrow, 0 : r.enc_lengths.shape[1]] = r.enc_lengths[...]
        r.lengths_in[nrow : 2 * nrow, 0 : r.dec_lengths.shape[1]] = r.dec_lengths[...]
        r.table_in[...] = jnp.zeros_like(r.table_in)
        for k in range(r.bias_w.shape[0]):
            r.table_in[k : k + 1, 0 : r.bias_w.shape[2]] = r.bias_w[k]
        self.blocks(
            lambda i: (self.block_kept(i).start(), self.block_pass(r.rows.at[i], self.here.t).start()),
            lambda i: self.block_out(i).start(),
        )
        for copy in self.small_copies():
            copy.start()
        band(INNER, [r.inner_w[...]])
        band(OUTER, [r.outer_w[...]])
        band(CROSS, [r.first_w[...], r.second_w[...]])

    def small(self):
        for copy in self.small_copies():
            copy.wait()

    def rows(self):
        r, t = self.r, self.here.t
        takes = lax.div(t, r.rows.shape[0]) == self.here.core
        for s in range(self.tensor):

            @pl.when(jnp.logical_and(takes, s != t))
            def _():
                pltpu.make_async_remote_copy(
                    r.rows.at[0], r.x.at[:, s], r.block_send.at[0], r.block_recv.at[s],
                    device_id=self.sibling, device_id_type=MESH,
                ).wait_recv()
                self.block_pass(r.x.at[:, s], s).start()

        self.blocks(lambda i: self.block_kept(i).wait(), nothing)
        for s in range(self.tensor):

            @pl.when(jnp.logical_not(takes))
            def _():
                self.block_pass(r.x.at[:, s], s).wait_recv()

    def close(self):
        r, t = self.r, self.here.t
        takes = lax.div(t, r.rows.shape[0]) == self.here.core
        self.blocks(
            lambda i: self.block_pass(r.rows.at[i], t).wait_send(),
            lambda i: self.block_out(i).wait_send(),
        )
        for s in range(self.tensor):

            @pl.when(jnp.logical_and(takes, s != t))
            def _():
                self.block_pass(r.x.at[:, s], s).wait_send()

        for group in self.groups:
            self.sends_done(group)
            all_over(r, self.landing[group], group, self.here, self.depth).wait_send()


class Sums:
    def __init__(self, r, here, tensor, dp):
        self.r, self.here, self.tensor, self.dp = r, here, tensor, dp
        self.depth = r.value_w.shape[0]
        self.hops = here.chips // 2
        self.count = 2 * self.hops - 3
        self.sibling = here.sibling()
        self.targets = [here.neighbour(1), here.neighbour(-1)]
        self.box = {CROSS: r.raw_c, OUTER: r.raw_a, INNER: r.inner, ATTN: r.outer}
        self.kept = {CROSS: r.own_cross, OUTER: r.own_outer, INNER: r.own_inner, ATTN: r.ff}
        self.groups = []

    def order(self, *groups):
        self.groups = list(groups)

    def free(self, k):
        for device in self.targets + [self.sibling]:
            pl.semaphore_signal(self.r.free_sem.at[k], inc=1, device_id=device, device_id_type=MESH)

    def allow(self, k):
        pl.semaphore_wait(self.r.free_sem.at[k], 3)

    def boxed(self, group, index, first, height):
        if isinstance(index, int):
            return (index // self.dp, pl.ds(pl.multiple_of(index % self.dp * self.depth + first, 16), height), slice(None))
        at = pl.ds(pl.multiple_of(lax.rem(index, self.dp) * self.depth + first, 16), height)
        return (lax.div(index, self.dp), at, slice(None))

    def taken(self, group, step, part, first, height):
        index = step + part * (self.hops - 1) if step else 0
        return self.boxed(group, index, first, height)

    def theirs(self, group, ring, first, height):
        return self.boxed(group, self.here.chips - 1 + ring, first, height)

    def own(self, group, ring, first, height):
        return (ring, pl.ds(first, height), slice(None))

    def ring_of(self, line, at):
        return line * self.tensor + at + (line % 2) * (self.tensor - 1 - 2 * at)

    def pieces(self, group, tt, slot):
        r, depth = self.r, self.depth
        wide = self.box[group].shape[2]
        made = []
        for line in range(self.here.groups):
            ring = self.ring_of(line, tt)

            def rows_of(core):
                return r.stage.at[slot, pl.ds(pl.multiple_of((line * CORES + core) * depth, 16), depth), pl.ds(0, wide)]

            made.append(
                pltpu.make_async_copy(
                    rows_of(self.here.core), self.kept[group].at[self.own(group, ring, 0, depth)], r.kept_sem.at[slot, line]
                )
            )
            made.append(
                pltpu.make_async_remote_copy(
                    rows_of(1 - self.here.core), self.box[group].at[self.theirs(group, ring, 0, depth)],
                    r.pair_send.at[slot, line], r.over_recv.at[group], device_id=self.sibling, device_id_type=MESH,
                )
            )
        return made

    def emit(self, group, tt, slot):
        for piece in self.pieces(group, tt, slot):
            piece.start()

    def release(self, group, tt, slot):
        for k, piece in enumerate(self.pieces(group, tt, slot)):
            if k % 2:
                piece.wait_send()
            else:
                piece.wait()


    def rows_at(self, sub):
        half = self.depth // 2
        return half * sub, half

    def source(self, step, part):
        way = -1 if part else 1
        return lax.rem(self.here.ring + way * (self.hops - step) + self.here.chips, self.here.chips)

    def onward(self, group, step, part, sub):
        r = self.r
        first, height = self.rows_at(sub)
        return pltpu.make_async_remote_copy(
            self.kept[group].at[self.own(group, self.source(step, part), first, height)],
            self.box[group].at[self.taken(group, step, part, first, height)],
            r.ring_send.at[group, part], r.ring_recv.at[group, part, sub, step],
            device_id=self.targets[part], device_id_type=MESH,
        )

    def here_sum(self, group, ring, first, height):
        value = self.kept[group][self.own(group, ring, first, height)].astype(F32)
        return value + self.box[group][self.theirs(group, ring, first, height)].astype(F32)

    def advance(self, group, step, part, sub, fresh=False):
        if not fresh:
            self.onward(group, step - 1, part, sub).wait_recv()
        ring = self.source(step, part)

        def add(first, height):
            value = self.here_sum(group, ring, first, height)
            if not fresh:
                value = value + self.box[group][self.taken(group, step - 1, part, first, height)].astype(F32)
            self.kept[group][self.own(group, ring, first, height)] = value.astype(BF16)

        self.in_pieces(sub, add)
        self.onward(group, step, part, sub).start()

    def in_pieces(self, sub, body):
        start, height = self.rows_at(sub)

        @pl.loop(0, height // 16)
        def _(k):
            body(pl.multiple_of(start + 16 * k, 16), 16)

    def begin(self, group):
        all_over(self.r, self.box[group], group, self.here, self.depth).wait_recv()
        for part in range(2):
            self.advance(group, 0, part, part, True)
        for part in range(2):
            self.advance(group, 1, part, 1 - part, True)
        if group == ATTN:
            self.small_across().wait_recv()
            self.small_advance(0, 0, True)
            self.small_advance(1, 1, True)

    def tick(self, group, n):
        step, leads = (n + 1) // 2 + 1, n % 2
        for part in range(2):
            self.advance(group, step, part, 1 - part if leads else part)
        if group == ATTN and not leads:
            self.small_advance(step, 0)
            if step > 1:
                self.small_advance(step, 1)

    def sends_done(self, group):
        all_sends(self.r, self.box[group], group, self.depth, self.hops, self.targets)

    def rest(self, group):
        self.end(group)
        for group in (ATTN, CROSS, INNER, OUTER):
            self.sends_done(group)

    def end(self, group):
        r, last = self.r, self.hops - 1
        for sub in range(2):
            for part in range(2):
                self.onward(group, last, part, sub).wait_recv()
            target = r.inner_out if group == INNER else r.total

            def add(first, height):
                value = self.here_sum(group, self.here.ring, first, height)
                for part in range(2):
                    value = value + self.box[group][self.taken(group, last, part, first, height)].astype(F32)
                target[pl.ds(first, height), 0 : self.box[group].shape[2]] = value

            self.in_pieces(sub, add)
        block = r.value_w.shape[1]
        done = {ATTN: ("pair_out", "value_out", "out_out", "tiny_out"), CROSS: ("first_out", "second_out")}
        if group == ATTN:
            r.pair_out[1] = r.total[:, 0:block]
            r.value_out[...] = r.total[:, block : 2 * block]
            r.pair_out[0] = r.total[:, 2 * block : 3 * block]
            r.out_out[...] = r.total[:, 3 * block : 4 * block].T
            at = self.small_at(self.here.ring)
            value = r.small[at] + r.small_theirs[at]
            for part in range(2):
                self.small_onward(last, part).wait_recv()
                value = value + r.small_taken[part, last]
            r.tiny_out[...] = value
        if group == CROSS:
            r.first_out[...] = r.total[:, 0:block]
            r.second_out[...] = r.total[:, block : 2 * block]
        if group == OUTER:
            r.outer_out[...] = r.total[...]
        for name in done.get(group, ("inner_out",) if group == INNER else ("outer_out",)):
            self.result(name).start()

    def result(self, name):
        r = self.r
        return pltpu.make_async_copy(getattr(r, name), getattr(r, name + "_hbm"), r.result_sem.at[r.results.index(name)])


    def small_at(self, ring):
        line, at = self.here.at(ring)
        return at, line * CORES + self.here.core

    def small_across(self):
        r = self.r
        return pltpu.make_async_remote_copy(
            r.small, r.small_theirs, r.small_sem.at[0], r.small_sem.at[1], device_id=self.sibling, device_id_type=MESH
        )

    def small_onward(self, step, part):
        r = self.r
        return pltpu.make_async_remote_copy(
            r.small_sent.at[part, step], r.small_taken.at[part, step], r.tiny_send.at[part, step], r.tiny_recv.at[part, step],
            device_id=self.targets[part], device_id_type=MESH,
        )

    def small_advance(self, step, part, fresh=False):
        at = self.small_at(self.source(step, part))
        value = self.r.small[at] + self.r.small_theirs[at]
        if not fresh:
            self.small_onward(step - 1, part).wait_recv()
            value = value + self.r.small_taken[part, step - 1]
        self.r.small_sent[part, step] = value
        self.small_onward(step, part).start()

    def small_begin(self):
        r, depth = self.r, self.depth
        r.small[...] = jnp.zeros_like(r.small)
        kinds = r.onehot.shape[0] // self.dp
        heads_at = self.heads_at
        for tt in range(self.tensor):
            for d in range(self.dp):
                r.small[tt, d, 0:3, 0:depth] = r.gains_out[0:3, d * depth : (d + 1) * depth]
                r.small[tt, d, 3 : 3 + heads_at, 0:kinds] = r.bias_out[
                    8 * tt : 8 * tt + heads_at, d * kinds : (d + 1) * kinds
                ]
        self.small_across().start()


    def home_copy(self, k):
        r, here, tensor = self.r, self.here, self.tensor
        nrow, half, places = r.home_in.shape[0], tensor // 2, r.home_in.shape[2]
        place = here.pipe * (here.core * half + k % half) + (1 - here.pipe) * k
        which = here.pipe * (k // half) + (1 - here.pipe) * here.core
        owner = lax.div(here.t, nrow)
        source = r.rows_out.at[pl.ds(k * places, places)]
        slot = r.home_in.at[lax.rem(here.t, nrow), which]
        recv = r.home_recv.at[lax.rem(here.t, nrow), which]
        return (
            jnp.logical_and(place == here.t, owner == here.core),
            lambda: pltpu.make_async_copy(source, slot, recv),
            lambda: pltpu.make_async_remote_copy(
                source, slot, r.home_send.at[k], recv,
                device_id={"dp": here.group * CORES + owner, "tensor": place}, device_id_type=MESH,
            ),
        )

    def home(self):
        for k in range(self.tensor):
            stays, inside, away = self.home_copy(k)

            @pl.when(stays)
            def _():
                inside().start()

            @pl.when(jnp.logical_not(stays))
            def _():
                away().start()

    def home_done(self, unused=None):
        r = self.r
        places = r.home_in.shape[2]
        for i in range(r.home_in.shape[0]):
            for which in range(2):
                pltpu.make_async_copy(
                    r.rows_out.at[pl.ds(0, places)], r.home_in.at[i, which], r.home_recv.at[i, which]
                ).wait()
                r.home_out[i, which] = r.home_in[i, which].astype(F32)
        self.result("home_out").start()

    def close(self):
        r = self.r
        for k in range(self.tensor):
            stays, inside, away = self.home_copy(k)

            @pl.when(jnp.logical_not(stays))
            def _():
                away().wait_send()

        for name in r.results:
            self.result(name).wait()
        self.small_across().wait_send()

        for part in range(2):
            for step in range(part, self.hops):
                self.small_onward(step, part).wait_send()


def fits_fused(tensor, dp, depth, units, width):
    chips = tensor * dp // CORES
    return (
        depth % 32 == 0
        and 4 * depth <= width
        and chips <= 2 * tensor
        and chips == 2 * tensor == 8
        and chips * depth == 2 * width
        and units == width == 6 * LANES
    )


def fused_kernel(tensor, dp, heads_at, results, names, *refs):
    here = Place(tensor, dp)
    r = types.SimpleNamespace(**dict(zip(names, refs)))
    line = [
        {"dp": here.group * CORES + lax.rem(here.core + j, CORES), "tensor": lax.rem(here.t + k, tensor)}
        for j in range(CORES)
        for k in range(tensor)
        if j + k > 0
    ]
    across = [{"pipe": 1 - here.pipe, "dp": here.group * CORES + k} for k in range(CORES)]
    r.results = results
    given = [name for name in names if name + "_hbm" in names and name not in results]
    copies = [
        pltpu.make_async_copy(getattr(r, name + "_hbm"), getattr(r, name), r.given_sem.at[k]) for k, name in enumerate(given)
    ]
    for copy in copies:
        copy.start()
    meet([here.neighbour(1), here.neighbour(-1)] + line + across)
    for copy in copies:
        copy.wait()
    supply, drain = Rings(r, here, tensor, dp), Sums(r, here, tensor, dp)
    drain.heads_at = heads_at
    work(r, here, supply, drain, tensor, heads_at)


def fused(tensor, dp, rows, enc_lengths, dec_lengths, gains, bias, buckets, weights):
    nrow, two, places, width = rows.shape
    depth, block = weights[1].shape
    units = weights[5].shape[1]
    heads_at, _, kinds = bias.shape
    chips = tensor * dp // CORES
    wide = -(-max(depth, kinds // dp) // LANES) * LANES
    sems = pltpu.SemaphoreType.DMA
    ranges = -(-buckets[0].shape[1] // LANES) * LANES
    scratch = arrays(tensor, heads_at, places, width, units, ranges, kinds)
    given = dict(enc_lengths=enc_lengths, dec_lengths=dec_lengths, gains=gains, bias_w=bias)
    given.update(enc_buckets=buckets[0], dec_buckets=buckets[1])
    names = ("query_key_w", "value_w", "out_w", "first_w", "second_w", "inner_w", "outer_w")
    given.update(zip(names, weights))
    scratch.update({name: pltpu.VMEM(array.shape, array.dtype) for name, array in given.items()})
    scratch.update(
        lengths_in=held(8, LANES, dtype=jnp.int32),
        table_in=held(8, LANES, dtype=F32),
        lengths=held(CORES, 8, LANES, dtype=jnp.int32),
        tables=held(tensor, 8, LANES, dtype=F32),
        own_cross=held(chips, depth, 2 * block),
        own_outer=held(chips, depth, units),
        own_inner=held(chips, depth, units),
        total=held(depth, units, dtype=F32),
        rows_out=held(tensor * places, width),
        gains_out=held(8, width, dtype=F32),
        bias_out=held(8 * tensor, LANES, dtype=F32),
        home_in=held(nrow, two, places, width),
        small=held(tensor, dp, 8, wide, dtype=F32),
        small_theirs=held(tensor, dp, 8, wide, dtype=F32),
        small_sent=held(2, chips // 2, 8, wide, dtype=F32),
        small_taken=held(2, chips // 2, 8, wide, dtype=F32),
        block_send=sems((nrow,)), block_recv=sems((tensor,)), pass_send=sems((tensor,)), pass_recv=sems((tensor,)),
        local_sem=sems((3,)), small_send=sems((tensor,)), small_recv=sems((tensor,)), own_sem=sems((4,)),
        ring_send=sems((4, 2)), ring_recv=sems((4, 2, 2, chips // 2)),
        over_send=sems((4,)), over_recv=sems((4,)), kept_sem=sems((2, dp // CORES)), pair_send=sems((2, dp // CORES)),
        small_sem=sems((2,)), tiny_send=sems((2, chips // 2)), tiny_recv=sems((2, chips // 2)),
        home_send=sems((tensor,)), home_recv=sems((nrow, two)),
        free_sem=pltpu.SemaphoreType.REGULAR((3,)), given_sem=sems((len(given),)),
    )
    inputs = ["rows"] + [name + "_hbm" for name in given]
    outputs = dict(
        home_out=rows.shape, tiny_out=(8, wide), pair_out=(2, depth, block), value_out=(depth, block),
        out_out=(block, depth), first_out=(depth, block), second_out=(depth, block), inner_out=(depth, units),
        outer_out=(depth, units),
    )
    scratch.update({name: held(*shape, dtype=F32) for name, shape in outputs.items()})
    scratch["result_sem"] = sems((len(outputs),))
    return pl.pallas_call(
        functools.partial(fused_kernel, tensor, dp, heads_at, list(outputs), inputs + [name + "_hbm" for name in outputs] + list(scratch)),
        out_shape=tuple(jax.ShapeDtypeStruct(shape, F32) for shape in outputs.values()),
        in_specs=[ANY] * (1 + len(given)),
        out_specs=(ANY,) * len(outputs),
        scratch_shapes=list(scratch.values()),
        compiler_params=pltpu.CompilerParams(collective_id=3, has_side_effects=True, vmem_limit_bytes=VMEM_LIMIT),
        name="fused",
    )(rows, *given.values())


def pad_to(array, *shape):
    return jnp.pad(array, [(0, full - have) for full, have in zip(shape, array.shape)])


def shards(
    tensor, dp, section_rows, enc_lengths, dec_lengths, enc_buckets, dec_buckets, norm_gains, rel_bias,
    query_key_w, value_w, attn_out_w, cross_first, cross_second, ff_in, ff_out,
):
    depth = value_w.shape[1]
    width = section_rows.shape[-1]
    buckets = (enc_buckets[None], dec_buckets[None])
    gains = norm_gains.transpose(1, 0, 2)
    bias = rel_bias.transpose(2, 0, 1)
    weights = (query_key_w[0], value_w[0], attn_out_w[0], cross_first[0], cross_second[0], ff_in[0], ff_out[0].T)
    run = fused if fits_fused(tensor, dp, depth, ff_in.shape[2], width) else in_three
    home, tiny, *grads = run(tensor, dp, section_rows[0], enc_lengths, dec_lengths, gains, bias, buckets, weights)
    gain, kind, home, *grads, outer = copied(depth, bias.shape[0], bias.shape[2] // dp, tiny, home, *grads)
    return (
        (home[None], gain.transpose(1, 0, 2), kind.transpose(1, 2, 0))
        + tuple(grad[None] for grad in grads)
        + (outer.T[None],)
    )


def copied(depth, heads_at, kinds, tiny, *results):
    count = len(results)

    def kernel(*refs):
        sources, refs = refs[: count + 1], refs[count + 1 :]
        targets, refs = refs[: count + 2], refs[count + 2 :]
        held_here, (tiny_ref, in_sem, out_sem) = refs[: count + 2], refs[count + 2 :]
        ins = [
            pltpu.make_async_copy(source, there, in_sem.at[k])
            for k, (source, there) in enumerate(zip(sources, (tiny_ref,) + tuple(held_here[2:])))
        ]
        outs = [pltpu.make_async_copy(there, target, out_sem.at[k]) for k, (there, target) in enumerate(zip(held_here, targets))]
        for copy in ins:
            copy.start()
        for copy, out in zip(ins[1:], outs[2:]):
            copy.wait()
            out.start()
        ins[0].wait()
        for k in range(3):
            held_here[0][k] = tiny_ref[k : k + 1, 0:depth]
        for k in range(heads_at):
            held_here[1][k] = tiny_ref[3 + k : 4 + k, 0:kinds]
        outs[0].start()
        outs[1].start()
        for out in outs:
            out.wait()

    shapes = [(3, 1, depth), (heads_at, 1, kinds)] + [result.shape for result in results]
    sems = pltpu.SemaphoreType.DMA
    return pl.pallas_call(
        kernel,
        out_shape=tuple(jax.ShapeDtypeStruct(shape, F32) for shape in shapes),
        in_specs=[ANY] * (count + 1),
        out_specs=(ANY,) * (count + 2),
        scratch_shapes=[held(*shape, dtype=F32) for shape in shapes + [tiny.shape]] + [sems((count + 1,)), sems((count + 2,))],
        compiler_params=pltpu.CompilerParams(vmem_limit_bytes=VMEM_LIMIT),
        name="copied",
    )(tiny, *results)


def in_three(tensor, dp, section_rows, enc_lengths, dec_lengths, gains, bias, buckets, weights):
    query_key, value, out, first, second, inner, outer = weights
    nrow, _, _, width = section_rows.shape
    heads_at, _, kinds = bias.shape
    lengths = pad_to(jnp.concatenate([enc_lengths, dec_lengths], axis=0), 8, LANES)
    table = pad_to(bias[:, 0], 8, LANES)
    depth, block = value.shape
    units = inner.shape[1]
    pack = jnp.concatenate([query_key[1], value, query_key[0], out.T, first, second, inner, outer], axis=1)
    rows, gathered, lengths, tables = gather(tensor, dp, section_rows, pack, lengths, table)
    grads, finished, gain_grads, bias = blocks(
        tensor, dp, heads_at, kinds, rows, gathered.reshape(tensor, width, -1), gains, lengths, tables, buckets
    )
    held_kinds = kinds // dp
    wide = -(-max(depth, held_kinds) // LANES) * LANES
    gain_part = pad_to(gain_grads[:3].reshape(3, dp, depth).transpose(1, 0, 2), dp, 3, wide)
    bias_part = bias.reshape(tensor, 8, LANES)[:, :heads_at, :kinds].reshape(tensor, heads_at, dp, held_kinds)
    bias_part = pad_to(bias_part.transpose(0, 2, 1, 3), tensor, dp, 5, wide)
    small = jnp.concatenate([jnp.broadcast_to(gain_part[None], (tensor,) + gain_part.shape), bias_part], axis=2)
    total, tiny, home = scatter(
        tensor, dp, grads.reshape(tensor, dp, depth, -1), small, finished.reshape(tensor, -1, width), nrow
    )
    key, value, query, out, first, second = [total[:, k * block : (k + 1) * block] for k in range(6)]
    inner, outer = total[:, 6 * block : 6 * block + units], total[:, 6 * block + units :]
    return (
        home.astype(F32), tiny,
        jnp.stack([query, key]), value, out.T, first, second, inner, outer,
    )


def solution(mesh):
    sizes = dict(mesh.shape)
    return jax.shard_map(
        functools.partial(shards, sizes["tensor"], sizes["dp"]),
        mesh=mesh,
        in_specs=(
            P("pipe", "dp", None, "tensor", None),
            P("dp", None),
            P("dp", None),
            P(),
            P(),
            P("pipe", None, None),
            P("pipe", None, "tensor"),
            P("pipe", None, "dp", "tensor"),
            P("pipe", "dp", "tensor"),
            P("pipe", "tensor", "dp"),
            P("pipe", "dp", "tensor"),
            P("pipe", "dp", "tensor"),
            P("pipe", "dp", "tensor"),
            P("pipe", "tensor", "dp"),
        ),
        out_specs=(
            P("pipe", "dp", None, "tensor", None),
            P("pipe", None, "dp"),
            P("pipe", "dp", "tensor"),
            P("pipe", None, "dp", "tensor"),
            P("pipe", "dp", "tensor"),
            P("pipe", "tensor", "dp"),
            P("pipe", "dp", "tensor"),
            P("pipe", "dp", "tensor"),
            P("pipe", "dp", "tensor"),
            P("pipe", "tensor", "dp"),
        ),
        check_vma=False,
    )
```

```python
import functools
import types

import jax
import jax.numpy as jnp
from jax import lax
from jax.experimental import pallas as pl
from jax.experimental.pallas import tpu as pltpu
from jax.sharding import PartitionSpec as P

MESH = pl.DeviceIdType.MESH
F32 = jnp.float32
BF16 = jnp.bfloat16
EPSILON = 1e-06
NEGATIVE = -1000000000.0
HEAD_DIM = 64
CORES = 2
LANES = 128
VMEM_LIMIT = 62 << 20
ANY = pl.BlockSpec(memory_space=pl.ANY)
VMEM = pl.BlockSpec(memory_space=pltpu.VMEM)


def nn(a, b):
    return lax.dot_general(a, b, (((1,), (0,)), ((), ())), preferred_element_type=F32)


def nt(a, b):
    return lax.dot_general(a, b, (((1,), (1,)), ((), ())), preferred_element_type=F32)


def tn(a, b):
    return lax.dot_general(a, b, (((0,), (0,)), ((), ())), preferred_element_type=F32)


class Place:
    def __init__(self, tensor, dp):
        self.tensor = tensor
        self.groups = dp // CORES
        self.chips = tensor * self.groups
        self.pipe = lax.axis_index("pipe")
        self.d = lax.axis_index("dp")
        self.t = lax.axis_index("tensor")
        self.core = lax.rem(self.d, CORES)
        self.group = self.d // CORES
        odd = lax.rem(self.group, 2)
        self.ring = self.group * tensor + self.t + odd * (tensor - 1 - 2 * self.t)

    def at(self, ring):
        group = ring // self.tensor
        along = lax.rem(ring, self.tensor)
        odd = lax.rem(group, 2)
        return group, along + odd * (self.tensor - 1 - 2 * along)

    def neighbour(self, step):
        group, t = self.at(lax.rem(self.ring + step + self.chips, self.chips))
        return {"dp": group * CORES + self.core, "tensor": t}

    def sibling(self):
        return {"dp": self.group * CORES + 1 - self.core}


def meet(devices):
    barrier = pltpu.get_barrier_semaphore()
    for device in devices:
        pl.semaphore_signal(barrier, inc=1, device_id=device, device_id_type=MESH)
    pl.semaphore_wait(barrier, len(devices))


def halves(rows, columns):
    if rows % 32 == 0:
        return [(pl.ds(k * (rows // 2), rows // 2), pl.ds(0, columns)) for k in range(2)]
    cut = columns // LANES // 2 * LANES
    return [(pl.ds(0, rows), pl.ds(0, cut)), (pl.ds(0, rows), pl.ds(cut, columns - cut))]


def gather_kernel(
    tensor, dp, rows_ref, pack_ref, length_ref, table_ref, x_ref, w_ref, lengths_ref, tables_ref,
    local_sem, block_send, block_recv, pass_send, pass_recv, small_send, small_recv,
    ring_send, ring_recv, core_send, core_recv,
):
    here = Place(tensor, dp)
    c, t, chips = here.core, here.t, here.chips
    nrow = rows_ref.shape[0]
    sibling = here.sibling()
    to_right, to_left = here.neighbour(1), here.neighbour(-1)
    others = [{"tensor": lax.rem(t + k, tensor)} for k in range(1, tensor)]
    meet([to_right, to_left, sibling] + others)

    lengths = pltpu.make_async_remote_copy(
        length_ref, lengths_ref.at[c], small_send.at[0], small_recv.at[0], device_id=sibling, device_id_type=MESH
    )
    lengths.start()
    own_lengths = pltpu.make_async_copy(length_ref, lengths_ref.at[c], local_sem.at[0])
    own_lengths.start()
    own_table = pltpu.make_async_copy(table_ref, tables_ref.at[t], local_sem.at[1])
    own_table.start()
    tables = []
    for k in range(1, tensor):
        tables.append(
            pltpu.make_async_remote_copy(
                table_ref, tables_ref.at[t], small_send.at[k], small_recv.at[k], device_id=others[k - 1], device_id_type=MESH
            )
        )
        tables[-1].start()

    def to_chip(i):
        return pltpu.make_async_remote_copy(
            rows_ref.at[i], x_ref.at[:, t], block_send.at[i], block_recv.at[t],
            device_id={"tensor": nrow * c + i}, device_id_type=MESH,
        )

    def kept(i):
        return pltpu.make_async_copy(rows_ref.at[i], x_ref.at[:, t], local_sem.at[2])

    def kept_pass(i):
        return pltpu.make_async_remote_copy(
            rows_ref.at[i], x_ref.at[:, t], pass_send.at[t], pass_recv.at[t], device_id=sibling, device_id_type=MESH
        )

    def passed(s):
        return pltpu.make_async_remote_copy(
            x_ref.at[:, s], x_ref.at[:, s], pass_send.at[s], pass_recv.at[s], device_id=sibling, device_id_type=MESH
        )

    for i in range(nrow):
        mine = nrow * c + i == t

        @pl.when(mine)
        def _():
            kept(i).start()
            kept_pass(i).start()

        @pl.when(jnp.logical_not(mine))
        def _():
            to_chip(i).start()

    parts = halves(*pack_ref.shape)
    own_pack = pltpu.make_async_copy(pack_ref, w_ref.at[t, here.d], local_sem.at[3])
    own_pack.start()

    def shard(ring, part):
        group, at = here.at(ring)
        return w_ref.at[at, group * CORES + c, parts[part][0], parts[part][1]]

    def source(step, part):
        return lax.rem(here.ring + (1 if part else -1) * step + chips, chips)

    def onward(step, part, first=False):
        slot = shard(source(step, part), part)
        return pltpu.make_async_remote_copy(
            pack_ref.at[parts[part][0], parts[part][1]] if first else slot, slot,
            ring_send.at[part, step], ring_recv.at[part, step],
            device_id=to_left if part else to_right, device_id_type=MESH,
        )

    def across(step, part, first=False):
        slot = shard(source(step, part), part)
        return pltpu.make_async_remote_copy(
            pack_ref.at[parts[part][0], parts[part][1]] if first else slot, slot,
            core_send.at[part, step], core_recv.at[part, step], device_id=sibling, device_id_type=MESH,
        )

    for part in range(2):
        onward(0, part, True).start()
        across(0, part, True).start()

    takes = t // nrow == c
    for s in range(tensor):

        @pl.when(jnp.logical_and(takes, s != t))
        def _():
            pltpu.make_async_remote_copy(
                rows_ref.at[0], x_ref.at[:, s], block_send.at[0], block_recv.at[s], device_id=sibling, device_id_type=MESH
            ).wait_recv()
            passed(s).start()

    @pl.loop(1, chips)
    def _(step):
        for part in range(2):
            onward(step - 1, part).wait_recv()

            @pl.when(step < chips - 1)
            def _():
                onward(step, part).start()

            across(step, part).start()

    @pl.loop(0, chips)
    def _(step):
        for part in range(2):

            @pl.when(step < chips - 1)
            def _():
                onward(step, part).wait_send()

            across(step, part).wait_send()
            across(step, part).wait_recv()

    for i in range(nrow):
        mine = nrow * c + i == t

        @pl.when(mine)
        def _():
            kept(i).wait()
            kept_pass(i).wait_send()

        @pl.when(jnp.logical_not(mine))
        def _():
            to_chip(i).wait_send()

    for s in range(tensor):

        @pl.when(jnp.logical_and(takes, s != t))
        def _():
            passed(s).wait_send()

        @pl.when(jnp.logical_not(takes))
        def _():
            passed(s).wait_recv()

    lengths.wait()
    own_lengths.wait()
    own_table.wait()
    own_pack.wait()
    for table in tables:
        table.wait()


def gather(tensor, dp, rows, pack, lengths, table):
    chips = tensor * dp // CORES
    nrow, two, places, width = rows.shape
    sems = pltpu.SemaphoreType.DMA
    return pl.pallas_call(
        functools.partial(gather_kernel, tensor, dp),
        out_shape=(
            jax.ShapeDtypeStruct((two, tensor, places, width), rows.dtype),
            jax.ShapeDtypeStruct((tensor, dp) + pack.shape, pack.dtype),
            jax.ShapeDtypeStruct((CORES,) + lengths.shape, lengths.dtype),
            jax.ShapeDtypeStruct((tensor,) + table.shape, table.dtype),
        ),
        in_specs=[ANY] * 4,
        out_specs=(ANY,) * 4,
        scratch_shapes=[
            sems((4,)), sems((nrow,)), sems((tensor,)), sems((tensor,)), sems((tensor,)), sems((tensor,)), sems((tensor,)),
            sems((2, chips)), sems((2, chips)), sems((2, chips)), sems((2, chips)),
        ],
        compiler_params=pltpu.CompilerParams(collective_id=0, has_side_effects=True),
        name="gather",
    )(rows, pack, lengths, table)


def scatter_kernel(
    tensor, dp, grads_ref, small_ref, rows_ref, out_ref, small_out, rows_out,
    own, theirs, taken, small_own, small_theirs, small_taken, total,
    own_sem, core_send, core_recv, ring_send, ring_recv,
    sown_sem, score_send, score_recv, sring_send, sring_recv, block_send, block_recv, local_sem,
):
    here = Place(tensor, dp)
    c, t, chips = here.core, here.t, here.chips
    nrow = rows_out.shape[0]
    sibling = here.sibling()
    to_right, to_left = here.neighbour(1), here.neighbour(-1)
    line = [
        {"dp": here.group * CORES + lax.rem(c + j, CORES), "tensor": lax.rem(t + k, tensor)}
        for j in range(CORES)
        for k in range(tensor)
        if j + k > 0
    ]
    meet([to_right, to_left] + line)

    half = tensor // 2
    owner = t // nrow

    def block(k):
        place = here.pipe * (c * half + k % half) + (1 - here.pipe) * k
        which = here.pipe * (k // half) + (1 - here.pipe) * c
        return place, which

    def home(k):
        place, which = block(k)
        slot = rows_out.at[lax.rem(t, nrow), which]
        recv = block_recv.at[lax.rem(t, nrow), which]
        return (
            jnp.logical_and(place == t, owner == c),
            lambda: pltpu.make_async_copy(rows_ref.at[k], slot, recv),
            lambda: pltpu.make_async_remote_copy(
                rows_ref.at[k], slot, block_send.at[k], recv,
                device_id={"dp": here.group * CORES + owner, "tensor": place}, device_id_type=MESH,
            ),
        )

    for k in range(tensor):
        stays, inside, away = home(k)

        @pl.when(stays)
        def _():
            inside().start()

        @pl.when(jnp.logical_not(stays))
        def _():
            away().start()

    def across(ring):
        group, at = here.at(ring)
        return (
            pltpu.make_async_remote_copy(
                grads_ref.at[at, group * CORES + 1 - c], theirs.at[ring], core_send.at[ring], core_recv.at[ring],
                device_id=sibling, device_id_type=MESH,
            ),
            pltpu.make_async_remote_copy(
                small_ref.at[at, group * CORES + 1 - c], small_theirs.at[ring], score_send.at[ring], score_recv.at[ring],
                device_id=sibling, device_id_type=MESH,
            ),
        )

    def fetch(ring):
        group, at = here.at(ring)
        return (
            pltpu.make_async_copy(grads_ref.at[at, group * CORES + c], own.at[ring], own_sem.at[ring]),
            pltpu.make_async_copy(small_ref.at[at, group * CORES + c], small_own.at[ring], sown_sem.at[ring]),
        )

    def behind(step):
        return lax.rem(here.ring - step + chips, chips)

    def order(k):
        off = (2 * lax.rem(k, 2) - 1) * (k // 2 + 1) * (1 - k // (chips - 1))
        return lax.rem(here.ring + chips + off, chips)

    @pl.loop(0, chips)
    def _(k):
        for copy in across(order(k)) + fetch(order(k)):
            copy.start()

    rows, columns = out_ref.shape
    parts = halves(rows, columns)

    def add(ring, part, step, last):
        height = parts[part][0].size
        piece = 16 if height % 16 == 0 else height

        @pl.loop(0, height // piece)
        def _(k):
            at = pl.ds(pl.multiple_of(parts[part][0].start + k * piece, 8), piece)
            where = (at, parts[part][1])
            value = own[(ring,) + where].astype(F32) + theirs[(ring,) + where].astype(F32)
            if step is not None:
                value = value + taken[(step,) + where].astype(F32)
            if last:
                total[where] = value
            else:
                own[(ring,) + where] = value.astype(BF16)

    def onward(ring, step, part):
        where = (parts[part][0], parts[part][1])
        return pltpu.make_async_remote_copy(
            own.at[(ring,) + where], taken.at[(step,) + where], ring_send.at[part, step], ring_recv.at[part, step],
            device_id=to_left if part else to_right, device_id_type=MESH,
        )

    def small_onward(ring, step):
        return pltpu.make_async_remote_copy(
            small_own.at[ring], small_taken.at[step], sring_send.at[step], sring_recv.at[step],
            device_id=to_right, device_id_type=MESH,
        )

    def ready(ring):
        for copy in across(ring):
            copy.wait_recv()
        for copy in fetch(ring):
            copy.wait()

    def ahead(step):
        return lax.rem(here.ring + step, chips)

    half_chips = chips // 2

    @pl.loop(0, chips - 1)
    def _(step):
        right, left = behind(step + 1), ahead(step + 1)

        @pl.when(step < half_chips)
        def _():
            ready(right)

        @pl.when(step < chips - 1 - half_chips)
        def _():
            ready(left)

        @pl.when(step == 0)
        def _():
            add(right, 0, None, False)
            add(left, 1, None, False)
            small_own[right] = small_own[right] + small_theirs[right]

        @pl.when(step > 0)
        def _():
            onward(right, step - 1, 0).wait_recv()
            add(right, 0, step - 1, False)
            onward(right, step, 0).start()
            onward(left, step - 1, 1).wait_recv()
            add(left, 1, step - 1, False)
            onward(left, step, 1).start()
            small_onward(right, step - 1).wait_recv()
            small_own[right] = small_own[right] + small_theirs[right] + small_taken[step - 1]
            small_onward(right, step).start()

        @pl.when(step == 0)
        def _():
            onward(right, 0, 0).start()
            onward(left, 0, 1).start()
            small_onward(right, 0).start()

    ready(here.ring)
    for part in range(2):
        onward(here.ring, chips - 2, part).wait_recv()
        add(here.ring, part, chips - 2, True)
    small_onward(here.ring, chips - 2).wait_recv()
    small_out[...] = small_own[here.ring] + small_theirs[here.ring] + small_taken[chips - 2]
    finish = pltpu.make_async_copy(total, out_ref, local_sem.at[0])
    finish.start()

    @pl.loop(0, chips)
    def _(step):
        @pl.when(step < chips - 1)
        def _():
            onward(behind(step + 1), step, 0).wait_send()
            onward(ahead(step + 1), step, 1).wait_send()
            small_onward(behind(step + 1), step).wait_send()

        for copy in across(step):
            copy.wait_send()

    for k in range(tensor):
        stays, inside, away = home(k)

        @pl.when(jnp.logical_not(stays))
        def _():
            away().wait_send()

    for i in range(nrow):
        for which in range(2):
            pltpu.make_async_copy(rows_ref.at[0], rows_out.at[i, which], block_recv.at[i, which]).wait()
    finish.wait()


def scatter(tensor, dp, grads, small, rows, nrow):
    chips = tensor * dp // CORES
    shard = grads.shape[2:]
    tiny = small.shape[2:]
    sems = pltpu.SemaphoreType.DMA
    return pl.pallas_call(
        functools.partial(scatter_kernel, tensor, dp),
        out_shape=(
            jax.ShapeDtypeStruct(shard, F32),
            jax.ShapeDtypeStruct(tiny, F32),
            jax.ShapeDtypeStruct((nrow, 2) + rows.shape[1:], rows.dtype),
        ),
        in_specs=[ANY] * 3,
        out_specs=(ANY, VMEM, ANY),
        scratch_shapes=[
            pltpu.VMEM((chips,) + shard, BF16),
            pltpu.VMEM((chips,) + shard, BF16),
            pltpu.VMEM((chips - 1,) + shard, BF16),
            pltpu.VMEM((chips,) + tiny, F32),
            pltpu.VMEM((chips,) + tiny, F32),
            pltpu.VMEM((chips - 1,) + tiny, F32),
            pltpu.VMEM(shard, F32),
            sems((chips,)), sems((chips,)), sems((chips,)), sems((2, chips)), sems((2, chips)),
            sems((chips,)), sems((chips,)), sems((chips,)), sems((chips,)), sems((chips,)),
            sems((tensor,)), sems((nrow, 2)), sems((1,)),
        ],
        compiler_params=pltpu.CompilerParams(collective_id=1, has_side_effects=True, vmem_limit_bytes=VMEM_LIMIT),
        name="scatter",
    )(grads, small, rows)


KEY, VALUE, QUERY, OUT, FIRST, SECOND = range(6)
ATTN, CROSS, INNER, OUTER = range(4)
SEGS_HELD = 6


def rms(value):
    return lax.rsqrt(jnp.mean(value * value, axis=-1, keepdims=True) + EPSILON)


def in_rows(count, body, piece=128):
    @pl.loop(0, count // piece)
    def _(k):
        body(pl.ds(pl.multiple_of(k * piece, piece), piece))


def columns_of(count, body, piece=768):
    piece = min(piece, count)

    @pl.loop(0, count // piece)
    def _(k):
        body(pl.ds(pl.multiple_of(k * piece, piece), piece))


def normalize(source, gain, target, count):
    def body(at):
        value = source[at, :].astype(F32)
        target[at, :] = (value * rms(value) * gain).astype(BF16)

    in_rows(count, body)


def normalize_back(source, gain, incoming, total, gain_parts, count, fresh):
    gain_parts[...] = jnp.zeros_like(gain_parts)

    def body(at):
        value, back = source[at, :].astype(F32), incoming[at, :]
        scale = rms(value)
        unit = value * scale
        gain_parts[...] += jnp.sum((back * unit).reshape(-1, 8, back.shape[-1]), axis=0)
        back = back * gain
        back = scale * (back - unit * jnp.mean(back * unit, axis=-1, keepdims=True))
        total[at, :] = back if fresh else total[at, :] + back

    in_rows(count, body)


def project(left, weight, target, count):
    def body(at):
        target[0:count, at] = nn(left[0:count, :], weight[:, at]).astype(target.dtype)

    columns_of(weight.shape[1], body)


def project_back(left, weight, total, count, fresh):
    def body(at):
        value = nt(left[0:count, :], weight[at, :])
        total[0:count, at] = value if fresh else total[0:count, at] + value

    columns_of(weight.shape[0], body)


def to_bf16(source, target, rows):
    def body(at):
        target[at, :] = source[at, :].astype(BF16)

    in_rows(rows, body)


def turn(left, turned, rows):
    def body(at):
        turned[at, 0:rows] = left[0:rows, at].T

    columns_of(left.shape[1], body, LANES)


def lane_half(shape, part):
    return lax.broadcasted_iota(jnp.int32, shape, 1) // HEAD_DIM == part


def attend(keys, values, queries, mixture, probs, rows, span, pairs, mask, bias, after):
    @pl.loop(0, pairs)
    def _(pair):
        lanes = pl.ds(pl.multiple_of(pair * LANES, LANES), LANES)
        key, query = keys[0:span, lanes], queries[0:rows, lanes]
        value_t = values[0:span, lanes].T
        mixed = []
        for part in range(2):
            one = jnp.where(lane_half(query.shape, part), query, jnp.zeros_like(query))
            scores = nt(key, one) + mask[0:span, 0:rows]
            if bias is not None:
                scores = scores + bias(2 * pair + part)
            scores = jnp.exp(scores - jnp.max(scores, axis=0, keepdims=True))
            scores = (scores * (1.0 / jnp.sum(scores, axis=0, keepdims=True))).astype(BF16)
            probs[2 * pair + part, 0:span, 0:rows] = scores
            mixed.append(nn(value_t[part * HEAD_DIM : (part + 1) * HEAD_DIM, :], scores))
        mixture[0:rows, lanes] = jnp.concatenate(mixed, axis=0).T.astype(BF16)
        after(pair)


def attend_back(keys, values, queries, back, probs, rows, span, pairs, each, before, after):
    @pl.loop(0, pairs)
    def _(pair):
        before(pair)
        lanes = pl.ds(pl.multiple_of(pair * LANES, LANES), LANES)
        key, value = keys[0:span, lanes], values[0:span, lanes]
        query, given = queries[0:rows, lanes], back[0:rows, lanes]
        key_t = key.T
        d_key, d_value, d_query = None, None, []
        for part in range(2):
            side = lane_half(query.shape, part)
            query_one = jnp.where(side, query, jnp.zeros_like(query))
            given_one = jnp.where(side, given, jnp.zeros_like(given))
            prob = probs[2 * pair + part, 0:span, 0:rows]
            wide = prob.astype(F32)
            d_prob = nt(value, given_one)
            d_score = (wide * (d_prob - jnp.sum(wide * d_prob, axis=0, keepdims=True))).astype(BF16)
            if each is not None:
                each(2 * pair + part, d_score)
            of_key, of_value = nn(d_score, query_one), nn(prob, given_one)
            d_key = of_key if d_key is None else d_key + of_key
            d_value = of_value if d_value is None else d_value + of_value
            d_query.append(nn(key_t[part * HEAD_DIM : (part + 1) * HEAD_DIM, :], d_score))
        keys[0:span, lanes] = d_key.astype(BF16)
        values[0:span, lanes] = d_value.astype(BF16)
        queries[0:rows, lanes] = jnp.concatenate(d_query, axis=0).T.astype(BF16)
        after(pair)


def segments(lengths_row, shape, axis, first):
    lane = lax.broadcasted_iota(jnp.int32, lengths_row.shape, 1)
    places = lax.broadcasted_iota(jnp.int32, shape, axis) + first
    ids = jnp.zeros(shape, jnp.int32)
    for c in range(SEGS_HELD):
        bound = jnp.sum(jnp.where(lane <= c, lengths_row, 0), axis=1, keepdims=True)
        ids = ids + (places >= bound).astype(jnp.int32)
    return ids


def masked(allowed):
    return jnp.where(allowed, 0.0, NEGATIVE).astype(F32)


def nothing(*unused, **named):
    pass


def work(r, here, supply, drain, tensor, heads_at):
    c, t = here.core, here.t
    width = r.hidden.shape[1]
    tall = r.hidden.shape[0]
    block = width // tensor
    half_width = width // 2
    units = r.inner.shape[2]
    places = r.x.shape[2]
    sibling = here.sibling()
    across = [{"pipe": 1 - here.pipe, "dp": here.group * CORES + k} for k in range(CORES)]
    nrow = tensor // CORES
    rows_e, span_e, rows_d, span_d = tall // 2, tall, tall // 4, tall // 2
    pairs_here = half_width // LANES
    near_lanes = pl.ds(pl.multiple_of(c * half_width, half_width), half_width)
    far_lanes = pl.ds(pl.multiple_of((1 - c) * half_width, half_width), half_width)
    lane_halves = [slice(k * half_width, (k + 1) * half_width) for k in range(CORES)]

    def move(source, target, sends, recvs, device):
        return pltpu.make_async_remote_copy(
            source, target, r.send_sem.at[sends], r.recv_sem.at[recvs], device_id=device, device_id_type=MESH
        )

    def lengths_row(first):
        return r.lengths[t // nrow, pl.ds(first + lax.rem(t, nrow), 1), :]

    def pair_lanes(pair):
        return pl.ds(pair * LANES if isinstance(pair, int) else pl.multiple_of(pair * LANES, LANES), LANES)

    def vector_row(head):
        return (head // heads_at) * 8 + lax.rem(head, heads_at)

    def bias_vectors():
        enc, dec = r.enc_buckets.shape[1], r.dec_buckets.shape[1]
        r.buckets[...] = jnp.zeros_like(r.buckets)

        @pl.when(here.pipe == 0)
        def _():
            r.buckets[0:1, 0:enc] = r.enc_buckets[...]

        @pl.when(here.pipe == 1)
        def _():
            r.buckets[0:1, dec - 1 : 2 * dec - 1] = r.dec_buckets[...]

        buckets = lax.broadcasted_iota(jnp.int32, r.onehot.shape, 0) == r.buckets[0:1, :]
        r.onehot[...] = buckets.astype(F32)
        for tt in range(tensor):
            r.vectors[pl.ds(8 * tt, 8), :] = lax.dot_general(
                r.tables[tt][:, 0 : r.onehot.shape[0]], r.onehot[...], (((1,), (0,)), ((), ())),
                precision=lax.Precision.HIGHEST, preferred_element_type=F32,
            )

    def rows_ready(span, rows, first_block):
        @pl.loop(0, span // places)
        def _(k):
            value = r.x[k // tensor, lax.rem(k, tensor)].astype(F32)
            at = pl.ds(pl.multiple_of(k * places, places), places)
            r.hidden[at, :] = (value * rms(value) * r.gains[0]).astype(BF16)

        for k in range(rows // places):
            r.own_x[k * places : (k + 1) * places, :] = r.x[first_block // tensor, lax.rem(first_block, tensor) + k]

    def untangle(source, first, count):
        def body(at):
            for tt in range(tensor):
                for k in range(count):
                    r.square[first + k, at, tt * block : (tt + 1) * block] = source[tt, at, k * block : (k + 1) * block]

        in_rows(width, body, 128)

    def self_forward(span, rows, first_row, group):
        def bias(head):
            pieces = []
            for j in range(span // LANES):
                start = pl.multiple_of(first_row + span - LANES - j * LANES, LANES)
                row = r.vectors[pl.ds(vector_row(head), 1), pl.ds(start, rows + LANES)]
                wide = jnp.broadcast_to(row, (LANES, rows + LANES))
                pieces.append(pltpu.roll(wide, rows + 1, 1, stride=1, stride_axis=0)[:, 0:rows])
            return jnp.concatenate(pieces, axis=0)

        untangle(r.raw_a, KEY, 2)
        untangle(r.raw_a.at[:, :, pl.ds(2 * block, 2 * block)], QUERY, 2)
        project(r.hidden, r.square.at[KEY], r.keys, span)
        supply.pump()
        project(r.hidden, r.square.at[VALUE], r.values, span)
        project(r.hidden.at[pl.ds(first_row, rows)], r.square.at[QUERY], r.queries, rows)
        supply.pump()
        after = at_each(range(width // LANES), supply.pump)

        attend(r.keys, r.values, r.queries, r.mixture, r.probs, rows, span, width // LANES, r.mask, bias, after)
        project_back(r.mixture, r.square.at[OUT], r.resid_mid, rows, True)

        def add(at):
            r.resid_mid[at, :] += r.own_x[at, :].astype(F32)

        in_rows(rows, add)
        supply.pump(until=group)
        supply.finish(group)

    def at_each(places, do):
        def hook(n):
            for place in places:

                @pl.when(n == place)
                def _():
                    do()

        return hook

    def feed_forward(rows, hook=nothing):
        @pl.loop(0, tensor)
        def _(tt):
            def body(at):
                value = nn(r.second[0:rows, :], r.inner[tt, :, at])
                cdf = 0.5 * (1.0 + lax.erf(value * 0.7071067811865476))
                r.ff[tt, 0:rows, at] = (value * cdf).astype(BF16)
                slope = cdf + value * jnp.exp(-0.5 * value * value) * 0.3989422804014327
                r.ff[tensor + tt, 0:rows, at] = slope.astype(BF16)

            columns_of(units, body)
            hook(tt)

    def feed_out(target, rows, hook=nothing):
        @pl.loop(0, tensor)
        def _(tt):
            def body(at):
                target[0:rows, at] += nt(r.ff[tt, 0:rows, :], r.outer[tt, at, :])

            columns_of(width, body)
            hook(tt)

    def feed_back(rows, ready, hook=nothing):
        r.summed[0:rows, :] = jnp.zeros((rows, width), F32)

        @pl.loop(0, tensor)
        def _(tt):
            def body(at):
                if ready:
                    value = r.ff[tensor + tt, rows : 2 * rows, at].astype(F32)
                else:
                    value = nn(r.d_branch[0:rows, :], r.outer[tt, :, at])
                r.ff[tensor + tt, 0:rows, at] = (value * r.ff[tensor + tt, 0:rows, at].astype(F32)).astype(BF16)

            columns_of(units, body)

            def back(at):
                r.summed[0:rows, at] += nt(r.ff[tensor + tt, 0:rows, :], r.inner[tt, at, :])

            columns_of(width, back)
            hook(tt)

    def feed_grads(rows, turned, first, which, hook=nothing):
        @pl.loop(0, tensor)
        def _(tt):
            slot = lax.rem(tt, 2)

            @pl.when(tt >= 2)
            def _():
                drain.release(which, tt - 2, slot)

            def body(at):
                r.stage[slot, :, at] = nn(turned[:, 0:rows], r.ff[first + tt, 0:rows, at]).astype(BF16)

            columns_of(units, body)
            drain.emit(which, tt, slot)
            hook(tt)

        for tt in range(tensor - 2, tensor):
            drain.release(which, tt, tt % 2)

    def square_grads(rows, which, products, hook):
        wide = len(products) * block
        apart = tensor // 2 * wide <= r.stage.shape[2]
        for k in range(tensor // 2):
            place = k if apart else 0
            for j, (turned, right) in enumerate(products):

                def body(at):
                    value = nn(turned[at, 0:rows], right[0:rows, 2 * k * block : 2 * (k + 1) * block]).astype(BF16)
                    for slot in range(2):
                        first = place * wide + j * block
                        r.stage[slot, at, first : first + block] = value[:, slot * block : (slot + 1) * block]

                in_rows(width, body, 256)
            for slot in range(2):
                drain.emit(which, 2 * k + slot, slot, place)
            hook(k)
            if not apart:
                for slot in range(2):
                    drain.release(which, 2 * k + slot, slot)
        if apart:
            for k in range(tensor // 2):
                for slot in range(2):
                    drain.release(which, 2 * k + slot, slot, k)

    def gain_done(which):
        r.gains_out[which : which + 1, :] = jnp.sum(r.gain_parts[...], axis=0, keepdims=True)

    def self_backward(span, rows, first_row, steps, send_rows):
        mirror = (
            lax.broadcasted_iota(jnp.int32, (LANES, LANES), 0) + lax.broadcasted_iota(jnp.int32, (LANES, LANES), 1)
            == LANES - 1
        ).astype(BF16)
        to_bf16(r.d_resid, r.branch, rows)
        project(r.branch, r.square.at[OUT], r.d_branch, rows)
        r.diagonals[...] = jnp.zeros_like(r.diagonals)

        def each(head, d_score):
            for j in range(span // LANES):
                start = pl.multiple_of(first_row + span - LANES - j * LANES, LANES)
                piece = nn(mirror, d_score[j * LANES : (j + 1) * LANES, :])
                piece = jnp.concatenate([piece, jnp.zeros((LANES, LANES), F32)], axis=1)
                piece = pltpu.roll(piece, 0, 1, stride=1, stride_axis=0)
                at = (pl.ds(vector_row(head), 1), pl.ds(start, rows + LANES))
                r.diagonals[at] += jnp.sum(piece, axis=0, keepdims=True)

        pairs = width // LANES
        attend_back(
            r.keys, r.values, r.queries, r.d_branch, r.probs, rows, span, pairs, each, nothing,
            at_each(range(pairs), steps),
        )
        far = pl.ds(pl.multiple_of((1 - c) * rows, rows), rows)
        near = pl.ds(pl.multiple_of(c * rows, rows), rows)
        trades = [
            move(source.at[far], r.taken_pair.at[k, pl.ds(0, rows)], 12 + k, 12 + k, sibling)
            for k, source in enumerate((r.keys, r.values))
        ]
        for trade in trades:
            trade.start()
        steps()
        turn(r.branch, r.turned, rows)
        turn(r.hidden.at[pl.ds(first_row, rows)], r.turned_more, rows)
        for tt in range(tensor):
            at = pl.ds(8 * tt, 8)
            r.bias_out[at, 0 : r.onehot.shape[0]] = lax.dot_general(
                r.diagonals[at, :], r.onehot[...], (((1,), (1,)), ((), ())),
                precision=lax.Precision.HIGHEST, preferred_element_type=F32,
            )
        steps()
        project_back(r.queries, r.square.at[QUERY], r.summed, rows, True)
        for trade in trades:
            trade.wait_recv()
        steps()
        for k, source in enumerate((r.keys, r.values)):
            r.d_pair[k, 0:rows, :] = (source[near, :].astype(F32) + r.taken_pair[k, 0:rows, :].astype(F32)).astype(BF16)
        project_back(r.d_pair.at[0], r.square.at[KEY], r.summed, rows, False)
        project_back(r.d_pair.at[1], r.square.at[VALUE], r.summed, rows, False)
        steps()
        normalize_back(r.own_x, r.gains[0], r.summed, r.d_resid, r.gain_parts, rows, False)
        gain_done(0)
        steps()
        send_rows()
        drain.small_begin()
        drain.allow(2)
        products = [(r.turned_more, r.d_pair.at[0]), (r.turned_more, r.d_pair.at[1]), (r.turned_more, r.queries), (r.turned, r.mixture)]
        square_grads(rows, ATTN, products, nothing)
        for trade in trades:
            trade.wait_send()
        steps()
        drain.begin(ATTN)
        steps()
        drain.rest(ATTN)

    def parts_of(array):
        return [array.at[pl.ds(k * rows_d, rows_d)] for k in range(CORES)]

    def part_here(array):
        return array.at[pl.ds(pl.multiple_of(c * rows_d, rows_d), rows_d)]

    r.gains_out[...] = jnp.zeros_like(r.gains_out)
    r.bias_out[...] = jnp.zeros_like(r.bias_out)
    supply.start()

    def entry():
        supply.pump(2)
        supply.small()
        bias_vectors()
        supply.pump(2)
        supply.rows()

    def schedule(*items):
        left = list(items)

        def steps():
            for name, group, *n in left.pop(0) if left else ():
                getattr(drain, name)(group, *n)

        return steps

    @pl.when(here.pipe == 0)
    def _():
        supply.resume(ATTN, INNER, OUTER, CROSS)
        drain.order(CROSS, OUTER, INNER, ATTN)
        entry()
        rows, span = rows_e, span_e
        first_row = pl.multiple_of(c * rows, rows)
        seg_rows = segments(lengths_row(0), (span, 1), 0, 0)
        r.mask[...] = masked(seg_rows == segments(lengths_row(0), (1, rows), 1, first_row))
        supply.pump()
        rows_ready(span, rows, c * tensor)
        supply.pump(until=ATTN)
        supply.finish(ATTN)
        self_forward(span, rows, first_row, INNER)
        normalize(r.resid_mid, r.gains[1], r.second, rows)
        feed_forward(rows, at_each((1, 2, 3), supply.pump))
        supply.pump(until=OUTER)
        supply.finish(OUTER)
        r.resid_top[...] = r.resid_mid[...]
        feed_out(r.resid_top, rows, at_each((1, 2, 3), supply.pump))
        normalize(r.resid_top, r.gains[2], r.third, rows)
        r.mask[...] = masked(seg_rows == segments(lengths_row(nrow), (1, span_d), 1, 0))
        supply.pump(until=CROSS)
        supply.finish(CROSS)
        untangle(r.raw_c, FIRST, 2)
        mine = pl.ds(first_row, rows)
        other = pl.ds(pl.multiple_of((1 - c) * rows, rows), rows)
        trades = []
        for k, held in enumerate((r.cross_keys, r.cross_values)):
            r.send_pair[k] = nn(r.third[...], r.square[FIRST + k, :, far_lanes]).astype(BF16)
            trades.append(move(r.send_pair.at[k], held.at[mine], k, k, sibling))
            trades[-1].start()
        for k, held in enumerate((r.cross_keys, r.cross_values)):
            held[mine, :] = nn(r.third[...], r.square[FIRST + k, :, near_lanes]).astype(BF16)
        for k, part in enumerate(parts_of(r.cross_queries)):
            move(part, part, 2 + k, 2 + k, across[k]).wait_recv()
        for k, held in enumerate((r.cross_keys, r.cross_values)):
            move(r.send_pair.at[k], held.at[other], k, k, sibling).wait_recv()

        def mixtures(pair):
            at = pair_lanes(pair)
            return [
                pltpu.make_async_remote_copy(
                    r.cross_mixture.at[pl.ds(k * rows_d, rows_d), at], r.cross_in.at[c, :, at],
                    r.mix_send.at[k, pair], r.mix_recv.at[c, pair], device_id=across[k], device_id_type=MESH,
                )
                for k in range(CORES)
            ]

        def arrived(pair):
            for k in range(CORES):
                part = r.cross_back.at[pl.ds(k * rows_d, rows_d), pair_lanes(pair)]
                pltpu.make_async_remote_copy(
                    part, part, r.back_send.at[k, pair], r.back_recv.at[k, pair], device_id=across[k], device_id_type=MESH
                ).wait_recv()

        def returns(pair):
            at = pair_lanes(pair)
            return [
                pltpu.make_async_remote_copy(
                    d_cross.at[other, at], r.cross_taken.at[k, :, at],
                    r.give_send.at[k, pair], r.give_recv.at[k, pair], device_id=sibling, device_id_type=MESH,
                )
                for k, d_cross in enumerate((r.cross_keys, r.cross_values))
            ]

        attend(
            r.cross_keys, r.cross_values, r.cross_queries, r.cross_mixture, r.cross_probs, span_d, span, pairs_here,
            r.mask, None, lambda pair: [mix.start() for mix in mixtures(pair)],
        )
        supply.close()
        drain.free(0)
        turn(r.third, r.turned, rows)
        attend_back(
            r.cross_keys, r.cross_values, r.cross_queries, r.cross_back, r.cross_probs, span_d, span, pairs_here, None,
            arrived, lambda pair: [back.start() for back in returns(pair)],
        )
        answers = [
            move(part, r.cross_in_back.at[c], 8 + k, 8 + c, across[k]) for k, part in enumerate(parts_of(r.cross_queries))
        ]
        for answer in answers:
            answer.start()
        for k, d_cross in enumerate((r.cross_keys, r.cross_values)):
            r.d_pair[k, :, near_lanes] = d_cross[mine, :]
        for pair in range(pairs_here):
            for back in returns(pair):
                back.wait_recv()
        for k in range(2):
            r.d_pair[k, :, far_lanes] = r.cross_taken[k]
        drain.allow(0)
        square_grads(rows, CROSS, [(r.turned, r.d_pair.at[0]), (r.turned, r.d_pair.at[1])], nothing)
        drain.begin(CROSS)
        project_back(r.d_pair.at[0], r.square.at[FIRST], r.summed, rows, True)
        project_back(r.d_pair.at[1], r.square.at[SECOND], r.summed, rows, False)
        normalize_back(r.resid_top, r.gains[2], r.summed, r.d_resid, r.gain_parts, rows, True)
        gain_done(2)
        to_bf16(r.d_resid, r.d_branch, rows)
        turn(r.d_branch, r.turned, rows)
        feed_grads(rows, r.turned, 0, OUTER, at_each((2,), lambda: drain.tick(CROSS, 0)))
        drain.tick(CROSS, 1)
        drain.begin(OUTER)
        feed_back(rows, False, at_each((1, 2), schedule([("tick", CROSS, 2)], [("tick", CROSS, 3)])))
        drain.free(1)
        drain.free(2)
        turn(r.second, r.turned, rows)
        drain.allow(1)
        feed_grads(rows, r.turned, tensor, INNER, at_each((1,), lambda: drain.tick(OUTER, 0)))
        normalize_back(r.resid_mid, r.gains[1], r.summed, r.d_resid, r.gain_parts, rows, False)
        gain_done(1)
        for copy in trades + answers:
            copy.wait_send()
        for pair in range(pairs_here):
            for copy in mixtures(pair) + returns(pair):
                copy.wait_send()

        def send_rows():
            to_bf16(r.d_resid, r.rows_out, rows)
            drain.home()

        steps = schedule(
            [("tick", CROSS, 4), ("begin", INNER)], [("tick", OUTER, 1)],
            [], [("end", CROSS)], [], [("tick", OUTER, 2)],
            [("tick", INNER, 0)], [], [("tick", INNER, 1)], [], [("tick", OUTER, 3)], [("tick", OUTER, 4)],
            [("tick", INNER, 2), ("tick", ATTN, 0), ("end", OUTER), ("tick", INNER, 3), ("tick", ATTN, 1), ("tick", ATTN, 2)]
            + [("home_done", None), ("tick", INNER, 4), ("tick", ATTN, 3), ("tick", ATTN, 4), ("end", INNER)],
        )
        self_backward(span, rows, first_row, steps, send_rows)

    @pl.when(here.pipe == 1)
    def _():
        supply.resume(ATTN, CROSS, INNER, OUTER)
        drain.order(OUTER, INNER, CROSS, ATTN)
        entry()
        rows, span = rows_d, span_d
        first_row = pl.multiple_of(c * rows, rows)
        key_at = lax.broadcasted_iota(jnp.int32, (span, rows), 0)
        query_at = lax.broadcasted_iota(jnp.int32, (span, rows), 1) + first_row
        same = segments(lengths_row(nrow), (span, 1), 0, 0) == segments(lengths_row(nrow), (1, rows), 1, first_row)
        r.mask[0:span, 0:rows] = masked(same & (query_at >= key_at))
        supply.pump()
        first_block = c * (tensor // 2)
        rows_ready(span, rows, first_block)
        for k in range(rows // places):
            r.d_branch[k * places : (k + 1) * places, :] = r.x[1, first_block + k]
        supply.pump(until=ATTN)
        supply.finish(ATTN)
        self_forward(span, rows, first_row, CROSS)
        untangle(r.raw_c, FIRST, 2)
        normalize(r.resid_mid, r.gains[1], r.third, rows)
        project(r.third, r.square.at[FIRST], r.joined, rows)
        asks = []
        for k in range(CORES):
            r.send_pair[k, 0:rows, :] = r.joined[:, lane_halves[k]]
            asks.append(move(r.send_pair.at[k, pl.ds(0, rows)], part_here(r.cross_queries), 2 + k, 2 + c, across[k]))
            asks[-1].start()
        supply.pump(until=INNER)
        supply.finish(INNER)
        supply.pump(until=OUTER)
        supply.finish(OUTER)

        @pl.loop(0, tensor)
        def _(tt):
            def body(at):
                r.ff[tensor + tt, rows : 2 * rows, at] = nn(r.d_branch[0:rows, :], r.outer[tt, :, at]).astype(BF16)

            columns_of(units, body)

        supply.close()
        drain.free(0)
        r.resid_top[0:rows, :] = r.resid_mid[0:rows, :]
        for k in range(CORES):
            for pair in range(pairs_here):
                part = r.cross_in.at[k, :, pair_lanes(pair)]
                pltpu.make_async_remote_copy(
                    part, part, r.mix_send.at[k, pair], r.mix_recv.at[k, pair], device_id=across[k], device_id_type=MESH
                ).wait_recv()
            r.joined[:, lane_halves[k]] = r.cross_in[k]
        project_back(r.joined, r.square.at[SECOND], r.resid_top, rows, False)
        normalize(r.resid_top, r.gains[2], r.second, rows)
        feed_forward(rows)
        feed_back(rows, True)
        r.d_resid[0:rows, :] = r.d_branch[0:rows, :].astype(F32)
        normalize_back(r.resid_top, r.gains[2], r.summed, r.d_resid, r.gain_parts, rows, False)
        gain_done(2)
        to_bf16(r.d_resid, r.branch, rows)
        tells = []
        for pair in range(pairs_here):
            at = pair_lanes(pair)
            firsts = [k * half_width + pair * LANES for k in range(CORES)]
            both = jnp.concatenate([r.square[SECOND, :, first : first + LANES] for first in firsts], axis=1)
            value = nn(r.branch[0:rows, :], both).astype(BF16)
            for k in range(CORES):
                r.send_back[k, :, at] = value[:, k * LANES : (k + 1) * LANES]
                tells.append(
                    pltpu.make_async_remote_copy(
                        r.send_back.at[k, :, at], r.cross_back.at[pl.ds(pl.multiple_of(c * rows, rows), rows), at],
                        r.back_send.at[k, pair], r.back_recv.at[c, pair], device_id=across[k], device_id_type=MESH,
                    )
                )
                tells[-1].start()
        drain.free(1)
        turn(r.d_branch, r.turned, rows)
        drain.allow(0)
        feed_grads(rows, r.turned, 0, OUTER)
        drain.begin(OUTER)
        turn(r.second, r.turned, rows)
        drain.allow(1)
        feed_grads(rows, r.turned, tensor, INNER)
        drain.begin(INNER)
        feed_out(r.resid_top, rows, at_each((1,), lambda: drain.tick(OUTER, 0)))
        drain.free(2)
        to_bf16(r.resid_top, r.rows_out, rows)
        turn(r.branch, r.turned, rows)
        turn(r.third, r.turned_more, rows)
        for k in range(CORES):
            move(r.cross_in_back.at[k], r.cross_in_back.at[k], 8 + k, 8 + k, across[k]).wait_recv()
            r.d_pair[1, 0:rows, lane_halves[k]] = r.cross_in_back[k]
        project_back(r.d_pair.at[1], r.square.at[FIRST], r.summed, rows, True)
        square_grads(rows, CROSS, [(r.turned_more, r.d_pair.at[1]), (r.turned, r.joined)], nothing)
        drain.tick(OUTER, 1)
        normalize_back(r.resid_mid, r.gains[1], r.summed, r.d_resid, r.gain_parts, rows, False)
        gain_done(1)
        for copy in asks + tells:
            copy.wait_send()

        def send_rows():
            to_bf16(r.d_resid, r.rows_out.at[pl.ds(rows, rows)], rows)
            drain.home()

        steps = schedule(
            [], [("tick", INNER, 0)], [], [("tick", INNER, 1)], [("tick", OUTER, 2)], [],
            [("tick", OUTER, 3)], [], [("tick", INNER, 2), ("tick", OUTER, 4)], [("begin", CROSS)],
            [("tick", INNER, 3), ("tick", INNER, 4)], [],
            [("end", OUTER), ("tick", CROSS, 0), ("tick", ATTN, 0), ("tick", CROSS, 1), ("end", INNER), ("tick", ATTN, 1)]
            + [("tick", ATTN, 2), ("tick", CROSS, 2), ("home_done", None), ("tick", ATTN, 3), ("tick", ATTN, 4)]
            + [("tick", CROSS, 3), ("tick", CROSS, 4), ("end", CROSS)],
        )
        self_backward(span, rows, first_row, steps, send_rows)

    drain.close()


def held(*shape, dtype=BF16):
    return pltpu.VMEM(shape, dtype)


def arrays(tensor, heads_at, places, width, units, ranges, kinds):
    tall = 2 * tensor * places
    block = width // tensor
    half_rows, half_width = tall // 2, width // 2
    heads = heads_at * tensor
    return dict(
        x=held(2, tensor, places, width),
        own_x=held(half_rows, width),
        raw_a=held(tensor, width, 4 * block),
        raw_c=held(tensor, width, 2 * block),
        square=held(6, width, width),
        inner=held(tensor, width, units),
        outer=held(tensor, width, units),
        hidden=held(tall, width),
        keys=held(tall, width),
        values=held(tall, width),
        queries=held(half_rows, width),
        probs=held(heads, tall, half_rows),
        mask=held(tall, half_rows, dtype=F32),
        mixture=held(half_rows, width),
        resid_mid=held(half_rows, width, dtype=F32),
        resid_top=held(half_rows, width, dtype=F32),
        d_resid=held(half_rows, width, dtype=F32),
        summed=held(half_rows, width, dtype=F32),
        second=held(half_rows, width),
        third=held(half_rows, width),
        ff=held(2 * tensor, half_rows, units),
        d_branch=held(half_rows, width),
        branch=held(half_rows, width),
        cross_keys=held(tall, half_width),
        cross_values=held(tall, half_width),
        cross_queries=held(half_rows, half_width),
        cross_mixture=held(half_rows, half_width),
        cross_probs=held(heads // CORES, tall, half_rows),
        cross_back=held(half_rows, half_width),
        cross_in=held(CORES, half_rows // 2, half_width),
        cross_in_back=held(CORES, half_rows // 2, half_width),
        cross_taken=held(CORES, half_rows, half_width),
        send_pair=held(CORES, half_rows, half_width),
        send_back=held(CORES, half_rows // 2, half_width),
        joined=held(half_rows // 2, width),
        taken_pair=held(2, half_rows, width),
        d_pair=held(2, half_rows, width),
        turned=held(width, half_rows),
        turned_more=held(width, half_rows),
        stage=held(2, width, units),
        vectors=held(8 * tensor, ranges, dtype=F32),
        diagonals=held(8 * tensor, ranges, dtype=F32),
        onehot=held(kinds, ranges, dtype=F32),
        buckets=held(8, ranges, dtype=jnp.int32),
        gain_parts=held(8, width, dtype=F32),
        send_sem=pltpu.SemaphoreType.DMA((14,)),
        recv_sem=pltpu.SemaphoreType.DMA((14,)),
        **{
            name: pltpu.SemaphoreType.DMA((CORES, half_width // LANES))
            for name in ("mix_send", "mix_recv", "back_send", "back_recv", "give_send", "give_recv")
        },
    )


def group_columns(block, units):
    return {ATTN: (0, 4 * block), CROSS: (4 * block, 2 * block), INNER: (6 * block, units), OUTER: (6 * block + units, units)}


def landing(r):
    return {ATTN: r.raw_a, CROSS: r.raw_c, INNER: r.inner, OUTER: r.outer}


class Loads:
    def __init__(self, r, tensor, x_hbm, w_hbm, sems):
        columns = group_columns(r.raw_a.shape[2] // 4, r.inner.shape[2])
        self.x = pltpu.make_async_copy(x_hbm, r.x, sems.at[4, 0])
        self.weights = [
            [
                pltpu.make_async_copy(w_hbm.at[tt, :, pl.ds(*columns[group])], target.at[tt], sems.at[group, tt])
                for tt in range(tensor)
            ]
            for group, target in landing(r).items()
        ]

    def start(self):
        self.x.start()
        for group in self.weights:
            for copy in group:
                copy.start()

    def rows(self):
        self.x.wait()

    def finish(self, group):
        for copy in self.weights[group]:
            copy.wait()

    small = resume = pump = close = nothing


class Stores:
    def __init__(self, r, grads_hbm, sems):
        self.columns = group_columns(r.raw_a.shape[2] // 4, r.inner.shape[2])
        self.r, self.grads, self.sems = r, grads_hbm, sems

    def copy(self, group, tt, slot, place):
        first, wide = self.columns[group]
        return pltpu.make_async_copy(
            self.r.stage.at[slot, :, pl.ds(place * wide, wide)], self.grads.at[tt, :, pl.ds(first, wide)],
            self.sems.at[slot + 2 * place],
        )

    def emit(self, group, tt, slot, place=0):
        self.copy(group, tt, slot, place).start()

    def release(self, group, tt, slot, place=0):
        self.copy(group, tt, slot, place).wait()

    order = free = allow = begin = tick = rest = end = home = home_done = small_begin = close = nothing


def blocks_kernel(tensor, dp, heads_at, names, *refs):
    here = Place(tensor, dp)
    r = types.SimpleNamespace(**dict(zip(names, refs)))
    across = [{"pipe": 1 - here.pipe, "dp": here.group * CORES + k} for k in range(CORES)]
    meet([here.sibling()] + across)
    work(r, here, Loads(r, tensor, r.x_hbm, r.w_hbm, r.load_sem), Stores(r, r.grads_hbm, r.stage_sem), tensor, heads_at)


def blocks(tensor, dp, heads_at, kinds, rows, weights, gains, lengths, tables, buckets):
    places, width = rows.shape[2:]
    units = (weights.shape[2] - 6 * (width // tensor)) // 2
    half_rows = tensor * places
    ranges = -(-buckets[0].shape[1] // LANES) * LANES
    scratch = arrays(tensor, heads_at, places, width, units, ranges, kinds)
    scratch["load_sem"] = pltpu.SemaphoreType.DMA((5, tensor))
    scratch["stage_sem"] = pltpu.SemaphoreType.DMA((4,))
    names = ["x_hbm", "w_hbm", "gains", "lengths", "tables", "enc_buckets", "dec_buckets", "grads_hbm", "rows_out", "gains_out", "bias_out"]
    return pl.pallas_call(
        functools.partial(blocks_kernel, tensor, dp, heads_at, names + list(scratch)),
        out_shape=(
            jax.ShapeDtypeStruct(weights.shape, BF16),
            jax.ShapeDtypeStruct((half_rows, width), BF16),
            jax.ShapeDtypeStruct((8, width), F32),
            jax.ShapeDtypeStruct((8 * tensor, LANES), F32),
        ),
        in_specs=[ANY, ANY] + [VMEM] * 5,
        out_specs=(ANY, VMEM, VMEM, VMEM),
        scratch_shapes=list(scratch.values()),
        compiler_params=pltpu.CompilerParams(collective_id=2, has_side_effects=True, vmem_limit_bytes=VMEM_LIMIT),
        name="blocks",
    )(rows, weights, gains, lengths, tables, *buckets)


def all_sends(r, box, group, depth, hops, targets):
    for part in range(2):
        sent = box.at[0, pl.ds(0, (2 * hops - 1) * depth // 2), :]
        pltpu.make_async_remote_copy(
            sent, sent, r.ring_send.at[group, part], r.ring_recv.at[group, part, 0, 0],
            device_id=targets[part], device_id_type=MESH,
        ).wait_send()


def all_over(r, box, group, here, depth):
    whole = box.at[pl.ds(0, here.chips * depth // box.shape[1])]
    return pltpu.make_async_remote_copy(
        whole, whole, r.over_send.at[group], r.over_recv.at[group], device_id=here.sibling(), device_id_type=MESH
    )


class Rings:
    def __init__(self, r, here, tensor, dp):
        self.r, self.here, self.tensor, self.dp = r, here, tensor, dp
        self.depth = r.value_w.shape[0]
        self.hops = here.chips // 2
        self.count = 2 * self.hops - 1
        self.sibling = here.sibling()
        self.targets = [here.neighbour(1), here.neighbour(-1)]
        self.landing = landing(r)
        self.groups = []
        self.plan = []


    def order(self, *groups):
        steps = []
        for k, group in enumerate(groups):
            steps.append((4 * k - 0.5, k, self.begin, group, None))
            late = {self.count - 3: 3.6, self.count - 2: 3.7, self.count - 1: 5.5}
            steps += [(4 * k + late.get(n, n), k, self.tick, group, n) for n in range(self.count)]
        steps.sort(key=lambda step: step[:2])
        self.groups = list(groups)
        self.plan = [step[2:] for step in steps]

    def resume(self, *groups):
        self.order(*groups)
        self.plan.pop(0)

    def pump(self, count=1, until=None):
        while self.plan and (count > 0 if until is None else any(step[1] == until for step in self.plan)):
            do, group, n = self.plan.pop(0)
            do(group) if n is None else do(group, n)
            count -= 0 if n is None else 1


    def block_out(self, i):
        r, t, c = self.r, self.here.t, self.here.core
        return pltpu.make_async_remote_copy(
            r.rows.at[i], r.x.at[:, t], r.block_send.at[i], r.block_recv.at[t],
            device_id={"tensor": r.rows.shape[0] * c + i}, device_id_type=MESH,
        )

    def block_kept(self, i):
        return pltpu.make_async_copy(self.r.rows.at[i], self.r.x.at[:, self.here.t], self.r.local_sem.at[0])

    def block_pass(self, source, s):
        r = self.r
        return pltpu.make_async_remote_copy(
            source, r.x.at[:, s], r.pass_send.at[s], r.pass_recv.at[s], device_id=self.sibling, device_id_type=MESH
        )

    def blocks(self, mine, others):
        for i in range(self.r.rows.shape[0]):
            here = self.r.rows.shape[0] * self.here.core + i == self.here.t

            @pl.when(here)
            def _():
                mine(i)

            @pl.when(jnp.logical_not(here))
            def _():
                others(i)

    def small_copies(self):
        r, t = self.r, self.here.t
        copies = [
            pltpu.make_async_remote_copy(
                r.lengths_in, r.lengths.at[self.here.core], r.small_send.at[0], r.small_recv.at[0],
                device_id=self.sibling, device_id_type=MESH,
            ),
            pltpu.make_async_copy(r.lengths_in, r.lengths.at[self.here.core], r.local_sem.at[1]),
            pltpu.make_async_copy(r.table_in, r.tables.at[t], r.local_sem.at[2]),
        ]
        for k in range(1, self.tensor):
            copies.append(
                pltpu.make_async_remote_copy(
                    r.table_in, r.tables.at[t], r.small_send.at[k], r.small_recv.at[k],
                    device_id={"tensor": lax.rem(t + k, self.tensor)}, device_id_type=MESH,
                )
            )
        return copies


    def rows_of(self, ring):
        line, at = self.here.at(ring)
        return at, pl.multiple_of((line * CORES + self.here.core) * self.depth, 16)

    def ring_at(self, step, part):
        way = -1 if part else 1
        return lax.rem(self.here.ring - way * step + self.here.chips, self.here.chips)

    def onward(self, group, step, part, sub):
        r, half = self.r, self.depth // 2
        at, first = self.rows_of(self.ring_at(step, part))
        target = self.landing[group]
        slot = target.at[at, pl.ds(pl.multiple_of(first + half * sub, 16), half), :]
        packed = r.stage.at[0, pl.ds(group * self.depth + half * sub, half), pl.ds(0, target.shape[2])]
        return pltpu.make_async_remote_copy(
            packed if step == 0 else slot, slot, r.ring_send.at[group, part], r.ring_recv.at[group, part, sub, step],
            device_id=self.targets[part], device_id_type=MESH,
        )

    def over(self, group, ring, first_time=False):
        r = self.r
        at, first = self.rows_of(ring)
        target = self.landing[group]
        slot = target.at[at, pl.ds(first, self.depth), :]
        packed = r.stage.at[0, pl.ds(group * self.depth, self.depth), pl.ds(0, target.shape[2])]
        return pltpu.make_async_remote_copy(
            packed if first_time else slot, slot, r.over_send.at[group], r.over_recv.at[group],
            device_id=self.sibling, device_id_type=MESH,
        )

    def own(self, group):
        wide = self.landing[group].shape[2]
        first = pl.multiple_of(self.here.d * self.depth, 16)
        return pltpu.make_async_copy(
            self.r.stage.at[0, pl.ds(group * self.depth, self.depth), pl.ds(0, wide)],
            self.landing[group].at[self.here.t, pl.ds(first, self.depth), :],
            self.r.own_sem.at[group],
        )

    def begin(self, group):
        for sub in range(2):
            for part in range(2):
                self.onward(group, 0, part, sub).start()
        self.over(group, self.here.ring, True).start()
        self.own(group).start()

    def tick(self, group, n):
        step, last = n // 2 + 1, n == self.count - 1
        for part in range(2):
            sub = part if last else n % 2
            self.onward(group, step - 1, part, sub).wait_recv()
            if not last and (step < self.hops - 1 or sub == part):
                self.onward(group, step, part, sub).start()
        if last:
            self.over(group, self.ring_at(step, 0)).start()
        elif n % 2:
            for part in range(2):
                self.over(group, self.ring_at(step, part)).start()

    def sends_done(self, group):
        all_sends(self.r, self.landing[group], group, self.depth, self.hops, self.targets)

    def finish(self, group):
        all_over(self.r, self.landing[group], group, self.here, self.depth).wait_recv()
        self.own(group).wait()

    def start(self):
        r, depth = self.r, self.depth
        block = r.value_w.shape[1]

        def band(group, pieces):
            wide = pieces[0].shape[1]
            for k, piece in enumerate(pieces):
                r.stage[0, group * depth : (group + 1) * depth, k * wide : (k + 1) * wide] = piece

        band(ATTN, [r.query_key_w[1], r.value_w[...], r.query_key_w[0], r.out_w[...].T])
        self.order(ATTN)
        self.begin(ATTN)
        nrow = r.rows.shape[0]
        r.lengths_in[...] = jnp.zeros_like(r.lengths_in)
        r.lengths_in[0:nrow, 0 : r.enc_lengths.shape[1]] = r.enc_lengths[...]
        r.lengths_in[nrow : 2 * nrow, 0 : r.dec_lengths.shape[1]] = r.dec_lengths[...]
        r.table_in[...] = jnp.zeros_like(r.table_in)
        for k in range(r.bias_w.shape[0]):
            r.table_in[k : k + 1, 0 : r.bias_w.shape[2]] = r.bias_w[k]
        self.blocks(
            lambda i: (self.block_kept(i).start(), self.block_pass(r.rows.at[i], self.here.t).start()),
            lambda i: self.block_out(i).start(),
        )
        for copy in self.small_copies():
            copy.start()
        band(INNER, [r.inner_w[...]])
        band(OUTER, [r.outer_w[...]])
        band(CROSS, [r.first_w[...], r.second_w[...]])

    def small(self):
        for copy in self.small_copies():
            copy.wait()

    def rows(self):
        r, t = self.r, self.here.t
        takes = lax.div(t, r.rows.shape[0]) == self.here.core
        for s in range(self.tensor):

            @pl.when(jnp.logical_and(takes, s != t))
            def _():
                pltpu.make_async_remote_copy(
                    r.rows.at[0], r.x.at[:, s], r.block_send.at[0], r.block_recv.at[s],
                    device_id=self.sibling, device_id_type=MESH,
                ).wait_recv()
                self.block_pass(r.x.at[:, s], s).start()

        self.blocks(lambda i: self.block_kept(i).wait(), nothing)
        for s in range(self.tensor):

            @pl.when(jnp.logical_not(takes))
            def _():
                self.block_pass(r.x.at[:, s], s).wait_recv()

    def close(self):
        r, t = self.r, self.here.t
        takes = lax.div(t, r.rows.shape[0]) == self.here.core
        self.blocks(
            lambda i: self.block_pass(r.rows.at[i], t).wait_send(),
            lambda i: self.block_out(i).wait_send(),
        )
        for s in range(self.tensor):

            @pl.when(jnp.logical_and(takes, s != t))
            def _():
                self.block_pass(r.x.at[:, s], s).wait_send()

        for group in self.groups:
            self.sends_done(group)
            all_over(r, self.landing[group], group, self.here, self.depth).wait_send()


class Sums:
    def __init__(self, r, here, tensor, dp):
        self.r, self.here, self.tensor, self.dp = r, here, tensor, dp
        self.depth = r.value_w.shape[0]
        self.hops = here.chips // 2
        self.count = 2 * self.hops - 3
        self.sibling = here.sibling()
        self.targets = [here.neighbour(1), here.neighbour(-1)]
        self.box = {CROSS: r.raw_c, OUTER: r.raw_a, INNER: r.inner, ATTN: r.outer}
        self.kept = {CROSS: r.own_cross, OUTER: r.own_outer, INNER: r.own_inner, ATTN: r.ff}
        self.groups = []

    def order(self, *groups):
        self.groups = list(groups)

    def free(self, k):
        for device in self.targets + [self.sibling]:
            pl.semaphore_signal(self.r.free_sem.at[k], inc=1, device_id=device, device_id_type=MESH)

    def allow(self, k):
        pl.semaphore_wait(self.r.free_sem.at[k], 3)

    def boxed(self, group, index, first, height):
        if isinstance(index, int):
            return (index // self.dp, pl.ds(pl.multiple_of(index % self.dp * self.depth + first, 16), height), slice(None))
        at = pl.ds(pl.multiple_of(lax.rem(index, self.dp) * self.depth + first, 16), height)
        return (lax.div(index, self.dp), at, slice(None))

    def taken(self, group, step, part, first, height):
        index = step + part * (self.hops - 1) if step else 0
        return self.boxed(group, index, first, height)

    def theirs(self, group, ring, first, height):
        return self.boxed(group, self.here.chips - 1 + ring, first, height)

    def own(self, group, ring, first, height):
        return (ring, pl.ds(first, height), slice(None))

    def ring_of(self, line, at):
        return line * self.tensor + at + (line % 2) * (self.tensor - 1 - 2 * at)

    def pieces(self, group, tt, slot, place=0):
        r, depth = self.r, self.depth
        wide = self.box[group].shape[2]
        sem = slot + 2 * place
        made = []
        for line in range(self.here.groups):
            ring = self.ring_of(line, tt)

            def rows_of(core):
                return r.stage.at[slot, pl.ds(pl.multiple_of((line * CORES + core) * depth, 16), depth), pl.ds(place * wide, wide)]

            made.append(
                pltpu.make_async_copy(
                    rows_of(self.here.core), self.kept[group].at[self.own(group, ring, 0, depth)], r.kept_sem.at[sem, line]
                )
            )
            made.append(
                pltpu.make_async_remote_copy(
                    rows_of(1 - self.here.core), self.box[group].at[self.theirs(group, ring, 0, depth)],
                    r.pair_send.at[sem, line], r.over_recv.at[group], device_id=self.sibling, device_id_type=MESH,
                )
            )
        return made

    def emit(self, group, tt, slot, place=0):
        for piece in self.pieces(group, tt, slot, place):
            piece.start()

    def release(self, group, tt, slot, place=0):
        for k, piece in enumerate(self.pieces(group, tt, slot, place)):
            if k % 2:
                piece.wait_send()
            else:
                piece.wait()


    def rows_at(self, sub):
        half = self.depth // 2
        return half * sub, half

    def source(self, step, part):
        way = -1 if part else 1
        return lax.rem(self.here.ring + way * (self.hops - step) + self.here.chips, self.here.chips)

    def onward(self, group, step, part, sub):
        r = self.r
        first, height = self.rows_at(sub)
        return pltpu.make_async_remote_copy(
            self.kept[group].at[self.own(group, self.source(step, part), first, height)],
            self.box[group].at[self.taken(group, step, part, first, height)],
            r.ring_send.at[group, part], r.ring_recv.at[group, part, sub, step],
            device_id=self.targets[part], device_id_type=MESH,
        )

    def here_sum(self, group, ring, first, height):
        value = self.kept[group][self.own(group, ring, first, height)].astype(F32)
        return value + self.box[group][self.theirs(group, ring, first, height)].astype(F32)

    def advance(self, group, step, part, sub, fresh=False):
        if not fresh:
            self.onward(group, step - 1, part, sub).wait_recv()
        ring = self.source(step, part)

        def add(first, height):
            value = self.here_sum(group, ring, first, height)
            if not fresh:
                value = value + self.box[group][self.taken(group, step - 1, part, first, height)].astype(F32)
            self.kept[group][self.own(group, ring, first, height)] = value.astype(BF16)

        self.in_pieces(sub, add)
        self.onward(group, step, part, sub).start()

    def in_pieces(self, sub, body):
        start, height = self.rows_at(sub)

        @pl.loop(0, height // 32)
        def _(k):
            body(pl.multiple_of(start + 32 * k, 32), 32)

    def begin(self, group):
        all_over(self.r, self.box[group], group, self.here, self.depth).wait_recv()
        for part in range(2):
            self.advance(group, 0, part, part, True)
        for part in range(2):
            self.advance(group, 1, part, 1 - part, True)
        if group == ATTN:
            self.small_across().wait_recv()
            self.small_advance(0, 0, True)
            self.small_advance(1, 1, True)

    def tick(self, group, n):
        step, leads = (n + 1) // 2 + 1, n % 2
        for part in range(2):
            self.advance(group, step, part, 1 - part if leads else part)
        if group == ATTN and not leads:
            self.small_advance(step, 0)
            if step > 1:
                self.small_advance(step, 1)

    def sends_done(self, group):
        all_sends(self.r, self.box[group], group, self.depth, self.hops, self.targets)

    def rest(self, group):
        self.end(group)
        for group in (ATTN, CROSS, INNER, OUTER):
            self.sends_done(group)

    def end(self, group):
        r, last = self.r, self.hops - 1
        for sub in range(2):
            for part in range(2):
                self.onward(group, last, part, sub).wait_recv()
            target = r.inner_out if group == INNER else r.total

            def add(first, height):
                value = self.here_sum(group, self.here.ring, first, height)
                for part in range(2):
                    value = value + self.box[group][self.taken(group, last, part, first, height)].astype(F32)
                target[pl.ds(first, height), 0 : self.box[group].shape[2]] = value

            self.in_pieces(sub, add)
        block = r.value_w.shape[1]
        done = {ATTN: ("pair_out", "value_out", "out_out", "tiny_out"), CROSS: ("first_out", "second_out")}
        if group == ATTN:
            r.pair_out[1] = r.total[:, 0:block]
            r.value_out[...] = r.total[:, block : 2 * block]
            r.pair_out[0] = r.total[:, 2 * block : 3 * block]
            r.out_out[...] = r.total[:, 3 * block : 4 * block].T
            at = self.small_at(self.here.ring)
            value = r.small[at] + r.small_theirs[at]
            for part in range(2):
                self.small_onward(last, part).wait_recv()
                value = value + r.small_taken[part, last]
            r.tiny_out[...] = value
        if group == CROSS:
            r.first_out[...] = r.total[:, 0:block]
            r.second_out[...] = r.total[:, block : 2 * block]
        if group == OUTER:
            r.outer_out[...] = r.total[...]
        for name in done.get(group, ("inner_out",) if group == INNER else ("outer_out",)):
            self.result(name).start()

    def result(self, name):
        r = self.r
        return pltpu.make_async_copy(getattr(r, name), getattr(r, name + "_hbm"), r.result_sem.at[r.results.index(name)])


    def small_at(self, ring):
        line, at = self.here.at(ring)
        return at, line * CORES + self.here.core

    def small_across(self):
        r = self.r
        return pltpu.make_async_remote_copy(
            r.small, r.small_theirs, r.small_sem.at[0], r.small_sem.at[1], device_id=self.sibling, device_id_type=MESH
        )

    def small_onward(self, step, part):
        r = self.r
        return pltpu.make_async_remote_copy(
            r.small_sent.at[part, step], r.small_taken.at[part, step], r.tiny_send.at[part, step], r.tiny_recv.at[part, step],
            device_id=self.targets[part], device_id_type=MESH,
        )

    def small_advance(self, step, part, fresh=False):
        at = self.small_at(self.source(step, part))
        value = self.r.small[at] + self.r.small_theirs[at]
        if not fresh:
            self.small_onward(step - 1, part).wait_recv()
            value = value + self.r.small_taken[part, step - 1]
        self.r.small_sent[part, step] = value
        self.small_onward(step, part).start()

    def small_begin(self):
        r, depth = self.r, self.depth
        r.small[...] = jnp.zeros_like(r.small)
        kinds = r.onehot.shape[0] // self.dp
        heads_at = self.heads_at
        for tt in range(self.tensor):
            for d in range(self.dp):
                r.small[tt, d, 0:3, 0:depth] = r.gains_out[0:3, d * depth : (d + 1) * depth]
                r.small[tt, d, 3 : 3 + heads_at, 0:kinds] = r.bias_out[
                    8 * tt : 8 * tt + heads_at, d * kinds : (d + 1) * kinds
                ]
        self.small_across().start()


    def home_copy(self, k):
        r, here, tensor = self.r, self.here, self.tensor
        nrow, half, places = r.home_in.shape[0], tensor // 2, r.home_in.shape[2]
        place = here.pipe * (here.core * half + k % half) + (1 - here.pipe) * k
        which = here.pipe * (k // half) + (1 - here.pipe) * here.core
        owner = lax.div(here.t, nrow)
        source = r.rows_out.at[pl.ds(k * places, places)]
        slot = r.home_in.at[lax.rem(here.t, nrow), which]
        recv = r.home_recv.at[lax.rem(here.t, nrow), which]
        return (
            jnp.logical_and(place == here.t, owner == here.core),
            lambda: pltpu.make_async_copy(source, slot, recv),
            lambda: pltpu.make_async_remote_copy(
                source, slot, r.home_send.at[k], recv,
                device_id={"dp": here.group * CORES + owner, "tensor": place}, device_id_type=MESH,
            ),
        )

    def home(self):
        for k in range(self.tensor):
            stays, inside, away = self.home_copy(k)

            @pl.when(stays)
            def _():
                inside().start()

            @pl.when(jnp.logical_not(stays))
            def _():
                away().start()

    def home_done(self, unused=None):
        r = self.r
        places = r.home_in.shape[2]
        for i in range(r.home_in.shape[0]):
            for which in range(2):
                pltpu.make_async_copy(
                    r.rows_out.at[pl.ds(0, places)], r.home_in.at[i, which], r.home_recv.at[i, which]
                ).wait()
                r.home_out[i, which] = r.home_in[i, which].astype(F32)
        self.result("home_out").start()

    def close(self):
        r = self.r
        for k in range(self.tensor):
            stays, inside, away = self.home_copy(k)

            @pl.when(jnp.logical_not(stays))
            def _():
                away().wait_send()

        for name in r.results:
            self.result(name).wait()
        self.small_across().wait_send()

        for part in range(2):
            for step in range(part, self.hops):
                self.small_onward(step, part).wait_send()


def fits_fused(tensor, dp, depth, units, width):
    chips = tensor * dp // CORES
    return (
        depth % 32 == 0
        and 4 * depth <= width
        and chips <= 2 * tensor
        and chips == 2 * tensor == 8
        and chips * depth == 2 * width
        and units == width == 6 * LANES
    )


def fused_kernel(tensor, dp, heads_at, results, names, *refs):
    here = Place(tensor, dp)
    r = types.SimpleNamespace(**dict(zip(names, refs)))
    line = [
        {"dp": here.group * CORES + lax.rem(here.core + j, CORES), "tensor": lax.rem(here.t + k, tensor)}
        for j in range(CORES)
        for k in range(tensor)
        if j + k > 0
    ]
    across = [{"pipe": 1 - here.pipe, "dp": here.group * CORES + k} for k in range(CORES)]
    r.results = results
    given = [name for name in names if name + "_hbm" in names and name not in results]
    copies = [
        pltpu.make_async_copy(getattr(r, name + "_hbm"), getattr(r, name), r.given_sem.at[k]) for k, name in enumerate(given)
    ]
    for copy in copies:
        copy.start()
    meet([here.neighbour(1), here.neighbour(-1)] + line + across)
    for copy in copies:
        copy.wait()
    supply, drain = Rings(r, here, tensor, dp), Sums(r, here, tensor, dp)
    drain.heads_at = heads_at
    work(r, here, supply, drain, tensor, heads_at)


def fused(tensor, dp, rows, enc_lengths, dec_lengths, gains, bias, buckets, weights):
    nrow, two, places, width = rows.shape
    depth, block = weights[1].shape
    units = weights[5].shape[1]
    heads_at, _, kinds = bias.shape
    chips = tensor * dp // CORES
    wide = -(-max(depth, kinds // dp) // LANES) * LANES
    sems = pltpu.SemaphoreType.DMA
    ranges = -(-buckets[0].shape[1] // LANES) * LANES
    scratch = arrays(tensor, heads_at, places, width, units, ranges, kinds)
    given = dict(enc_lengths=enc_lengths, dec_lengths=dec_lengths, gains=gains, bias_w=bias)
    given.update(enc_buckets=buckets[0], dec_buckets=buckets[1])
    names = ("query_key_w", "value_w", "out_w", "first_w", "second_w", "inner_w", "outer_w")
    given.update(zip(names, weights))
    scratch.update({name: pltpu.VMEM(array.shape, array.dtype) for name, array in given.items()})
    scratch.update(
        lengths_in=held(8, LANES, dtype=jnp.int32),
        table_in=held(8, LANES, dtype=F32),
        lengths=held(CORES, 8, LANES, dtype=jnp.int32),
        tables=held(tensor, 8, LANES, dtype=F32),
        own_cross=held(chips, depth, 2 * block),
        own_outer=held(chips, depth, units),
        own_inner=held(chips, depth, units),
        total=held(depth, units, dtype=F32),
        rows_out=held(tensor * places, width),
        gains_out=held(8, width, dtype=F32),
        bias_out=held(8 * tensor, LANES, dtype=F32),
        home_in=held(nrow, two, places, width),
        small=held(tensor, dp, 8, wide, dtype=F32),
        small_theirs=held(tensor, dp, 8, wide, dtype=F32),
        small_sent=held(2, chips // 2, 8, wide, dtype=F32),
        small_taken=held(2, chips // 2, 8, wide, dtype=F32),
        block_send=sems((nrow,)), block_recv=sems((tensor,)), pass_send=sems((tensor,)), pass_recv=sems((tensor,)),
        local_sem=sems((3,)), small_send=sems((tensor,)), small_recv=sems((tensor,)), own_sem=sems((4,)),
        ring_send=sems((4, 2)), ring_recv=sems((4, 2, 2, chips // 2)),
        over_send=sems((4,)), over_recv=sems((4,)), kept_sem=sems((4, dp // CORES)), pair_send=sems((4, dp // CORES)),
        small_sem=sems((2,)), tiny_send=sems((2, chips // 2)), tiny_recv=sems((2, chips // 2)),
        home_send=sems((tensor,)), home_recv=sems((nrow, two)),
        free_sem=pltpu.SemaphoreType.REGULAR((3,)), given_sem=sems((len(given),)),
    )
    inputs = ["rows"] + [name + "_hbm" for name in given]
    outputs = dict(
        home_out=rows.shape, tiny_out=(8, wide), pair_out=(2, depth, block), value_out=(depth, block),
        out_out=(block, depth), first_out=(depth, block), second_out=(depth, block), inner_out=(depth, units),
        outer_out=(depth, units),
    )
    scratch.update({name: held(*shape, dtype=F32) for name, shape in outputs.items()})
    scratch["result_sem"] = sems((len(outputs),))
    return pl.pallas_call(
        functools.partial(fused_kernel, tensor, dp, heads_at, list(outputs), inputs + [name + "_hbm" for name in outputs] + list(scratch)),
        out_shape=tuple(jax.ShapeDtypeStruct(shape, F32) for shape in outputs.values()),
        in_specs=[ANY] * (1 + len(given)),
        out_specs=(ANY,) * len(outputs),
        scratch_shapes=list(scratch.values()),
        compiler_params=pltpu.CompilerParams(collective_id=3, has_side_effects=True, vmem_limit_bytes=VMEM_LIMIT),
        name="fused",
    )(rows, *given.values())


def pad_to(array, *shape):
    return jnp.pad(array, [(0, full - have) for full, have in zip(shape, array.shape)])


def shards(
    tensor, dp, section_rows, enc_lengths, dec_lengths, enc_buckets, dec_buckets, norm_gains, rel_bias,
    query_key_w, value_w, attn_out_w, cross_first, cross_second, ff_in, ff_out,
):
    depth = value_w.shape[1]
    width = section_rows.shape[-1]
    buckets = (enc_buckets[None], dec_buckets[None])
    gains = norm_gains.transpose(1, 0, 2)
    bias = rel_bias.transpose(2, 0, 1)
    weights = (query_key_w[0], value_w[0], attn_out_w[0], cross_first[0], cross_second[0], ff_in[0], ff_out[0].T)
    run = fused if fits_fused(tensor, dp, depth, ff_in.shape[2], width) else in_three
    home, tiny, *grads = run(tensor, dp, section_rows[0], enc_lengths, dec_lengths, gains, bias, buckets, weights)
    gain, kind, home, *grads, outer = copied(depth, bias.shape[0], bias.shape[2] // dp, tiny, home, *grads)
    return (
        (home[None], gain.transpose(1, 0, 2), kind.transpose(1, 2, 0))
        + tuple(grad[None] for grad in grads)
        + (outer.T[None],)
    )


def copied(depth, heads_at, kinds, tiny, *results):
    count = len(results)

    def kernel(*refs):
        sources, refs = refs[: count + 1], refs[count + 1 :]
        targets, refs = refs[: count + 2], refs[count + 2 :]
        held_here, (tiny_ref, in_sem, out_sem) = refs[: count + 2], refs[count + 2 :]
        ins = [
            pltpu.make_async_copy(source, there, in_sem.at[k])
            for k, (source, there) in enumerate(zip(sources, (tiny_ref,) + tuple(held_here[2:])))
        ]
        outs = [pltpu.make_async_copy(there, target, out_sem.at[k]) for k, (there, target) in enumerate(zip(held_here, targets))]
        for copy in ins:
            copy.start()
        for copy, out in zip(ins[1:], outs[2:]):
            copy.wait()
            out.start()
        ins[0].wait()
        for k in range(3):
            held_here[0][k] = tiny_ref[k : k + 1, 0:depth]
        for k in range(heads_at):
            held_here[1][k] = tiny_ref[3 + k : 4 + k, 0:kinds]
        outs[0].start()
        outs[1].start()
        for out in outs:
            out.wait()

    shapes = [(3, 1, depth), (heads_at, 1, kinds)] + [result.shape for result in results]
    sems = pltpu.SemaphoreType.DMA
    return pl.pallas_call(
        kernel,
        out_shape=tuple(jax.ShapeDtypeStruct(shape, F32) for shape in shapes),
        in_specs=[ANY] * (count + 1),
        out_specs=(ANY,) * (count + 2),
        scratch_shapes=[held(*shape, dtype=F32) for shape in shapes + [tiny.shape]] + [sems((count + 1,)), sems((count + 2,))],
        compiler_params=pltpu.CompilerParams(vmem_limit_bytes=VMEM_LIMIT),
        name="copied",
    )(tiny, *results)


def in_three(tensor, dp, section_rows, enc_lengths, dec_lengths, gains, bias, buckets, weights):
    query_key, value, out, first, second, inner, outer = weights
    nrow, _, _, width = section_rows.shape
    heads_at, _, kinds = bias.shape
    lengths = pad_to(jnp.concatenate([enc_lengths, dec_lengths], axis=0), 8, LANES)
    table = pad_to(bias[:, 0], 8, LANES)
    depth, block = value.shape
    units = inner.shape[1]
    pack = jnp.concatenate([query_key[1], value, query_key[0], out.T, first, second, inner, outer], axis=1)
    rows, gathered, lengths, tables = gather(tensor, dp, section_rows, pack, lengths, table)
    grads, finished, gain_grads, bias = blocks(
        tensor, dp, heads_at, kinds, rows, gathered.reshape(tensor, width, -1), gains, lengths, tables, buckets
    )
    held_kinds = kinds // dp
    wide = -(-max(depth, held_kinds) // LANES) * LANES
    gain_part = pad_to(gain_grads[:3].reshape(3, dp, depth).transpose(1, 0, 2), dp, 3, wide)
    bias_part = bias.reshape(tensor, 8, LANES)[:, :heads_at, :kinds].reshape(tensor, heads_at, dp, held_kinds)
    bias_part = pad_to(bias_part.transpose(0, 2, 1, 3), tensor, dp, 5, wide)
    small = jnp.concatenate([jnp.broadcast_to(gain_part[None], (tensor,) + gain_part.shape), bias_part], axis=2)
    total, tiny, home = scatter(
        tensor, dp, grads.reshape(tensor, dp, depth, -1), small, finished.reshape(tensor, -1, width), nrow
    )
    key, value, query, out, first, second = [total[:, k * block : (k + 1) * block] for k in range(6)]
    inner, outer = total[:, 6 * block : 6 * block + units], total[:, 6 * block + units :]
    return (
        home.astype(F32), tiny,
        jnp.stack([query, key]), value, out.T, first, second, inner, outer,
    )


def solution(mesh):
    sizes = dict(mesh.shape)
    return jax.shard_map(
        functools.partial(shards, sizes["tensor"], sizes["dp"]),
        mesh=mesh,
        in_specs=(
            P("pipe", "dp", None, "tensor", None),
            P("dp", None),
            P("dp", None),
            P(),
            P(),
            P("pipe", None, None),
            P("pipe", None, "tensor"),
            P("pipe", None, "dp", "tensor"),
            P("pipe", "dp", "tensor"),
            P("pipe", "tensor", "dp"),
            P("pipe", "dp", "tensor"),
            P("pipe", "dp", "tensor"),
            P("pipe", "dp", "tensor"),
            P("pipe", "tensor", "dp"),
        ),
        out_specs=(
            P("pipe", "dp", None, "tensor", None),
            P("pipe", None, "dp"),
            P("pipe", "dp", "tensor"),
            P("pipe", None, "dp", "tensor"),
            P("pipe", "dp", "tensor"),
            P("pipe", "tensor", "dp"),
            P("pipe", "dp", "tensor"),
            P("pipe", "dp", "tensor"),
            P("pipe", "dp", "tensor"),
            P("pipe", "tensor", "dp"),
        ),
        check_vma=False,
    )
```

```python
import functools
import types

import jax
import jax.numpy as jnp
from jax import lax
from jax.experimental import pallas as pl
from jax.experimental.pallas import tpu as pltpu
from jax.sharding import PartitionSpec as P

MESH = pl.DeviceIdType.MESH
F32 = jnp.float32
BF16 = jnp.bfloat16
EPSILON = 1e-06
NEGATIVE = -1000000000.0
HEAD_DIM = 64
CORES = 2
LANES = 128
VMEM_LIMIT = 62 << 20
ANY = pl.BlockSpec(memory_space=pl.ANY)
VMEM = pl.BlockSpec(memory_space=pltpu.VMEM)


def nn(a, b):
    return lax.dot_general(a, b, (((1,), (0,)), ((), ())), preferred_element_type=F32)


def nt(a, b):
    return lax.dot_general(a, b, (((1,), (1,)), ((), ())), preferred_element_type=F32)


def tn(a, b):
    return lax.dot_general(a, b, (((0,), (0,)), ((), ())), preferred_element_type=F32)


class Place:
    def __init__(self, tensor, dp):
        self.tensor = tensor
        self.groups = dp // CORES
        self.chips = tensor * self.groups
        self.pipe = lax.axis_index("pipe")
        self.d = lax.axis_index("dp")
        self.t = lax.axis_index("tensor")
        self.core = lax.rem(self.d, CORES)
        self.group = self.d // CORES
        odd = lax.rem(self.group, 2)
        self.ring = self.group * tensor + self.t + odd * (tensor - 1 - 2 * self.t)

    def at(self, ring):
        group = ring // self.tensor
        along = lax.rem(ring, self.tensor)
        odd = lax.rem(group, 2)
        return group, along + odd * (self.tensor - 1 - 2 * along)

    def neighbour(self, step):
        group, t = self.at(lax.rem(self.ring + step + self.chips, self.chips))
        return {"dp": group * CORES + self.core, "tensor": t}

    def sibling(self):
        return {"dp": self.group * CORES + 1 - self.core}


def meet(devices):
    barrier = pltpu.get_barrier_semaphore()
    for device in devices:
        pl.semaphore_signal(barrier, inc=1, device_id=device, device_id_type=MESH)
    pl.semaphore_wait(barrier, len(devices))


def halves(rows, columns):
    if rows % 32 == 0:
        return [(pl.ds(k * (rows // 2), rows // 2), pl.ds(0, columns)) for k in range(2)]
    cut = columns // LANES // 2 * LANES
    return [(pl.ds(0, rows), pl.ds(0, cut)), (pl.ds(0, rows), pl.ds(cut, columns - cut))]


def gather_kernel(
    tensor, dp, rows_ref, pack_ref, length_ref, table_ref, x_ref, w_ref, lengths_ref, tables_ref,
    local_sem, block_send, block_recv, pass_send, pass_recv, small_send, small_recv,
    ring_send, ring_recv, core_send, core_recv,
):
    here = Place(tensor, dp)
    c, t, chips = here.core, here.t, here.chips
    nrow = rows_ref.shape[0]
    sibling = here.sibling()
    to_right, to_left = here.neighbour(1), here.neighbour(-1)
    others = [{"tensor": lax.rem(t + k, tensor)} for k in range(1, tensor)]
    meet([to_right, to_left, sibling] + others)

    lengths = pltpu.make_async_remote_copy(
        length_ref, lengths_ref.at[c], small_send.at[0], small_recv.at[0], device_id=sibling, device_id_type=MESH
    )
    lengths.start()
    own_lengths = pltpu.make_async_copy(length_ref, lengths_ref.at[c], local_sem.at[0])
    own_lengths.start()
    own_table = pltpu.make_async_copy(table_ref, tables_ref.at[t], local_sem.at[1])
    own_table.start()
    tables = []
    for k in range(1, tensor):
        tables.append(
            pltpu.make_async_remote_copy(
                table_ref, tables_ref.at[t], small_send.at[k], small_recv.at[k], device_id=others[k - 1], device_id_type=MESH
            )
        )
        tables[-1].start()

    def to_chip(i):
        return pltpu.make_async_remote_copy(
            rows_ref.at[i], x_ref.at[:, t], block_send.at[i], block_recv.at[t],
            device_id={"tensor": nrow * c + i}, device_id_type=MESH,
        )

    def kept(i):
        return pltpu.make_async_copy(rows_ref.at[i], x_ref.at[:, t], local_sem.at[2])

    def kept_pass(i):
        return pltpu.make_async_remote_copy(
            rows_ref.at[i], x_ref.at[:, t], pass_send.at[t], pass_recv.at[t], device_id=sibling, device_id_type=MESH
        )

    def passed(s):
        return pltpu.make_async_remote_copy(
            x_ref.at[:, s], x_ref.at[:, s], pass_send.at[s], pass_recv.at[s], device_id=sibling, device_id_type=MESH
        )

    for i in range(nrow):
        mine = nrow * c + i == t

        @pl.when(mine)
        def _():
            kept(i).start()
            kept_pass(i).start()

        @pl.when(jnp.logical_not(mine))
        def _():
            to_chip(i).start()

    parts = halves(*pack_ref.shape)
    own_pack = pltpu.make_async_copy(pack_ref, w_ref.at[t, here.d], local_sem.at[3])
    own_pack.start()

    def shard(ring, part):
        group, at = here.at(ring)
        return w_ref.at[at, group * CORES + c, parts[part][0], parts[part][1]]

    def source(step, part):
        return lax.rem(here.ring + (1 if part else -1) * step + chips, chips)

    def onward(step, part, first=False):
        slot = shard(source(step, part), part)
        return pltpu.make_async_remote_copy(
            pack_ref.at[parts[part][0], parts[part][1]] if first else slot, slot,
            ring_send.at[part, step], ring_recv.at[part, step],
            device_id=to_left if part else to_right, device_id_type=MESH,
        )

    def across(step, part, first=False):
        slot = shard(source(step, part), part)
        return pltpu.make_async_remote_copy(
            pack_ref.at[parts[part][0], parts[part][1]] if first else slot, slot,
            core_send.at[part, step], core_recv.at[part, step], device_id=sibling, device_id_type=MESH,
        )

    for part in range(2):
        onward(0, part, True).start()
        across(0, part, True).start()

    takes = t // nrow == c
    for s in range(tensor):

        @pl.when(jnp.logical_and(takes, s != t))
        def _():
            pltpu.make_async_remote_copy(
                rows_ref.at[0], x_ref.at[:, s], block_send.at[0], block_recv.at[s], device_id=sibling, device_id_type=MESH
            ).wait_recv()
            passed(s).start()

    @pl.loop(1, chips)
    def _(step):
        for part in range(2):
            onward(step - 1, part).wait_recv()

            @pl.when(step < chips - 1)
            def _():
                onward(step, part).start()

            across(step, part).start()

    @pl.loop(0, chips)
    def _(step):
        for part in range(2):

            @pl.when(step < chips - 1)
            def _():
                onward(step, part).wait_send()

            across(step, part).wait_send()
            across(step, part).wait_recv()

    for i in range(nrow):
        mine = nrow * c + i == t

        @pl.when(mine)
        def _():
            kept(i).wait()
            kept_pass(i).wait_send()

        @pl.when(jnp.logical_not(mine))
        def _():
            to_chip(i).wait_send()

    for s in range(tensor):

        @pl.when(jnp.logical_and(takes, s != t))
        def _():
            passed(s).wait_send()

        @pl.when(jnp.logical_not(takes))
        def _():
            passed(s).wait_recv()

    lengths.wait()
    own_lengths.wait()
    own_table.wait()
    own_pack.wait()
    for table in tables:
        table.wait()


def gather(tensor, dp, rows, pack, lengths, table):
    chips = tensor * dp // CORES
    nrow, two, places, width = rows.shape
    sems = pltpu.SemaphoreType.DMA
    return pl.pallas_call(
        functools.partial(gather_kernel, tensor, dp),
        out_shape=(
            jax.ShapeDtypeStruct((two, tensor, places, width), rows.dtype),
            jax.ShapeDtypeStruct((tensor, dp) + pack.shape, pack.dtype),
            jax.ShapeDtypeStruct((CORES,) + lengths.shape, lengths.dtype),
            jax.ShapeDtypeStruct((tensor,) + table.shape, table.dtype),
        ),
        in_specs=[ANY] * 4,
        out_specs=(ANY,) * 4,
        scratch_shapes=[
            sems((4,)), sems((nrow,)), sems((tensor,)), sems((tensor,)), sems((tensor,)), sems((tensor,)), sems((tensor,)),
            sems((2, chips)), sems((2, chips)), sems((2, chips)), sems((2, chips)),
        ],
        compiler_params=pltpu.CompilerParams(collective_id=0, has_side_effects=True),
        name="gather",
    )(rows, pack, lengths, table)


def scatter_kernel(
    tensor, dp, grads_ref, small_ref, rows_ref, out_ref, small_out, rows_out,
    own, theirs, taken, small_own, small_theirs, small_taken, total,
    own_sem, core_send, core_recv, ring_send, ring_recv,
    sown_sem, score_send, score_recv, sring_send, sring_recv, block_send, block_recv, local_sem,
):
    here = Place(tensor, dp)
    c, t, chips = here.core, here.t, here.chips
    nrow = rows_out.shape[0]
    sibling = here.sibling()
    to_right, to_left = here.neighbour(1), here.neighbour(-1)
    line = [
        {"dp": here.group * CORES + lax.rem(c + j, CORES), "tensor": lax.rem(t + k, tensor)}
        for j in range(CORES)
        for k in range(tensor)
        if j + k > 0
    ]
    meet([to_right, to_left] + line)

    half = tensor // 2
    owner = t // nrow

    def block(k):
        place = here.pipe * (c * half + k % half) + (1 - here.pipe) * k
        which = here.pipe * (k // half) + (1 - here.pipe) * c
        return place, which

    def home(k):
        place, which = block(k)
        slot = rows_out.at[lax.rem(t, nrow), which]
        recv = block_recv.at[lax.rem(t, nrow), which]
        return (
            jnp.logical_and(place == t, owner == c),
            lambda: pltpu.make_async_copy(rows_ref.at[k], slot, recv),
            lambda: pltpu.make_async_remote_copy(
                rows_ref.at[k], slot, block_send.at[k], recv,
                device_id={"dp": here.group * CORES + owner, "tensor": place}, device_id_type=MESH,
            ),
        )

    for k in range(tensor):
        stays, inside, away = home(k)

        @pl.when(stays)
        def _():
            inside().start()

        @pl.when(jnp.logical_not(stays))
        def _():
            away().start()

    def across(ring):
        group, at = here.at(ring)
        return (
            pltpu.make_async_remote_copy(
                grads_ref.at[at, group * CORES + 1 - c], theirs.at[ring], core_send.at[ring], core_recv.at[ring],
                device_id=sibling, device_id_type=MESH,
            ),
            pltpu.make_async_remote_copy(
                small_ref.at[at, group * CORES + 1 - c], small_theirs.at[ring], score_send.at[ring], score_recv.at[ring],
                device_id=sibling, device_id_type=MESH,
            ),
        )

    def fetch(ring):
        group, at = here.at(ring)
        return (
            pltpu.make_async_copy(grads_ref.at[at, group * CORES + c], own.at[ring], own_sem.at[ring]),
            pltpu.make_async_copy(small_ref.at[at, group * CORES + c], small_own.at[ring], sown_sem.at[ring]),
        )

    def behind(step):
        return lax.rem(here.ring - step + chips, chips)

    def order(k):
        off = (2 * lax.rem(k, 2) - 1) * (k // 2 + 1) * (1 - k // (chips - 1))
        return lax.rem(here.ring + chips + off, chips)

    @pl.loop(0, chips)
    def _(k):
        for copy in across(order(k)) + fetch(order(k)):
            copy.start()

    rows, columns = out_ref.shape
    parts = halves(rows, columns)

    def add(ring, part, step, last):
        height = parts[part][0].size
        piece = 16 if height % 16 == 0 else height

        @pl.loop(0, height // piece)
        def _(k):
            at = pl.ds(pl.multiple_of(parts[part][0].start + k * piece, 8), piece)
            where = (at, parts[part][1])
            value = own[(ring,) + where].astype(F32) + theirs[(ring,) + where].astype(F32)
            if step is not None:
                value = value + taken[(step,) + where].astype(F32)
            if last:
                total[where] = value
            else:
                own[(ring,) + where] = value.astype(BF16)

    def onward(ring, step, part):
        where = (parts[part][0], parts[part][1])
        return pltpu.make_async_remote_copy(
            own.at[(ring,) + where], taken.at[(step,) + where], ring_send.at[part, step], ring_recv.at[part, step],
            device_id=to_left if part else to_right, device_id_type=MESH,
        )

    def small_onward(ring, step):
        return pltpu.make_async_remote_copy(
            small_own.at[ring], small_taken.at[step], sring_send.at[step], sring_recv.at[step],
            device_id=to_right, device_id_type=MESH,
        )

    def ready(ring):
        for copy in across(ring):
            copy.wait_recv()
        for copy in fetch(ring):
            copy.wait()

    def ahead(step):
        return lax.rem(here.ring + step, chips)

    half_chips = chips // 2

    @pl.loop(0, chips - 1)
    def _(step):
        right, left = behind(step + 1), ahead(step + 1)

        @pl.when(step < half_chips)
        def _():
            ready(right)

        @pl.when(step < chips - 1 - half_chips)
        def _():
            ready(left)

        @pl.when(step == 0)
        def _():
            add(right, 0, None, False)
            add(left, 1, None, False)
            small_own[right] = small_own[right] + small_theirs[right]

        @pl.when(step > 0)
        def _():
            onward(right, step - 1, 0).wait_recv()
            add(right, 0, step - 1, False)
            onward(right, step, 0).start()
            onward(left, step - 1, 1).wait_recv()
            add(left, 1, step - 1, False)
            onward(left, step, 1).start()
            small_onward(right, step - 1).wait_recv()
            small_own[right] = small_own[right] + small_theirs[right] + small_taken[step - 1]
            small_onward(right, step).start()

        @pl.when(step == 0)
        def _():
            onward(right, 0, 0).start()
            onward(left, 0, 1).start()
            small_onward(right, 0).start()

    ready(here.ring)
    for part in range(2):
        onward(here.ring, chips - 2, part).wait_recv()
        add(here.ring, part, chips - 2, True)
    small_onward(here.ring, chips - 2).wait_recv()
    small_out[...] = small_own[here.ring] + small_theirs[here.ring] + small_taken[chips - 2]
    finish = pltpu.make_async_copy(total, out_ref, local_sem.at[0])
    finish.start()

    @pl.loop(0, chips)
    def _(step):
        @pl.when(step < chips - 1)
        def _():
            onward(behind(step + 1), step, 0).wait_send()
            onward(ahead(step + 1), step, 1).wait_send()
            small_onward(behind(step + 1), step).wait_send()

        for copy in across(step):
            copy.wait_send()

    for k in range(tensor):
        stays, inside, away = home(k)

        @pl.when(jnp.logical_not(stays))
        def _():
            away().wait_send()

    for i in range(nrow):
        for which in range(2):
            pltpu.make_async_copy(rows_ref.at[0], rows_out.at[i, which], block_recv.at[i, which]).wait()
    finish.wait()


def scatter(tensor, dp, grads, small, rows, nrow):
    chips = tensor * dp // CORES
    shard = grads.shape[2:]
    tiny = small.shape[2:]
    sems = pltpu.SemaphoreType.DMA
    return pl.pallas_call(
        functools.partial(scatter_kernel, tensor, dp),
        out_shape=(
            jax.ShapeDtypeStruct(shard, F32),
            jax.ShapeDtypeStruct(tiny, F32),
            jax.ShapeDtypeStruct((nrow, 2) + rows.shape[1:], rows.dtype),
        ),
        in_specs=[ANY] * 3,
        out_specs=(ANY, VMEM, ANY),
        scratch_shapes=[
            pltpu.VMEM((chips,) + shard, BF16),
            pltpu.VMEM((chips,) + shard, BF16),
            pltpu.VMEM((chips - 1,) + shard, BF16),
            pltpu.VMEM((chips,) + tiny, F32),
            pltpu.VMEM((chips,) + tiny, F32),
            pltpu.VMEM((chips - 1,) + tiny, F32),
            pltpu.VMEM(shard, F32),
            sems((chips,)), sems((chips,)), sems((chips,)), sems((2, chips)), sems((2, chips)),
            sems((chips,)), sems((chips,)), sems((chips,)), sems((chips,)), sems((chips,)),
            sems((tensor,)), sems((nrow, 2)), sems((1,)),
        ],
        compiler_params=pltpu.CompilerParams(collective_id=1, has_side_effects=True, vmem_limit_bytes=VMEM_LIMIT),
        name="scatter",
    )(grads, small, rows)


KEY, VALUE, QUERY, OUT, FIRST, SECOND = range(6)
ATTN, CROSS, INNER, OUTER = range(4)
SEGS_HELD = 6


def rms(value):
    return lax.rsqrt(jnp.mean(value * value, axis=-1, keepdims=True) + EPSILON)


def in_rows(count, body, piece=128):
    @pl.loop(0, count // piece)
    def _(k):
        body(pl.ds(pl.multiple_of(k * piece, piece), piece))


def columns_of(count, body, piece=768):
    piece = min(piece, count)

    @pl.loop(0, count // piece)
    def _(k):
        body(pl.ds(pl.multiple_of(k * piece, piece), piece))


def normalize(source, gain, target, count):
    def body(at):
        value = source[at, :].astype(F32)
        target[at, :] = (value * rms(value) * gain).astype(BF16)

    in_rows(count, body)


def normalize_back(source, gain, incoming, total, gain_parts, count, fresh):
    gain_parts[...] = jnp.zeros_like(gain_parts)

    def body(at):
        value, back = source[at, :].astype(F32), incoming[at, :]
        scale = rms(value)
        unit = value * scale
        gain_parts[...] += jnp.sum((back * unit).reshape(-1, 8, back.shape[-1]), axis=0)
        back = back * gain
        back = scale * (back - unit * jnp.mean(back * unit, axis=-1, keepdims=True))
        total[at, :] = back if fresh else total[at, :] + back

    in_rows(count, body)


def project(left, weight, target, count):
    def body(at):
        target[0:count, at] = nn(left[0:count, :], weight[:, at]).astype(target.dtype)

    columns_of(weight.shape[1], body)


def project_back(left, weight, total, count, fresh):
    def body(at):
        value = nt(left[0:count, :], weight[at, :])
        total[0:count, at] = value if fresh else total[0:count, at] + value

    columns_of(weight.shape[0], body)


def to_bf16(source, target, rows):
    def body(at):
        target[at, :] = source[at, :].astype(BF16)

    in_rows(rows, body)


def turn(left, turned, rows):
    def body(at):
        turned[at, 0:rows] = left[0:rows, at].T

    columns_of(left.shape[1], body, LANES)


def lane_half(shape, part):
    return lax.broadcasted_iota(jnp.int32, shape, 1) // HEAD_DIM == part


def attend(keys, values, queries, mixture, probs, rows, span, pairs, mask, bias, after, unroll=1):
    @pl.loop(0, pairs, unroll=unroll)
    def _(pair):
        lanes = pl.ds(pl.multiple_of(pair * LANES, LANES), LANES)
        key, query = keys[0:span, lanes], queries[0:rows, lanes]
        value_t = values[0:span, lanes].T
        mixed = []
        for part in range(2):
            one = jnp.where(lane_half(query.shape, part), query, jnp.zeros_like(query))
            scores = nt(key, one) + mask[0:span, 0:rows]
            if bias is not None:
                scores = scores + bias(2 * pair + part)
            scores = jnp.exp(scores - jnp.max(scores, axis=0, keepdims=True))
            scores = (scores * (1.0 / jnp.sum(scores, axis=0, keepdims=True))).astype(BF16)
            probs[2 * pair + part, 0:span, 0:rows] = scores
            mixed.append(nn(value_t[part * HEAD_DIM : (part + 1) * HEAD_DIM, :], scores))
        mixture[0:rows, lanes] = jnp.concatenate(mixed, axis=0).T.astype(BF16)
        after(pair)


def attend_back(keys, values, queries, back, probs, rows, span, pairs, each, before, after):
    @pl.loop(0, pairs)
    def _(pair):
        before(pair)
        lanes = pl.ds(pl.multiple_of(pair * LANES, LANES), LANES)
        key, value = keys[0:span, lanes], values[0:span, lanes]
        query, given = queries[0:rows, lanes], back[0:rows, lanes]
        key_t = key.T
        d_key, d_value, d_query = None, None, []
        for part in range(2):
            side = lane_half(query.shape, part)
            query_one = jnp.where(side, query, jnp.zeros_like(query))
            given_one = jnp.where(side, given, jnp.zeros_like(given))
            prob = probs[2 * pair + part, 0:span, 0:rows]
            wide = prob.astype(F32)
            d_prob = nt(value, given_one)
            d_score = (wide * (d_prob - jnp.sum(wide * d_prob, axis=0, keepdims=True))).astype(BF16)
            if each is not None:
                each(2 * pair + part, d_score)
            of_key, of_value = nn(d_score, query_one), nn(prob, given_one)
            d_key = of_key if d_key is None else d_key + of_key
            d_value = of_value if d_value is None else d_value + of_value
            d_query.append(nn(key_t[part * HEAD_DIM : (part + 1) * HEAD_DIM, :], d_score))
        keys[0:span, lanes] = d_key.astype(BF16)
        values[0:span, lanes] = d_value.astype(BF16)
        queries[0:rows, lanes] = jnp.concatenate(d_query, axis=0).T.astype(BF16)
        after(pair)


def segments(lengths_row, shape, axis, first):
    lane = lax.broadcasted_iota(jnp.int32, lengths_row.shape, 1)
    places = lax.broadcasted_iota(jnp.int32, shape, axis) + first
    ids = jnp.zeros(shape, jnp.int32)
    for c in range(SEGS_HELD):
        bound = jnp.sum(jnp.where(lane <= c, lengths_row, 0), axis=1, keepdims=True)
        ids = ids + (places >= bound).astype(jnp.int32)
    return ids


def masked(allowed):
    return jnp.where(allowed, 0.0, NEGATIVE).astype(F32)


def nothing(*unused, **named):
    pass


def work(r, here, supply, drain, tensor, heads_at):
    c, t = here.core, here.t
    width = r.hidden.shape[1]
    tall = r.hidden.shape[0]
    block = width // tensor
    half_width = width // 2
    units = r.inner.shape[2]
    places = r.x.shape[2]
    sibling = here.sibling()
    across = [{"pipe": 1 - here.pipe, "dp": here.group * CORES + k} for k in range(CORES)]
    nrow = tensor // CORES
    rows_e, span_e, rows_d, span_d = tall // 2, tall, tall // 4, tall // 2
    pairs_here = half_width // LANES
    near_lanes = pl.ds(pl.multiple_of(c * half_width, half_width), half_width)
    far_lanes = pl.ds(pl.multiple_of((1 - c) * half_width, half_width), half_width)
    lane_halves = [slice(k * half_width, (k + 1) * half_width) for k in range(CORES)]

    def move(source, target, sends, recvs, device):
        return pltpu.make_async_remote_copy(
            source, target, r.send_sem.at[sends], r.recv_sem.at[recvs], device_id=device, device_id_type=MESH
        )

    def lengths_row(first):
        return r.lengths[t // nrow, pl.ds(first + lax.rem(t, nrow), 1), :]

    def pair_lanes(pair):
        return pl.ds(pair * LANES if isinstance(pair, int) else pl.multiple_of(pair * LANES, LANES), LANES)

    def vector_row(head):
        return (head // heads_at) * 8 + lax.rem(head, heads_at)

    def bias_vectors():
        enc, dec = r.enc_buckets.shape[1], r.dec_buckets.shape[1]
        r.buckets[...] = jnp.zeros_like(r.buckets)

        @pl.when(here.pipe == 0)
        def _():
            r.buckets[0:1, 0:enc] = r.enc_buckets[...]

        @pl.when(here.pipe == 1)
        def _():
            r.buckets[0:1, dec - 1 : 2 * dec - 1] = r.dec_buckets[...]

        buckets = lax.broadcasted_iota(jnp.int32, r.onehot.shape, 0) == r.buckets[0:1, :]
        r.onehot[...] = buckets.astype(F32)
        for tt in range(tensor):
            r.vectors[pl.ds(8 * tt, 8), :] = lax.dot_general(
                r.tables[tt][:, 0 : r.onehot.shape[0]], r.onehot[...], (((1,), (0,)), ((), ())),
                precision=lax.Precision.HIGHEST, preferred_element_type=F32,
            )

    def rows_ready(span, rows, first_block):
        @pl.loop(0, span // places)
        def _(k):
            value = r.x[k // tensor, lax.rem(k, tensor)].astype(F32)
            at = pl.ds(pl.multiple_of(k * places, places), places)
            r.hidden[at, :] = (value * rms(value) * r.gains[0]).astype(BF16)

        for k in range(rows // places):
            r.own_x[k * places : (k + 1) * places, :] = r.x[first_block // tensor, lax.rem(first_block, tensor) + k]

    def untangle(source, first, count):
        def body(at):
            for tt in range(tensor):
                for k in range(count):
                    r.square[first + k, at, tt * block : (tt + 1) * block] = source[tt, at, k * block : (k + 1) * block]

        in_rows(width, body, 128)

    def self_forward(span, rows, first_row, group):
        def bias(head):
            pieces = []
            for j in range(span // LANES):
                start = pl.multiple_of(first_row + span - LANES - j * LANES, LANES)
                row = r.vectors[pl.ds(vector_row(head), 1), pl.ds(start, rows + LANES)]
                wide = jnp.broadcast_to(row, (LANES, rows + LANES))
                pieces.append(pltpu.roll(wide, rows + 1, 1, stride=1, stride_axis=0)[:, 0:rows])
            return jnp.concatenate(pieces, axis=0)

        untangle(r.raw_a, KEY, 2)
        untangle(r.raw_a.at[:, :, pl.ds(2 * block, 2 * block)], QUERY, 2)
        project(r.hidden, r.square.at[KEY], r.keys, span)
        supply.pump()
        project(r.hidden, r.square.at[VALUE], r.values, span)
        project(r.hidden.at[pl.ds(first_row, rows)], r.square.at[QUERY], r.queries, rows)
        supply.pump()
        after = at_each(range(width // LANES), supply.pump)

        attend(r.keys, r.values, r.queries, r.mixture, r.probs, rows, span, width // LANES, r.mask, bias, after)
        project_back(r.mixture, r.square.at[OUT], r.resid_mid, rows, True)

        def add(at):
            r.resid_mid[at, :] += r.own_x[at, :].astype(F32)

        in_rows(rows, add)
        supply.pump(until=group)
        supply.finish(group)

    def at_each(places, do):
        def hook(n):
            for place in places:

                @pl.when(n == place)
                def _():
                    do()

        return hook

    def feed_forward(rows, hook=nothing):
        @pl.loop(0, tensor)
        def _(tt):
            def body(at):
                value = nn(r.second[0:rows, :], r.inner[tt, :, at])
                cdf = 0.5 * (1.0 + lax.erf(value * 0.7071067811865476))
                r.ff[tt, 0:rows, at] = (value * cdf).astype(BF16)
                slope = cdf + value * jnp.exp(-0.5 * value * value) * 0.3989422804014327
                r.ff[tensor + tt, 0:rows, at] = slope.astype(BF16)

            columns_of(units, body)
            hook(tt)

    def feed_out(target, rows, hook=nothing):
        @pl.loop(0, tensor)
        def _(tt):
            def body(at):
                target[0:rows, at] += nt(r.ff[tt, 0:rows, :], r.outer[tt, at, :])

            columns_of(width, body)
            hook(tt)

    def feed_back(rows, ready, hook=nothing):
        r.summed[0:rows, :] = jnp.zeros((rows, width), F32)

        @pl.loop(0, tensor)
        def _(tt):
            def body(at):
                if ready:
                    value = r.ff[tensor + tt, rows : 2 * rows, at].astype(F32)
                else:
                    value = nn(r.d_branch[0:rows, :], r.outer[tt, :, at])
                r.ff[tensor + tt, 0:rows, at] = (value * r.ff[tensor + tt, 0:rows, at].astype(F32)).astype(BF16)

            columns_of(units, body)

            def back(at):
                r.summed[0:rows, at] += nt(r.ff[tensor + tt, 0:rows, :], r.inner[tt, at, :])

            columns_of(width, back)
            hook(tt)

    def feed_grads(rows, turned, first, which, hook=nothing):
        @pl.loop(0, tensor)
        def _(tt):
            slot = lax.rem(tt, 2)

            @pl.when(tt >= 2)
            def _():
                drain.release(which, tt - 2, slot)

            def body(at):
                r.stage[slot, :, at] = nn(turned[:, 0:rows], r.ff[first + tt, 0:rows, at]).astype(BF16)

            columns_of(units, body)
            drain.emit(which, tt, slot)
            hook(tt)

        for tt in range(tensor - 2, tensor):
            drain.release(which, tt, tt % 2)

    def square_grads(rows, which, products, hook):
        wide = len(products) * block
        apart = tensor // 2 * wide <= r.stage.shape[2]
        for k in range(tensor // 2):
            place = k if apart else 0
            for j, (turned, right) in enumerate(products):

                def body(at):
                    value = nn(turned[at, 0:rows], right[0:rows, 2 * k * block : 2 * (k + 1) * block]).astype(BF16)
                    for slot in range(2):
                        first = place * wide + j * block
                        r.stage[slot, at, first : first + block] = value[:, slot * block : (slot + 1) * block]

                in_rows(width, body, 256)
            for slot in range(2):
                drain.emit(which, 2 * k + slot, slot, place)
            hook(k)
            if not apart:
                for slot in range(2):
                    drain.release(which, 2 * k + slot, slot)
        if apart:
            for k in range(tensor // 2):
                for slot in range(2):
                    drain.release(which, 2 * k + slot, slot, k)

    def gain_done(which):
        r.gains_out[which : which + 1, :] = jnp.sum(r.gain_parts[...], axis=0, keepdims=True)

    def self_backward(span, rows, first_row, steps, send_rows):
        mirror = (
            lax.broadcasted_iota(jnp.int32, (LANES, LANES), 0) + lax.broadcasted_iota(jnp.int32, (LANES, LANES), 1)
            == LANES - 1
        ).astype(BF16)
        to_bf16(r.d_resid, r.branch, rows)
        project(r.branch, r.square.at[OUT], r.d_branch, rows)
        r.diagonals[...] = jnp.zeros_like(r.diagonals)

        def each(head, d_score):
            for j in range(span // LANES):
                start = pl.multiple_of(first_row + span - LANES - j * LANES, LANES)
                piece = nn(mirror, d_score[j * LANES : (j + 1) * LANES, :])
                piece = jnp.concatenate([piece, jnp.zeros((LANES, LANES), F32)], axis=1)
                piece = pltpu.roll(piece, 0, 1, stride=1, stride_axis=0)
                at = (pl.ds(vector_row(head), 1), pl.ds(start, rows + LANES))
                r.diagonals[at] += jnp.sum(piece, axis=0, keepdims=True)

        pairs = width // LANES
        attend_back(
            r.keys, r.values, r.queries, r.d_branch, r.probs, rows, span, pairs, each, nothing,
            at_each(range(pairs), steps),
        )
        far = pl.ds(pl.multiple_of((1 - c) * rows, rows), rows)
        near = pl.ds(pl.multiple_of(c * rows, rows), rows)
        trades = [
            move(source.at[far], r.taken_pair.at[k, pl.ds(0, rows)], 12 + k, 12 + k, sibling)
            for k, source in enumerate((r.keys, r.values))
        ]
        for trade in trades:
            trade.start()
        steps()
        turn(r.branch, r.turned, rows)
        turn(r.hidden.at[pl.ds(first_row, rows)], r.turned_more, rows)
        for tt in range(tensor):
            at = pl.ds(8 * tt, 8)
            r.bias_out[at, 0 : r.onehot.shape[0]] = lax.dot_general(
                r.diagonals[at, :], r.onehot[...], (((1,), (1,)), ((), ())),
                precision=lax.Precision.HIGHEST, preferred_element_type=F32,
            )
        steps()
        project_back(r.queries, r.square.at[QUERY], r.summed, rows, True)
        for trade in trades:
            trade.wait_recv()
        steps()
        for k, source in enumerate((r.keys, r.values)):
            r.d_pair[k, 0:rows, :] = (source[near, :].astype(F32) + r.taken_pair[k, 0:rows, :].astype(F32)).astype(BF16)
        project_back(r.d_pair.at[0], r.square.at[KEY], r.summed, rows, False)
        project_back(r.d_pair.at[1], r.square.at[VALUE], r.summed, rows, False)
        steps()
        normalize_back(r.own_x, r.gains[0], r.summed, r.d_resid, r.gain_parts, rows, False)
        gain_done(0)
        steps()
        send_rows()
        drain.small_begin()
        drain.allow(2)
        products = [(r.turned_more, r.d_pair.at[0]), (r.turned_more, r.d_pair.at[1]), (r.turned_more, r.queries), (r.turned, r.mixture)]
        square_grads(rows, ATTN, products, nothing)
        for trade in trades:
            trade.wait_send()
        steps()
        drain.begin(ATTN)
        steps()
        drain.rest(ATTN)

    def parts_of(array):
        return [array.at[pl.ds(k * rows_d, rows_d)] for k in range(CORES)]

    def part_here(array):
        return array.at[pl.ds(pl.multiple_of(c * rows_d, rows_d), rows_d)]

    r.gains_out[...] = jnp.zeros_like(r.gains_out)
    r.bias_out[...] = jnp.zeros_like(r.bias_out)
    supply.start()

    def entry():
        supply.pump(2)
        supply.small()
        bias_vectors()
        supply.pump(2)
        supply.rows()

    def schedule(*items):
        left = list(items)

        def steps():
            for name, group, *n in left.pop(0) if left else ():
                getattr(drain, name)(group, *n)

        return steps

    @pl.when(here.pipe == 0)
    def _():
        supply.resume(ATTN, INNER, OUTER, CROSS)
        drain.order(CROSS, OUTER, INNER, ATTN)
        entry()
        rows, span = rows_e, span_e
        first_row = pl.multiple_of(c * rows, rows)
        seg_rows = segments(lengths_row(0), (span, 1), 0, 0)
        r.mask[...] = masked(seg_rows == segments(lengths_row(0), (1, rows), 1, first_row))
        supply.pump()
        rows_ready(span, rows, c * tensor)
        supply.pump(until=ATTN)
        supply.finish(ATTN)
        self_forward(span, rows, first_row, INNER)
        normalize(r.resid_mid, r.gains[1], r.second, rows)
        feed_forward(rows, at_each((1, 2, 3), supply.pump))
        supply.pump(until=OUTER)
        supply.finish(OUTER)
        r.resid_top[...] = r.resid_mid[...]
        feed_out(r.resid_top, rows, at_each((1, 2, 3), supply.pump))
        normalize(r.resid_top, r.gains[2], r.third, rows)
        r.mask[...] = masked(seg_rows == segments(lengths_row(nrow), (1, span_d), 1, 0))
        supply.pump(until=CROSS)
        supply.finish(CROSS)
        untangle(r.raw_c, FIRST, 2)
        mine = pl.ds(first_row, rows)
        other = pl.ds(pl.multiple_of((1 - c) * rows, rows), rows)
        trades = []
        for k, held in enumerate((r.cross_keys, r.cross_values)):
            r.send_pair[k] = nn(r.third[...], r.square[FIRST + k, :, far_lanes]).astype(BF16)
            trades.append(move(r.send_pair.at[k], held.at[mine], k, k, sibling))
            trades[-1].start()
        for k, held in enumerate((r.cross_keys, r.cross_values)):
            held[mine, :] = nn(r.third[...], r.square[FIRST + k, :, near_lanes]).astype(BF16)
        for k, part in enumerate(parts_of(r.cross_queries)):
            move(part, part, 2 + k, 2 + k, across[k]).wait_recv()
        for k, held in enumerate((r.cross_keys, r.cross_values)):
            move(r.send_pair.at[k], held.at[other], k, k, sibling).wait_recv()

        def mixtures(pair):
            at = pair_lanes(pair)
            return [
                pltpu.make_async_remote_copy(
                    r.cross_mixture.at[pl.ds(k * rows_d, rows_d), at], r.cross_in.at[c, :, at],
                    r.mix_send.at[k, pair], r.mix_recv.at[c, pair], device_id=across[k], device_id_type=MESH,
                )
                for k in range(CORES)
            ]

        def arrived(pair):
            for k in range(CORES):
                part = r.cross_back.at[pl.ds(k * rows_d, rows_d), pair_lanes(pair)]
                pltpu.make_async_remote_copy(
                    part, part, r.back_send.at[k, pair], r.back_recv.at[k, pair], device_id=across[k], device_id_type=MESH
                ).wait_recv()

        def returns(pair):
            at = pair_lanes(pair)
            return [
                pltpu.make_async_remote_copy(
                    d_cross.at[other, at], r.cross_taken.at[k, :, at],
                    r.give_send.at[k, pair], r.give_recv.at[k, pair], device_id=sibling, device_id_type=MESH,
                )
                for k, d_cross in enumerate((r.cross_keys, r.cross_values))
            ]

        attend(
            r.cross_keys, r.cross_values, r.cross_queries, r.cross_mixture, r.cross_probs, span_d, span, pairs_here,
            r.mask, None, lambda pair: [mix.start() for mix in mixtures(pair)], pairs_here,
        )
        supply.close()
        drain.free(0)
        turn(r.third, r.turned, rows)
        attend_back(
            r.cross_keys, r.cross_values, r.cross_queries, r.cross_back, r.cross_probs, span_d, span, pairs_here, None,
            arrived, lambda pair: [back.start() for back in returns(pair)],
        )
        answers = [
            move(part, r.cross_in_back.at[c], 8 + k, 8 + c, across[k]) for k, part in enumerate(parts_of(r.cross_queries))
        ]
        for answer in answers:
            answer.start()
        for k, d_cross in enumerate((r.cross_keys, r.cross_values)):
            r.d_pair[k, :, near_lanes] = d_cross[mine, :]
        for pair in range(pairs_here):
            for back in returns(pair):
                back.wait_recv()
        for k in range(2):
            r.d_pair[k, :, far_lanes] = r.cross_taken[k]
        drain.allow(0)
        square_grads(rows, CROSS, [(r.turned, r.d_pair.at[0]), (r.turned, r.d_pair.at[1])], nothing)
        drain.begin(CROSS)
        project_back(r.d_pair.at[0], r.square.at[FIRST], r.summed, rows, True)
        project_back(r.d_pair.at[1], r.square.at[SECOND], r.summed, rows, False)
        normalize_back(r.resid_top, r.gains[2], r.summed, r.d_resid, r.gain_parts, rows, True)
        gain_done(2)
        to_bf16(r.d_resid, r.d_branch, rows)
        turn(r.d_branch, r.turned, rows)
        feed_grads(rows, r.turned, 0, OUTER, at_each((2,), lambda: drain.tick(CROSS, 0)))
        drain.tick(CROSS, 1)
        drain.begin(OUTER)
        feed_back(rows, False, at_each((1, 2), schedule([("tick", CROSS, 2)], [("tick", CROSS, 3)])))
        drain.free(1)
        drain.free(2)
        turn(r.second, r.turned, rows)
        drain.allow(1)
        feed_grads(rows, r.turned, tensor, INNER, at_each((1,), lambda: drain.tick(OUTER, 0)))
        normalize_back(r.resid_mid, r.gains[1], r.summed, r.d_resid, r.gain_parts, rows, False)
        gain_done(1)
        for copy in trades + answers:
            copy.wait_send()
        for pair in range(pairs_here):
            for copy in mixtures(pair) + returns(pair):
                copy.wait_send()

        def send_rows():
            to_bf16(r.d_resid, r.rows_out, rows)
            drain.home()

        steps = schedule(
            [("tick", CROSS, 4), ("begin", INNER)], [("tick", OUTER, 1)],
            [], [("end", CROSS)], [], [("tick", OUTER, 2)],
            [("tick", INNER, 0)], [], [("tick", INNER, 1)], [], [("tick", OUTER, 3)], [("tick", OUTER, 4)],
            [("tick", INNER, 2), ("tick", ATTN, 0), ("end", OUTER), ("tick", INNER, 3), ("tick", ATTN, 1), ("tick", ATTN, 2)]
            + [("home_done", None), ("tick", INNER, 4), ("tick", ATTN, 3), ("tick", ATTN, 4), ("end", INNER)],
        )
        self_backward(span, rows, first_row, steps, send_rows)

    @pl.when(here.pipe == 1)
    def _():
        supply.resume(ATTN, CROSS, INNER, OUTER)
        drain.order(OUTER, INNER, CROSS, ATTN)
        entry()
        rows, span = rows_d, span_d
        first_row = pl.multiple_of(c * rows, rows)
        key_at = lax.broadcasted_iota(jnp.int32, (span, rows), 0)
        query_at = lax.broadcasted_iota(jnp.int32, (span, rows), 1) + first_row
        same = segments(lengths_row(nrow), (span, 1), 0, 0) == segments(lengths_row(nrow), (1, rows), 1, first_row)
        r.mask[0:span, 0:rows] = masked(same & (query_at >= key_at))
        supply.pump()
        first_block = c * (tensor // 2)
        rows_ready(span, rows, first_block)
        for k in range(rows // places):
            r.d_branch[k * places : (k + 1) * places, :] = r.x[1, first_block + k]
        supply.pump(until=ATTN)
        supply.finish(ATTN)
        self_forward(span, rows, first_row, CROSS)
        untangle(r.raw_c, FIRST, 2)
        normalize(r.resid_mid, r.gains[1], r.third, rows)
        project(r.third, r.square.at[FIRST], r.joined, rows)
        asks = []
        for k in range(CORES):
            r.send_pair[k, 0:rows, :] = r.joined[:, lane_halves[k]]
            asks.append(move(r.send_pair.at[k, pl.ds(0, rows)], part_here(r.cross_queries), 2 + k, 2 + c, across[k]))
            asks[-1].start()
        supply.pump(until=INNER)
        supply.finish(INNER)
        supply.pump(until=OUTER)
        supply.finish(OUTER)

        @pl.loop(0, tensor)
        def _(tt):
            def body(at):
                r.ff[tensor + tt, rows : 2 * rows, at] = nn(r.d_branch[0:rows, :], r.outer[tt, :, at]).astype(BF16)

            columns_of(units, body)

        supply.close()
        drain.free(0)
        r.resid_top[0:rows, :] = r.resid_mid[0:rows, :]
        for k in range(CORES):
            for pair in range(pairs_here):
                part = r.cross_in.at[k, :, pair_lanes(pair)]
                pltpu.make_async_remote_copy(
                    part, part, r.mix_send.at[k, pair], r.mix_recv.at[k, pair], device_id=across[k], device_id_type=MESH
                ).wait_recv()
            r.joined[:, lane_halves[k]] = r.cross_in[k]
        project_back(r.joined, r.square.at[SECOND], r.resid_top, rows, False)
        normalize(r.resid_top, r.gains[2], r.second, rows)
        feed_forward(rows)
        feed_back(rows, True)
        r.d_resid[0:rows, :] = r.d_branch[0:rows, :].astype(F32)
        normalize_back(r.resid_top, r.gains[2], r.summed, r.d_resid, r.gain_parts, rows, False)
        gain_done(2)
        to_bf16(r.d_resid, r.branch, rows)
        tells = []
        for pair in range(pairs_here):
            at = pair_lanes(pair)
            firsts = [k * half_width + pair * LANES for k in range(CORES)]
            both = jnp.concatenate([r.square[SECOND, :, first : first + LANES] for first in firsts], axis=1)
            value = nn(r.branch[0:rows, :], both).astype(BF16)
            for k in range(CORES):
                r.send_back[k, :, at] = value[:, k * LANES : (k + 1) * LANES]
                tells.append(
                    pltpu.make_async_remote_copy(
                        r.send_back.at[k, :, at], r.cross_back.at[pl.ds(pl.multiple_of(c * rows, rows), rows), at],
                        r.back_send.at[k, pair], r.back_recv.at[c, pair], device_id=across[k], device_id_type=MESH,
                    )
                )
                tells[-1].start()
        drain.free(1)
        turn(r.d_branch, r.turned, rows)
        drain.allow(0)
        feed_grads(rows, r.turned, 0, OUTER)
        drain.begin(OUTER)
        turn(r.second, r.turned, rows)
        drain.allow(1)
        feed_grads(rows, r.turned, tensor, INNER)
        drain.begin(INNER)
        feed_out(r.resid_top, rows, at_each((1,), lambda: drain.tick(OUTER, 0)))
        drain.free(2)
        to_bf16(r.resid_top, r.rows_out, rows)
        turn(r.branch, r.turned, rows)
        turn(r.third, r.turned_more, rows)
        for k in range(CORES):
            move(r.cross_in_back.at[k], r.cross_in_back.at[k], 8 + k, 8 + k, across[k]).wait_recv()
            r.d_pair[1, 0:rows, lane_halves[k]] = r.cross_in_back[k]
        project_back(r.d_pair.at[1], r.square.at[FIRST], r.summed, rows, True)
        square_grads(rows, CROSS, [(r.turned_more, r.d_pair.at[1]), (r.turned, r.joined)], nothing)
        drain.tick(OUTER, 1)
        normalize_back(r.resid_mid, r.gains[1], r.summed, r.d_resid, r.gain_parts, rows, False)
        gain_done(1)
        for copy in asks + tells:
            copy.wait_send()

        def send_rows():
            to_bf16(r.d_resid, r.rows_out.at[pl.ds(rows, rows)], rows)
            drain.home()

        steps = schedule(
            [], [("tick", INNER, 0)], [], [("tick", INNER, 1)], [("tick", OUTER, 2)], [],
            [("tick", OUTER, 3)], [], [("tick", INNER, 2), ("tick", OUTER, 4)], [("begin", CROSS)],
            [("tick", INNER, 3), ("tick", INNER, 4)], [],
            [("end", OUTER), ("tick", CROSS, 0), ("tick", ATTN, 0), ("tick", CROSS, 1), ("end", INNER), ("tick", ATTN, 1)]
            + [("tick", ATTN, 2), ("tick", CROSS, 2), ("home_done", None), ("tick", ATTN, 3), ("tick", ATTN, 4)]
            + [("tick", CROSS, 3), ("tick", CROSS, 4), ("end", CROSS)],
        )
        self_backward(span, rows, first_row, steps, send_rows)

    drain.close()


def held(*shape, dtype=BF16):
    return pltpu.VMEM(shape, dtype)


def arrays(tensor, heads_at, places, width, units, ranges, kinds):
    tall = 2 * tensor * places
    block = width // tensor
    half_rows, half_width = tall // 2, width // 2
    heads = heads_at * tensor
    return dict(
        x=held(2, tensor, places, width),
        own_x=held(half_rows, width),
        raw_a=held(tensor, width, 4 * block),
        raw_c=held(tensor, width, 2 * block),
        square=held(6, width, width),
        inner=held(tensor, width, units),
        outer=held(tensor, width, units),
        hidden=held(tall, width),
        keys=held(tall, width),
        values=held(tall, width),
        queries=held(half_rows, width),
        probs=held(heads, tall, half_rows),
        mask=held(tall, half_rows, dtype=F32),
        mixture=held(half_rows, width),
        resid_mid=held(half_rows, width, dtype=F32),
        resid_top=held(half_rows, width, dtype=F32),
        d_resid=held(half_rows, width, dtype=F32),
        summed=held(half_rows, width, dtype=F32),
        second=held(half_rows, width),
        third=held(half_rows, width),
        ff=held(2 * tensor, half_rows, units),
        d_branch=held(half_rows, width),
        branch=held(half_rows, width),
        cross_keys=held(tall, half_width),
        cross_values=held(tall, half_width),
        cross_queries=held(half_rows, half_width),
        cross_mixture=held(half_rows, half_width),
        cross_probs=held(heads // CORES, tall, half_rows),
        cross_back=held(half_rows, half_width),
        cross_in=held(CORES, half_rows // 2, half_width),
        cross_in_back=held(CORES, half_rows // 2, half_width),
        cross_taken=held(CORES, half_rows, half_width),
        send_pair=held(CORES, half_rows, half_width),
        send_back=held(CORES, half_rows // 2, half_width),
        joined=held(half_rows // 2, width),
        taken_pair=held(2, half_rows, width),
        d_pair=held(2, half_rows, width),
        turned=held(width, half_rows),
        turned_more=held(width, half_rows),
        stage=held(2, width, units),
        vectors=held(8 * tensor, ranges, dtype=F32),
        diagonals=held(8 * tensor, ranges, dtype=F32),
        onehot=held(kinds, ranges, dtype=F32),
        buckets=held(8, ranges, dtype=jnp.int32),
        gain_parts=held(8, width, dtype=F32),
        send_sem=pltpu.SemaphoreType.DMA((14,)),
        recv_sem=pltpu.SemaphoreType.DMA((14,)),
        **{
            name: pltpu.SemaphoreType.DMA((CORES, half_width // LANES))
            for name in ("mix_send", "mix_recv", "back_send", "back_recv", "give_send", "give_recv")
        },
    )


def group_columns(block, units):
    return {ATTN: (0, 4 * block), CROSS: (4 * block, 2 * block), INNER: (6 * block, units), OUTER: (6 * block + units, units)}


def landing(r):
    return {ATTN: r.raw_a, CROSS: r.raw_c, INNER: r.inner, OUTER: r.outer}


class Loads:
    def __init__(self, r, tensor, x_hbm, w_hbm, sems):
        columns = group_columns(r.raw_a.shape[2] // 4, r.inner.shape[2])
        self.x = pltpu.make_async_copy(x_hbm, r.x, sems.at[4, 0])
        self.weights = [
            [
                pltpu.make_async_copy(w_hbm.at[tt, :, pl.ds(*columns[group])], target.at[tt], sems.at[group, tt])
                for tt in range(tensor)
            ]
            for group, target in landing(r).items()
        ]

    def start(self):
        self.x.start()
        for group in self.weights:
            for copy in group:
                copy.start()

    def rows(self):
        self.x.wait()

    def finish(self, group):
        for copy in self.weights[group]:
            copy.wait()

    small = resume = pump = close = nothing


class Stores:
    def __init__(self, r, grads_hbm, sems):
        self.columns = group_columns(r.raw_a.shape[2] // 4, r.inner.shape[2])
        self.r, self.grads, self.sems = r, grads_hbm, sems

    def copy(self, group, tt, slot, place):
        first, wide = self.columns[group]
        return pltpu.make_async_copy(
            self.r.stage.at[slot, :, pl.ds(place * wide, wide)], self.grads.at[tt, :, pl.ds(first, wide)],
            self.sems.at[slot + 2 * place],
        )

    def emit(self, group, tt, slot, place=0):
        self.copy(group, tt, slot, place).start()

    def release(self, group, tt, slot, place=0):
        self.copy(group, tt, slot, place).wait()

    order = free = allow = begin = tick = rest = end = home = home_done = small_begin = close = nothing


def blocks_kernel(tensor, dp, heads_at, names, *refs):
    here = Place(tensor, dp)
    r = types.SimpleNamespace(**dict(zip(names, refs)))
    across = [{"pipe": 1 - here.pipe, "dp": here.group * CORES + k} for k in range(CORES)]
    meet([here.sibling()] + across)
    work(r, here, Loads(r, tensor, r.x_hbm, r.w_hbm, r.load_sem), Stores(r, r.grads_hbm, r.stage_sem), tensor, heads_at)


def blocks(tensor, dp, heads_at, kinds, rows, weights, gains, lengths, tables, buckets):
    places, width = rows.shape[2:]
    units = (weights.shape[2] - 6 * (width // tensor)) // 2
    half_rows = tensor * places
    ranges = -(-buckets[0].shape[1] // LANES) * LANES
    scratch = arrays(tensor, heads_at, places, width, units, ranges, kinds)
    scratch["load_sem"] = pltpu.SemaphoreType.DMA((5, tensor))
    scratch["stage_sem"] = pltpu.SemaphoreType.DMA((4,))
    names = ["x_hbm", "w_hbm", "gains", "lengths", "tables", "enc_buckets", "dec_buckets", "grads_hbm", "rows_out", "gains_out", "bias_out"]
    return pl.pallas_call(
        functools.partial(blocks_kernel, tensor, dp, heads_at, names + list(scratch)),
        out_shape=(
            jax.ShapeDtypeStruct(weights.shape, BF16),
            jax.ShapeDtypeStruct((half_rows, width), BF16),
            jax.ShapeDtypeStruct((8, width), F32),
            jax.ShapeDtypeStruct((8 * tensor, LANES), F32),
        ),
        in_specs=[ANY, ANY] + [VMEM] * 5,
        out_specs=(ANY, VMEM, VMEM, VMEM),
        scratch_shapes=list(scratch.values()),
        compiler_params=pltpu.CompilerParams(collective_id=2, has_side_effects=True, vmem_limit_bytes=VMEM_LIMIT),
        name="blocks",
    )(rows, weights, gains, lengths, tables, *buckets)


def all_sends(r, box, group, depth, hops, targets):
    for part in range(2):
        sent = box.at[0, pl.ds(0, (2 * hops - 1) * depth // 2), :]
        pltpu.make_async_remote_copy(
            sent, sent, r.ring_send.at[group, part], r.ring_recv.at[group, part, 0, 0],
            device_id=targets[part], device_id_type=MESH,
        ).wait_send()


def all_over(r, box, group, here, depth):
    whole = box.at[pl.ds(0, here.chips * depth // box.shape[1])]
    return pltpu.make_async_remote_copy(
        whole, whole, r.over_send.at[group], r.over_recv.at[group], device_id=here.sibling(), device_id_type=MESH
    )


class Rings:
    def __init__(self, r, here, tensor, dp):
        self.r, self.here, self.tensor, self.dp = r, here, tensor, dp
        self.depth = r.value_w.shape[0]
        self.hops = here.chips // 2
        self.count = 2 * self.hops - 1
        self.sibling = here.sibling()
        self.targets = [here.neighbour(1), here.neighbour(-1)]
        self.landing = landing(r)
        self.groups = []
        self.plan = []


    def order(self, *groups):
        steps = []
        for k, group in enumerate(groups):
            steps.append((4 * k - 0.5, k, self.begin, group, None))
            late = {self.count - 3: 3.6, self.count - 2: 3.7, self.count - 1: 5.5}
            steps += [(4 * k + late.get(n, n), k, self.tick, group, n) for n in range(self.count)]
        steps.sort(key=lambda step: step[:2])
        self.groups = list(groups)
        self.plan = [step[2:] for step in steps]

    def resume(self, *groups):
        self.order(*groups)
        self.plan.pop(0)

    def pump(self, count=1, until=None):
        while self.plan and (count > 0 if until is None else any(step[1] == until for step in self.plan)):
            do, group, n = self.plan.pop(0)
            do(group) if n is None else do(group, n)
            count -= 0 if n is None else 1


    def block_out(self, i):
        r, t, c = self.r, self.here.t, self.here.core
        return pltpu.make_async_remote_copy(
            r.rows.at[i], r.x.at[:, t], r.block_send.at[i], r.block_recv.at[t],
            device_id={"tensor": r.rows.shape[0] * c + i}, device_id_type=MESH,
        )

    def block_kept(self, i):
        return pltpu.make_async_copy(self.r.rows.at[i], self.r.x.at[:, self.here.t], self.r.local_sem.at[0])

    def block_pass(self, source, s):
        r = self.r
        return pltpu.make_async_remote_copy(
            source, r.x.at[:, s], r.pass_send.at[s], r.pass_recv.at[s], device_id=self.sibling, device_id_type=MESH
        )

    def blocks(self, mine, others):
        for i in range(self.r.rows.shape[0]):
            here = self.r.rows.shape[0] * self.here.core + i == self.here.t

            @pl.when(here)
            def _():
                mine(i)

            @pl.when(jnp.logical_not(here))
            def _():
                others(i)

    def small_copies(self):
        r, t = self.r, self.here.t
        copies = [
            pltpu.make_async_remote_copy(
                r.lengths_in, r.lengths.at[self.here.core], r.small_send.at[0], r.small_recv.at[0],
                device_id=self.sibling, device_id_type=MESH,
            ),
            pltpu.make_async_copy(r.lengths_in, r.lengths.at[self.here.core], r.local_sem.at[1]),
            pltpu.make_async_copy(r.table_in, r.tables.at[t], r.local_sem.at[2]),
        ]
        for k in range(1, self.tensor):
            copies.append(
                pltpu.make_async_remote_copy(
                    r.table_in, r.tables.at[t], r.small_send.at[k], r.small_recv.at[k],
                    device_id={"tensor": lax.rem(t + k, self.tensor)}, device_id_type=MESH,
                )
            )
        return copies


    def rows_of(self, ring):
        line, at = self.here.at(ring)
        return at, pl.multiple_of((line * CORES + self.here.core) * self.depth, 16)

    def ring_at(self, step, part):
        way = -1 if part else 1
        return lax.rem(self.here.ring - way * step + self.here.chips, self.here.chips)

    def onward(self, group, step, part, sub):
        r, half = self.r, self.depth // 2
        at, first = self.rows_of(self.ring_at(step, part))
        target = self.landing[group]
        slot = target.at[at, pl.ds(pl.multiple_of(first + half * sub, 16), half), :]
        packed = r.stage.at[0, pl.ds(group * self.depth + half * sub, half), pl.ds(0, target.shape[2])]
        return pltpu.make_async_remote_copy(
            packed if step == 0 else slot, slot, r.ring_send.at[group, part], r.ring_recv.at[group, part, sub, step],
            device_id=self.targets[part], device_id_type=MESH,
        )

    def over(self, group, ring, first_time=False):
        r = self.r
        at, first = self.rows_of(ring)
        target = self.landing[group]
        slot = target.at[at, pl.ds(first, self.depth), :]
        packed = r.stage.at[0, pl.ds(group * self.depth, self.depth), pl.ds(0, target.shape[2])]
        return pltpu.make_async_remote_copy(
            packed if first_time else slot, slot, r.over_send.at[group], r.over_recv.at[group],
            device_id=self.sibling, device_id_type=MESH,
        )

    def own(self, group):
        wide = self.landing[group].shape[2]
        first = pl.multiple_of(self.here.d * self.depth, 16)
        return pltpu.make_async_copy(
            self.r.stage.at[0, pl.ds(group * self.depth, self.depth), pl.ds(0, wide)],
            self.landing[group].at[self.here.t, pl.ds(first, self.depth), :],
            self.r.own_sem.at[group],
        )

    def begin(self, group):
        for sub in range(2):
            for part in range(2):
                self.onward(group, 0, part, sub).start()
        self.over(group, self.here.ring, True).start()
        self.own(group).start()

    def tick(self, group, n):
        step, last = n // 2 + 1, n == self.count - 1
        for part in range(2):
            sub = part if last else n % 2
            self.onward(group, step - 1, part, sub).wait_recv()
            if not last and (step < self.hops - 1 or sub == part):
                self.onward(group, step, part, sub).start()
        if last:
            self.over(group, self.ring_at(step, 0)).start()
        elif n % 2:
            for part in range(2):
                self.over(group, self.ring_at(step, part)).start()

    def sends_done(self, group):
        all_sends(self.r, self.landing[group], group, self.depth, self.hops, self.targets)

    def finish(self, group):
        all_over(self.r, self.landing[group], group, self.here, self.depth).wait_recv()
        self.own(group).wait()

    def start(self):
        r, depth = self.r, self.depth
        block = r.value_w.shape[1]

        def band(group, pieces):
            wide = pieces[0].shape[1]
            for k, piece in enumerate(pieces):
                r.stage[0, group * depth : (group + 1) * depth, k * wide : (k + 1) * wide] = piece

        band(ATTN, [r.query_key_w[1], r.value_w[...], r.query_key_w[0], r.out_w[...].T])
        self.order(ATTN)
        self.begin(ATTN)
        nrow = r.rows.shape[0]
        r.lengths_in[...] = jnp.zeros_like(r.lengths_in)
        r.lengths_in[0:nrow, 0 : r.enc_lengths.shape[1]] = r.enc_lengths[...]
        r.lengths_in[nrow : 2 * nrow, 0 : r.dec_lengths.shape[1]] = r.dec_lengths[...]
        r.table_in[...] = jnp.zeros_like(r.table_in)
        for k in range(r.bias_w.shape[0]):
            r.table_in[k : k + 1, 0 : r.bias_w.shape[2]] = r.bias_w[k]
        self.blocks(
            lambda i: (self.block_kept(i).start(), self.block_pass(r.rows.at[i], self.here.t).start()),
            lambda i: self.block_out(i).start(),
        )
        for copy in self.small_copies():
            copy.start()
        band(INNER, [r.inner_w[...]])
        band(OUTER, [r.outer_w[...]])
        band(CROSS, [r.first_w[...], r.second_w[...]])

    def small(self):
        for copy in self.small_copies():
            copy.wait()

    def rows(self):
        r, t = self.r, self.here.t
        takes = lax.div(t, r.rows.shape[0]) == self.here.core
        for s in range(self.tensor):

            @pl.when(jnp.logical_and(takes, s != t))
            def _():
                pltpu.make_async_remote_copy(
                    r.rows.at[0], r.x.at[:, s], r.block_send.at[0], r.block_recv.at[s],
                    device_id=self.sibling, device_id_type=MESH,
                ).wait_recv()
                self.block_pass(r.x.at[:, s], s).start()

        self.blocks(lambda i: self.block_kept(i).wait(), nothing)
        for s in range(self.tensor):

            @pl.when(jnp.logical_not(takes))
            def _():
                self.block_pass(r.x.at[:, s], s).wait_recv()

    def close(self):
        r, t = self.r, self.here.t
        takes = lax.div(t, r.rows.shape[0]) == self.here.core
        self.blocks(
            lambda i: self.block_pass(r.rows.at[i], t).wait_send(),
            lambda i: self.block_out(i).wait_send(),
        )
        for s in range(self.tensor):

            @pl.when(jnp.logical_and(takes, s != t))
            def _():
                self.block_pass(r.x.at[:, s], s).wait_send()

        for group in self.groups:
            self.sends_done(group)
            all_over(r, self.landing[group], group, self.here, self.depth).wait_send()


class Sums:
    def __init__(self, r, here, tensor, dp):
        self.r, self.here, self.tensor, self.dp = r, here, tensor, dp
        self.depth = r.value_w.shape[0]
        self.hops = here.chips // 2
        self.count = 2 * self.hops - 3
        self.sibling = here.sibling()
        self.targets = [here.neighbour(1), here.neighbour(-1)]
        self.box = {CROSS: r.raw_c, OUTER: r.raw_a, INNER: r.inner, ATTN: r.outer}
        self.kept = {CROSS: r.own_cross, OUTER: r.own_outer, INNER: r.own_inner, ATTN: r.ff}
        self.groups = []

    def order(self, *groups):
        self.groups = list(groups)

    def free(self, k):
        for device in self.targets + [self.sibling]:
            pl.semaphore_signal(self.r.free_sem.at[k], inc=1, device_id=device, device_id_type=MESH)

    def allow(self, k):
        pl.semaphore_wait(self.r.free_sem.at[k], 3)

    def boxed(self, group, index, first, height):
        if isinstance(index, int):
            return (index // self.dp, pl.ds(pl.multiple_of(index % self.dp * self.depth + first, 16), height), slice(None))
        at = pl.ds(pl.multiple_of(lax.rem(index, self.dp) * self.depth + first, 16), height)
        return (lax.div(index, self.dp), at, slice(None))

    def taken(self, group, step, part, first, height):
        index = step + part * (self.hops - 1) if step else 0
        return self.boxed(group, index, first, height)

    def theirs(self, group, ring, first, height):
        return self.boxed(group, self.here.chips - 1 + ring, first, height)

    def own(self, group, ring, first, height):
        return (ring, pl.ds(first, height), slice(None))

    def ring_of(self, line, at):
        return line * self.tensor + at + (line % 2) * (self.tensor - 1 - 2 * at)

    def pieces(self, group, tt, slot, place=0):
        r, depth = self.r, self.depth
        wide = self.box[group].shape[2]
        sem = slot + 2 * place
        made = []
        for line in range(self.here.groups):
            ring = self.ring_of(line, tt)

            def rows_of(core):
                return r.stage.at[slot, pl.ds(pl.multiple_of((line * CORES + core) * depth, 16), depth), pl.ds(place * wide, wide)]

            made.append(
                pltpu.make_async_copy(
                    rows_of(self.here.core), self.kept[group].at[self.own(group, ring, 0, depth)], r.kept_sem.at[sem, line]
                )
            )
            made.append(
                pltpu.make_async_remote_copy(
                    rows_of(1 - self.here.core), self.box[group].at[self.theirs(group, ring, 0, depth)],
                    r.pair_send.at[sem, line], r.over_recv.at[group], device_id=self.sibling, device_id_type=MESH,
                )
            )
        return made

    def emit(self, group, tt, slot, place=0):
        for piece in self.pieces(group, tt, slot, place):
            piece.start()

    def release(self, group, tt, slot, place=0):
        for k, piece in enumerate(self.pieces(group, tt, slot, place)):
            if k % 2:
                piece.wait_send()
            else:
                piece.wait()


    def rows_at(self, sub):
        half = self.depth // 2
        return half * sub, half

    def source(self, step, part):
        way = -1 if part else 1
        return lax.rem(self.here.ring + way * (self.hops - step) + self.here.chips, self.here.chips)

    def onward(self, group, step, part, sub):
        r = self.r
        first, height = self.rows_at(sub)
        return pltpu.make_async_remote_copy(
            self.kept[group].at[self.own(group, self.source(step, part), first, height)],
            self.box[group].at[self.taken(group, step, part, first, height)],
            r.ring_send.at[group, part], r.ring_recv.at[group, part, sub, step],
            device_id=self.targets[part], device_id_type=MESH,
        )

    def here_sum(self, group, ring, first, height):
        value = self.kept[group][self.own(group, ring, first, height)].astype(F32)
        return value + self.box[group][self.theirs(group, ring, first, height)].astype(F32)

    def advance(self, group, step, part, sub, fresh=False):
        if not fresh:
            self.onward(group, step - 1, part, sub).wait_recv()
        ring = self.source(step, part)

        def add(first, height):
            value = self.here_sum(group, ring, first, height)
            if not fresh:
                value = value + self.box[group][self.taken(group, step - 1, part, first, height)].astype(F32)
            self.kept[group][self.own(group, ring, first, height)] = value.astype(BF16)

        self.in_pieces(sub, add)
        self.onward(group, step, part, sub).start()

    def in_pieces(self, sub, body):
        start, height = self.rows_at(sub)

        @pl.loop(0, height // 32)
        def _(k):
            body(pl.multiple_of(start + 32 * k, 32), 32)

    def begin(self, group):
        all_over(self.r, self.box[group], group, self.here, self.depth).wait_recv()
        for part in range(2):
            self.advance(group, 0, part, part, True)
        for part in range(2):
            self.advance(group, 1, part, 1 - part, True)
        if group == ATTN:
            self.small_across().wait_recv()
            self.small_advance(0, 0, True)
            self.small_advance(1, 1, True)

    def tick(self, group, n):
        step, leads = (n + 1) // 2 + 1, n % 2
        for part in range(2):
            self.advance(group, step, part, 1 - part if leads else part)
        if group == ATTN and not leads:
            self.small_advance(step, 0)
            if step > 1:
                self.small_advance(step, 1)

    def sends_done(self, group):
        all_sends(self.r, self.box[group], group, self.depth, self.hops, self.targets)

    def rest(self, group):
        self.end(group)
        for group in (ATTN, CROSS, INNER, OUTER):
            self.sends_done(group)

    def end(self, group):
        r, last = self.r, self.hops - 1
        for sub in range(2):
            for part in range(2):
                self.onward(group, last, part, sub).wait_recv()
            target = r.inner_out if group == INNER else r.total

            def add(first, height):
                value = self.here_sum(group, self.here.ring, first, height)
                for part in range(2):
                    value = value + self.box[group][self.taken(group, last, part, first, height)].astype(F32)
                target[pl.ds(first, height), 0 : self.box[group].shape[2]] = value

            self.in_pieces(sub, add)
        block = r.value_w.shape[1]
        done = {ATTN: ("pair_out", "value_out", "out_out", "tiny_out"), CROSS: ("first_out", "second_out")}
        if group == ATTN:
            r.pair_out[1] = r.total[:, 0:block]
            r.value_out[...] = r.total[:, block : 2 * block]
            r.pair_out[0] = r.total[:, 2 * block : 3 * block]
            r.out_out[...] = r.total[:, 3 * block : 4 * block].T
            at = self.small_at(self.here.ring)
            value = r.small[at] + r.small_theirs[at]
            for part in range(2):
                self.small_onward(last, part).wait_recv()
                value = value + r.small_taken[part, last]
            r.tiny_out[...] = value
        if group == CROSS:
            r.first_out[...] = r.total[:, 0:block]
            r.second_out[...] = r.total[:, block : 2 * block]
        if group == OUTER:
            r.outer_out[...] = r.total[...]
        for name in done.get(group, ("inner_out",) if group == INNER else ("outer_out",)):
            self.result(name).start()

    def result(self, name):
        r = self.r
        return pltpu.make_async_copy(getattr(r, name), getattr(r, name + "_hbm"), r.result_sem.at[r.results.index(name)])


    def small_at(self, ring):
        line, at = self.here.at(ring)
        return at, line * CORES + self.here.core

    def small_across(self):
        r = self.r
        return pltpu.make_async_remote_copy(
            r.small, r.small_theirs, r.small_sem.at[0], r.small_sem.at[1], device_id=self.sibling, device_id_type=MESH
        )

    def small_onward(self, step, part):
        r = self.r
        return pltpu.make_async_remote_copy(
            r.small_sent.at[part, step], r.small_taken.at[part, step], r.tiny_send.at[part, step], r.tiny_recv.at[part, step],
            device_id=self.targets[part], device_id_type=MESH,
        )

    def small_advance(self, step, part, fresh=False):
        at = self.small_at(self.source(step, part))
        value = self.r.small[at] + self.r.small_theirs[at]
        if not fresh:
            self.small_onward(step - 1, part).wait_recv()
            value = value + self.r.small_taken[part, step - 1]
        self.r.small_sent[part, step] = value
        self.small_onward(step, part).start()

    def small_begin(self):
        r, depth = self.r, self.depth
        r.small[...] = jnp.zeros_like(r.small)
        kinds = r.onehot.shape[0] // self.dp
        heads_at = self.heads_at
        for tt in range(self.tensor):
            for d in range(self.dp):
                r.small[tt, d, 0:3, 0:depth] = r.gains_out[0:3, d * depth : (d + 1) * depth]
                r.small[tt, d, 3 : 3 + heads_at, 0:kinds] = r.bias_out[
                    8 * tt : 8 * tt + heads_at, d * kinds : (d + 1) * kinds
                ]
        self.small_across().start()


    def home_copy(self, k):
        r, here, tensor = self.r, self.here, self.tensor
        nrow, half, places = r.home_in.shape[0], tensor // 2, r.home_in.shape[2]
        place = here.pipe * (here.core * half + k % half) + (1 - here.pipe) * k
        which = here.pipe * (k // half) + (1 - here.pipe) * here.core
        owner = lax.div(here.t, nrow)
        source = r.rows_out.at[pl.ds(k * places, places)]
        slot = r.home_in.at[lax.rem(here.t, nrow), which]
        recv = r.home_recv.at[lax.rem(here.t, nrow), which]
        return (
            jnp.logical_and(place == here.t, owner == here.core),
            lambda: pltpu.make_async_copy(source, slot, recv),
            lambda: pltpu.make_async_remote_copy(
                source, slot, r.home_send.at[k], recv,
                device_id={"dp": here.group * CORES + owner, "tensor": place}, device_id_type=MESH,
            ),
        )

    def home(self):
        for k in range(self.tensor):
            stays, inside, away = self.home_copy(k)

            @pl.when(stays)
            def _():
                inside().start()

            @pl.when(jnp.logical_not(stays))
            def _():
                away().start()

    def home_done(self, unused=None):
        r = self.r
        places = r.home_in.shape[2]
        for i in range(r.home_in.shape[0]):
            for which in range(2):
                pltpu.make_async_copy(
                    r.rows_out.at[pl.ds(0, places)], r.home_in.at[i, which], r.home_recv.at[i, which]
                ).wait()
                r.home_out[i, which] = r.home_in[i, which].astype(F32)
        self.result("home_out").start()

    def close(self):
        r = self.r
        for k in range(self.tensor):
            stays, inside, away = self.home_copy(k)

            @pl.when(jnp.logical_not(stays))
            def _():
                away().wait_send()

        for name in r.results:
            self.result(name).wait()
        self.small_across().wait_send()

        for part in range(2):
            for step in range(part, self.hops):
                self.small_onward(step, part).wait_send()


def fits_fused(tensor, dp, depth, units, width):
    chips = tensor * dp // CORES
    return (
        depth % 32 == 0
        and 4 * depth <= width
        and chips <= 2 * tensor
        and chips == 2 * tensor == 8
        and chips * depth == 2 * width
        and units == width == 6 * LANES
    )


def fused_kernel(tensor, dp, heads_at, results, names, *refs):
    here = Place(tensor, dp)
    r = types.SimpleNamespace(**dict(zip(names, refs)))
    line = [
        {"dp": here.group * CORES + lax.rem(here.core + j, CORES), "tensor": lax.rem(here.t + k, tensor)}
        for j in range(CORES)
        for k in range(tensor)
        if j + k > 0
    ]
    across = [{"pipe": 1 - here.pipe, "dp": here.group * CORES + k} for k in range(CORES)]
    r.results = results
    given = [name for name in names if name + "_hbm" in names and name not in results]
    copies = [
        pltpu.make_async_copy(getattr(r, name + "_hbm"), getattr(r, name), r.given_sem.at[k]) for k, name in enumerate(given)
    ]
    for copy in copies:
        copy.start()
    meet([here.neighbour(1), here.neighbour(-1)] + line + across)
    for copy in copies:
        copy.wait()
    supply, drain = Rings(r, here, tensor, dp), Sums(r, here, tensor, dp)
    drain.heads_at = heads_at
    work(r, here, supply, drain, tensor, heads_at)


def fused(tensor, dp, rows, enc_lengths, dec_lengths, gains, bias, buckets, weights):
    nrow, two, places, width = rows.shape
    depth, block = weights[1].shape
    units = weights[5].shape[1]
    heads_at, _, kinds = bias.shape
    chips = tensor * dp // CORES
    wide = -(-max(depth, kinds // dp) // LANES) * LANES
    sems = pltpu.SemaphoreType.DMA
    ranges = -(-buckets[0].shape[1] // LANES) * LANES
    scratch = arrays(tensor, heads_at, places, width, units, ranges, kinds)
    given = dict(enc_lengths=enc_lengths, dec_lengths=dec_lengths, gains=gains, bias_w=bias)
    given.update(enc_buckets=buckets[0], dec_buckets=buckets[1])
    names = ("query_key_w", "value_w", "out_w", "first_w", "second_w", "inner_w", "outer_w")
    given.update(zip(names, weights))
    scratch.update({name: pltpu.VMEM(array.shape, array.dtype) for name, array in given.items()})
    scratch.update(
        lengths_in=held(8, LANES, dtype=jnp.int32),
        table_in=held(8, LANES, dtype=F32),
        lengths=held(CORES, 8, LANES, dtype=jnp.int32),
        tables=held(tensor, 8, LANES, dtype=F32),
        own_cross=held(chips, depth, 2 * block),
        own_outer=held(chips, depth, units),
        own_inner=held(chips, depth, units),
        total=held(depth, units, dtype=F32),
        rows_out=held(tensor * places, width),
        gains_out=held(8, width, dtype=F32),
        bias_out=held(8 * tensor, LANES, dtype=F32),
        home_in=held(nrow, two, places, width),
        small=held(tensor, dp, 8, wide, dtype=F32),
        small_theirs=held(tensor, dp, 8, wide, dtype=F32),
        small_sent=held(2, chips // 2, 8, wide, dtype=F32),
        small_taken=held(2, chips // 2, 8, wide, dtype=F32),
        block_send=sems((nrow,)), block_recv=sems((tensor,)), pass_send=sems((tensor,)), pass_recv=sems((tensor,)),
        local_sem=sems((3,)), small_send=sems((tensor,)), small_recv=sems((tensor,)), own_sem=sems((4,)),
        ring_send=sems((4, 2)), ring_recv=sems((4, 2, 2, chips // 2)),
        over_send=sems((4,)), over_recv=sems((4,)), kept_sem=sems((4, dp // CORES)), pair_send=sems((4, dp // CORES)),
        small_sem=sems((2,)), tiny_send=sems((2, chips // 2)), tiny_recv=sems((2, chips // 2)),
        home_send=sems((tensor,)), home_recv=sems((nrow, two)),
        free_sem=pltpu.SemaphoreType.REGULAR((3,)), given_sem=sems((len(given),)),
    )
    inputs = ["rows"] + [name + "_hbm" for name in given]
    outputs = dict(
        home_out=rows.shape, tiny_out=(8, wide), pair_out=(2, depth, block), value_out=(depth, block),
        out_out=(block, depth), first_out=(depth, block), second_out=(depth, block), inner_out=(depth, units),
        outer_out=(depth, units),
    )
    scratch.update({name: held(*shape, dtype=F32) for name, shape in outputs.items()})
    scratch["result_sem"] = sems((len(outputs),))
    return pl.pallas_call(
        functools.partial(fused_kernel, tensor, dp, heads_at, list(outputs), inputs + [name + "_hbm" for name in outputs] + list(scratch)),
        out_shape=tuple(jax.ShapeDtypeStruct(shape, F32) for shape in outputs.values()),
        in_specs=[ANY] * (1 + len(given)),
        out_specs=(ANY,) * len(outputs),
        scratch_shapes=list(scratch.values()),
        compiler_params=pltpu.CompilerParams(collective_id=3, has_side_effects=True, vmem_limit_bytes=VMEM_LIMIT),
        name="fused",
    )(rows, *given.values())


def pad_to(array, *shape):
    return jnp.pad(array, [(0, full - have) for full, have in zip(shape, array.shape)])


def shards(
    tensor, dp, section_rows, enc_lengths, dec_lengths, enc_buckets, dec_buckets, norm_gains, rel_bias,
    query_key_w, value_w, attn_out_w, cross_first, cross_second, ff_in, ff_out,
):
    depth = value_w.shape[1]
    width = section_rows.shape[-1]
    buckets = (enc_buckets[None], dec_buckets[None])
    gains = norm_gains.transpose(1, 0, 2)
    bias = rel_bias.transpose(2, 0, 1)
    weights = (query_key_w[0], value_w[0], attn_out_w[0], cross_first[0], cross_second[0], ff_in[0], ff_out[0].T)
    run = fused if fits_fused(tensor, dp, depth, ff_in.shape[2], width) else in_three
    home, tiny, *grads = run(tensor, dp, section_rows[0], enc_lengths, dec_lengths, gains, bias, buckets, weights)
    gain, kind, home, *grads, outer = copied(depth, bias.shape[0], bias.shape[2] // dp, tiny, home, *grads)
    return (
        (home[None], gain.transpose(1, 0, 2), kind.transpose(1, 2, 0))
        + tuple(grad[None] for grad in grads)
        + (outer.T[None],)
    )


def copied(depth, heads_at, kinds, tiny, *results):
    count = len(results)

    def kernel(*refs):
        sources, refs = refs[: count + 1], refs[count + 1 :]
        targets, refs = refs[: count + 2], refs[count + 2 :]
        held_here, (tiny_ref, in_sem, out_sem) = refs[: count + 2], refs[count + 2 :]
        ins = [
            pltpu.make_async_copy(source, there, in_sem.at[k])
            for k, (source, there) in enumerate(zip(sources, (tiny_ref,) + tuple(held_here[2:])))
        ]
        outs = [pltpu.make_async_copy(there, target, out_sem.at[k]) for k, (there, target) in enumerate(zip(held_here, targets))]
        for copy in ins:
            copy.start()
        for copy, out in zip(ins[1:], outs[2:]):
            copy.wait()
            out.start()
        ins[0].wait()
        for k in range(3):
            held_here[0][k] = tiny_ref[k : k + 1, 0:depth]
        for k in range(heads_at):
            held_here[1][k] = tiny_ref[3 + k : 4 + k, 0:kinds]
        outs[0].start()
        outs[1].start()
        for out in outs:
            out.wait()

    shapes = [(3, 1, depth), (heads_at, 1, kinds)] + [result.shape for result in results]
    sems = pltpu.SemaphoreType.DMA
    return pl.pallas_call(
        kernel,
        out_shape=tuple(jax.ShapeDtypeStruct(shape, F32) for shape in shapes),
        in_specs=[ANY] * (count + 1),
        out_specs=(ANY,) * (count + 2),
        scratch_shapes=[held(*shape, dtype=F32) for shape in shapes + [tiny.shape]] + [sems((count + 1,)), sems((count + 2,))],
        compiler_params=pltpu.CompilerParams(vmem_limit_bytes=VMEM_LIMIT),
        name="copied",
    )(tiny, *results)


def in_three(tensor, dp, section_rows, enc_lengths, dec_lengths, gains, bias, buckets, weights):
    query_key, value, out, first, second, inner, outer = weights
    nrow, _, _, width = section_rows.shape
    heads_at, _, kinds = bias.shape
    lengths = pad_to(jnp.concatenate([enc_lengths, dec_lengths], axis=0), 8, LANES)
    table = pad_to(bias[:, 0], 8, LANES)
    depth, block = value.shape
    units = inner.shape[1]
    pack = jnp.concatenate([query_key[1], value, query_key[0], out.T, first, second, inner, outer], axis=1)
    rows, gathered, lengths, tables = gather(tensor, dp, section_rows, pack, lengths, table)
    grads, finished, gain_grads, bias = blocks(
        tensor, dp, heads_at, kinds, rows, gathered.reshape(tensor, width, -1), gains, lengths, tables, buckets
    )
    held_kinds = kinds // dp
    wide = -(-max(depth, held_kinds) // LANES) * LANES
    gain_part = pad_to(gain_grads[:3].reshape(3, dp, depth).transpose(1, 0, 2), dp, 3, wide)
    bias_part = bias.reshape(tensor, 8, LANES)[:, :heads_at, :kinds].reshape(tensor, heads_at, dp, held_kinds)
    bias_part = pad_to(bias_part.transpose(0, 2, 1, 3), tensor, dp, 5, wide)
    small = jnp.concatenate([jnp.broadcast_to(gain_part[None], (tensor,) + gain_part.shape), bias_part], axis=2)
    total, tiny, home = scatter(
        tensor, dp, grads.reshape(tensor, dp, depth, -1), small, finished.reshape(tensor, -1, width), nrow
    )
    key, value, query, out, first, second = [total[:, k * block : (k + 1) * block] for k in range(6)]
    inner, outer = total[:, 6 * block : 6 * block + units], total[:, 6 * block + units :]
    return (
        home.astype(F32), tiny,
        jnp.stack([query, key]), value, out.T, first, second, inner, outer,
    )


def solution(mesh):
    sizes = dict(mesh.shape)
    return jax.shard_map(
        functools.partial(shards, sizes["tensor"], sizes["dp"]),
        mesh=mesh,
        in_specs=(
            P("pipe", "dp", None, "tensor", None),
            P("dp", None),
            P("dp", None),
            P(),
            P(),
            P("pipe", None, None),
            P("pipe", None, "tensor"),
            P("pipe", None, "dp", "tensor"),
            P("pipe", "dp", "tensor"),
            P("pipe", "tensor", "dp"),
            P("pipe", "dp", "tensor"),
            P("pipe", "dp", "tensor"),
            P("pipe", "dp", "tensor"),
            P("pipe", "tensor", "dp"),
        ),
        out_specs=(
            P("pipe", "dp", None, "tensor", None),
            P("pipe", None, "dp"),
            P("pipe", "dp", "tensor"),
            P("pipe", None, "dp", "tensor"),
            P("pipe", "dp", "tensor"),
            P("pipe", "tensor", "dp"),
            P("pipe", "dp", "tensor"),
            P("pipe", "dp", "tensor"),
            P("pipe", "dp", "tensor"),
            P("pipe", "tensor", "dp"),
        ),
        check_vma=False,
    )
```
